32 devices in a mesh: dp: 8 (over y, x, core), tp: 4 (over z).
Axes of the slice: x: 2, y: 2, z: 4, core: 2. Of those that a mesh axis runs over, the one named last changes fastest.
Arguments:
- tokens: bfloat16 [8192, 1536], P(('dp', 'tp')), may hold values from -6 to 6
- out_grad: bfloat16 [8192, 1536], P(('dp', 'tp')), may hold values from -6 to 6
- segment_ids: int32 [8192], replicated, may hold values from 0 to 3, never falling along the last dimension, each value on 1 to 4096 neighbouring positions
- attn_gain: bfloat16 [1536], replicated, may hold values from 0.5 to 1.5
- query_weight: bfloat16 [1536, 1536], P(None, 'tp'), may hold values from -0.15625 to 0.15625
- key_matrix: bfloat16 [1536, 768], P(None, 'tp'), may hold values from -0.15625 to 0.15625
- value_matrix: bfloat16 [1536, 768], P(None, 'tp'), may hold values from -0.15625 to 0.15625
- output_weight: bfloat16 [1536, 1536], P('tp'), may hold values from -2.5 to 2.5
- mlp_gain: bfloat16 [1536], replicated, may hold values from 0.5 to 1.5
- gate_weight: bfloat16 [1536, 4096], P(None, 'tp'), may hold values from -0.15625 to 0.15625
- up_weight: bfloat16 [1536, 4096], P(None, 'tp'), may hold values from -0.15625 to 0.15625
- down_weight: bfloat16 [4096, 1536], P('tp'), may hold values from -0.09375 to 0.09375
Outputs:
- output: bfloat16 [8192, 1536], P(('dp', 'tp'))
- input_grad: float32 [8192, 1536], P(('dp', 'tp'))
- attn_gain_grad: float32 [1536], P('dp')
- query_weight_grad: float32 [1536, 1536], P('dp', 'tp')
- key_weight_grad: float32 [1536, 768], P('dp', 'tp')
- value_weight_grad: float32 [1536, 768], P('dp', 'tp')
- output_weight_grad: float32 [1536, 1536], P('tp', 'dp')
- mlp_gain_grad: float32 [1536], P('dp')
- gate_weight_grad: float32 [1536, 4096], P('dp', 'tp')
- up_weight_grad: float32 [1536, 4096], P('dp', 'tp')
- down_weight_grad: float32 [4096, 1536], P('tp', 'dp')
The draws below stay inside these ranges and needn't reach their ends.
Inputs may be any that keep to these rules, and one draw needn't show every extreme that they name: segment_ids never fall along the packed batch; every item has 1 to 4096 tokens and the longest has exactly 4096, so the keys of a token lie in its own row or the 4 rows before it.
All inputs are finite; a program needn't handle non-finite values.
Results may differ from the reference program's by a relative error of at most 0.025.
Values may be sent and summed in bfloat16 or wider, within the bound.
A program may use at most 192 MiB of HBM per device.

```python
import math
import jax
import jax.numpy as jnp
import numpy as np
from jax import lax

MODEL_WIDTH = 1536
QUERY_HEAD_COUNT = 16
KEY_VALUE_HEADS = 8
HEAD_WIDTH = 96
FF = 4096
ROW_TOKENS = 1024
SPAN = 4
TOKENS = 8192
MOST_LEN = 4096
SEGS = 4


def level_of(stream_key, dims, pieces, low, largest):
    gain = 1.0
    for dim, parts in pieces:
        steps = jax.random.uniform(jax.random.fold_in(jax.random.fold_in(stream_key, 6), dim), (parts,), jnp.float32, low / len(pieces), largest / len(pieces))
        gain = gain * jnp.repeat(jnp.exp(steps), dims[dim] // parts).reshape((-1,) + (1,) * (len(dims) - 1 - dim))
    return gain


def length_profile(number_of, total, reach, slope):
    loads = [(1 << 20) // math.isqrt(standing ** slope) + 1 for standing in range(2, number_of + 1)]
    surplus, holding = total - reach - (number_of - 1), [1] * (number_of - 1)
    while surplus > 0:
        free = [i for i in range(number_of - 1) if holding[i] < reach]
        mass, budget = sum([loads[i] for i in free]), surplus
        for i in free:
            extra = min(reach - holding[i], max(1, budget * loads[i] // mass), surplus)
            holding[i] = holding[i] + extra
            surplus = surplus - extra
    return np.array([reach] + holding)


def ragged_sizes(own_key, amount, total, limit, slope):
    if amount == 2:
        one = jax.random.randint(own_key, (), max(1, total - limit), min(limit, total - 1) + 1)
        return jnp.stack([one, total - one])
    sizes = jnp.asarray(length_profile(amount, total, limit, slope), jnp.int32)
    pairs = (amount - 1) // 2
    donor, taker = sizes[1:1 + 2 * pairs:2], sizes[2:2 + 2 * pairs:2]
    room = jnp.minimum(donor - 1, limit - taker)
    passed = jax.random.randint(jax.random.fold_in(own_key, 1), (pairs,), 0, 1 << 20) % (room + 1)
    sizes = sizes.at[1:1 + 2 * pairs:2].set(donor - passed).at[2:2 + 2 * pairs:2].set(taker + passed)
    return sizes[jax.random.permutation(jax.random.fold_in(own_key, 2), amount)]


def bell_draw(rng, extent, scale, limit, shards=(), kind=jnp.bfloat16):
    entries = jax.random.normal(rng, extent, jnp.float32) * scale
    if len(shards) > 0:
        entries = level_of(rng, extent, shards, -0.22, 0.18) * entries
    return jnp.clip(entries, min=-limit, max=limit).astype(kind)


def setup_inputs(seed: int = 0) -> dict:
    streams_of = jax.random.split(jax.random.key(seed), 13)
    return {
        "tokens": bell_draw(streams_of[0], (TOKENS, MODEL_WIDTH), 1.0, 6.0, ((0, 32),)),
        "out_grad": bell_draw(streams_of[1], (TOKENS, MODEL_WIDTH), 1.0, 6.0, ((0, 32),)),
        "segment_ids": jnp.searchsorted(jnp.cumsum(ragged_sizes(streams_of[2], SEGS, TOKENS, MOST_LEN, 2)), jnp.arange(TOKENS), side="right").astype(jnp.int32),
        "attn_gain": jnp.clip(1.0 + 0.1 * jax.random.normal(streams_of[3], (MODEL_WIDTH,), jnp.float32), 0.5, 1.5).astype(jnp.bfloat16),
        "query_weight": bell_draw(streams_of[4], (MODEL_WIDTH, QUERY_HEAD_COUNT * HEAD_WIDTH), MODEL_WIDTH ** -0.5, 0.15625, ((1, 4),)),
        "key_matrix": bell_draw(streams_of[5], (MODEL_WIDTH, KEY_VALUE_HEADS * HEAD_WIDTH), MODEL_WIDTH ** -0.5, 0.15625, ((1, 4),)),
        "value_matrix": bell_draw(streams_of[6], (MODEL_WIDTH, KEY_VALUE_HEADS * HEAD_WIDTH), MODEL_WIDTH ** -0.5, 0.15625, ((1, 4),)),
        "output_weight": bell_draw(streams_of[7], (QUERY_HEAD_COUNT * HEAD_WIDTH, MODEL_WIDTH), (max(1, QUERY_HEAD_COUNT * HEAD_WIDTH // 256)) ** -0.5, 2.5, ((0, 4),)),
        "mlp_gain": jnp.clip(1.0 + 0.1 * jax.random.normal(streams_of[8], (MODEL_WIDTH,), jnp.float32), 0.5, 1.5).astype(jnp.bfloat16),
        "gate_weight": bell_draw(streams_of[9], (MODEL_WIDTH, FF), MODEL_WIDTH ** -0.5, 0.15625, ((1, 4),)),
        "up_weight": bell_draw(streams_of[10], (MODEL_WIDTH, FF), MODEL_WIDTH ** -0.5, 0.15625, ((1, 4),)),
        "down_weight": bell_draw(streams_of[11], (FF, MODEL_WIDTH), FF ** -0.5, 0.09375, ((0, 4),)),
    }


@jax.custom_vjp
def lower_bound(v):
    return lax.optimization_barrier(v.astype(jnp.bfloat16)).astype(jnp.float32)

@jax.custom_vjp
def low_back(v):
    return v

def low_keep(v):
    return (lower_bound(v), None)

def low_pass(kept, grad):
    return (grad,)

def back_keep(v):
    return (v, None)

def back_low(kept, grad):
    return (lower_bound(grad),)
lower_bound.defvjp(low_keep, low_pass)
low_back.defvjp(back_keep, back_low)
eps_norm = 1e-05
rope_base = 100000.0
precise = lax.Precision.HIGHEST

def rms_scale(value_vectors, gain_vec):
    return value_vectors * lax.rsqrt(lax.optimization_barrier(jnp.mean(value_vectors * value_vectors, axis=-1, keepdims=True)) + eps_norm) * gain_vec

def rotary_turn(value_vectors, token_positions, heads):
    half_width = HEAD_WIDTH // 2
    inverse = 1.0 / rope_base ** (jnp.arange(half_width, dtype=jnp.float32) * 2.0 / HEAD_WIDTH)
    angles = token_positions.astype(jnp.float32)[:, None] * inverse[None, :]
    cosine = jnp.cos(angles)[:, None, :]
    sine_part = jnp.sin(angles)[:, None, :]
    shaped = value_vectors.reshape(value_vectors.shape[0], heads, HEAD_WIDTH)
    first_half = shaped[..., :half_width]
    second = shaped[..., half_width:]
    turned = jnp.concatenate([first_half * cosine - second * sine_part, second * cosine + first_half * sine_part], axis=-1)
    return turned.reshape(value_vectors.shape)

def swiglu(gate_pre, up_pre):
    return jax.nn.silu(gate_pre) * up_pre

def positions_of(segment_ids):
    token_index = jnp.arange(segment_ids.shape[0], dtype=jnp.int32)
    before = jnp.concatenate([jnp.full((1,), -1, jnp.int32), segment_ids[:-1]])
    starts = jnp.where(segment_ids != before, token_index, 0)
    return token_index - lax.cummax(starts)

def attend(query_vectors, key_vectors, value_vectors, segment_ids):
    totals = query_vectors.shape[0]
    group_width = QUERY_HEAD_COUNT // KEY_VALUE_HEADS
    border_slack = SPAN * ROW_TOKENS
    attend_span = border_slack + ROW_TOKENS
    score_scale = HEAD_WIDTH ** (-0.5)
    keys_padded = jnp.concatenate([jnp.zeros((border_slack, KEY_VALUE_HEADS * HEAD_WIDTH), jnp.float32), key_vectors])
    values_padded = jnp.concatenate([jnp.zeros((border_slack, KEY_VALUE_HEADS * HEAD_WIDTH), jnp.float32), value_vectors])
    segs_pad = jnp.concatenate([jnp.full((border_slack,), -1, jnp.int32), segment_ids])

    def one_row(row_index):
        leading_row = (row_index * ROW_TOKENS).astype(jnp.int32)
        query_row_block = lax.dynamic_slice_in_dim(query_vectors, leading_row, ROW_TOKENS, 0).reshape(ROW_TOKENS, KEY_VALUE_HEADS, group_width, HEAD_WIDTH)
        key_row_block = lax.dynamic_slice_in_dim(keys_padded, leading_row, attend_span, 0).reshape(attend_span, KEY_VALUE_HEADS, HEAD_WIDTH)
        value_row_block = lax.dynamic_slice_in_dim(values_padded, leading_row, attend_span, 0).reshape(attend_span, KEY_VALUE_HEADS, HEAD_WIDTH)
        seg_query = lax.dynamic_slice_in_dim(segment_ids, leading_row, ROW_TOKENS, 0)
        seg_keys = lax.dynamic_slice_in_dim(segs_pad, leading_row, attend_span, 0)
        query_index = leading_row + jnp.arange(ROW_TOKENS, dtype=jnp.int32)
        key_index = leading_row - border_slack + jnp.arange(attend_span, dtype=jnp.int32)
        allowed = (seg_keys[None, :] == seg_query[:, None]) & (key_index[None, :] <= query_index[:, None])

        def one_head(operands):
            query_head, key_head, value_head = operands
            raw_scores = jnp.einsum('qgd,kd->gqk', query_head, key_head, precision=precise)
            scores = jnp.where(allowed[None], low_back(raw_scores * score_scale), -jnp.inf)
            log_total = jnp.log(lax.optimization_barrier(jnp.sum(jnp.exp(scores), axis=-1, keepdims=True)))
            weights = lower_bound(jnp.exp(scores - log_total))
            return jnp.einsum('gqk,kd->qgd', weights, value_head, precision=precise)
        heads_out = lax.map(jax.checkpoint(one_head), (jnp.moveaxis(query_row_block, 1, 0), jnp.moveaxis(key_row_block, 1, 0), jnp.moveaxis(value_row_block, 1, 0)))
        return jnp.moveaxis(heads_out, 0, 1).reshape(ROW_TOKENS, QUERY_HEAD_COUNT * HEAD_WIDTH)
    rows_out = lax.map(jax.checkpoint(one_row), jnp.arange(totals // ROW_TOKENS, dtype=jnp.int32))
    return rows_out.reshape(totals, QUERY_HEAD_COUNT * HEAD_WIDTH)

def reference(tokens, out_grad, segment_ids, attn_gain, query_weight, key_matrix, value_matrix, output_weight, mlp_gain, gate_weight, up_weight, down_weight):
    token_positions = positions_of(segment_ids)

    def block_layer(tokens32, gain_attn, weight_q, weight_k, weight_v, weight_o, gain_mlp, weight_gate, weight_up, weight_down):
        normed = lower_bound(rms_scale(tokens32, gain_attn))
        q_linear = low_back(jnp.dot(normed, weight_q, precision=precise))
        key_linear_out = low_back(jnp.dot(normed, weight_k, precision=precise))
        v_linear = low_back(jnp.dot(normed, weight_v, precision=precise))
        query_vectors = lower_bound(rotary_turn(q_linear, token_positions, QUERY_HEAD_COUNT))
        key_vectors = lower_bound(rotary_turn(key_linear_out, token_positions, KEY_VALUE_HEADS))
        value_vectors = lower_bound(v_linear)
        context = low_back(lower_bound(attend(query_vectors, key_vectors, value_vectors, segment_ids)))
        residual = tokens32 + low_back(jnp.dot(context, weight_o, precision=precise))
        mlp_normed = lower_bound(rms_scale(residual, gain_mlp))
        gate_pre = low_back(jnp.dot(mlp_normed, weight_gate, precision=precise))
        up_pre = low_back(jnp.dot(mlp_normed, weight_up, precision=precise))
        hidden = lower_bound(swiglu(gate_pre, up_pre))
        return residual + low_back(jnp.dot(hidden, weight_down, precision=precise))
    primals = (tokens.astype(jnp.float32), attn_gain.astype(jnp.float32), query_weight.astype(jnp.float32), key_matrix.astype(jnp.float32), value_matrix.astype(jnp.float32), output_weight.astype(jnp.float32), mlp_gain.astype(jnp.float32), gate_weight.astype(jnp.float32), up_weight.astype(jnp.float32), down_weight.astype(jnp.float32))
    output, pullback = jax.vjp(block_layer, *primals)
    gradients = pullback(out_grad.astype(jnp.float32))
    return (output.astype(jnp.bfloat16), gradients[0], gradients[1], gradients[2], gradients[3], gradients[4], gradients[5], gradients[6], gradients[7], gradients[8], gradients[9])
```

```python
import jax
import jax.numpy as jnp
from jax import lax
from jax.sharding import PartitionSpec as P

HEAD_WIDTH = 96


eps_norm = 1e-05
rope_base = 100000.0
reach_limit = 8


def shifted(block, axis, distance):
    devices = range(lax.axis_size(axis))
    route = [(i - distance, i) for i in devices if i - distance in devices]
    return lax.ppermute(block, axis, route)


def rms_scale(value_vectors, gain_vec):
    return (
        value_vectors
        * lax.rsqrt(jnp.mean(value_vectors * value_vectors, axis=-1, keepdims=True) + eps_norm)
        * gain_vec
    )


def rotary_turn(value_vectors, token_positions, heads):
    half_width = HEAD_WIDTH // 2
    inverse = 1.0 / rope_base ** (jnp.arange(half_width, dtype=jnp.float32) * 2.0 / HEAD_WIDTH)
    angles = token_positions.astype(jnp.float32)[:, None] * inverse[None, :]
    cosine = jnp.cos(angles)[:, None, :]
    sine_part = jnp.sin(angles)[:, None, :]
    shaped = value_vectors.reshape(value_vectors.shape[0], heads, HEAD_WIDTH)
    first_half = shaped[..., :half_width]
    second = shaped[..., half_width:]
    turned = jnp.concatenate(
        [first_half * cosine - second * sine_part, second * cosine + first_half * sine_part],
        axis=-1,
    )
    return turned.reshape(value_vectors.shape)


def swiglu(gate_pre, up_pre):
    return jax.nn.silu(gate_pre) * up_pre


def contract_rows(left_side, right_side):
    return lax.dot_general(
        left_side, right_side, (((0,), (0,)), ((), ())), preferred_element_type=jnp.float32
    )


def contract_cols(left_side, right_side):
    return lax.dot_general(
        left_side, right_side, (((1,), (1,)), ((), ())), preferred_element_type=jnp.float32
    )


def local(
    tokens,
    out_grad,
    segment_ids,
    attn_gain,
    query_weight,
    key_matrix,
    value_matrix,
    output_weight,
    mlp_gain,
    gate_weight,
    up_weight,
    down_weight,
):
    floats = jnp.float32
    halves = jnp.bfloat16
    shard_rows = tokens.shape[0]
    row_len = shard_rows * lax.axis_size("tp")
    row_index = lax.axis_index("dp")
    reach = min(reach_limit, lax.axis_size("dp") // 2)
    heads_q = query_weight.shape[1] // HEAD_WIDTH
    heads_kv = key_matrix.shape[1] // HEAD_WIDTH
    group_width = heads_q // heads_kv
    q_cols = heads_q * HEAD_WIDTH
    kv_cols = heads_kv * HEAD_WIDTH
    score_scale = HEAD_WIDTH ** (-0.5)
    row_first = row_index * row_len
    seg_row = lax.dynamic_slice_in_dim(segment_ids, row_first, row_len)
    index_row = row_first + jnp.arange(row_len, dtype=jnp.int32)
    every_index = jnp.arange(segment_ids.shape[0], dtype=jnp.int32)
    marks = (segment_ids[1:] != segment_ids[:-1]).astype(jnp.int32)
    starts = jnp.concatenate([jnp.zeros((1,), jnp.int32), marks * every_index[1:]])
    is_at = (starts[None, :] <= index_row[:, None]).astype(jnp.int32)
    token_positions = index_row - jnp.max(is_at * starts[None, :], axis=1)
    tokens32 = tokens.astype(floats)
    gain_attn = attn_gain.astype(floats)
    gain_mlp = mlp_gain.astype(floats)
    normed = rms_scale(tokens32, gain_attn).astype(halves)
    normed_full = lax.all_gather(normed, "tp", axis=0, tiled=True)
    joined = jnp.concatenate([query_weight, key_matrix, value_matrix], axis=1)
    projected = jnp.dot(normed_full, joined, preferred_element_type=floats)
    q_linear = projected[:, :q_cols]
    key_linear_out = projected[:, q_cols : q_cols + kv_cols]
    query_vectors = rotary_turn(q_linear, token_positions, heads_q).astype(halves)
    key_vectors = rotary_turn(key_linear_out, token_positions, heads_kv).astype(halves)
    value_vectors = projected[:, q_cols + kv_cols :].astype(halves)
    query_heads = query_vectors.reshape(row_len, heads_kv, group_width, HEAD_WIDTH)
    held_blocks = [(key_vectors, value_vectors)]
    moving = (key_vectors, value_vectors)
    for step_hop in range(reach):
        moving = shifted((moving[0], moving[1]), "dp", 1)
        held_blocks.append(moving)

    def block_mask(step_hop):
        key_row = row_index - step_hop
        seg_keys = lax.dynamic_slice_in_dim(segment_ids, jnp.maximum(key_row, 0) * row_len, row_len)
        key_index = key_row * row_len + jnp.arange(row_len, dtype=jnp.int32)
        return (seg_keys[None, :] == seg_row[:, None]) & (key_index[None, :] <= index_row[:, None])

    def block_needed(step_hop):
        last_key = jnp.maximum((row_index - step_hop + 1) * row_len - 1, 0)
        return (row_index >= step_hop) & (segment_ids[last_key] == seg_row[0])

    block_masks = [block_mask(step_hop) for step_hop in range(reach + 1)]

    def apply_block(step_hop, update, state_in):
        key_block, value_block = held_blocks[step_hop]
        if step_hop == 0:
            return update(state_in, key_block, value_block, block_masks[0])
        return lax.cond(
            block_needed(step_hop),
            update,
            lambda state_kept, key_skip, value_skip, mask_skip: state_kept,
            state_in,
            key_block,
            value_block,
            block_masks[step_hop],
        )

    def scores(key_block, allowed):
        raw_scores = jnp.einsum(
            "qhgd,khd->hgqk",
            query_heads,
            key_block.reshape(row_len, heads_kv, HEAD_WIDTH),
            preferred_element_type=floats,
        )
        return jnp.where(allowed, raw_scores * score_scale, -jnp.inf)

    def add_online(state_in, key_block, value_block, allowed):
        run_max, run_total, run_sum = state_in
        block_scores = scores(key_block, allowed)
        new_max = jnp.maximum(run_max, jnp.max(block_scores, axis=-1))
        factor = jnp.exp(run_max - new_max)
        weights = jnp.exp(block_scores - new_max[..., None])
        run_total = run_total * factor + jnp.sum(weights, axis=-1)
        run_sum = run_sum * jnp.moveaxis(factor, 2, 0)[..., None] + jnp.einsum(
            "hgqk,khd->qhgd",
            weights.astype(halves),
            value_block.reshape(row_len, heads_kv, HEAD_WIDTH),
            preferred_element_type=floats,
        )
        return (new_max, run_total, run_sum)

    online = (
        jnp.full((heads_kv, group_width, row_len), -jnp.inf, floats),
        jnp.zeros((heads_kv, group_width, row_len), floats),
        jnp.zeros((row_len, heads_kv, group_width, HEAD_WIDTH), floats),
    )
    for step_hop in range(reach + 1):
        online = apply_block(step_hop, add_online, online)
    run_max, run_total, run_sum = online
    log_total = (run_max + jnp.log(run_total))[..., None]
    context_heads = (run_sum / jnp.moveaxis(run_total, 2, 0)[..., None]).astype(halves)
    context = context_heads.reshape(row_len, q_cols)
    residual = tokens32 + lax.psum_scatter(
        jnp.dot(context, output_weight, preferred_element_type=floats).astype(jnp.bfloat16),
        "tp",
        scatter_dimension=0,
        tiled=True,
    ).astype(jnp.float32)
    mlp_normed = rms_scale(residual, gain_mlp).astype(halves)
    mlp_full = lax.all_gather(mlp_normed, "tp", axis=0, tiled=True)
    gate_pre = jnp.dot(mlp_full, gate_weight, preferred_element_type=floats)
    up_pre = jnp.dot(mlp_full, up_weight, preferred_element_type=floats)
    hidden = swiglu(gate_pre, up_pre).astype(halves)
    output = residual + lax.psum_scatter(
        jnp.dot(hidden, down_weight, preferred_element_type=floats).astype(jnp.bfloat16),
        "tp",
        scatter_dimension=0,
        tiled=True,
    ).astype(jnp.float32)
    grad_full = lax.all_gather(out_grad, "tp", axis=0, tiled=True)
    grad_hidden = contract_cols(grad_full, down_weight)
    down_grad = contract_rows(grad_full, hidden)
    silu_back = jax.vjp(swiglu, gate_pre, up_pre)[1]
    grad_gate, grad_up = silu_back(grad_hidden)
    grad_gate = grad_gate.astype(halves)
    grad_up = grad_up.astype(halves)
    gate_grad = contract_rows(mlp_full, grad_gate)
    up_grad = contract_rows(mlp_full, grad_up)
    grad_mlp_normed = lax.psum_scatter(
        (contract_cols(grad_gate, gate_weight) + contract_cols(grad_up, up_weight)).astype(
            jnp.bfloat16
        ),
        "tp",
        scatter_dimension=0,
        tiled=True,
    ).astype(jnp.float32)
    mlp_norm_back = jax.vjp(rms_scale, residual, gain_mlp)[1]
    grad_residual_part, mlp_gain_part = mlp_norm_back(grad_mlp_normed)
    grad_residual = out_grad.astype(floats) + grad_residual_part
    attn_grad_full = lax.all_gather(grad_residual.astype(halves), "tp", axis=0, tiled=True)
    output_grad = contract_rows(attn_grad_full, context)
    grad_context = (
        contract_cols(attn_grad_full, output_weight)
        .astype(halves)
        .reshape(row_len, heads_kv, group_width, HEAD_WIDTH)
    )
    delta_col = jnp.einsum(
        "qhgd,qhgd->hgq", grad_context, context_heads, preferred_element_type=floats
    )[..., None]

    def add_grads(state_in, key_block, value_block, allowed):
        query_acc, key_acc, value_acc = state_in
        probabilities = jnp.exp(scores(key_block, allowed) - log_total)
        grad_probs = jnp.einsum(
            "qhgd,khd->hgqk",
            grad_context,
            value_block.reshape(row_len, heads_kv, HEAD_WIDTH),
            preferred_element_type=floats,
        )
        grad_scores = (probabilities * (grad_probs - delta_col)).astype(halves)
        key_heads = key_block.reshape(row_len, heads_kv, HEAD_WIDTH)
        query_acc = (
            query_acc
            + jnp.einsum("hgqk,khd->qhgd", grad_scores, key_heads, preferred_element_type=floats)
            * score_scale
        )
        key_acc = (
            key_acc
            + jnp.einsum(
                "hgqk,qhgd->khd", grad_scores, query_heads, preferred_element_type=floats
            ).reshape(row_len, kv_cols)
            * score_scale
        )
        value_acc = value_acc + jnp.einsum(
            "hgqk,qhgd->khd",
            probabilities.astype(halves),
            grad_context,
            preferred_element_type=floats,
        ).reshape(row_len, kv_cols)
        return (query_acc, key_acc, value_acc)

    query_acc = jnp.zeros((row_len, heads_kv, group_width, HEAD_WIDTH), floats)
    carried = (jnp.zeros((row_len, kv_cols), floats), jnp.zeros((row_len, kv_cols), floats))
    for step_hop in range(reach, 0, -1):
        query_acc, key_acc, value_acc = apply_block(
            step_hop, add_grads, (query_acc, carried[0], carried[1])
        )
        carried = (
            shifted(key_acc.astype(jnp.bfloat16), "dp", -1).astype(key_acc.dtype),
            shifted(value_acc.astype(jnp.bfloat16), "dp", -1).astype(value_acc.dtype),
        )
    query_acc, key_total, value_total = apply_block(
        0, add_grads, (query_acc, carried[0], carried[1])
    )
    query_back = jax.vjp(lambda linear: rotary_turn(linear, token_positions, heads_q), q_linear)[1]
    key_back = jax.vjp(
        lambda linear: rotary_turn(linear, token_positions, heads_kv), key_linear_out
    )[1]
    grad_q_linear = query_back(query_acc.reshape(row_len, q_cols))[0]
    grad_k_linear = key_back(key_total)[0]
    grads_joined = jnp.concatenate([grad_q_linear, grad_k_linear, value_total], axis=1).astype(
        halves
    )
    proj_grad = contract_rows(normed_full, grads_joined)
    grad_normed = lax.psum_scatter(
        contract_cols(grads_joined, joined).astype(jnp.bfloat16),
        "tp",
        scatter_dimension=0,
        tiled=True,
    ).astype(jnp.float32)
    attn_norm_back = jax.vjp(rms_scale, tokens32, gain_attn)[1]
    grad_tokens_part, attn_gain_part = attn_norm_back(grad_normed)
    input_grad = grad_residual + grad_tokens_part
    def scatter_rows(grad):
        return lax.psum_scatter(
            grad.astype(halves), "dp", scatter_dimension=0, tiled=True
        ).astype(floats)

    mlp_sums = scatter_rows(jnp.concatenate([gate_grad, up_grad, down_grad], axis=1))
    ff_cols = gate_weight.shape[1]
    gate_sum = mlp_sums[:, :ff_cols]
    up_sum = mlp_sums[:, ff_cols : 2 * ff_cols]
    down_sum = mlp_sums[:, 2 * ff_cols :]
    attn_sums = scatter_rows(jnp.concatenate([proj_grad, output_grad], axis=1))
    query_sum = attn_sums[:, :q_cols]
    key_sum = attn_sums[:, q_cols : q_cols + kv_cols]
    value_sum = attn_sums[:, q_cols + kv_cols : q_cols + 2 * kv_cols]
    output_sum = attn_sums[:, q_cols + 2 * kv_cols :]
    attn_gain_sum = lax.psum_scatter(attn_gain_part, "dp", scatter_dimension=0, tiled=True)
    mlp_gain_sum = lax.psum_scatter(mlp_gain_part, "dp", scatter_dimension=0, tiled=True)
    attn_gain_total, mlp_gain_total = lax.psum((attn_gain_sum, mlp_gain_sum), "tp")
    return (
        output.astype(halves),
        input_grad,
        attn_gain_total,
        query_sum,
        key_sum,
        value_sum,
        output_sum.T,
        mlp_gain_total,
        gate_sum,
        up_sum,
        down_sum.T,
    )


def solution(mesh):
    return jax.shard_map(
        local,
        mesh=mesh,
        in_specs=(
            P(("dp", "tp"), None),
            P(("dp", "tp"), None),
            P(),
            P(),
            P(None, "tp"),
            P(None, "tp"),
            P(None, "tp"),
            P("tp", None),
            P(),
            P(None, "tp"),
            P(None, "tp"),
            P("tp", None),
        ),
        out_specs=(
            P(("dp", "tp"), None),
            P(("dp", "tp"), None),
            P("dp"),
            P("dp", "tp"),
            P("dp", "tp"),
            P("dp", "tp"),
            P("tp", "dp"),
            P("dp"),
            P("dp", "tp"),
            P("dp", "tp"),
            P("tp", "dp"),
        ),
        check_vma=False,
    )
```

```python
import functools

import jax
import jax.numpy as jnp
from jax import lax
from jax.experimental import pallas as pl
from jax.experimental.pallas import tpu as pltpu
from jax.sharding import PartitionSpec as P

HEAD_WIDTH = 96
BLK = 256
LOG2E = 1.4426950408889634
SCORE = LOG2E * HEAD_WIDTH ** (-0.5)
VSCALE = 2.0 ** -9
floats = jnp.float32
halves = jnp.bfloat16


def dot_nn(a, b):
    return jnp.dot(a, b, preferred_element_type=floats)


def dot_nt(a, b):
    return lax.dot_general(a, b, (((1,), (1,)), ((), ())), preferred_element_type=floats)


def pair_state(sc, kb, qb):
    key_base = sc[0, kb]
    q_base, least, most = sc[1, qb], sc[2, qb], sc[3, qb]
    needed = (key_base <= q_base + (BLK - 1)) & (key_base + (BLK - 1) >= least)
    whole = (key_base + (BLK - 1) <= q_base) & (key_base >= most)
    return key_base, needed, whole


def allowed_mask(key_base, tok_ref, start_ref, lanes):
    keys = key_base + lax.broadcasted_iota(jnp.int32, (BLK, BLK), 0)
    return (keys <= tok_ref[0:1, lanes]) & (keys >= start_ref[0:1, lanes])


def fwd_kernel(n, width, first, last, sc, q_ref, tok_ref, start_ref, *refs):
    pieces = refs[:n]
    refs = refs[n:]
    if not first:
        acc_in, sum_in = refs[:2]
        refs = refs[2:]
    out_acc, out_sum = refs[:2]
    kv, keys_nat, acc, total, q_wide, sem = refs[2:]
    per = width // BLK
    for i in range(n):
        pltpu.make_async_copy(pieces[i], kv.at[i], sem.at[i]).start()
    if first:
        acc[...] = jnp.zeros_like(acc)
        total[...] = jnp.zeros_like(total)
    else:
        acc[...] = acc_in[...]
        total[...] = sum_in[...]
    for i in range(n):
        pltpu.make_async_copy(pieces[i], kv.at[i], sem.at[i]).wait()
    heads_kv = pieces[0].shape[0] // (2 * HEAD_WIDTH)
    group = q_ref.shape[0] // (heads_kv * HEAD_WIDTH)
    v_off = heads_kv * HEAD_WIDTH
    places = [
        (h, slice((h * group + g) * HEAD_WIDTH, (h * group + g + 1) * HEAD_WIDTH), slice(qb * BLK, (qb + 1) * BLK),
         slice(h * HEAD_WIDTH, (h + 1) * HEAD_WIDTH), slice((qb * group + g) * BLK, (qb * group + g + 1) * BLK), h * group + g)
        for h in range(heads_kv) for g in range(group) for qb in range(q_ref.shape[1] // BLK)
    ]
    for h, rows, lanes, wrows, wlanes, hd in places:
        q_wide[wrows, wlanes] = q_ref[rows, lanes]

    def key_block(kb, carry):
        piece = kb // per
        klanes = pl.ds(pl.multiple_of((kb % per) * BLK, BLK), BLK)
        for h in range(heads_kv):
            keys_nat[h] = kv[piece, h * HEAD_WIDTH : (h + 1) * HEAD_WIDTH, klanes].T

        def query_block(qb, carry):
            key_base, needed, whole = pair_state(sc, kb, qb)
            lanes = pl.ds(pl.multiple_of(qb * BLK, BLK), BLK)

            def unit(masked):
                wide = pl.ds(pl.multiple_of(qb * (group * BLK), group * BLK), group * BLK)
                if masked:
                    allowed = allowed_mask(key_base, tok_ref, start_ref, lanes)
                    allowed = jnp.concatenate([allowed] * group, axis=1)
                scores = [
                    dot_nn(keys_nat[h], q_wide[h * HEAD_WIDTH : (h + 1) * HEAD_WIDTH, wide])
                    for h in range(heads_kv)
                ]
                weights = [jnp.exp2(s * SCORE) for s in scores]
                if masked:
                    weights = [jnp.where(allowed, w, 0.0) for w in weights]
                sums = [jnp.sum(w, axis=0, keepdims=True) for w in weights]
                parts = [
                    dot_nn(
                        kv[piece, v_off + h * HEAD_WIDTH : v_off + (h + 1) * HEAD_WIDTH, klanes],
                        weights[h].astype(halves),
                    )
                    for h in range(heads_kv)
                ]
                for h in range(heads_kv):
                    total[h : h + 1, wide] += sums[h]
                    acc[h * HEAD_WIDTH : (h + 1) * HEAD_WIDTH, wide] += parts[h]

            pl.when(needed & whole)(lambda: unit(False))
            pl.when(needed & jnp.logical_not(whole))(lambda: unit(True))
            return carry

        return lax.fori_loop(0, q_ref.shape[1] // BLK, query_block, carry)

    lax.fori_loop(0, n * per, key_block, 0)
    if last:
        for h, rows, lanes, wrows, wlanes, hd in places:
            row = total[h : h + 1, wlanes]
            out_acc[rows, lanes] = (acc[wrows, wlanes] * ((1.0 / VSCALE) / row)).astype(halves)
            out_sum[hd : hd + 1, lanes] = jnp.log2(row)
    else:
        out_acc[...] = acc[...]
        out_sum[...] = total[...]


VM = pl.BlockSpec(memory_space=pltpu.VMEM)
SM = pl.BlockSpec(memory_space=pltpu.SMEM)
HB = pl.BlockSpec(memory_space=pl.ANY)


def attend_forward(sc, q_t, tok, start, pieces, state=None, last=True):
    n, width = len(pieces), pieces[0].shape[1]
    heads = q_t.shape[0] // HEAD_WIDTH
    heads_kv = pieces[0].shape[0] // (2 * HEAD_WIDTH)
    first = state is None
    tokens = q_t.shape[1]
    out_shape = (
        jax.ShapeDtypeStruct(q_t.shape, halves if last else floats),
        jax.ShapeDtypeStruct((heads, tokens), floats),
    )
    return pl.pallas_call(
        functools.partial(fwd_kernel, n, width, first, last),
        out_shape=out_shape,
        in_specs=[SM, VM, VM, VM] + [HB] * n + ([] if first else [VM, VM]),
        out_specs=(VM, VM),
        scratch_shapes=[
            pltpu.VMEM((n,) + pieces[0].shape, halves),
            pltpu.VMEM((heads_kv, BLK, HEAD_WIDTH), halves),
            pltpu.VMEM((heads_kv * HEAD_WIDTH, tokens * heads // heads_kv), floats),
            pltpu.VMEM((heads_kv, tokens * heads // heads_kv), floats),
            pltpu.VMEM((heads_kv * HEAD_WIDTH, tokens * heads // heads_kv), halves),
            pltpu.SemaphoreType.DMA((n,)),
        ],
        compiler_params=pltpu.CompilerParams(vmem_limit_bytes=40 << 20),
        name="attend_forward",
    )(sc, q_t, tok, start, *pieces, *(() if first else state))


def bwd_kernel(n, width, first, sc, q_ref, do_ref, log_ref, delta_ref, tok_ref, start_ref, *refs):
    pieces = refs[:n]
    refs = refs[n:]
    if not first:
        dq_in = refs[0]
        refs = refs[1:]
    dq_out = refs[0]
    douts = refs[1 : 1 + n]
    kv, dkv, keys_nat, vals_nat, acc, q_wide, do_wide, log_wide, delta_wide, dq_wide, sem, osem = refs[1 + n :]
    per = width // BLK
    for i in range(n):
        pltpu.make_async_copy(pieces[i], kv.at[i], sem.at[i]).start()
    for i in range(n):
        pltpu.make_async_copy(pieces[i], kv.at[i], sem.at[i]).wait()
    heads_kv = pieces[0].shape[0] // (2 * HEAD_WIDTH)
    group = q_ref.shape[0] // (heads_kv * HEAD_WIDTH)
    v_off = heads_kv * HEAD_WIDTH
    places = [
        (h, slice((h * group + g) * HEAD_WIDTH, (h * group + g + 1) * HEAD_WIDTH), slice(qb * BLK, (qb + 1) * BLK),
         slice(h * HEAD_WIDTH, (h + 1) * HEAD_WIDTH), slice((qb * group + g) * BLK, (qb * group + g + 1) * BLK), h * group + g)
        for h in range(heads_kv) for g in range(group) for qb in range(q_ref.shape[1] // BLK)
    ]
    for h, rows, lanes, wrows, wlanes, hd in places:
        q_wide[wrows, wlanes] = q_ref[rows, lanes]
        do_wide[wrows, wlanes] = do_ref[rows, lanes]
        log_wide[h : h + 1, wlanes] = log_ref[hd : hd + 1, lanes]
        delta_wide[h : h + 1, wlanes] = delta_ref[hd : hd + 1, lanes]
        dq_wide[wrows, wlanes] = jnp.zeros((HEAD_WIDTH, BLK), floats) if first else dq_in[rows, lanes]
    out_scale = (1.0 / VSCALE) * HEAD_WIDTH ** (-0.5)

    def key_block(kb, carry):
        piece = kb // per
        klanes = pl.ds(pl.multiple_of((kb % per) * BLK, BLK), BLK)
        for h in range(heads_kv):
            keys_nat[h] = kv[piece, h * HEAD_WIDTH : (h + 1) * HEAD_WIDTH, klanes].T
            vals_nat[h] = kv[piece, v_off + h * HEAD_WIDTH : v_off + (h + 1) * HEAD_WIDTH, klanes].T
        acc[...] = jnp.zeros_like(acc)

        def query_block(qb, carry):
            key_base, needed, whole = pair_state(sc, kb, qb)
            lanes = pl.ds(pl.multiple_of(qb * BLK, BLK), BLK)

            def unit(masked):
                wide = pl.ds(pl.multiple_of(qb * (group * BLK), group * BLK), group * BLK)
                if masked:
                    allowed = allowed_mask(key_base, tok_ref, start_ref, lanes)
                    allowed = jnp.concatenate([allowed] * group, axis=1)
                heads = range(heads_kv)
                krows = [slice(h * HEAD_WIDTH, (h + 1) * HEAD_WIDTH) for h in heads]
                vrows = [slice(v_off + h * HEAD_WIDTH, v_off + (h + 1) * HEAD_WIDTH) for h in heads]
                qt = [q_wide[krows[h], wide] for h in heads]
                dot = [do_wide[krows[h], wide] for h in heads]
                scores = [dot_nn(keys_nat[h], qt[h]) for h in heads]
                dprobs = [dot_nn(vals_nat[h], dot[h]) for h in heads]
                weights = [
                    jnp.exp2(scores[h] * SCORE - log_wide[h : h + 1, wide]) for h in heads
                ]
                if masked:
                    weights = [jnp.where(allowed, w, 0.0) for w in weights]
                ds = [
                    (weights[h] * (dprobs[h] - delta_wide[h : h + 1, wide])).astype(halves)
                    for h in heads
                ]
                dv = [dot_nt(dot[h], weights[h].astype(halves)) for h in heads]
                dk = [dot_nt(qt[h], ds[h]) for h in heads]
                dq = [dot_nn(kv[piece, krows[h], klanes], ds[h]) for h in heads]
                for h in heads:
                    acc[vrows[h], :] += dv[h]
                    acc[krows[h], :] += dk[h]
                    dq_wide[krows[h], wide] += dq[h]

            pl.when(needed & whole)(lambda: unit(False))
            pl.when(needed & jnp.logical_not(whole))(lambda: unit(True))
            return carry

        carry = lax.fori_loop(0, q_ref.shape[1] // BLK, query_block, carry)
        dkv[piece, 0:v_off, klanes] = (acc[0:v_off, :] * out_scale).astype(halves)
        dkv[piece, v_off:, klanes] = acc[v_off:, :].astype(halves)
        return carry

    lax.fori_loop(0, n * per, key_block, 0)
    for i in range(n):
        pltpu.make_async_copy(dkv.at[i], douts[i], osem.at[i]).start()
    for h, rows, lanes, wrows, wlanes, hd in places:
        dq_out[rows, lanes] = dq_wide[wrows, wlanes] * out_scale
    for i in range(n):
        pltpu.make_async_copy(dkv.at[i], douts[i], osem.at[i]).wait()


def attend_backward(sc, q_t, do_t, log_total, delta, tok, start, pieces):
    n, width = len(pieces), pieces[0].shape[1]
    heads_kv = pieces[0].shape[0] // (2 * HEAD_WIDTH)
    wide = q_t.shape[0] // (heads_kv * HEAD_WIDTH) * q_t.shape[1]
    outs = pl.pallas_call(
        functools.partial(bwd_kernel, n, width, True),
        out_shape=(jax.ShapeDtypeStruct(q_t.shape, floats),)
        + tuple(jax.ShapeDtypeStruct(p.shape, halves) for p in pieces),
        in_specs=[SM] + [VM] * 6 + [HB] * n,
        out_specs=(VM,) + (HB,) * n,
        scratch_shapes=[
            pltpu.VMEM((n,) + pieces[0].shape, halves),
            pltpu.VMEM((n,) + pieces[0].shape, halves),
            pltpu.VMEM((heads_kv, BLK, HEAD_WIDTH), halves),
            pltpu.VMEM((heads_kv, BLK, HEAD_WIDTH), halves),
            pltpu.VMEM((pieces[0].shape[0], BLK), floats),
            pltpu.VMEM((heads_kv * HEAD_WIDTH, wide), halves),
            pltpu.VMEM((heads_kv * HEAD_WIDTH, wide), halves),
            pltpu.VMEM((heads_kv, wide), floats),
            pltpu.VMEM((heads_kv, wide), floats),
            pltpu.VMEM((heads_kv * HEAD_WIDTH, wide), floats),
            pltpu.SemaphoreType.DMA((n,)),
            pltpu.SemaphoreType.DMA((n,)),
        ],
        compiler_params=pltpu.CompilerParams(vmem_limit_bytes=44 << 20),
        name="attend_backward",
    )(sc, q_t, do_t, log_total, delta, tok, start, *pieces)
    return outs[0], list(outs[1:])


eps_norm = 1e-05
rope_base = 100000.0
reach_limit = 8


def shifted(block, axis, distance):
    devices = range(lax.axis_size(axis))
    route = [(i - distance, i) for i in devices if i - distance in devices]
    return lax.ppermute(block, axis, route)


def rms_scale(value_vectors, gain_vec):
    return (
        value_vectors
        * lax.rsqrt(jnp.mean(value_vectors * value_vectors, axis=-1, keepdims=True) + eps_norm)
        * gain_vec
    )


def rotary_turn(value_vectors, token_positions, heads):
    half_width = HEAD_WIDTH // 2
    inverse = 1.0 / rope_base ** (jnp.arange(half_width, dtype=jnp.float32) * 2.0 / HEAD_WIDTH)
    angles = token_positions.astype(jnp.float32)[:, None] * inverse[None, :]
    cosine = jnp.cos(angles)[:, None, :]
    sine_part = jnp.sin(angles)[:, None, :]
    shaped = value_vectors.reshape(value_vectors.shape[0], heads, HEAD_WIDTH)
    first_half = shaped[..., :half_width]
    second = shaped[..., half_width:]
    turned = jnp.concatenate(
        [first_half * cosine - second * sine_part, second * cosine + first_half * sine_part],
        axis=-1,
    )
    return turned.reshape(value_vectors.shape)


def swiglu(gate_pre, up_pre):
    return jax.nn.silu(gate_pre) * up_pre


def contract_rows(left_side, right_side):
    return lax.dot_general(
        left_side, right_side, (((0,), (0,)), ((), ())), preferred_element_type=jnp.float32
    )


def contract_cols(left_side, right_side):
    return lax.dot_general(
        left_side, right_side, (((1,), (1,)), ((), ())), preferred_element_type=jnp.float32
    )


def local(
    tokens,
    out_grad,
    segment_ids,
    attn_gain,
    query_weight,
    key_matrix,
    value_matrix,
    output_weight,
    mlp_gain,
    gate_weight,
    up_weight,
    down_weight,
):
    floats = jnp.float32
    halves = jnp.bfloat16
    shard_rows = tokens.shape[0]
    row_len = shard_rows * lax.axis_size("tp")
    row_index = lax.axis_index("dp")
    reach = min(reach_limit, lax.axis_size("dp") // 2)
    heads_q = query_weight.shape[1] // HEAD_WIDTH
    heads_kv = key_matrix.shape[1] // HEAD_WIDTH
    group_width = heads_q // heads_kv
    q_cols = heads_q * HEAD_WIDTH
    kv_cols = heads_kv * HEAD_WIDTH
    score_scale = HEAD_WIDTH ** (-0.5)
    row_first = row_index * row_len
    seg_row = lax.dynamic_slice_in_dim(segment_ids, row_first, row_len)
    index_row = row_first + jnp.arange(row_len, dtype=jnp.int32)
    every_index = jnp.arange(segment_ids.shape[0], dtype=jnp.int32)
    marks = (segment_ids[1:] != segment_ids[:-1]).astype(jnp.int32)
    starts = jnp.concatenate([jnp.zeros((1,), jnp.int32), marks * every_index[1:]])
    is_at = (starts[None, :] <= index_row[:, None]).astype(jnp.int32)
    token_positions = index_row - jnp.max(is_at * starts[None, :], axis=1)
    tokens32 = tokens.astype(floats)
    gain_attn = attn_gain.astype(floats)
    gain_mlp = mlp_gain.astype(floats)
    normed = rms_scale(tokens32, gain_attn).astype(halves)
    normed_full = lax.all_gather(normed, "tp", axis=0, tiled=True)
    joined = jnp.concatenate([query_weight, key_matrix, value_matrix], axis=1)
    projected = jnp.dot(normed_full, joined, preferred_element_type=floats)
    q_linear = projected[:, :q_cols]
    key_linear_out = projected[:, q_cols : q_cols + kv_cols]
    query_vectors = rotary_turn(q_linear, token_positions, heads_q).astype(halves)
    key_vectors = rotary_turn(key_linear_out, token_positions, heads_kv).astype(halves)
    value_vectors = projected[:, q_cols + kv_cols :].astype(halves)
    query_heads = query_vectors.reshape(row_len, heads_kv, group_width, HEAD_WIDTH)
    held_blocks = [(key_vectors, value_vectors)]
    moving = (key_vectors, value_vectors)
    for step_hop in range(reach):
        moving = shifted((moving[0], moving[1]), "dp", 1)
        held_blocks.append(moving)

    def block_mask(step_hop):
        key_row = row_index - step_hop
        seg_keys = lax.dynamic_slice_in_dim(segment_ids, jnp.maximum(key_row, 0) * row_len, row_len)
        key_index = key_row * row_len + jnp.arange(row_len, dtype=jnp.int32)
        return (seg_keys[None, :] == seg_row[:, None]) & (key_index[None, :] <= index_row[:, None])

    def block_needed(step_hop):
        last_key = jnp.maximum((row_index - step_hop + 1) * row_len - 1, 0)
        return (row_index >= step_hop) & (segment_ids[last_key] == seg_row[0])

    block_masks = [block_mask(step_hop) for step_hop in range(reach + 1)]

    def apply_block(step_hop, update, state_in):
        key_block, value_block = held_blocks[step_hop]
        if step_hop == 0:
            return update(state_in, key_block, value_block, block_masks[0])
        return lax.cond(
            block_needed(step_hop),
            update,
            lambda state_kept, key_skip, value_skip, mask_skip: state_kept,
            state_in,
            key_block,
            value_block,
            block_masks[step_hop],
        )

    def scores(key_block, allowed):
        raw_scores = jnp.einsum(
            "qhgd,khd->hgqk",
            query_heads,
            key_block.reshape(row_len, heads_kv, HEAD_WIDTH),
            preferred_element_type=floats,
        )
        return jnp.where(allowed, raw_scores * score_scale, -jnp.inf)

    def add_online(state_in, key_block, value_block, allowed):
        run_max, run_total, run_sum = state_in
        block_scores = scores(key_block, allowed)
        new_max = jnp.maximum(run_max, jnp.max(block_scores, axis=-1))
        factor = jnp.exp(run_max - new_max)
        weights = jnp.exp(block_scores - new_max[..., None])
        run_total = run_total * factor + jnp.sum(weights, axis=-1)
        run_sum = run_sum * jnp.moveaxis(factor, 2, 0)[..., None] + jnp.einsum(
            "hgqk,khd->qhgd",
            weights.astype(halves),
            value_block.reshape(row_len, heads_kv, HEAD_WIDTH),
            preferred_element_type=floats,
        )
        return (new_max, run_total, run_sum)

    online = (
        jnp.full((heads_kv, group_width, row_len), -jnp.inf, floats),
        jnp.zeros((heads_kv, group_width, row_len), floats),
        jnp.zeros((row_len, heads_kv, group_width, HEAD_WIDTH), floats),
    )
    for step_hop in range(reach + 1):
        online = apply_block(step_hop, add_online, online)
    run_max, run_total, run_sum = online
    log_total = (run_max + jnp.log(run_total))[..., None]
    context_heads = (run_sum / jnp.moveaxis(run_total, 2, 0)[..., None]).astype(halves)
    context = context_heads.reshape(row_len, q_cols)
    residual = tokens32 + lax.psum_scatter(
        jnp.dot(context, output_weight, preferred_element_type=floats).astype(jnp.bfloat16),
        "tp",
        scatter_dimension=0,
        tiled=True,
    ).astype(jnp.float32)
    mlp_normed = rms_scale(residual, gain_mlp).astype(halves)
    mlp_full = lax.all_gather(mlp_normed, "tp", axis=0, tiled=True)
    gate_pre = jnp.dot(mlp_full, gate_weight, preferred_element_type=floats)
    up_pre = jnp.dot(mlp_full, up_weight, preferred_element_type=floats)
    hidden = swiglu(gate_pre, up_pre).astype(halves)
    output = residual + lax.psum_scatter(
        jnp.dot(hidden, down_weight, preferred_element_type=floats).astype(jnp.bfloat16),
        "tp",
        scatter_dimension=0,
        tiled=True,
    ).astype(jnp.float32)
    grad_full = lax.all_gather(out_grad, "tp", axis=0, tiled=True)
    grad_hidden = contract_cols(grad_full, down_weight)
    down_grad = contract_rows(grad_full, hidden)
    silu_back = jax.vjp(swiglu, gate_pre, up_pre)[1]
    grad_gate, grad_up = silu_back(grad_hidden)
    grad_gate = grad_gate.astype(halves)
    grad_up = grad_up.astype(halves)
    gate_grad = contract_rows(mlp_full, grad_gate)
    up_grad = contract_rows(mlp_full, grad_up)
    grad_mlp_normed = lax.psum_scatter(
        (contract_cols(grad_gate, gate_weight) + contract_cols(grad_up, up_weight)).astype(
            jnp.bfloat16
        ),
        "tp",
        scatter_dimension=0,
        tiled=True,
    ).astype(jnp.float32)
    mlp_norm_back = jax.vjp(rms_scale, residual, gain_mlp)[1]
    grad_residual_part, mlp_gain_part = mlp_norm_back(grad_mlp_normed)
    grad_residual = out_grad.astype(floats) + grad_residual_part
    attn_grad_full = lax.all_gather(grad_residual.astype(halves), "tp", axis=0, tiled=True)
    output_grad = contract_rows(attn_grad_full, context)
    grad_context = (
        contract_cols(attn_grad_full, output_weight)
        .astype(halves)
        .reshape(row_len, heads_kv, group_width, HEAD_WIDTH)
    )
    delta_col = jnp.einsum(
        "qhgd,qhgd->hgq", grad_context, context_heads, preferred_element_type=floats
    )[..., None]

    def add_grads(state_in, key_block, value_block, allowed):
        query_acc, key_acc, value_acc = state_in
        probabilities = jnp.exp(scores(key_block, allowed) - log_total)
        grad_probs = jnp.einsum(
            "qhgd,khd->hgqk",
            grad_context,
            value_block.reshape(row_len, heads_kv, HEAD_WIDTH),
            preferred_element_type=floats,
        )
        grad_scores = (probabilities * (grad_probs - delta_col)).astype(halves)
        key_heads = key_block.reshape(row_len, heads_kv, HEAD_WIDTH)
        query_acc = (
            query_acc
            + jnp.einsum("hgqk,khd->qhgd", grad_scores, key_heads, preferred_element_type=floats)
            * score_scale
        )
        key_acc = (
            key_acc
            + jnp.einsum(
                "hgqk,qhgd->khd", grad_scores, query_heads, preferred_element_type=floats
            ).reshape(row_len, kv_cols)
            * score_scale
        )
        value_acc = value_acc + jnp.einsum(
            "hgqk,qhgd->khd",
            probabilities.astype(halves),
            grad_context,
            preferred_element_type=floats,
        ).reshape(row_len, kv_cols)
        return (query_acc, key_acc, value_acc)

    query_acc = jnp.zeros((row_len, heads_kv, group_width, HEAD_WIDTH), floats)
    carried = (jnp.zeros((row_len, kv_cols), floats), jnp.zeros((row_len, kv_cols), floats))
    for step_hop in range(reach, 0, -1):
        query_acc, key_acc, value_acc = apply_block(
            step_hop, add_grads, (query_acc, carried[0], carried[1])
        )
        carried = (
            shifted(key_acc.astype(jnp.bfloat16), "dp", -1).astype(key_acc.dtype),
            shifted(value_acc.astype(jnp.bfloat16), "dp", -1).astype(value_acc.dtype),
        )
    query_acc, key_total, value_total = apply_block(
        0, add_grads, (query_acc, carried[0], carried[1])
    )
    query_back = jax.vjp(lambda linear: rotary_turn(linear, token_positions, heads_q), q_linear)[1]
    key_back = jax.vjp(
        lambda linear: rotary_turn(linear, token_positions, heads_kv), key_linear_out
    )[1]
    grad_q_linear = query_back(query_acc.reshape(row_len, q_cols))[0]
    grad_k_linear = key_back(key_total)[0]
    grads_joined = jnp.concatenate([grad_q_linear, grad_k_linear, value_total], axis=1).astype(
        halves
    )
    proj_grad = contract_rows(normed_full, grads_joined)
    grad_normed = lax.psum_scatter(
        contract_cols(grads_joined, joined).astype(jnp.bfloat16),
        "tp",
        scatter_dimension=0,
        tiled=True,
    ).astype(jnp.float32)
    attn_norm_back = jax.vjp(rms_scale, tokens32, gain_attn)[1]
    grad_tokens_part, attn_gain_part = attn_norm_back(grad_normed)
    input_grad = grad_residual + grad_tokens_part
    def scatter_rows(grad):
        return lax.psum_scatter(
            grad.astype(halves), "dp", scatter_dimension=0, tiled=True
        ).astype(floats)

    mlp_sums = scatter_rows(jnp.concatenate([gate_grad, up_grad, down_grad], axis=1))
    ff_cols = gate_weight.shape[1]
    gate_sum = mlp_sums[:, :ff_cols]
    up_sum = mlp_sums[:, ff_cols : 2 * ff_cols]
    down_sum = mlp_sums[:, 2 * ff_cols :]
    attn_sums = scatter_rows(jnp.concatenate([proj_grad, output_grad], axis=1))
    query_sum = attn_sums[:, :q_cols]
    key_sum = attn_sums[:, q_cols : q_cols + kv_cols]
    value_sum = attn_sums[:, q_cols + kv_cols : q_cols + 2 * kv_cols]
    output_sum = attn_sums[:, q_cols + 2 * kv_cols :]
    attn_gain_sum = lax.psum_scatter(attn_gain_part, "dp", scatter_dimension=0, tiled=True)
    mlp_gain_sum = lax.psum_scatter(mlp_gain_part, "dp", scatter_dimension=0, tiled=True)
    attn_gain_total, mlp_gain_total = lax.psum((attn_gain_sum, mlp_gain_sum), "tp")
    return (
        output.astype(halves),
        input_grad,
        attn_gain_total,
        query_sum,
        key_sum,
        value_sum,
        output_sum.T,
        mlp_gain_total,
        gate_sum,
        up_sum,
        down_sum.T,
    )


def routes(target):
    pairs = []
    for index in range(32):
        dp, z = divmod(index, 4)
        there = target(dp // 4, dp // 2 % 2, dp % 2, z)
        if there is not None:
            y, x, c, z = there
            pairs.append((index, (y * 4 + x * 2 + c) * 4 + z))
    return pairs


ROUTES = {
    "core": routes(lambda y, x, c, z: (y, x, 1 - c, z)),
    "x": routes(lambda y, x, c, z: (y, 1 - x, c, z)),
    "y": routes(lambda y, x, c, z: (1 - y, x, c, z)),
    "near": routes(lambda y, x, c, z: (y, x, c, z ^ 1)),
    "far": routes(lambda y, x, c, z: (y, x, c, z ^ 2)),
    "cross": routes(lambda y, x, c, z: (y, x, 1 - c, z ^ 2)),
    "odd_far": routes(lambda y, x, c, z: (y, x, c, z ^ 2) if c else None),
    "odd_x": routes(lambda y, x, c, z: (y, 1 - x, c, z) if c else None),
    "odd_y": routes(lambda y, x, c, z: (1 - y, x, c, z) if c else None),
    "odd_xy": routes(lambda y, x, c, z: (1 - y, 1 - x, c, z) if c else None),
    "home": routes(lambda y, x, c, z: (y, x, 0, z ^ 2) if c else (y, x, 1, z)),
    "x_up": routes(lambda y, x, c, z: None if x else (y, 1, c, z)),
    "y_up": routes(lambda y, x, c, z: None if y else (1, x, c, z)),
    "x_down": routes(lambda y, x, c, z: (y, 0, c, z) if x else None),
    "y_down": routes(lambda y, x, c, z: (0, x, c, z) if y else None),
    "relay": routes(lambda y, x, c, z: (1, 0, c, z) if x and y else None),
    "unrelay": routes(lambda y, x, c, z: (1, 1, c, z) if y and not x else None),
}
FAR_BASE = 1 << 24


def send(block, way):
    return lax.ppermute(block, ("dp", "tp"), ROUTES[way])


def assemble_kernel(where, own_ref, a_ref, x_ref, y_ref, xy_ref, out_ref, sem):
    odd, y, x = where[0], where[1], where[2]
    rows = a_ref.shape[0]

    @pl.when(odd == 0)
    def _():
        copy = pltpu.make_async_copy(own_ref, out_ref, sem.at[0])
        copy.start()
        copy.wait()

    @pl.when(odd != 0)
    def _():
        copies = []
        for i, (ref, slot) in enumerate(
            (
                (a_ref, 2 * y + x),
                (x_ref, 2 * y + (1 - x)),
                (y_ref, 2 * (1 - y) + x),
                (xy_ref, 2 * (1 - y) + (1 - x)),
            )
        ):
            copies.append(
                pltpu.make_async_copy(ref, out_ref.at[pl.ds(slot * rows, rows)], sem.at[i])
            )
        for copy in copies:
            copy.start()
        for copy in copies:
            copy.wait()


def fetch_quarter(weight, where, slot):
    rows = weight.shape[0] // 4
    part = send(lax.dynamic_slice_in_dim(weight, slot * rows, rows), "odd_far")
    pieces = (part, send(part, "odd_x"), send(part, "odd_y"), send(part, "odd_xy"))
    return pl.pallas_call(
        assemble_kernel,
        out_shape=jax.ShapeDtypeStruct(weight.shape, weight.dtype),
        in_specs=[SM] + [HB] * 5,
        out_specs=HB,
        scratch_shapes=[pltpu.SemaphoreType.DMA((4,))],
        compiler_params=pltpu.CompilerParams(vmem_limit_bytes=4 << 20),
        name="assemble",
    )(where, weight, *pieces)


def gather_group(block):
    near = send(block, "near")
    beside = send(block, "core")
    return jnp.concatenate([block, beside]), jnp.concatenate([near, send(near, "core")])


def scatter_group(here, there):
    rows = here.shape[0] // 2
    there_sum = there[:rows] + send(there[rows:].astype(halves), "core").astype(floats)
    here_sum = here[:rows] + send(here[rows:].astype(halves), "core").astype(floats)
    return here_sum + send(there_sum.astype(halves), "near").astype(floats)


def dot_tt(a, b):
    return lax.dot_general(a, b, (((0,), (1,)), ((), ())), preferred_element_type=floats)


def rope_tables(positions):
    half_width = HEAD_WIDTH // 2
    inverse = 1.0 / rope_base ** (jnp.arange(half_width, dtype=floats) * 2.0 / HEAD_WIDTH)
    angles = inverse[:, None] * positions.astype(floats)[None, :]
    return jnp.cos(angles), jnp.sin(angles)


def turn(linear, cosine, sine):
    shaped = linear.reshape(-1, 2, HEAD_WIDTH // 2, linear.shape[-1])
    one, two = shaped[:, 0], shaped[:, 1]
    turned = jnp.stack([one * cosine - two * sine, two * cosine + one * sine], axis=1)
    return turned.reshape(linear.shape)


def norm_back(vectors, gain, grad):
    root = lax.rsqrt(jnp.mean(vectors * vectors, axis=-1, keepdims=True) + eps_norm)
    weighted = grad * gain
    slope = jnp.mean(weighted * vectors, axis=-1, keepdims=True)
    back = root * weighted - vectors * (root * root * root * slope)
    return back, jnp.sum(grad * vectors * root, axis=0)


def sum_rows_over_plane(grad, x, y, x_first):
    shaped = grad.reshape(2, 2, -1, grad.shape[-1])

    def pick(array, at, axis):
        return lax.dynamic_index_in_dim(array, at, axis, keepdims=False)

    axes = (("x", x, 1), ("y", y, 0)) if x_first else (("y", y, 0), ("x", x, 1))
    (way, at, axis), (way_two, at_two, _) = axes
    come = send(pick(shaped, 1 - at, axis), way)
    half = pick(shaped, at, axis).astype(floats) + come.astype(floats)
    come = send(pick(half, 1 - at_two, 0).astype(halves), way_two)
    return pick(half, at_two, 0) + come.astype(floats)


def sum_rows_home(part, odd):
    rows = part.shape[0] // 2
    first, second = part[:rows], part[rows:]
    one = send(jnp.where(odd, first, second).astype(halves), "home").astype(floats)
    two = send(second.astype(halves), "odd_far").astype(floats)
    return jnp.where(odd, one + two, first + one)


def local_regrouped(
    tokens,
    out_grad,
    segment_ids,
    attn_gain,
    query_weight,
    key_matrix,
    value_matrix,
    output_weight,
    mlp_gain,
    gate_weight,
    up_weight,
    down_weight,
):
    block = tokens.shape[0]
    row_len = 4 * block
    dp, z = lax.axis_index("dp"), lax.axis_index("tp")
    y, x, c = dp // 4, dp // 2 % 2, dp % 2
    j = dp // 2
    odd = c == 1
    pair, side = z // 2, z % 2
    q_cols, kv_cols = query_weight.shape[1], key_matrix.shape[1]
    heads = q_cols // HEAD_WIDTH
    group_width = q_cols // kv_cols
    ff_cols = gate_weight.shape[1]
    gain_attn, gain_mlp = attn_gain.astype(floats), mlp_gain.astype(floats)

    def base(j_of, core, pair_of, side_of):
        return (2 * j_of + core) * row_len + (2 * pair_of + side_of) * block

    where = jnp.stack([c, y, x]).astype(jnp.int32)
    slot = 2 * y + x
    joined = fetch_quarter(
        jnp.concatenate([query_weight, key_matrix, value_matrix], axis=1), where, slot
    )
    weight_o = fetch_quarter(output_weight, where, slot)
    weight_gate = fetch_quarter(gate_weight, where, slot)
    weight_up = fetch_quarter(up_weight, where, slot)
    weight_down = fetch_quarter(down_weight, where, slot)

    bases = [
        base(j, c, pair, side),
        base(j, 1 - c, pair, side),
        base(j, c, pair, 1 - side),
        base(j, 1 - c, pair, 1 - side),
    ]
    counts = [jnp.sum((segment_ids < item).astype(jnp.int32)) for item in range(1, 4)]
    segs = jnp.concatenate([lax.dynamic_slice_in_dim(segment_ids, b, block) for b in bases])
    index = jnp.concatenate([b + jnp.arange(block, dtype=jnp.int32) for b in bases])
    start = jnp.zeros_like(segs)
    for item in range(1, 4):
        start = jnp.where(segs == item, counts[item - 1], start)
    cosine, sine = rope_tables(index - start)
    index_row, start_row = index[None, :], start[None, :]
    starts4 = start.reshape(4, block)

    tokens32 = tokens.astype(floats)
    normed = rms_scale(tokens32, gain_attn).astype(halves)
    here_n, there_n = gather_group(normed)
    qs, kvs = [], []
    for n, part in enumerate((here_n, there_n)):
        lanes = slice(2 * n * block, 2 * (n + 1) * block)
        linear = dot_tt(joined, part)
        cos_n, sin_n = cosine[:, lanes], sine[:, lanes]
        turned = turn(linear[: q_cols + kv_cols], cos_n, sin_n)
        qs.append(turned[:q_cols].astype(halves))
        kvs.append(
            jnp.concatenate(
                [
                    turned[q_cols:].astype(halves),
                    (linear[q_cols + kv_cols :].astype(halves) * VSCALE).astype(halves),
                ]
            )
        )
    q_t = jnp.concatenate(qs, axis=1)

    pieces, piece_bases = [], []

    def there_or_far(present, value):
        return jnp.where(present, value, FAR_BASE)

    for n in range(2):
        side_n = side if n == 0 else 1 - side
        for cross in range(2):
            block_kv = kvs[n] if cross == 0 else send(kvs[n], "cross")
            from_x = send(block_kv, "x_up")
            from_y = send(block_kv, "y_up")
            from_relay = send(from_y, "relay")
            cores = (c, 1 - c) if cross == 0 else (1 - c, c)
            pair_of = pair if cross == 0 else 1 - pair
            for piece, j_of, present in (
                (block_kv, j, None),
                (from_x, j - 1, x == 1),
                (from_y, j - 2, y == 1),
                (from_relay, j - 1, (y == 1) & (x == 0)),
            ):
                pieces.append(piece)
                for core in cores:
                    where_from = base(j_of, core, pair_of, side_n)
                    piece_bases.append(
                        where_from if present is None else there_or_far(present, where_from)
                    )
    total_blocks = len(piece_bases)

    def padded(values):
        values = jnp.stack(values).astype(jnp.int32)
        return jnp.pad(values, (0, total_blocks - values.shape[0]))

    sc = jnp.stack(
        [
            padded(piece_bases),
            padded(bases),
            jnp.pad(starts4[:, 0], (0, total_blocks - 4)),
            jnp.pad(starts4[:, -1], (0, total_blocks - 4)),
        ]
    )
    context_t, log_total = attend_forward(sc, q_t, index_row, start_row, pieces)

    def halves_of(product):
        return product(slice(0, 2 * block)), product(slice(2 * block, 4 * block))

    here_o, there_o = halves_of(
        lambda lanes: lax.dot_general(
            context_t[:, lanes], weight_o, (((0,), (0,)), ((), ())), preferred_element_type=floats
        )
    )
    residual = tokens32 + scatter_group(here_o, there_o)

    mlp_normed = rms_scale(residual, gain_mlp).astype(halves)
    here_m, there_m = gather_group(mlp_normed)
    here_g, there_g = gather_group(out_grad)
    hiddens, d_gates, d_ups, outs, d_norms = [], [], [], [], []
    for part, grad in ((here_m, here_g), (there_m, there_g)):
        gate_pre = jnp.dot(part, weight_gate, preferred_element_type=floats)
        up_pre = jnp.dot(part, weight_up, preferred_element_type=floats)
        d_hidden = contract_cols(grad, weight_down)
        sigma = jax.nn.sigmoid(gate_pre)
        silu = gate_pre * sigma
        hiddens.append((silu * up_pre).astype(halves))
        d_gates.append(
            (d_hidden * up_pre * (sigma * (1.0 + gate_pre * (1.0 - sigma)))).astype(halves)
        )
        d_ups.append((d_hidden * silu).astype(halves))
    for n in range(2):
        d_norms.append(contract_cols(d_gates[n], weight_gate) + contract_cols(d_ups[n], weight_up))
    for n in range(2):
        outs.append(jnp.dot(hiddens[n], weight_down, preferred_element_type=floats))
    grad_mlp_normed = scatter_group(*d_norms)
    output = residual + scatter_group(*outs)
    mlp_full = jnp.concatenate([here_m, there_m])
    grad_full = jnp.concatenate([here_g, there_g])
    gate_grad = contract_rows(mlp_full, jnp.concatenate(d_gates)).astype(halves)
    up_grad = contract_rows(mlp_full, jnp.concatenate(d_ups)).astype(halves)
    down_grad = contract_rows(grad_full, jnp.concatenate(hiddens)).astype(halves)
    gate_sum = sum_rows_home(sum_rows_over_plane(gate_grad, x, y, True), odd)
    up_sum = sum_rows_home(sum_rows_over_plane(up_grad, x, y, False), odd)
    down_sum = sum_rows_home(sum_rows_over_plane(down_grad, x, y, True), odd)

    grad_part, mlp_gain_part = norm_back(residual, gain_mlp, grad_mlp_normed)
    grad_residual = out_grad.astype(floats) + grad_part
    here_e, there_e = gather_group(grad_residual.astype(halves))

    d_context_t = jnp.concatenate(
        [contract_cols(weight_o, here_e), contract_cols(weight_o, there_e)], axis=1
    ).astype(halves)
    attn_grad_full = jnp.concatenate([here_e, there_e])
    output_grad = dot_tt(attn_grad_full, context_t).astype(halves)
    output_sum = sum_rows_home(sum_rows_over_plane(output_grad, x, y, False), odd)
    delta = jnp.sum(
        (d_context_t.astype(floats) * context_t.astype(floats)).reshape(heads, HEAD_WIDTH, -1), axis=1
    )
    d_query_t, d_pieces = attend_backward(
        sc, q_t, d_context_t, log_total, delta * VSCALE, index_row, start_row, pieces
    )
    d_halves = []
    for n in range(2):
        sums = []
        for cross in range(2):
            own, from_x, from_y, from_relay = d_pieces[8 * n + 4 * cross : 8 * n + 4 * cross + 4]
            back = send(from_relay, "unrelay").astype(floats)
            from_y = (from_y.astype(floats) + back).astype(halves)
            sums.append(
                own.astype(floats)
                + send(from_x, "x_down").astype(floats)
                + send(from_y, "y_down").astype(floats)
            )
        d_halves.append(sums[0] + send(sums[1].astype(halves), "cross").astype(floats))
    d_kv = jnp.concatenate(d_halves, axis=1)
    d_turned = turn(jnp.concatenate([d_query_t, d_kv[:kv_cols]]), cosine, -sine)
    d_linear = jnp.concatenate([d_turned, d_kv[kv_cols:]]).astype(halves)
    normed_full = jnp.concatenate([here_n, there_n])
    here_d, there_d = halves_of(lambda lanes: dot_tt(d_linear[:, lanes], joined))
    grad_normed = scatter_group(here_d, there_d)
    proj_grad = lax.dot_general(
        normed_full, d_linear, (((0,), (1,)), ((), ())), preferred_element_type=floats
    ).astype(halves)
    proj_sum = sum_rows_home(sum_rows_over_plane(proj_grad, x, y, True), odd)
    grad_tokens_part, attn_gain_part = norm_back(tokens32, gain_attn, grad_normed)
    input_grad = grad_residual + grad_tokens_part

    gains = jnp.stack([attn_gain_part, mlp_gain_part])
    for way in ("core", "x", "y", "near", "far"):
        gains = gains + send(gains, way)
    per = gains.shape[1] // 8
    gains = lax.dynamic_slice_in_dim(gains, dp * per, per, axis=1)
    return (
        output.astype(halves),
        input_grad,
        gains[0],
        proj_sum[:, :q_cols],
        proj_sum[:, q_cols : q_cols + kv_cols],
        proj_sum[:, q_cols + kv_cols :],
        output_sum.T,
        gains[1],
        gate_sum,
        up_sum,
        down_sum.T,
    )


def solution(mesh):
    regroup = mesh.shape["dp"] == 8 and mesh.shape["tp"] == 4
    chosen = local_regrouped if regroup else local
    return jax.shard_map(
        chosen,
        mesh=mesh,
        in_specs=(
            P(("dp", "tp"), None),
            P(("dp", "tp"), None),
            P(),
            P(),
            P(None, "tp"),
            P(None, "tp"),
            P(None, "tp"),
            P("tp", None),
            P(),
            P(None, "tp"),
            P(None, "tp"),
            P("tp", None),
        ),
        out_specs=(
            P(("dp", "tp"), None),
            P(("dp", "tp"), None),
            P("dp"),
            P("dp", "tp"),
            P("dp", "tp"),
            P("dp", "tp"),
            P("tp", "dp"),
            P("dp"),
            P("dp", "tp"),
            P("dp", "tp"),
            P("tp", "dp"),
        ),
        check_vma=False,
    )
```

```python
import functools

import jax
import jax.numpy as jnp
from jax import lax
from jax.experimental import pallas as pl
from jax.experimental.pallas import tpu as pltpu
from jax.sharding import PartitionSpec as P

HEAD_WIDTH = 96
BLK = 256
LOG2E = 1.4426950408889634
SCORE = LOG2E * HEAD_WIDTH ** (-0.5)
VSCALE = 2.0 ** -9
floats = jnp.float32
halves = jnp.bfloat16


def dot_nn(a, b):
    return jnp.dot(a, b, preferred_element_type=floats)


def dot_nt(a, b):
    return lax.dot_general(a, b, (((1,), (1,)), ((), ())), preferred_element_type=floats)


def pair_state(sc, kb, qb):
    key_base = sc[0, kb]
    q_base, least, most = sc[1, qb], sc[2, qb], sc[3, qb]
    needed = (key_base <= q_base + (BLK - 1)) & (key_base + (BLK - 1) >= least)
    whole = (key_base + (BLK - 1) <= q_base) & (key_base >= most)
    return key_base, needed, whole


def allowed_mask(key_base, tok_ref, start_ref, lanes):
    keys = key_base + lax.broadcasted_iota(jnp.int32, (BLK, BLK), 0)
    return (keys <= tok_ref[0:1, lanes]) & (keys >= start_ref[0:1, lanes])


def fwd_kernel(n, width, first, last, sc, q_ref, tok_ref, start_ref, *refs):
    pieces = refs[:n]
    refs = refs[n:]
    if not first:
        acc_in, sum_in = refs[:2]
        refs = refs[2:]
    out_acc, out_sum = refs[:2]
    kv, keys_nat, acc, total, q_wide, sem = refs[2:]
    per = width // BLK
    for i in range(n):
        pltpu.make_async_copy(pieces[i], kv.at[i], sem.at[i]).start()
    if first:
        acc[...] = jnp.zeros_like(acc)
        total[...] = jnp.zeros_like(total)
    else:
        acc[...] = acc_in[...]
        total[...] = sum_in[...]
    for i in range(n):
        pltpu.make_async_copy(pieces[i], kv.at[i], sem.at[i]).wait()
    heads_kv = pieces[0].shape[0] // (2 * HEAD_WIDTH)
    group = q_ref.shape[0] // (heads_kv * HEAD_WIDTH)
    v_off = heads_kv * HEAD_WIDTH
    places = [
        (h, slice((h * group + g) * HEAD_WIDTH, (h * group + g + 1) * HEAD_WIDTH), slice(qb * BLK, (qb + 1) * BLK),
         slice(h * HEAD_WIDTH, (h + 1) * HEAD_WIDTH), slice((qb * group + g) * BLK, (qb * group + g + 1) * BLK), h * group + g)
        for h in range(heads_kv) for g in range(group) for qb in range(q_ref.shape[1] // BLK)
    ]
    for h, rows, lanes, wrows, wlanes, hd in places:
        q_wide[wrows, wlanes] = q_ref[rows, lanes]

    def key_block(kb, carry):
        piece = kb // per
        klanes = pl.ds(pl.multiple_of((kb % per) * BLK, BLK), BLK)
        for h in range(heads_kv):
            keys_nat[h] = kv[piece, h * HEAD_WIDTH : (h + 1) * HEAD_WIDTH, klanes].T

        def query_block(qb, carry):
            key_base, needed, whole = pair_state(sc, kb, qb)
            lanes = pl.ds(pl.multiple_of(qb * BLK, BLK), BLK)

            def unit(masked):
                wide = pl.ds(pl.multiple_of(qb * (group * BLK), group * BLK), group * BLK)
                if masked:
                    allowed = allowed_mask(key_base, tok_ref, start_ref, lanes)
                    allowed = jnp.concatenate([allowed] * group, axis=1)
                scores = [
                    dot_nn(keys_nat[h], q_wide[h * HEAD_WIDTH : (h + 1) * HEAD_WIDTH, wide])
                    for h in range(heads_kv)
                ]
                weights = [jnp.exp2(s * SCORE) for s in scores]
                if masked:
                    weights = [jnp.where(allowed, w, 0.0) for w in weights]
                sums = [jnp.sum(w, axis=0, keepdims=True) for w in weights]
                parts = [
                    dot_nn(
                        kv[piece, v_off + h * HEAD_WIDTH : v_off + (h + 1) * HEAD_WIDTH, klanes],
                        weights[h].astype(halves),
                    )
                    for h in range(heads_kv)
                ]
                for h in range(heads_kv):
                    total[h : h + 1, wide] += sums[h]
                    acc[h * HEAD_WIDTH : (h + 1) * HEAD_WIDTH, wide] += parts[h]

            pl.when(needed & whole)(lambda: unit(False))
            pl.when(needed & jnp.logical_not(whole))(lambda: unit(True))
            return carry

        return lax.fori_loop(0, q_ref.shape[1] // BLK, query_block, carry)

    lax.fori_loop(0, n * per, key_block, 0)
    if last:
        for h, rows, lanes, wrows, wlanes, hd in places:
            row = total[h : h + 1, wlanes]
            out_acc[rows, lanes] = (acc[wrows, wlanes] * ((1.0 / VSCALE) / row)).astype(halves)
            out_sum[hd : hd + 1, lanes] = jnp.log2(row)
    else:
        out_acc[...] = acc[...]
        out_sum[...] = total[...]


VM = pl.BlockSpec(memory_space=pltpu.VMEM)
SM = pl.BlockSpec(memory_space=pltpu.SMEM)
HB = pl.BlockSpec(memory_space=pl.ANY)


def attend_forward(sc, q_t, tok, start, pieces, state=None, last=True):
    n, width = len(pieces), pieces[0].shape[1]
    heads = q_t.shape[0] // HEAD_WIDTH
    heads_kv = pieces[0].shape[0] // (2 * HEAD_WIDTH)
    first = state is None
    tokens = q_t.shape[1]
    out_shape = (
        jax.ShapeDtypeStruct(q_t.shape, halves if last else floats),
        jax.ShapeDtypeStruct((heads, tokens), floats),
    )
    return pl.pallas_call(
        functools.partial(fwd_kernel, n, width, first, last),
        out_shape=out_shape,
        in_specs=[SM, VM, VM, VM] + [HB] * n + ([] if first else [VM, VM]),
        out_specs=(VM, VM),
        scratch_shapes=[
            pltpu.VMEM((n,) + pieces[0].shape, halves),
            pltpu.VMEM((heads_kv, BLK, HEAD_WIDTH), halves),
            pltpu.VMEM((heads_kv * HEAD_WIDTH, tokens * heads // heads_kv), floats),
            pltpu.VMEM((heads_kv, tokens * heads // heads_kv), floats),
            pltpu.VMEM((heads_kv * HEAD_WIDTH, tokens * heads // heads_kv), halves),
            pltpu.SemaphoreType.DMA((n,)),
        ],
        compiler_params=pltpu.CompilerParams(vmem_limit_bytes=40 << 20),
        name="attend_forward",
    )(sc, q_t, tok, start, *pieces, *(() if first else state))


def bwd_kernel(n, width, first, sc, q_ref, do_ref, log_ref, delta_ref, tok_ref, start_ref, *refs):
    pieces = refs[:n]
    refs = refs[n:]
    if not first:
        dq_in = refs[0]
        refs = refs[1:]
    dq_out = refs[0]
    douts = refs[1 : 1 + n]
    kv, dkv, keys_nat, vals_nat, acc, q_wide, do_wide, log_wide, delta_wide, dq_wide, sem, osem = refs[1 + n :]
    per = width // BLK
    for i in range(n):
        pltpu.make_async_copy(pieces[i], kv.at[i], sem.at[i]).start()
    for i in range(n):
        pltpu.make_async_copy(pieces[i], kv.at[i], sem.at[i]).wait()
    heads_kv = pieces[0].shape[0] // (2 * HEAD_WIDTH)
    group = q_ref.shape[0] // (heads_kv * HEAD_WIDTH)
    v_off = heads_kv * HEAD_WIDTH
    places = [
        (h, slice((h * group + g) * HEAD_WIDTH, (h * group + g + 1) * HEAD_WIDTH), slice(qb * BLK, (qb + 1) * BLK),
         slice(h * HEAD_WIDTH, (h + 1) * HEAD_WIDTH), slice((qb * group + g) * BLK, (qb * group + g + 1) * BLK), h * group + g)
        for h in range(heads_kv) for g in range(group) for qb in range(q_ref.shape[1] // BLK)
    ]
    for h, rows, lanes, wrows, wlanes, hd in places:
        q_wide[wrows, wlanes] = q_ref[rows, lanes]
        do_wide[wrows, wlanes] = do_ref[rows, lanes]
        log_wide[h : h + 1, wlanes] = log_ref[hd : hd + 1, lanes]
        delta_wide[h : h + 1, wlanes] = delta_ref[hd : hd + 1, lanes]
        dq_wide[wrows, wlanes] = jnp.zeros((HEAD_WIDTH, BLK), floats) if first else dq_in[rows, lanes]
    out_scale = (1.0 / VSCALE) * HEAD_WIDTH ** (-0.5)

    def key_block(kb, carry):
        piece = kb // per
        klanes = pl.ds(pl.multiple_of((kb % per) * BLK, BLK), BLK)
        for h in range(heads_kv):
            keys_nat[h] = kv[piece, h * HEAD_WIDTH : (h + 1) * HEAD_WIDTH, klanes].T
            vals_nat[h] = kv[piece, v_off + h * HEAD_WIDTH : v_off + (h + 1) * HEAD_WIDTH, klanes].T
        acc[...] = jnp.zeros_like(acc)

        def query_block(qb, carry):
            key_base, needed, whole = pair_state(sc, kb, qb)
            lanes = pl.ds(pl.multiple_of(qb * BLK, BLK), BLK)

            def unit(masked):
                wide = pl.ds(pl.multiple_of(qb * (group * BLK), group * BLK), group * BLK)
                if masked:
                    allowed = allowed_mask(key_base, tok_ref, start_ref, lanes)
                    allowed = jnp.concatenate([allowed] * group, axis=1)
                heads = range(heads_kv)
                krows = [slice(h * HEAD_WIDTH, (h + 1) * HEAD_WIDTH) for h in heads]
                vrows = [slice(v_off + h * HEAD_WIDTH, v_off + (h + 1) * HEAD_WIDTH) for h in heads]
                qt = [q_wide[krows[h], wide] for h in heads]
                dot = [do_wide[krows[h], wide] for h in heads]
                scores = [dot_nn(keys_nat[h], qt[h]) for h in heads]
                dprobs = [dot_nn(vals_nat[h], dot[h]) for h in heads]
                weights = [
                    jnp.exp2(scores[h] * SCORE - log_wide[h : h + 1, wide]) for h in heads
                ]
                if masked:
                    weights = [jnp.where(allowed, w, 0.0) for w in weights]
                ds = [
                    (weights[h] * (dprobs[h] - delta_wide[h : h + 1, wide])).astype(halves)
                    for h in heads
                ]
                dv = [dot_nt(dot[h], weights[h].astype(halves)) for h in heads]
                dk = [dot_nt(qt[h], ds[h]) for h in heads]
                dq = [dot_nn(kv[piece, krows[h], klanes], ds[h]) for h in heads]
                for h in heads:
                    acc[vrows[h], :] += dv[h]
                    acc[krows[h], :] += dk[h]
                    dq_wide[krows[h], wide] += dq[h]

            pl.when(needed & whole)(lambda: unit(False))
            pl.when(needed & jnp.logical_not(whole))(lambda: unit(True))
            return carry

        carry = lax.fori_loop(0, q_ref.shape[1] // BLK, query_block, carry)
        dkv[piece, 0:v_off, klanes] = (acc[0:v_off, :] * out_scale).astype(halves)
        dkv[piece, v_off:, klanes] = acc[v_off:, :].astype(halves)
        return carry

    lax.fori_loop(0, n * per, key_block, 0)
    for i in range(n):
        pltpu.make_async_copy(dkv.at[i], douts[i], osem.at[i]).start()
    for h, rows, lanes, wrows, wlanes, hd in places:
        dq_out[rows, lanes] = dq_wide[wrows, wlanes] * out_scale
    for i in range(n):
        pltpu.make_async_copy(dkv.at[i], douts[i], osem.at[i]).wait()


def attend_backward(sc, q_t, do_t, log_total, delta, tok, start, pieces):
    n, width = len(pieces), pieces[0].shape[1]
    heads_kv = pieces[0].shape[0] // (2 * HEAD_WIDTH)
    wide = q_t.shape[0] // (heads_kv * HEAD_WIDTH) * q_t.shape[1]
    outs = pl.pallas_call(
        functools.partial(bwd_kernel, n, width, True),
        out_shape=(jax.ShapeDtypeStruct(q_t.shape, floats),)
        + tuple(jax.ShapeDtypeStruct(p.shape, halves) for p in pieces),
        in_specs=[SM] + [VM] * 6 + [HB] * n,
        out_specs=(VM,) + (HB,) * n,
        scratch_shapes=[
            pltpu.VMEM((n,) + pieces[0].shape, halves),
            pltpu.VMEM((n,) + pieces[0].shape, halves),
            pltpu.VMEM((heads_kv, BLK, HEAD_WIDTH), halves),
            pltpu.VMEM((heads_kv, BLK, HEAD_WIDTH), halves),
            pltpu.VMEM((pieces[0].shape[0], BLK), floats),
            pltpu.VMEM((heads_kv * HEAD_WIDTH, wide), halves),
            pltpu.VMEM((heads_kv * HEAD_WIDTH, wide), halves),
            pltpu.VMEM((heads_kv, wide), floats),
            pltpu.VMEM((heads_kv, wide), floats),
            pltpu.VMEM((heads_kv * HEAD_WIDTH, wide), floats),
            pltpu.SemaphoreType.DMA((n,)),
            pltpu.SemaphoreType.DMA((n,)),
        ],
        compiler_params=pltpu.CompilerParams(vmem_limit_bytes=44 << 20),
        name="attend_backward",
    )(sc, q_t, do_t, log_total, delta, tok, start, *pieces)
    return outs[0], list(outs[1:])


eps_norm = 1e-05
rope_base = 100000.0
reach_limit = 8


def shifted(block, axis, distance):
    devices = range(lax.axis_size(axis))
    route = [(i - distance, i) for i in devices if i - distance in devices]
    return lax.ppermute(block, axis, route)


def rms_scale(value_vectors, gain_vec):
    return (
        value_vectors
        * lax.rsqrt(jnp.mean(value_vectors * value_vectors, axis=-1, keepdims=True) + eps_norm)
        * gain_vec
    )


def rotary_turn(value_vectors, token_positions, heads):
    half_width = HEAD_WIDTH // 2
    inverse = 1.0 / rope_base ** (jnp.arange(half_width, dtype=jnp.float32) * 2.0 / HEAD_WIDTH)
    angles = token_positions.astype(jnp.float32)[:, None] * inverse[None, :]
    cosine = jnp.cos(angles)[:, None, :]
    sine_part = jnp.sin(angles)[:, None, :]
    shaped = value_vectors.reshape(value_vectors.shape[0], heads, HEAD_WIDTH)
    first_half = shaped[..., :half_width]
    second = shaped[..., half_width:]
    turned = jnp.concatenate(
        [first_half * cosine - second * sine_part, second * cosine + first_half * sine_part],
        axis=-1,
    )
    return turned.reshape(value_vectors.shape)


def swiglu(gate_pre, up_pre):
    return jax.nn.silu(gate_pre) * up_pre


def contract_rows(left_side, right_side):
    return lax.dot_general(
        left_side, right_side, (((0,), (0,)), ((), ())), preferred_element_type=jnp.float32
    )


def contract_cols(left_side, right_side):
    return lax.dot_general(
        left_side, right_side, (((1,), (1,)), ((), ())), preferred_element_type=jnp.float32
    )


def local(
    tokens,
    out_grad,
    segment_ids,
    attn_gain,
    query_weight,
    key_matrix,
    value_matrix,
    output_weight,
    mlp_gain,
    gate_weight,
    up_weight,
    down_weight,
):
    floats = jnp.float32
    halves = jnp.bfloat16
    shard_rows = tokens.shape[0]
    row_len = shard_rows * lax.axis_size("tp")
    row_index = lax.axis_index("dp")
    reach = min(reach_limit, lax.axis_size("dp") // 2)
    heads_q = query_weight.shape[1] // HEAD_WIDTH
    heads_kv = key_matrix.shape[1] // HEAD_WIDTH
    group_width = heads_q // heads_kv
    q_cols = heads_q * HEAD_WIDTH
    kv_cols = heads_kv * HEAD_WIDTH
    score_scale = HEAD_WIDTH ** (-0.5)
    row_first = row_index * row_len
    seg_row = lax.dynamic_slice_in_dim(segment_ids, row_first, row_len)
    index_row = row_first + jnp.arange(row_len, dtype=jnp.int32)
    every_index = jnp.arange(segment_ids.shape[0], dtype=jnp.int32)
    marks = (segment_ids[1:] != segment_ids[:-1]).astype(jnp.int32)
    starts = jnp.concatenate([jnp.zeros((1,), jnp.int32), marks * every_index[1:]])
    is_at = (starts[None, :] <= index_row[:, None]).astype(jnp.int32)
    token_positions = index_row - jnp.max(is_at * starts[None, :], axis=1)
    tokens32 = tokens.astype(floats)
    gain_attn = attn_gain.astype(floats)
    gain_mlp = mlp_gain.astype(floats)
    normed = rms_scale(tokens32, gain_attn).astype(halves)
    normed_full = lax.all_gather(normed, "tp", axis=0, tiled=True)
    joined = jnp.concatenate([query_weight, key_matrix, value_matrix], axis=1)
    projected = jnp.dot(normed_full, joined, preferred_element_type=floats)
    q_linear = projected[:, :q_cols]
    key_linear_out = projected[:, q_cols : q_cols + kv_cols]
    query_vectors = rotary_turn(q_linear, token_positions, heads_q).astype(halves)
    key_vectors = rotary_turn(key_linear_out, token_positions, heads_kv).astype(halves)
    value_vectors = projected[:, q_cols + kv_cols :].astype(halves)
    query_heads = query_vectors.reshape(row_len, heads_kv, group_width, HEAD_WIDTH)
    held_blocks = [(key_vectors, value_vectors)]
    moving = (key_vectors, value_vectors)
    for step_hop in range(reach):
        moving = shifted((moving[0], moving[1]), "dp", 1)
        held_blocks.append(moving)

    def block_mask(step_hop):
        key_row = row_index - step_hop
        seg_keys = lax.dynamic_slice_in_dim(segment_ids, jnp.maximum(key_row, 0) * row_len, row_len)
        key_index = key_row * row_len + jnp.arange(row_len, dtype=jnp.int32)
        return (seg_keys[None, :] == seg_row[:, None]) & (key_index[None, :] <= index_row[:, None])

    def block_needed(step_hop):
        last_key = jnp.maximum((row_index - step_hop + 1) * row_len - 1, 0)
        return (row_index >= step_hop) & (segment_ids[last_key] == seg_row[0])

    block_masks = [block_mask(step_hop) for step_hop in range(reach + 1)]

    def apply_block(step_hop, update, state_in):
        key_block, value_block = held_blocks[step_hop]
        if step_hop == 0:
            return update(state_in, key_block, value_block, block_masks[0])
        return lax.cond(
            block_needed(step_hop),
            update,
            lambda state_kept, key_skip, value_skip, mask_skip: state_kept,
            state_in,
            key_block,
            value_block,
            block_masks[step_hop],
        )

    def scores(key_block, allowed):
        raw_scores = jnp.einsum(
            "qhgd,khd->hgqk",
            query_heads,
            key_block.reshape(row_len, heads_kv, HEAD_WIDTH),
            preferred_element_type=floats,
        )
        return jnp.where(allowed, raw_scores * score_scale, -jnp.inf)

    def add_online(state_in, key_block, value_block, allowed):
        run_max, run_total, run_sum = state_in
        block_scores = scores(key_block, allowed)
        new_max = jnp.maximum(run_max, jnp.max(block_scores, axis=-1))
        factor = jnp.exp(run_max - new_max)
        weights = jnp.exp(block_scores - new_max[..., None])
        run_total = run_total * factor + jnp.sum(weights, axis=-1)
        run_sum = run_sum * jnp.moveaxis(factor, 2, 0)[..., None] + jnp.einsum(
            "hgqk,khd->qhgd",
            weights.astype(halves),
            value_block.reshape(row_len, heads_kv, HEAD_WIDTH),
            preferred_element_type=floats,
        )
        return (new_max, run_total, run_sum)

    online = (
        jnp.full((heads_kv, group_width, row_len), -jnp.inf, floats),
        jnp.zeros((heads_kv, group_width, row_len), floats),
        jnp.zeros((row_len, heads_kv, group_width, HEAD_WIDTH), floats),
    )
    for step_hop in range(reach + 1):
        online = apply_block(step_hop, add_online, online)
    run_max, run_total, run_sum = online
    log_total = (run_max + jnp.log(run_total))[..., None]
    context_heads = (run_sum / jnp.moveaxis(run_total, 2, 0)[..., None]).astype(halves)
    context = context_heads.reshape(row_len, q_cols)
    residual = tokens32 + lax.psum_scatter(
        jnp.dot(context, output_weight, preferred_element_type=floats).astype(jnp.bfloat16),
        "tp",
        scatter_dimension=0,
        tiled=True,
    ).astype(jnp.float32)
    mlp_normed = rms_scale(residual, gain_mlp).astype(halves)
    mlp_full = lax.all_gather(mlp_normed, "tp", axis=0, tiled=True)
    gate_pre = jnp.dot(mlp_full, gate_weight, preferred_element_type=floats)
    up_pre = jnp.dot(mlp_full, up_weight, preferred_element_type=floats)
    hidden = swiglu(gate_pre, up_pre).astype(halves)
    output = residual + lax.psum_scatter(
        jnp.dot(hidden, down_weight, preferred_element_type=floats).astype(jnp.bfloat16),
        "tp",
        scatter_dimension=0,
        tiled=True,
    ).astype(jnp.float32)
    grad_full = lax.all_gather(out_grad, "tp", axis=0, tiled=True)
    grad_hidden = contract_cols(grad_full, down_weight)
    down_grad = contract_rows(grad_full, hidden)
    silu_back = jax.vjp(swiglu, gate_pre, up_pre)[1]
    grad_gate, grad_up = silu_back(grad_hidden)
    grad_gate = grad_gate.astype(halves)
    grad_up = grad_up.astype(halves)
    gate_grad = contract_rows(mlp_full, grad_gate)
    up_grad = contract_rows(mlp_full, grad_up)
    grad_mlp_normed = lax.psum_scatter(
        (contract_cols(grad_gate, gate_weight) + contract_cols(grad_up, up_weight)).astype(
            jnp.bfloat16
        ),
        "tp",
        scatter_dimension=0,
        tiled=True,
    ).astype(jnp.float32)
    mlp_norm_back = jax.vjp(rms_scale, residual, gain_mlp)[1]
    grad_residual_part, mlp_gain_part = mlp_norm_back(grad_mlp_normed)
    grad_residual = out_grad.astype(floats) + grad_residual_part
    attn_grad_full = lax.all_gather(grad_residual.astype(halves), "tp", axis=0, tiled=True)
    output_grad = contract_rows(attn_grad_full, context)
    grad_context = (
        contract_cols(attn_grad_full, output_weight)
        .astype(halves)
        .reshape(row_len, heads_kv, group_width, HEAD_WIDTH)
    )
    delta_col = jnp.einsum(
        "qhgd,qhgd->hgq", grad_context, context_heads, preferred_element_type=floats
    )[..., None]

    def add_grads(state_in, key_block, value_block, allowed):
        query_acc, key_acc, value_acc = state_in
        probabilities = jnp.exp(scores(key_block, allowed) - log_total)
        grad_probs = jnp.einsum(
            "qhgd,khd->hgqk",
            grad_context,
            value_block.reshape(row_len, heads_kv, HEAD_WIDTH),
            preferred_element_type=floats,
        )
        grad_scores = (probabilities * (grad_probs - delta_col)).astype(halves)
        key_heads = key_block.reshape(row_len, heads_kv, HEAD_WIDTH)
        query_acc = (
            query_acc
            + jnp.einsum("hgqk,khd->qhgd", grad_scores, key_heads, preferred_element_type=floats)
            * score_scale
        )
        key_acc = (
            key_acc
            + jnp.einsum(
                "hgqk,qhgd->khd", grad_scores, query_heads, preferred_element_type=floats
            ).reshape(row_len, kv_cols)
            * score_scale
        )
        value_acc = value_acc + jnp.einsum(
            "hgqk,qhgd->khd",
            probabilities.astype(halves),
            grad_context,
            preferred_element_type=floats,
        ).reshape(row_len, kv_cols)
        return (query_acc, key_acc, value_acc)

    query_acc = jnp.zeros((row_len, heads_kv, group_width, HEAD_WIDTH), floats)
    carried = (jnp.zeros((row_len, kv_cols), floats), jnp.zeros((row_len, kv_cols), floats))
    for step_hop in range(reach, 0, -1):
        query_acc, key_acc, value_acc = apply_block(
            step_hop, add_grads, (query_acc, carried[0], carried[1])
        )
        carried = (
            shifted(key_acc.astype(jnp.bfloat16), "dp", -1).astype(key_acc.dtype),
            shifted(value_acc.astype(jnp.bfloat16), "dp", -1).astype(value_acc.dtype),
        )
    query_acc, key_total, value_total = apply_block(
        0, add_grads, (query_acc, carried[0], carried[1])
    )
    query_back = jax.vjp(lambda linear: rotary_turn(linear, token_positions, heads_q), q_linear)[1]
    key_back = jax.vjp(
        lambda linear: rotary_turn(linear, token_positions, heads_kv), key_linear_out
    )[1]
    grad_q_linear = query_back(query_acc.reshape(row_len, q_cols))[0]
    grad_k_linear = key_back(key_total)[0]
    grads_joined = jnp.concatenate([grad_q_linear, grad_k_linear, value_total], axis=1).astype(
        halves
    )
    proj_grad = contract_rows(normed_full, grads_joined)
    grad_normed = lax.psum_scatter(
        contract_cols(grads_joined, joined).astype(jnp.bfloat16),
        "tp",
        scatter_dimension=0,
        tiled=True,
    ).astype(jnp.float32)
    attn_norm_back = jax.vjp(rms_scale, tokens32, gain_attn)[1]
    grad_tokens_part, attn_gain_part = attn_norm_back(grad_normed)
    input_grad = grad_residual + grad_tokens_part
    def scatter_rows(grad):
        return lax.psum_scatter(
            grad.astype(halves), "dp", scatter_dimension=0, tiled=True
        ).astype(floats)

    mlp_sums = scatter_rows(jnp.concatenate([gate_grad, up_grad, down_grad], axis=1))
    ff_cols = gate_weight.shape[1]
    gate_sum = mlp_sums[:, :ff_cols]
    up_sum = mlp_sums[:, ff_cols : 2 * ff_cols]
    down_sum = mlp_sums[:, 2 * ff_cols :]
    attn_sums = scatter_rows(jnp.concatenate([proj_grad, output_grad], axis=1))
    query_sum = attn_sums[:, :q_cols]
    key_sum = attn_sums[:, q_cols : q_cols + kv_cols]
    value_sum = attn_sums[:, q_cols + kv_cols : q_cols + 2 * kv_cols]
    output_sum = attn_sums[:, q_cols + 2 * kv_cols :]
    attn_gain_sum = lax.psum_scatter(attn_gain_part, "dp", scatter_dimension=0, tiled=True)
    mlp_gain_sum = lax.psum_scatter(mlp_gain_part, "dp", scatter_dimension=0, tiled=True)
    attn_gain_total, mlp_gain_total = lax.psum((attn_gain_sum, mlp_gain_sum), "tp")
    return (
        output.astype(halves),
        input_grad,
        attn_gain_total,
        query_sum,
        key_sum,
        value_sum,
        output_sum.T,
        mlp_gain_total,
        gate_sum,
        up_sum,
        down_sum.T,
    )


MESH = pl.DeviceIdType.MESH


def group_devices():
    dp, z = lax.axis_index("dp"), lax.axis_index("tp")
    beside = (dp + 1 - 2 * lax.rem(dp, 2), z)
    near = (dp, z + 1 - 2 * lax.rem(z, 2))
    return beside, near


def meet(devices):
    barrier = pltpu.get_barrier_semaphore()
    for device in devices:
        pl.semaphore_signal(barrier, inc=1, device_id=device, device_id_type=MESH)
    pl.semaphore_wait(barrier, len(devices))


def tiles(total, step, body):
    def one(i, carry):
        body(pl.ds(pl.multiple_of(i * step, step), step))
        return carry

    lax.fori_loop(0, total // step, one, 0)


CHUNKS = 4


class GroupSum:
    copies = 2 + CHUNKS

    def __init__(self, first, sems, bufs, devices):
        self.first, (self.ss, self.rs), self.bufs = first, sems, bufs
        self.beside, self.near = devices

    def remote(self, i, src, dst, device):
        i = self.first + i
        return pltpu.make_async_remote_copy(
            src_ref=src, dst_ref=dst, send_sem=self.ss.at[i], recv_sem=self.rs.at[i],
            device_id=device, device_id_type=MESH,
        )

    def run(self, product):
        part_near, part_own, out_far, out_beside, out_near, in_near, in_own, in_sum = self.bufs

        def put_there(cols, value):
            rows = value.shape[0] // 2
            part_near[:, cols] = value[:rows]
            out_far[:, cols] = value[rows:].astype(halves)

        def put_here(cols, value):
            rows = value.shape[0] // 2
            part_own[:, cols] = value[:rows]
            out_beside[:, cols] = value[rows:].astype(halves)

        product(1, put_there)
        self.far = self.remote(0, out_far, in_near, self.beside)
        self.far.start()
        product(0, put_here)
        self.side = self.remote(1, out_beside, in_own, self.beside)
        self.side.start()
        self.far.wait_recv()
        rows = part_near.shape[0] // CHUNKS
        self.sums = []
        for k in range(CHUNKS):
            at = pl.ds(k * rows, rows)
            out_near[at, :] = (part_near[at, :] + in_near[at, :].astype(floats)).astype(halves)
            copy = self.remote(2 + k, out_near.at[at], in_sum.at[at], self.near)
            copy.start()
            self.sums.append(copy)

    def take(self, k):
        part_near, part_own, out_far, out_beside, out_near, in_near, in_own, in_sum = self.bufs
        if k == 0:
            self.side.wait_recv()
        self.sums[k].wait_recv()
        rows = part_own.shape[0] // CHUNKS
        at = pl.ds(k * rows, rows)
        return part_own[at, :] + in_own[at, :].astype(floats) + in_sum[at, :].astype(floats)

    def finish(self):
        for copy in (self.far, self.side, *self.sums):
            copy.wait_send()


class GroupGather:
    copies = 3 * CHUNKS

    def __init__(self, first, sems, full, block, devices):
        self.first, (self.ss, self.rs), self.full, self.block = first, sems, full, block
        self.beside, self.near = devices
        self.sent = []

    def remote(self, i, src, dst, device):
        i = self.first + i
        return pltpu.make_async_remote_copy(
            src_ref=src, dst_ref=dst, send_sem=self.ss.at[i], recv_sem=self.rs.at[i],
            device_id=device, device_id_type=MESH,
        )

    def slot(self, n, k):
        rows = self.block // CHUNKS
        return self.full.at[pl.ds(n * self.block + k * rows, rows)]

    def put(self, k):
        for i, (n, device) in enumerate(((2, self.near), (1, self.beside))):
            copy = self.remote(i * CHUNKS + k, self.slot(0, k), self.slot(n, k), device)
            copy.start()
            self.sent.append((i, copy))

    def wait_here(self):
        for i, copy in self.sent:
            if i == 1:
                copy.wait_recv()

    def wait_there(self):
        relays = []
        k = 0
        for i, copy in self.sent:
            if i == 0:
                copy.wait_recv()
                relay = self.remote(2 * CHUNKS + k, self.slot(2, k), self.slot(3, k), self.beside)
                relay.start()
                relays.append(relay)
                k += 1
        for relay in relays:
            relay.wait_recv()
        self.sent += [(2, relay) for relay in relays]

    def finish(self):
        for _, copy in self.sent:
            copy.wait_send()


def start_weight(odd, slots, own, pieces, out, sem):
    rows = pieces[0].shape[0]

    @pl.when(odd == 0)
    def _():
        pltpu.make_async_copy(own, out, sem.at[0]).start()

    @pl.when(odd != 0)
    def _():
        for i in range(4):
            pltpu.make_async_copy(pieces[i], out.at[pl.ds(slots[i] * rows, rows)], sem.at[i]).start()


def wait_weight(odd, slots, own, pieces, out, sem):
    rows = pieces[0].shape[0]

    @pl.when(odd == 0)
    def _():
        pltpu.make_async_copy(own, out, sem.at[0]).wait()

    @pl.when(odd != 0)
    def _():
        for i in range(4):
            pltpu.make_async_copy(pieces[i], out.at[pl.ds(slots[i] * rows, rows)], sem.at[i]).wait()


def mid_kernel(ctx_ref, tok_ref, gain_ref, grad_refs, weight_refs, outs, scratch):
    (res_out, gres_out, e_full, part_out, gate_out, up_out, down_out, dctx_out, delta_out, gain_out) = outs
    (ctx, g_full, m_full, dh, hid, dgate, dup, w_o, w_g, w_u, w_d, *bufs, ss, rs, wsem, gsem) = scratch
    dp = lax.axis_index("dp")
    odd = lax.rem(dp, 2)
    x, y = lax.rem(dp // 2, 2), dp // 4
    slots = (2 * y + x, 2 * y + 1 - x, 2 - 2 * y + x, 3 - 2 * y - x)
    devices = group_devices()
    block, width = tok_ref.shape
    two = 2 * block
    hidden = w_g.shape[1]
    weights = [
        (odd, slots, weight_refs[5 * i], weight_refs[5 * i + 1 : 5 * i + 5], out, wsem.at[i])
        for i, out in enumerate((w_o, w_d, w_g, w_u))
    ]
    start_weight(*weights[0])
    grads = [
        pltpu.make_async_copy(grad_refs[i], g_full.at[pl.ds(i * block, block)], gsem.at[i])
        for i in range(4)
    ]
    for copy in grads:
        copy.start()
    for weight in weights[1:]:
        start_weight(*weight)
    ctx[...] = ctx_ref[...].T
    meet(devices)

    sum_one = GroupSum(0, (ss, rs), bufs, devices)
    first = GroupSum.copies
    gather_one = GroupGather(first, (ss, rs), m_full, block, devices)
    first += GroupGather.copies
    sum_two = GroupSum(first, (ss, rs), bufs, devices)
    first += GroupSum.copies
    gather_two = GroupGather(first, (ss, rs), e_full, block, devices)

    def project(k, put):
        rows = slice(k * two, (k + 1) * two)
        tiles(width, 256, lambda cols: put(cols, dot_nn(ctx[rows, :], w_o[:, cols])))

    wait_weight(*weights[0])
    sum_one.run(project)
    wait_weight(*weights[1])
    for copy in grads:
        copy.wait()

    def back_hidden(cols):
        for rows in (slice(0, two), slice(two, 2 * two)):
            dh[rows, cols] = dot_nt(g_full[rows, :], w_d[cols, :]).astype(halves)

    tiles(hidden, 256, back_hidden)
    chunk = block // CHUNKS
    for k in range(CHUNKS):
        at = pl.ds(k * chunk, chunk)
        res = tok_ref[at, :].astype(floats) + sum_one.take(k)
        res_out[at, :] = res
        root = lax.rsqrt(jnp.mean(res * res, axis=-1, keepdims=True) + eps_norm)
        m_full[at, :] = (res * root * gain_ref[...]).astype(halves)
        gather_one.put(k)
    sum_one.finish()

    def activate(k):
        rows = slice(k * two, (k + 1) * two)

        def one(cols):
            gate_pre = dot_nn(m_full[rows, :], w_g[:, cols])
            up_pre = dot_nn(m_full[rows, :], w_u[:, cols])
            back = dh[rows, cols].astype(floats)
            sigma = 1.0 / (1.0 + jnp.exp(-gate_pre))
            silu = gate_pre * sigma
            hid[rows, cols] = (silu * up_pre).astype(halves)
            dgate[rows, cols] = (back * up_pre * (sigma + silu * (1.0 - sigma))).astype(halves)
            dup[rows, cols] = (back * silu).astype(halves)

        tiles(hidden, 256, one)

    def partial_out(k):
        rows = slice(k * two, (k + 1) * two)

        def one(cols):
            part_out[rows, cols] = dot_nn(hid[rows, :], w_d[:, cols]).astype(halves)

        tiles(width, 256, one)

    wait_weight(*weights[2])
    wait_weight(*weights[3])
    gather_one.wait_here()
    activate(0)
    partial_out(0)
    gather_one.wait_there()
    activate(1)
    gather_one.finish()

    def back_norm(k, put):
        rows = slice(k * two, (k + 1) * two)
        tiles(
            width,
            256,
            lambda cols: put(
                cols, dot_nt(dgate[rows, :], w_g[cols, :]) + dot_nt(dup[rows, :], w_u[cols, :])
            ),
        )

    def outer(left, right, out):
        def one(rows):
            out[rows, :] = lax.dot_general(
                left[:, rows], right[...], (((0,), (0,)), ((), ())), preferred_element_type=floats
            ).astype(halves)

        tiles(width, 256, one)

    sum_two.run(back_norm)
    partial_out(1)
    outer(g_full, hid, down_out)
    outer(m_full, dgate, gate_out)
    gain_out[...] = jnp.zeros_like(gain_out)
    for k in range(CHUNKS):
        at = pl.ds(k * chunk, chunk)
        back = sum_two.take(k)
        res = res_out[at, :]
        root = lax.rsqrt(jnp.mean(res * res, axis=-1, keepdims=True) + eps_norm)
        weighted = back * gain_ref[...]
        slope = jnp.mean(weighted * res, axis=-1, keepdims=True)
        grad = g_full[at, :].astype(floats) + root * weighted - res * (root * root * root * slope)
        gain_out[...] += jnp.sum(back * res * root, axis=0, keepdims=True)
        gres_out[at, :] = grad
        e_full[at, :] = grad.astype(halves)
        gather_two.put(k)
    sum_two.finish()
    outer(m_full, dup, up_out)

    def back_context(k):
        lanes = slice(k * two, (k + 1) * two)
        grad = dot_nt(w_o[...], e_full[lanes, :]).astype(halves)
        dctx_out[:, lanes] = grad
        prod = grad.astype(floats) * ctx_ref[:, lanes].astype(floats)
        for hd in range(delta_out.shape[0]):
            delta_out[hd : hd + 1, lanes] = VSCALE * jnp.sum(
                prod[hd * HEAD_WIDTH : (hd + 1) * HEAD_WIDTH], axis=0, keepdims=True
            )

    gather_two.wait_here()
    back_context(0)
    gather_two.wait_there()
    back_context(1)
    gather_two.finish()


def middle(context_t, tokens, gain, grads, weights):
    q_cols, group = context_t.shape
    block, width = tokens.shape
    hidden = weights[2][0].shape[1]
    flat = [ref for weight in weights for ref in weight]
    shape = jax.ShapeDtypeStruct
    out_shape = (
        shape((block, width), floats),
        shape((block, width), floats),
        shape((group, width), halves),
        shape((group, width), halves),
        shape((width, hidden), halves),
        shape((width, hidden), halves),
        shape((width, hidden), halves),
        shape((q_cols, group), halves),
        shape((q_cols // HEAD_WIDTH, group), floats),
        shape((1, width), floats),
    )
    copies = 2 * (GroupSum.copies + GroupGather.copies)
    scratch = [
        pltpu.VMEM((group, q_cols), halves),
        pltpu.VMEM((group, width), halves),
        pltpu.VMEM((group, width), halves),
        pltpu.VMEM((group, hidden), halves),
        pltpu.VMEM((group, hidden), halves),
        pltpu.VMEM((group, hidden), halves),
        pltpu.VMEM((group, hidden), halves),
        *[pltpu.VMEM(weight[0].shape, halves) for weight in (weights[0], weights[2], weights[3], weights[1])],
        *[pltpu.VMEM((block, width), floats)] * 2,
        *[pltpu.VMEM((block, width), halves)] * 6,
        pltpu.SemaphoreType.DMA((copies,)),
        pltpu.SemaphoreType.DMA((copies,)),
        pltpu.SemaphoreType.DMA((4, 4)),
        pltpu.SemaphoreType.DMA((4,)),
    ]

    def kernel(*refs):
        ctx_ref, tok_ref, gain_ref = refs[:3]
        rest = refs[3:]
        mid_kernel(
            ctx_ref, tok_ref, gain_ref, rest[:4], rest[4 : 4 + len(flat)],
            rest[4 + len(flat) : 14 + len(flat)], rest[14 + len(flat) :],
        )

    return pl.pallas_call(
        kernel,
        out_shape=out_shape,
        in_specs=[VM] * 3 + [HB] * (4 + len(flat)),
        out_specs=(VM,) * 10,
        scratch_shapes=scratch,
        compiler_params=pltpu.CompilerParams(
            collective_id=1, has_side_effects=True, vmem_limit_bytes=62 << 20
        ),
        name="middle",
    )(context_t, tokens, gain, *grads, *flat)


def routes(target):
    pairs = []
    for index in range(32):
        dp, z = divmod(index, 4)
        there = target(dp // 4, dp // 2 % 2, dp % 2, z)
        if there is not None:
            y, x, c, z = there
            pairs.append((index, (y * 4 + x * 2 + c) * 4 + z))
    return pairs


ROUTES = {
    "core": routes(lambda y, x, c, z: (y, x, 1 - c, z)),
    "x": routes(lambda y, x, c, z: (y, 1 - x, c, z)),
    "y": routes(lambda y, x, c, z: (1 - y, x, c, z)),
    "near": routes(lambda y, x, c, z: (y, x, c, z ^ 1)),
    "far": routes(lambda y, x, c, z: (y, x, c, z ^ 2)),
    "cross": routes(lambda y, x, c, z: (y, x, 1 - c, z ^ 2)),
    "odd_far": routes(lambda y, x, c, z: (y, x, c, z ^ 2) if c else None),
    "odd_x": routes(lambda y, x, c, z: (y, 1 - x, c, z) if c else None),
    "odd_y": routes(lambda y, x, c, z: (1 - y, x, c, z) if c else None),
    "odd_xy": routes(lambda y, x, c, z: (1 - y, 1 - x, c, z) if c else None),
    "home": routes(lambda y, x, c, z: (y, x, 0, z ^ 2) if c else (y, x, 1, z)),
    "x_up": routes(lambda y, x, c, z: None if x else (y, 1, c, z)),
    "y_up": routes(lambda y, x, c, z: None if y else (1, x, c, z)),
    "x_down": routes(lambda y, x, c, z: (y, 0, c, z) if x else None),
    "y_down": routes(lambda y, x, c, z: (0, x, c, z) if y else None),
    "relay": routes(lambda y, x, c, z: (1, 0, c, z) if x and y else None),
    "unrelay": routes(lambda y, x, c, z: (1, 1, c, z) if y and not x else None),
}
FAR_BASE = 1 << 24


def send(block, way):
    return lax.ppermute(block, ("dp", "tp"), ROUTES[way])


def assemble_kernel(where, own_ref, a_ref, x_ref, y_ref, xy_ref, out_ref, sem):
    odd, y, x = where[0], where[1], where[2]
    rows = a_ref.shape[0]

    @pl.when(odd == 0)
    def _():
        copy = pltpu.make_async_copy(own_ref, out_ref, sem.at[0])
        copy.start()
        copy.wait()

    @pl.when(odd != 0)
    def _():
        copies = []
        for i, (ref, slot) in enumerate(
            (
                (a_ref, 2 * y + x),
                (x_ref, 2 * y + (1 - x)),
                (y_ref, 2 * (1 - y) + x),
                (xy_ref, 2 * (1 - y) + (1 - x)),
            )
        ):
            copies.append(
                pltpu.make_async_copy(ref, out_ref.at[pl.ds(slot * rows, rows)], sem.at[i])
            )
        for copy in copies:
            copy.start()
        for copy in copies:
            copy.wait()


def fetch_quarter(weight, where, slot):
    rows = weight.shape[0] // 4
    part = send(lax.dynamic_slice_in_dim(weight, slot * rows, rows), "odd_far")
    pieces = (part, send(part, "odd_x"), send(part, "odd_y"), send(part, "odd_xy"))
    return pl.pallas_call(
        assemble_kernel,
        out_shape=jax.ShapeDtypeStruct(weight.shape, weight.dtype),
        in_specs=[SM] + [HB] * 5,
        out_specs=HB,
        scratch_shapes=[pltpu.SemaphoreType.DMA((4,))],
        compiler_params=pltpu.CompilerParams(vmem_limit_bytes=4 << 20),
        name="assemble",
    )(where, weight, *pieces)


def fetch_pieces(weight, slot):
    rows = weight.shape[0] // 4
    part = send(lax.dynamic_slice_in_dim(weight, slot * rows, rows), "odd_far")
    return weight, part, send(part, "odd_x"), send(part, "odd_y"), send(part, "odd_xy")


def gather_blocks(block):
    near = send(block, "near")
    return block, send(block, "core"), near, send(near, "core")


def gather_group(block):
    near = send(block, "near")
    beside = send(block, "core")
    return jnp.concatenate([block, beside]), jnp.concatenate([near, send(near, "core")])


def scatter_group(here, there):
    rows = here.shape[0] // 2
    there_sum = there[:rows] + send(there[rows:].astype(halves), "core").astype(floats)
    here_sum = here[:rows].astype(floats) + send(here[rows:].astype(halves), "core").astype(floats)
    return here_sum + send(there_sum.astype(halves), "near").astype(floats)


def dot_tt(a, b):
    return lax.dot_general(a, b, (((0,), (1,)), ((), ())), preferred_element_type=floats)


def rope_tables(positions):
    half_width = HEAD_WIDTH // 2
    inverse = 1.0 / rope_base ** (jnp.arange(half_width, dtype=floats) * 2.0 / HEAD_WIDTH)
    angles = inverse[:, None] * positions.astype(floats)[None, :]
    return jnp.cos(angles), jnp.sin(angles)


def turn(linear, cosine, sine):
    shaped = linear.reshape(-1, 2, HEAD_WIDTH // 2, linear.shape[-1])
    one, two = shaped[:, 0], shaped[:, 1]
    turned = jnp.stack([one * cosine - two * sine, two * cosine + one * sine], axis=1)
    return turned.reshape(linear.shape)


def norm_back(vectors, gain, grad):
    root = lax.rsqrt(jnp.mean(vectors * vectors, axis=-1, keepdims=True) + eps_norm)
    weighted = grad * gain
    slope = jnp.mean(weighted * vectors, axis=-1, keepdims=True)
    back = root * weighted - vectors * (root * root * root * slope)
    return back, jnp.sum(grad * vectors * root, axis=0)


def sum_rows_over_plane(grad, x, y, x_first):
    shaped = grad.reshape(2, 2, -1, grad.shape[-1])

    def pick(array, at, axis):
        return lax.dynamic_index_in_dim(array, at, axis, keepdims=False)

    axes = (("x", x, 1), ("y", y, 0)) if x_first else (("y", y, 0), ("x", x, 1))
    (way, at, axis), (way_two, at_two, _) = axes
    come = send(pick(shaped, 1 - at, axis), way)
    half = pick(shaped, at, axis).astype(floats) + come.astype(floats)
    come = send(pick(half, 1 - at_two, 0).astype(halves), way_two)
    return pick(half, at_two, 0) + come.astype(floats)


def sum_rows_home(part, odd):
    rows = part.shape[0] // 2
    first, second = part[:rows], part[rows:]
    one = send(jnp.where(odd, first, second).astype(halves), "home").astype(floats)
    two = send(second.astype(halves), "odd_far").astype(floats)
    return jnp.where(odd, one + two, first + one)


def local_regrouped(
    tokens,
    out_grad,
    segment_ids,
    attn_gain,
    query_weight,
    key_matrix,
    value_matrix,
    output_weight,
    mlp_gain,
    gate_weight,
    up_weight,
    down_weight,
):
    block = tokens.shape[0]
    row_len = 4 * block
    dp, z = lax.axis_index("dp"), lax.axis_index("tp")
    y, x, c = dp // 4, dp // 2 % 2, dp % 2
    j = dp // 2
    odd = c == 1
    pair, side = z // 2, z % 2
    q_cols, kv_cols = query_weight.shape[1], key_matrix.shape[1]
    heads = q_cols // HEAD_WIDTH
    group_width = q_cols // kv_cols
    ff_cols = gate_weight.shape[1]
    gain_attn, gain_mlp = attn_gain.astype(floats), mlp_gain.astype(floats)

    def base(j_of, core, pair_of, side_of):
        return (2 * j_of + core) * row_len + (2 * pair_of + side_of) * block

    where = jnp.stack([c, y, x]).astype(jnp.int32)
    slot = 2 * y + x
    joined = fetch_quarter(
        jnp.concatenate([query_weight, key_matrix, value_matrix], axis=1), where, slot
    )
    weights = [
        fetch_pieces(weight, slot) for weight in (output_weight, down_weight, gate_weight, up_weight)
    ]
    grads_g = gather_blocks(out_grad)

    bases = [
        base(j, c, pair, side),
        base(j, 1 - c, pair, side),
        base(j, c, pair, 1 - side),
        base(j, 1 - c, pair, 1 - side),
    ]
    counts = [jnp.sum((segment_ids < item).astype(jnp.int32)) for item in range(1, 4)]
    segs = jnp.concatenate([lax.dynamic_slice_in_dim(segment_ids, b, block) for b in bases])
    index = jnp.concatenate([b + jnp.arange(block, dtype=jnp.int32) for b in bases])
    start = jnp.zeros_like(segs)
    for item in range(1, 4):
        start = jnp.where(segs == item, counts[item - 1], start)
    cosine, sine = rope_tables(index - start)
    index_row, start_row = index[None, :], start[None, :]
    starts4 = start.reshape(4, block)

    tokens32 = tokens.astype(floats)
    normed = rms_scale(tokens32, gain_attn).astype(halves)
    here_n, there_n = gather_group(normed)
    qs, kvs = [], []
    for n, part in enumerate((here_n, there_n)):
        lanes = slice(2 * n * block, 2 * (n + 1) * block)
        linear = dot_tt(joined, part)
        cos_n, sin_n = cosine[:, lanes], sine[:, lanes]
        turned = turn(linear[: q_cols + kv_cols], cos_n, sin_n)
        qs.append(turned[:q_cols].astype(halves))
        kvs.append(
            jnp.concatenate(
                [
                    turned[q_cols:].astype(halves),
                    (linear[q_cols + kv_cols :].astype(halves) * VSCALE).astype(halves),
                ]
            )
        )
    q_t = jnp.concatenate(qs, axis=1)

    pieces, piece_bases = [], []

    def there_or_far(present, value):
        return jnp.where(present, value, FAR_BASE)

    for n in range(2):
        side_n = side if n == 0 else 1 - side
        for cross in range(2):
            block_kv = kvs[n] if cross == 0 else send(kvs[n], "cross")
            from_x = send(block_kv, "x_up")
            from_y = send(block_kv, "y_up")
            from_relay = send(from_y, "relay")
            cores = (c, 1 - c) if cross == 0 else (1 - c, c)
            pair_of = pair if cross == 0 else 1 - pair
            for piece, j_of, present in (
                (block_kv, j, None),
                (from_x, j - 1, x == 1),
                (from_y, j - 2, y == 1),
                (from_relay, j - 1, (y == 1) & (x == 0)),
            ):
                pieces.append(piece)
                for core in cores:
                    where_from = base(j_of, core, pair_of, side_n)
                    piece_bases.append(
                        where_from if present is None else there_or_far(present, where_from)
                    )
    total_blocks = len(piece_bases)

    def padded(values):
        values = jnp.stack(values).astype(jnp.int32)
        return jnp.pad(values, (0, total_blocks - values.shape[0]))

    sc = jnp.stack(
        [
            padded(piece_bases),
            padded(bases),
            jnp.pad(starts4[:, 0], (0, total_blocks - 4)),
            jnp.pad(starts4[:, -1], (0, total_blocks - 4)),
        ]
    )
    context_t, log_total = attend_forward(sc, q_t, index_row, start_row, pieces)

    (
        residual, grad_residual, attn_grad_full, part_out, gate_grad, up_grad, down_grad,
        d_context_t, delta, mlp_gain_part,
    ) = middle(context_t, tokens, gain_mlp[None, :], grads_g, weights)
    output = residual + scatter_group(part_out[: 2 * block], part_out[2 * block :])
    gate_sum = sum_rows_home(sum_rows_over_plane(gate_grad, x, y, True), odd)
    up_sum = sum_rows_home(sum_rows_over_plane(up_grad, x, y, False), odd)
    down_sum = sum_rows_home(sum_rows_over_plane(down_grad, x, y, True), odd)

    output_grad = dot_tt(attn_grad_full, context_t).astype(halves)
    output_sum = sum_rows_home(sum_rows_over_plane(output_grad, x, y, False), odd)
    d_query_t, d_pieces = attend_backward(
        sc, q_t, d_context_t, log_total, delta, index_row, start_row, pieces
    )
    d_halves = []
    for n in range(2):
        sums = []
        for cross in range(2):
            own, from_x, from_y, from_relay = d_pieces[8 * n + 4 * cross : 8 * n + 4 * cross + 4]
            back = send(from_relay, "unrelay").astype(floats)
            from_y = (from_y.astype(floats) + back).astype(halves)
            sums.append(
                own.astype(floats)
                + send(from_x, "x_down").astype(floats)
                + send(from_y, "y_down").astype(floats)
            )
        d_halves.append(sums[0] + send(sums[1].astype(halves), "cross").astype(floats))
    d_kv = jnp.concatenate(d_halves, axis=1)
    d_turned = turn(jnp.concatenate([d_query_t, d_kv[:kv_cols]]), cosine, -sine)
    d_linear = jnp.concatenate([d_turned, d_kv[kv_cols:]]).astype(halves)
    normed_full = jnp.concatenate([here_n, there_n])
    here_d = dot_tt(d_linear[:, : 2 * block], joined)
    there_d = dot_tt(d_linear[:, 2 * block :], joined)
    grad_normed = scatter_group(here_d, there_d)
    proj_grad = lax.dot_general(
        normed_full, d_linear, (((0,), (1,)), ((), ())), preferred_element_type=floats
    ).astype(halves)
    proj_sum = sum_rows_home(sum_rows_over_plane(proj_grad, x, y, True), odd)
    grad_tokens_part, attn_gain_part = norm_back(tokens32, gain_attn, grad_normed)
    input_grad = grad_residual + grad_tokens_part

    gains = jnp.stack([attn_gain_part, mlp_gain_part[0]])
    for way in ("core", "x", "y", "near", "far"):
        gains = gains + send(gains, way)
    per = gains.shape[1] // 8
    gains = lax.dynamic_slice_in_dim(gains, dp * per, per, axis=1)
    return (
        output.astype(halves),
        input_grad,
        gains[0],
        proj_sum[:, :q_cols],
        proj_sum[:, q_cols : q_cols + kv_cols],
        proj_sum[:, q_cols + kv_cols :],
        output_sum.T,
        gains[1],
        gate_sum,
        up_sum,
        down_sum.T,
    )


def solution(mesh):
    regroup = mesh.shape["dp"] == 8 and mesh.shape["tp"] == 4
    chosen = local_regrouped if regroup else local
    return jax.shard_map(
        chosen,
        mesh=mesh,
        in_specs=(
            P(("dp", "tp"), None),
            P(("dp", "tp"), None),
            P(),
            P(),
            P(None, "tp"),
            P(None, "tp"),
            P(None, "tp"),
            P("tp", None),
            P(),
            P(None, "tp"),
            P(None, "tp"),
            P("tp", None),
        ),
        out_specs=(
            P(("dp", "tp"), None),
            P(("dp", "tp"), None),
            P("dp"),
            P("dp", "tp"),
            P("dp", "tp"),
            P("dp", "tp"),
            P("tp", "dp"),
            P("dp"),
            P("dp", "tp"),
            P("dp", "tp"),
            P("tp", "dp"),
        ),
        check_vma=False,
    )
```

```python
import functools

import jax
import jax.numpy as jnp
from jax import lax
from jax.experimental import pallas as pl
from jax.experimental.pallas import tpu as pltpu
from jax.sharding import PartitionSpec as P

HEAD_WIDTH = 96
BLK = 256
LOG2E = 1.4426950408889634
SCORE = LOG2E * HEAD_WIDTH ** (-0.5)
VSCALE = 2.0 ** -9
floats = jnp.float32
halves = jnp.bfloat16


def dot_nn(a, b):
    return jnp.dot(a, b, preferred_element_type=floats)


def dot_nt(a, b):
    return lax.dot_general(a, b, (((1,), (1,)), ((), ())), preferred_element_type=floats)


def pair_state(sc, kb, qb):
    key_base = sc[0, kb]
    q_base, least, most = sc[1, qb], sc[2, qb], sc[3, qb]
    needed = (key_base <= q_base + (BLK - 1)) & (key_base + (BLK - 1) >= least)
    whole = (key_base + (BLK - 1) <= q_base) & (key_base >= most)
    return key_base, needed, whole


def allowed_mask(key_base, tok_ref, start_ref, lanes):
    keys = key_base + lax.broadcasted_iota(jnp.int32, (BLK, BLK), 0)
    return (keys <= tok_ref[0:1, lanes]) & (keys >= start_ref[0:1, lanes])


def fwd_kernel(n, width, first, last, sc, q_ref, tok_ref, start_ref, pieces, *refs):
    if not first:
        acc_in, sum_in = refs[:2]
        refs = refs[2:]
    out_acc, out_sum = refs[:2]
    kv, keys_nat, acc, total, q_wide, sem = refs[2:]
    per = width // BLK
    for i in range(n):
        pltpu.make_async_copy(pieces.at[i], kv.at[i], sem.at[i]).start()
    if first:
        acc[...] = jnp.zeros_like(acc)
        total[...] = jnp.zeros_like(total)
    else:
        acc[...] = acc_in[...]
        total[...] = sum_in[...]
    for i in range(n):
        pltpu.make_async_copy(pieces.at[i], kv.at[i], sem.at[i]).wait()
    heads_kv = pieces.shape[1] // (2 * HEAD_WIDTH)
    group = q_ref.shape[0] // (heads_kv * HEAD_WIDTH)
    v_off = heads_kv * HEAD_WIDTH
    places = [
        (h, slice((h * group + g) * HEAD_WIDTH, (h * group + g + 1) * HEAD_WIDTH), slice(qb * BLK, (qb + 1) * BLK),
         slice(h * HEAD_WIDTH, (h + 1) * HEAD_WIDTH), slice((qb * group + g) * BLK, (qb * group + g + 1) * BLK), h * group + g)
        for h in range(heads_kv) for g in range(group) for qb in range(q_ref.shape[1] // BLK)
    ]
    for h, rows, lanes, wrows, wlanes, hd in places:
        q_wide[wrows, wlanes] = q_ref[rows, lanes]

    def key_block(kb, carry):
        piece = kb // per
        klanes = pl.ds(pl.multiple_of((kb % per) * BLK, BLK), BLK)
        for h in range(heads_kv):
            keys_nat[h] = kv[piece, h * HEAD_WIDTH : (h + 1) * HEAD_WIDTH, klanes].T

        def query_block(qb, carry):
            key_base, needed, whole = pair_state(sc, kb, qb)
            lanes = pl.ds(pl.multiple_of(qb * BLK, BLK), BLK)

            def unit(masked):
                wide = pl.ds(pl.multiple_of(qb * (group * BLK), group * BLK), group * BLK)
                if masked:
                    allowed = allowed_mask(key_base, tok_ref, start_ref, lanes)
                    allowed = jnp.concatenate([allowed] * group, axis=1)
                scores = [
                    dot_nn(keys_nat[h], q_wide[h * HEAD_WIDTH : (h + 1) * HEAD_WIDTH, wide])
                    for h in range(heads_kv)
                ]
                weights = [jnp.exp2(s * SCORE) for s in scores]
                if masked:
                    weights = [jnp.where(allowed, w, 0.0) for w in weights]
                sums = [jnp.sum(w, axis=0, keepdims=True) for w in weights]
                parts = [
                    dot_nn(
                        kv[piece, v_off + h * HEAD_WIDTH : v_off + (h + 1) * HEAD_WIDTH, klanes],
                        weights[h].astype(halves),
                    )
                    for h in range(heads_kv)
                ]
                for h in range(heads_kv):
                    total[h : h + 1, wide] += sums[h]
                    acc[h * HEAD_WIDTH : (h + 1) * HEAD_WIDTH, wide] += parts[h]

            pl.when(needed & whole)(lambda: unit(False))
            pl.when(needed & jnp.logical_not(whole))(lambda: unit(True))
            return carry

        return lax.fori_loop(0, q_ref.shape[1] // BLK, query_block, carry)

    lax.fori_loop(0, n * per, key_block, 0)
    if last:
        for h, rows, lanes, wrows, wlanes, hd in places:
            row = total[h : h + 1, wlanes]
            out_acc[rows, lanes] = (acc[wrows, wlanes] * ((1.0 / VSCALE) / row)).astype(halves)
            out_sum[hd : hd + 1, lanes] = jnp.log2(row)
    else:
        out_acc[...] = acc[...]
        out_sum[...] = total[...]


VM = pl.BlockSpec(memory_space=pltpu.VMEM)
SM = pl.BlockSpec(memory_space=pltpu.SMEM)
HB = pl.BlockSpec(memory_space=pl.ANY)


def attend_forward(sc, q_t, tok, start, pieces, state=None, last=True):
    n, width = pieces.shape[0], pieces.shape[2]
    heads = q_t.shape[0] // HEAD_WIDTH
    heads_kv = pieces.shape[1] // (2 * HEAD_WIDTH)
    first = state is None
    tokens = q_t.shape[1]
    out_shape = (
        jax.ShapeDtypeStruct(q_t.shape, halves if last else floats),
        jax.ShapeDtypeStruct((heads, tokens), floats),
    )
    return pl.pallas_call(
        functools.partial(fwd_kernel, n, width, first, last),
        out_shape=out_shape,
        in_specs=[SM, VM, VM, VM] + [HB] + ([] if first else [VM, VM]),
        out_specs=(VM, VM),
        scratch_shapes=[
            pltpu.VMEM(pieces.shape, halves),
            pltpu.VMEM((heads_kv, BLK, HEAD_WIDTH), halves),
            pltpu.VMEM((heads_kv * HEAD_WIDTH, tokens * heads // heads_kv), floats),
            pltpu.VMEM((heads_kv, tokens * heads // heads_kv), floats),
            pltpu.VMEM((heads_kv * HEAD_WIDTH, tokens * heads // heads_kv), halves),
            pltpu.SemaphoreType.DMA((n,)),
        ],
        compiler_params=pltpu.CompilerParams(vmem_limit_bytes=40 << 20),
        name="attend_forward",
    )(sc, q_t, tok, start, pieces, *(() if first else state))


def bwd_kernel(n, width, first, sc, q_ref, do_ref, log_ref, delta_ref, tok_ref, start_ref, pieces, *refs):
    if not first:
        dq_in = refs[0]
        refs = refs[1:]
    dq_out = refs[0]
    dkv_out = refs[1]
    kv, dkv, keys_nat, vals_nat, acc, q_wide, do_wide, log_wide, delta_wide, dq_wide, sem, osem = refs[2:]
    per = width // BLK
    for i in range(n):
        pltpu.make_async_copy(pieces.at[i], kv.at[i], sem.at[i]).start()
    for i in range(n):
        pltpu.make_async_copy(pieces.at[i], kv.at[i], sem.at[i]).wait()
    heads_kv = pieces.shape[1] // (2 * HEAD_WIDTH)
    group = q_ref.shape[0] // (heads_kv * HEAD_WIDTH)
    v_off = heads_kv * HEAD_WIDTH
    places = [
        (h, slice((h * group + g) * HEAD_WIDTH, (h * group + g + 1) * HEAD_WIDTH), slice(qb * BLK, (qb + 1) * BLK),
         slice(h * HEAD_WIDTH, (h + 1) * HEAD_WIDTH), slice((qb * group + g) * BLK, (qb * group + g + 1) * BLK), h * group + g)
        for h in range(heads_kv) for g in range(group) for qb in range(q_ref.shape[1] // BLK)
    ]
    for h, rows, lanes, wrows, wlanes, hd in places:
        q_wide[wrows, wlanes] = q_ref[rows, lanes]
        do_wide[wrows, wlanes] = do_ref[rows, lanes]
        log_wide[h : h + 1, wlanes] = log_ref[hd : hd + 1, lanes]
        delta_wide[h : h + 1, wlanes] = delta_ref[hd : hd + 1, lanes]
        dq_wide[wrows, wlanes] = jnp.zeros((HEAD_WIDTH, BLK), floats) if first else dq_in[rows, lanes]
    out_scale = (1.0 / VSCALE) * HEAD_WIDTH ** (-0.5)

    def key_block(kb, carry):
        piece = kb // per
        klanes = pl.ds(pl.multiple_of((kb % per) * BLK, BLK), BLK)
        for h in range(heads_kv):
            keys_nat[h] = kv[piece, h * HEAD_WIDTH : (h + 1) * HEAD_WIDTH, klanes].T
            vals_nat[h] = kv[piece, v_off + h * HEAD_WIDTH : v_off + (h + 1) * HEAD_WIDTH, klanes].T
        acc[...] = jnp.zeros_like(acc)

        def query_block(qb, carry):
            key_base, needed, whole = pair_state(sc, kb, qb)
            lanes = pl.ds(pl.multiple_of(qb * BLK, BLK), BLK)

            def unit(masked):
                wide = pl.ds(pl.multiple_of(qb * (group * BLK), group * BLK), group * BLK)
                if masked:
                    allowed = allowed_mask(key_base, tok_ref, start_ref, lanes)
                    allowed = jnp.concatenate([allowed] * group, axis=1)
                heads = range(heads_kv)
                krows = [slice(h * HEAD_WIDTH, (h + 1) * HEAD_WIDTH) for h in heads]
                vrows = [slice(v_off + h * HEAD_WIDTH, v_off + (h + 1) * HEAD_WIDTH) for h in heads]
                qt = [q_wide[krows[h], wide] for h in heads]
                dot = [do_wide[krows[h], wide] for h in heads]
                scores = [dot_nn(keys_nat[h], qt[h]) for h in heads]
                dprobs = [dot_nn(vals_nat[h], dot[h]) for h in heads]
                weights = [
                    jnp.exp2(scores[h] * SCORE - log_wide[h : h + 1, wide]) for h in heads
                ]
                if masked:
                    weights = [jnp.where(allowed, w, 0.0) for w in weights]
                ds = [
                    (weights[h] * (dprobs[h] - delta_wide[h : h + 1, wide])).astype(halves)
                    for h in heads
                ]
                dv = [dot_nt(dot[h], weights[h].astype(halves)) for h in heads]
                dk = [dot_nt(qt[h], ds[h]) for h in heads]
                dq = [dot_nn(kv[piece, krows[h], klanes], ds[h]) for h in heads]
                for h in heads:
                    acc[vrows[h], :] += dv[h]
                    acc[krows[h], :] += dk[h]
                    dq_wide[krows[h], wide] += dq[h]

            pl.when(needed & whole)(lambda: unit(False))
            pl.when(needed & jnp.logical_not(whole))(lambda: unit(True))
            return carry

        carry = lax.fori_loop(0, q_ref.shape[1] // BLK, query_block, carry)
        dkv[piece, 0:v_off, klanes] = (acc[0:v_off, :] * out_scale).astype(halves)
        dkv[piece, v_off:, klanes] = acc[v_off:, :].astype(halves)
        return carry

    lax.fori_loop(0, n * per, key_block, 0)
    for i in range(n):
        pltpu.make_async_copy(dkv.at[i], dkv_out.at[i], osem.at[i]).start()
    for h, rows, lanes, wrows, wlanes, hd in places:
        dq_out[rows, lanes] = dq_wide[wrows, wlanes] * out_scale
    for i in range(n):
        pltpu.make_async_copy(dkv.at[i], dkv_out.at[i], osem.at[i]).wait()


def attend_backward(sc, q_t, do_t, log_total, delta, tok, start, pieces):
    n, width = pieces.shape[0], pieces.shape[2]
    heads_kv = pieces.shape[1] // (2 * HEAD_WIDTH)
    wide = q_t.shape[0] // (heads_kv * HEAD_WIDTH) * q_t.shape[1]
    outs = pl.pallas_call(
        functools.partial(bwd_kernel, n, width, True),
        out_shape=(
            jax.ShapeDtypeStruct(q_t.shape, floats),
            jax.ShapeDtypeStruct(pieces.shape, halves),
        ),
        in_specs=[SM] + [VM] * 6 + [HB],
        out_specs=(VM, HB),
        scratch_shapes=[
            pltpu.VMEM(pieces.shape, halves),
            pltpu.VMEM(pieces.shape, halves),
            pltpu.VMEM((heads_kv, BLK, HEAD_WIDTH), halves),
            pltpu.VMEM((heads_kv, BLK, HEAD_WIDTH), halves),
            pltpu.VMEM((pieces.shape[1], BLK), floats),
            pltpu.VMEM((heads_kv * HEAD_WIDTH, wide), halves),
            pltpu.VMEM((heads_kv * HEAD_WIDTH, wide), halves),
            pltpu.VMEM((heads_kv, wide), floats),
            pltpu.VMEM((heads_kv, wide), floats),
            pltpu.VMEM((heads_kv * HEAD_WIDTH, wide), floats),
            pltpu.SemaphoreType.DMA((n,)),
            pltpu.SemaphoreType.DMA((n,)),
        ],
        compiler_params=pltpu.CompilerParams(vmem_limit_bytes=44 << 20),
        name="attend_backward",
    )(sc, q_t, do_t, log_total, delta, tok, start, pieces)
    return outs


eps_norm = 1e-05
rope_base = 100000.0
reach_limit = 8


def shifted(block, axis, distance):
    devices = range(lax.axis_size(axis))
    route = [(i - distance, i) for i in devices if i - distance in devices]
    return lax.ppermute(block, axis, route)


def rms_scale(value_vectors, gain_vec):
    return (
        value_vectors
        * lax.rsqrt(jnp.mean(value_vectors * value_vectors, axis=-1, keepdims=True) + eps_norm)
        * gain_vec
    )


def rotary_turn(value_vectors, token_positions, heads):
    half_width = HEAD_WIDTH // 2
    inverse = 1.0 / rope_base ** (jnp.arange(half_width, dtype=jnp.float32) * 2.0 / HEAD_WIDTH)
    angles = token_positions.astype(jnp.float32)[:, None] * inverse[None, :]
    cosine = jnp.cos(angles)[:, None, :]
    sine_part = jnp.sin(angles)[:, None, :]
    shaped = value_vectors.reshape(value_vectors.shape[0], heads, HEAD_WIDTH)
    first_half = shaped[..., :half_width]
    second = shaped[..., half_width:]
    turned = jnp.concatenate(
        [first_half * cosine - second * sine_part, second * cosine + first_half * sine_part],
        axis=-1,
    )
    return turned.reshape(value_vectors.shape)


def swiglu(gate_pre, up_pre):
    return jax.nn.silu(gate_pre) * up_pre


def contract_rows(left_side, right_side):
    return lax.dot_general(
        left_side, right_side, (((0,), (0,)), ((), ())), preferred_element_type=jnp.float32
    )


def contract_cols(left_side, right_side):
    return lax.dot_general(
        left_side, right_side, (((1,), (1,)), ((), ())), preferred_element_type=jnp.float32
    )


def local(
    tokens,
    out_grad,
    segment_ids,
    attn_gain,
    query_weight,
    key_matrix,
    value_matrix,
    output_weight,
    mlp_gain,
    gate_weight,
    up_weight,
    down_weight,
):
    floats = jnp.float32
    halves = jnp.bfloat16
    shard_rows = tokens.shape[0]
    row_len = shard_rows * lax.axis_size("tp")
    row_index = lax.axis_index("dp")
    reach = min(reach_limit, lax.axis_size("dp") // 2)
    heads_q = query_weight.shape[1] // HEAD_WIDTH
    heads_kv = key_matrix.shape[1] // HEAD_WIDTH
    group_width = heads_q // heads_kv
    q_cols = heads_q * HEAD_WIDTH
    kv_cols = heads_kv * HEAD_WIDTH
    score_scale = HEAD_WIDTH ** (-0.5)
    row_first = row_index * row_len
    seg_row = lax.dynamic_slice_in_dim(segment_ids, row_first, row_len)
    index_row = row_first + jnp.arange(row_len, dtype=jnp.int32)
    every_index = jnp.arange(segment_ids.shape[0], dtype=jnp.int32)
    marks = (segment_ids[1:] != segment_ids[:-1]).astype(jnp.int32)
    starts = jnp.concatenate([jnp.zeros((1,), jnp.int32), marks * every_index[1:]])
    is_at = (starts[None, :] <= index_row[:, None]).astype(jnp.int32)
    token_positions = index_row - jnp.max(is_at * starts[None, :], axis=1)
    tokens32 = tokens.astype(floats)
    gain_attn = attn_gain.astype(floats)
    gain_mlp = mlp_gain.astype(floats)
    normed = rms_scale(tokens32, gain_attn).astype(halves)
    normed_full = lax.all_gather(normed, "tp", axis=0, tiled=True)
    joined = jnp.concatenate([query_weight, key_matrix, value_matrix], axis=1)
    projected = jnp.dot(normed_full, joined, preferred_element_type=floats)
    q_linear = projected[:, :q_cols]
    key_linear_out = projected[:, q_cols : q_cols + kv_cols]
    query_vectors = rotary_turn(q_linear, token_positions, heads_q).astype(halves)
    key_vectors = rotary_turn(key_linear_out, token_positions, heads_kv).astype(halves)
    value_vectors = projected[:, q_cols + kv_cols :].astype(halves)
    query_heads = query_vectors.reshape(row_len, heads_kv, group_width, HEAD_WIDTH)
    held_blocks = [(key_vectors, value_vectors)]
    moving = (key_vectors, value_vectors)
    for step_hop in range(reach):
        moving = shifted((moving[0], moving[1]), "dp", 1)
        held_blocks.append(moving)

    def block_mask(step_hop):
        key_row = row_index - step_hop
        seg_keys = lax.dynamic_slice_in_dim(segment_ids, jnp.maximum(key_row, 0) * row_len, row_len)
        key_index = key_row * row_len + jnp.arange(row_len, dtype=jnp.int32)
        return (seg_keys[None, :] == seg_row[:, None]) & (key_index[None, :] <= index_row[:, None])

    def block_needed(step_hop):
        last_key = jnp.maximum((row_index - step_hop + 1) * row_len - 1, 0)
        return (row_index >= step_hop) & (segment_ids[last_key] == seg_row[0])

    block_masks = [block_mask(step_hop) for step_hop in range(reach + 1)]

    def apply_block(step_hop, update, state_in):
        key_block, value_block = held_blocks[step_hop]
        if step_hop == 0:
            return update(state_in, key_block, value_block, block_masks[0])
        return lax.cond(
            block_needed(step_hop),
            update,
            lambda state_kept, key_skip, value_skip, mask_skip: state_kept,
            state_in,
            key_block,
            value_block,
            block_masks[step_hop],
        )

    def scores(key_block, allowed):
        raw_scores = jnp.einsum(
            "qhgd,khd->hgqk",
            query_heads,
            key_block.reshape(row_len, heads_kv, HEAD_WIDTH),
            preferred_element_type=floats,
        )
        return jnp.where(allowed, raw_scores * score_scale, -jnp.inf)

    def add_online(state_in, key_block, value_block, allowed):
        run_max, run_total, run_sum = state_in
        block_scores = scores(key_block, allowed)
        new_max = jnp.maximum(run_max, jnp.max(block_scores, axis=-1))
        factor = jnp.exp(run_max - new_max)
        weights = jnp.exp(block_scores - new_max[..., None])
        run_total = run_total * factor + jnp.sum(weights, axis=-1)
        run_sum = run_sum * jnp.moveaxis(factor, 2, 0)[..., None] + jnp.einsum(
            "hgqk,khd->qhgd",
            weights.astype(halves),
            value_block.reshape(row_len, heads_kv, HEAD_WIDTH),
            preferred_element_type=floats,
        )
        return (new_max, run_total, run_sum)

    online = (
        jnp.full((heads_kv, group_width, row_len), -jnp.inf, floats),
        jnp.zeros((heads_kv, group_width, row_len), floats),
        jnp.zeros((row_len, heads_kv, group_width, HEAD_WIDTH), floats),
    )
    for step_hop in range(reach + 1):
        online = apply_block(step_hop, add_online, online)
    run_max, run_total, run_sum = online
    log_total = (run_max + jnp.log(run_total))[..., None]
    context_heads = (run_sum / jnp.moveaxis(run_total, 2, 0)[..., None]).astype(halves)
    context = context_heads.reshape(row_len, q_cols)
    residual = tokens32 + lax.psum_scatter(
        jnp.dot(context, output_weight, preferred_element_type=floats).astype(jnp.bfloat16),
        "tp",
        scatter_dimension=0,
        tiled=True,
    ).astype(jnp.float32)
    mlp_normed = rms_scale(residual, gain_mlp).astype(halves)
    mlp_full = lax.all_gather(mlp_normed, "tp", axis=0, tiled=True)
    gate_pre = jnp.dot(mlp_full, gate_weight, preferred_element_type=floats)
    up_pre = jnp.dot(mlp_full, up_weight, preferred_element_type=floats)
    hidden = swiglu(gate_pre, up_pre).astype(halves)
    output = residual + lax.psum_scatter(
        jnp.dot(hidden, down_weight, preferred_element_type=floats).astype(jnp.bfloat16),
        "tp",
        scatter_dimension=0,
        tiled=True,
    ).astype(jnp.float32)
    grad_full = lax.all_gather(out_grad, "tp", axis=0, tiled=True)
    grad_hidden = contract_cols(grad_full, down_weight)
    down_grad = contract_rows(grad_full, hidden)
    silu_back = jax.vjp(swiglu, gate_pre, up_pre)[1]
    grad_gate, grad_up = silu_back(grad_hidden)
    grad_gate = grad_gate.astype(halves)
    grad_up = grad_up.astype(halves)
    gate_grad = contract_rows(mlp_full, grad_gate)
    up_grad = contract_rows(mlp_full, grad_up)
    grad_mlp_normed = lax.psum_scatter(
        (contract_cols(grad_gate, gate_weight) + contract_cols(grad_up, up_weight)).astype(
            jnp.bfloat16
        ),
        "tp",
        scatter_dimension=0,
        tiled=True,
    ).astype(jnp.float32)
    mlp_norm_back = jax.vjp(rms_scale, residual, gain_mlp)[1]
    grad_residual_part, mlp_gain_part = mlp_norm_back(grad_mlp_normed)
    grad_residual = out_grad.astype(floats) + grad_residual_part
    attn_grad_full = lax.all_gather(grad_residual.astype(halves), "tp", axis=0, tiled=True)
    output_grad = contract_rows(attn_grad_full, context)
    grad_context = (
        contract_cols(attn_grad_full, output_weight)
        .astype(halves)
        .reshape(row_len, heads_kv, group_width, HEAD_WIDTH)
    )
    delta_col = jnp.einsum(
        "qhgd,qhgd->hgq", grad_context, context_heads, preferred_element_type=floats
    )[..., None]

    def add_grads(state_in, key_block, value_block, allowed):
        query_acc, key_acc, value_acc = state_in
        probabilities = jnp.exp(scores(key_block, allowed) - log_total)
        grad_probs = jnp.einsum(
            "qhgd,khd->hgqk",
            grad_context,
            value_block.reshape(row_len, heads_kv, HEAD_WIDTH),
            preferred_element_type=floats,
        )
        grad_scores = (probabilities * (grad_probs - delta_col)).astype(halves)
        key_heads = key_block.reshape(row_len, heads_kv, HEAD_WIDTH)
        query_acc = (
            query_acc
            + jnp.einsum("hgqk,khd->qhgd", grad_scores, key_heads, preferred_element_type=floats)
            * score_scale
        )
        key_acc = (
            key_acc
            + jnp.einsum(
                "hgqk,qhgd->khd", grad_scores, query_heads, preferred_element_type=floats
            ).reshape(row_len, kv_cols)
            * score_scale
        )
        value_acc = value_acc + jnp.einsum(
            "hgqk,qhgd->khd",
            probabilities.astype(halves),
            grad_context,
            preferred_element_type=floats,
        ).reshape(row_len, kv_cols)
        return (query_acc, key_acc, value_acc)

    query_acc = jnp.zeros((row_len, heads_kv, group_width, HEAD_WIDTH), floats)
    carried = (jnp.zeros((row_len, kv_cols), floats), jnp.zeros((row_len, kv_cols), floats))
    for step_hop in range(reach, 0, -1):
        query_acc, key_acc, value_acc = apply_block(
            step_hop, add_grads, (query_acc, carried[0], carried[1])
        )
        carried = (
            shifted(key_acc.astype(jnp.bfloat16), "dp", -1).astype(key_acc.dtype),
            shifted(value_acc.astype(jnp.bfloat16), "dp", -1).astype(value_acc.dtype),
        )
    query_acc, key_total, value_total = apply_block(
        0, add_grads, (query_acc, carried[0], carried[1])
    )
    query_back = jax.vjp(lambda linear: rotary_turn(linear, token_positions, heads_q), q_linear)[1]
    key_back = jax.vjp(
        lambda linear: rotary_turn(linear, token_positions, heads_kv), key_linear_out
    )[1]
    grad_q_linear = query_back(query_acc.reshape(row_len, q_cols))[0]
    grad_k_linear = key_back(key_total)[0]
    grads_joined = jnp.concatenate([grad_q_linear, grad_k_linear, value_total], axis=1).astype(
        halves
    )
    proj_grad = contract_rows(normed_full, grads_joined)
    grad_normed = lax.psum_scatter(
        contract_cols(grads_joined, joined).astype(jnp.bfloat16),
        "tp",
        scatter_dimension=0,
        tiled=True,
    ).astype(jnp.float32)
    attn_norm_back = jax.vjp(rms_scale, tokens32, gain_attn)[1]
    grad_tokens_part, attn_gain_part = attn_norm_back(grad_normed)
    input_grad = grad_residual + grad_tokens_part
    def scatter_rows(grad):
        return lax.psum_scatter(
            grad.astype(halves), "dp", scatter_dimension=0, tiled=True
        ).astype(floats)

    mlp_sums = scatter_rows(jnp.concatenate([gate_grad, up_grad, down_grad], axis=1))
    ff_cols = gate_weight.shape[1]
    gate_sum = mlp_sums[:, :ff_cols]
    up_sum = mlp_sums[:, ff_cols : 2 * ff_cols]
    down_sum = mlp_sums[:, 2 * ff_cols :]
    attn_sums = scatter_rows(jnp.concatenate([proj_grad, output_grad], axis=1))
    query_sum = attn_sums[:, :q_cols]
    key_sum = attn_sums[:, q_cols : q_cols + kv_cols]
    value_sum = attn_sums[:, q_cols + kv_cols : q_cols + 2 * kv_cols]
    output_sum = attn_sums[:, q_cols + 2 * kv_cols :]
    attn_gain_sum = lax.psum_scatter(attn_gain_part, "dp", scatter_dimension=0, tiled=True)
    mlp_gain_sum = lax.psum_scatter(mlp_gain_part, "dp", scatter_dimension=0, tiled=True)
    attn_gain_total, mlp_gain_total = lax.psum((attn_gain_sum, mlp_gain_sum), "tp")
    return (
        output.astype(halves),
        input_grad,
        attn_gain_total,
        query_sum,
        key_sum,
        value_sum,
        output_sum.T,
        mlp_gain_total,
        gate_sum,
        up_sum,
        down_sum.T,
    )


MESH = pl.DeviceIdType.MESH


def meet(devices):
    barrier = pltpu.get_barrier_semaphore()
    for device in devices:
        pl.semaphore_signal(barrier, inc=1, device_id=device, device_id_type=MESH)
    pl.semaphore_wait(barrier, len(devices))


def tiles(total, step, body):
    def one(i, carry):
        body(pl.ds(pl.multiple_of(i * step, step), step))
        return carry

    lax.fori_loop(0, total // step, one, 0)


CHUNKS = 4


class GroupSum:
    def __init__(self, copies, bufs, place):
        self.copies, self.bufs, self.place = copies, bufs, place

    def run(self, product):
        part_near, part_own, out_far, out_beside, out_near, in_near, in_own, in_sum = self.bufs

        def put_there(cols, value):
            rows = value.shape[0] // 2
            part_near[:, cols] = value[:rows]
            out_far[:, cols] = value[rows:].astype(halves)

        def put_here(cols, value):
            rows = value.shape[0] // 2
            part_own[:, cols] = value[:rows]
            out_beside[:, cols] = value[rows:].astype(halves)

        product(1, put_there)
        self.far = self.copies.make(out_far, in_near, self.place.beside)
        self.far.start()
        product(0, put_here)
        self.side = self.copies.make(out_beside, in_own, self.place.beside)
        self.side.start()
        self.far.wait_recv()
        rows = part_near.shape[0] // CHUNKS
        self.sums = []
        for k in range(CHUNKS):
            at = pl.ds(k * rows, rows)
            out_near[at, :] = (part_near[at, :] + in_near[at, :].astype(floats)).astype(halves)
            copy = self.copies.make(out_near.at[at], in_sum.at[at], self.place.near)
            copy.start()
            self.sums.append(copy)

    def take(self, k):
        part_near, part_own, out_far, out_beside, out_near, in_near, in_own, in_sum = self.bufs
        if k == 0:
            self.side.wait_recv()
        self.sums[k].wait_recv()
        rows = part_own.shape[0] // CHUNKS
        at = pl.ds(k * rows, rows)
        return part_own[at, :] + in_own[at, :].astype(floats) + in_sum[at, :].astype(floats)

    def finish(self):
        for copy in (self.far, self.side, *self.sums):
            copy.wait_send()


class GroupGather:
    def __init__(self, copies, full, block, place):
        self.copies, self.full, self.block, self.place = copies, full, block, place
        self.sent = []

    def slot(self, n, k):
        rows = self.block // CHUNKS
        return self.full.at[pl.ds(n * self.block + k * rows, rows)]

    def put(self, k):
        for i, (n, device) in enumerate(((2, self.place.near), (1, self.place.beside))):
            copy = self.copies.make(self.slot(0, k), self.slot(n, k), device)
            copy.start()
            self.sent.append((i, copy))

    def wait_here(self):
        for i, copy in self.sent:
            if i == 1:
                copy.wait_recv()

    def wait_there(self):
        relays = []
        k = 0
        for i, copy in self.sent:
            if i == 0:
                copy.wait_recv()
                relay = self.copies.make(self.slot(2, k), self.slot(3, k), self.place.beside)
                relay.start()
                relays.append(relay)
                k += 1
        for relay in relays:
            relay.wait_recv()
        self.sent += [(2, relay) for relay in relays]

    def finish(self):
        for _, copy in self.sent:
            copy.wait_send()


class Copies:
    limit = 96

    def __init__(self, send_sems, recv_sems):
        self.send_sems, self.recv_sems, self.used = send_sems, recv_sems, 0

    def make(self, src, dst, device):
        i = self.used
        self.used += 1
        return pltpu.make_async_remote_copy(
            src_ref=src,
            dst_ref=dst,
            send_sem=self.send_sems.at[i],
            recv_sem=self.recv_sems.at[i],
            device_id=device,
            device_id_type=MESH,
        )


def copy_semaphores():
    return [pltpu.SemaphoreType.DMA((Copies.limit,)), pltpu.SemaphoreType.DMA((Copies.limit,))]


class Place:
    def __init__(self):
        dp, z = lax.axis_index("dp"), lax.axis_index("tp")
        self.dp, self.z = dp, z
        self.c = lax.rem(dp, 2)
        self.x = lax.rem(dp // 2, 2)
        self.y = dp // 4
        far_z = lax.rem(z + 2, 4)
        self.beside = (dp + 1 - 2 * self.c, z)
        self.near = (dp, z + 1 - 2 * lax.rem(z, 2))
        self.far = (dp, far_z)
        self.cross = (self.beside[0], far_z)
        self.over_x = (dp + 2 - 4 * self.x, z)
        self.over_y = (dp + 4 - 8 * self.y, z)
        self.slot = 2 * self.y + self.x
        self.slot_x = 2 * self.y + 1 - self.x
        self.slot_y = 2 - 2 * self.y + self.x
        self.odd = self.c == 1
        self.corner = (self.x == 1) & (self.y == 1)
        self.turn = (self.x == 0) & (self.y == 1)


class PlaneFetch:
    def __init__(self, copies, place, out, own=None):
        self.place, self.out = place, out
        rows = out.shape[0] // 8

        def part(slot, ch):
            return pl.ds(slot * (2 * rows) + ch * rows, rows)

        def remote(slot, ch, device):
            at = part(slot, ch)
            return copies.make(out.at[at], out.at[at], device)

        p = place
        self.hop = None
        if own is not None:
            self.hop = [
                copies.make(own.at[part(p.slot, ch)], out.at[part(p.slot, ch)], p.far)
                for ch in range(2)
            ]
        self.x = [remote(p.slot, ch, p.over_x) for ch in range(2)]
        self.y = [remote(p.slot, ch, p.over_y) for ch in range(2)]
        self.relay_y = remote(p.slot_x, 0, p.over_y)
        self.relay_x = remote(p.slot_y, 1, p.over_x)

    def start(self):
        @pl.when(self.place.odd)
        def _():
            for copy in self.hop:
                copy.start()

    def forward(self):
        @pl.when(self.place.odd)
        def _():
            for ch in range(2):
                if self.hop is not None:
                    self.hop[ch].wait_recv()
                self.x[ch].start()
                self.y[ch].start()

    def relay(self):
        @pl.when(self.place.odd)
        def _():
            self.x[0].wait_recv()
            self.relay_y.start()
            self.y[1].wait_recv()
            self.relay_x.start()

    def finish(self):
        @pl.when(self.place.odd)
        def _():
            self.x[1].wait_recv()
            self.y[0].wait_recv()
            self.relay_y.wait_recv()
            self.relay_x.wait_recv()

    def drain(self):
        @pl.when(self.place.odd)
        def _():
            for copy in (self.hop or []) + self.x + self.y + [self.relay_y, self.relay_x]:
                copy.wait_send()


class Spread:
    def __init__(self, copies, place, source, slots):
        self.place = place
        self.to_x = copies.make(source, slots[1], place.over_x)
        self.to_y = copies.make(source, slots[2], place.over_y)
        self.relayed = copies.make(slots[2], slots[3], place.over_x)

    def start(self):
        pl.when(self.place.x == 0)(self.to_x.start)
        pl.when(self.place.y == 0)(self.to_y.start)

    def relay(self):
        @pl.when(self.place.corner)
        def _():
            self.to_y.wait_recv()
            self.relayed.start()

    def finish(self):
        p = self.place
        pl.when(p.x == 1)(self.to_x.wait_recv)
        pl.when((p.y == 1) & (p.x == 0))(self.to_y.wait_recv)
        pl.when(p.turn)(self.relayed.wait_recv)
        pl.when(p.x == 0)(self.to_x.wait_send)
        pl.when(p.y == 0)(self.to_y.wait_send)
        pl.when(p.corner)(self.relayed.wait_send)


def first_kernel(
    tok_ref, grad_ref, gain_ref, cos_ref, sin_ref, joined_in, wo_in, wd_in,
    q_out, kv_out, n_full, g_full, joined, wo_out, wd_out,
    linear, kv_own, ss, rs, lsem,
):
    place = Place()
    copies = Copies(ss, rs)
    block, width = tok_ref.shape
    two = 2 * block
    q_cols = q_out.shape[0]
    kv_cols = kv_own.shape[1] // 2
    local = [
        pltpu.make_async_copy(src, dst, lsem.at[i])
        for i, (src, dst) in enumerate(((joined_in, joined), (wo_in, wo_out), (wd_in, wd_out)))
    ]

    @pl.when(place.c == 0)
    def _():
        for copy in local:
            copy.start()

    own_grad = pltpu.make_async_copy(grad_ref, g_full.at[pl.ds(0, block)], lsem.at[3])
    own_grad.start()
    meet((place.beside, place.near, place.far, place.cross, place.over_x, place.over_y))

    fetch_joined = PlaneFetch(copies, place, joined, joined_in)
    fetch_o = PlaneFetch(copies, place, wo_out, wo_in)
    fetch_d = PlaneFetch(copies, place, wd_out, wd_in)
    gather = GroupGather(copies, n_full, block, place)
    gather_g = GroupGather(copies, g_full, block, place)
    fetch_joined.start()
    chunk = block // CHUNKS
    for k in range(CHUNKS):
        at = pl.ds(k * chunk, chunk)
        tok = tok_ref[at, :].astype(floats)
        root = lax.rsqrt(jnp.mean(tok * tok, axis=-1, keepdims=True) + eps_norm)
        n_full[at, :] = (tok * root * gain_ref[...]).astype(halves)
        gather.put(k)
    fetch_joined.forward()
    fetch_o.start()
    fetch_d.start()
    fetch_joined.relay()
    gather.wait_here()
    fetch_joined.finish()
    pl.when(place.c == 0)(local[0].wait)

    def project(k):
        rows = slice(k * two, (k + 1) * two)

        def one(cols):
            linear[cols, :] = dot_nn(n_full[rows, :], joined[:, cols]).T

        tiles(joined.shape[1], 256, one)
        half_width = HEAD_WIDTH // 2
        for head in range((q_cols + kv_cols) // HEAD_WIDTH):
            low = slice(head * HEAD_WIDTH, head * HEAD_WIDTH + half_width)
            high = slice(head * HEAD_WIDTH + half_width, (head + 1) * HEAD_WIDTH)
            one_half, two_half = linear[low, :], linear[high, :]
            cosine, sine = cos_ref[:, rows], sin_ref[:, rows]
            first = (one_half * cosine - two_half * sine).astype(halves)
            second = (two_half * cosine + one_half * sine).astype(halves)
            if head * HEAD_WIDTH < q_cols:
                q_out[low, rows] = first
                q_out[high, rows] = second
            else:
                kv_own[k, low.start - q_cols : low.stop - q_cols, :] = first
                kv_own[k, high.start - q_cols : high.stop - q_cols, :] = second
        kv_own[k, kv_cols:, :] = (linear[q_cols + kv_cols :, :].astype(halves) * VSCALE).astype(halves)

    crossings, spreads_a, spreads_b, kept = [], [], [], []

    def share(k):
        slots = [kv_out.at[8 * k + i] for i in range(8)]
        keep = pltpu.make_async_copy(kv_own.at[k], slots[0], lsem.at[4 + k])
        keep.start()
        kept.append(keep)
        crossing = copies.make(kv_own.at[k], slots[4], place.cross)
        crossing.start()
        crossings.append(crossing)
        spread = Spread(copies, place, kv_own.at[k], slots[:4])
        spread.start()
        spreads_a.append(spread)
        spreads_b.append(Spread(copies, place, slots[4], slots[4:]))

    project(0)
    share(0)
    gather.wait_there()
    project(1)
    share(1)
    own_grad.wait()
    for k in range(CHUNKS):
        gather_g.put(k)
    fetch_o.forward()
    fetch_d.forward()
    spreads_a[0].relay()
    spreads_a[1].relay()
    fetch_o.relay()
    fetch_d.relay()
    crossings[0].wait_recv()
    spreads_b[0].start()
    gather_g.wait_there()
    spreads_b[0].relay()
    crossings[1].wait_recv()
    spreads_b[1].start()
    spreads_b[1].relay()
    fetch_o.finish()
    fetch_d.finish()
    gather_g.wait_here()
    for spread in spreads_a + spreads_b:
        spread.finish()
    for copy in kept:
        copy.wait()

    @pl.when(place.c == 0)
    def _():
        for copy in local[1:]:
            copy.wait()

    for copy in crossings:
        copy.wait_send()
    for fetch in (fetch_joined, fetch_o, fetch_d):
        fetch.drain()
    gather.finish()
    gather_g.finish()


def first_part(tokens, out_grad, gain, cosine, sine, joined, weight_o, weight_d, q_cols, kv_cols):
    block, width = tokens.shape
    group = 4 * block
    shape = jax.ShapeDtypeStruct
    out_shape = (
        shape((q_cols, group), halves),
        shape((16, 2 * kv_cols, 2 * block), halves),
        shape((group, width), halves),
        shape((group, width), halves),
        shape(joined.shape, halves),
        shape(weight_o.shape, halves),
        shape(weight_d.shape, halves),
    )
    return pl.pallas_call(
        first_kernel,
        out_shape=out_shape,
        in_specs=[VM] * 5 + [HB] * 3,
        out_specs=(VM, HB, VM, VM, VM, HB, HB),
        scratch_shapes=[
            pltpu.VMEM((joined.shape[1], 2 * block), floats),
            pltpu.VMEM((2, 2 * kv_cols, 2 * block), halves),
            *copy_semaphores(),
            pltpu.SemaphoreType.DMA((6,)),
        ],
        compiler_params=pltpu.CompilerParams(
            collective_id=2, has_side_effects=True, vmem_limit_bytes=40 << 20
        ),
        name="first",
    )(tokens, out_grad, gain, cosine, sine, joined, weight_o, weight_d)


def mid_kernel(ctx_ref, tok_ref, gain_ref, g_full, weight_refs, outs, scratch):
    (res_out, gres_out, e_full, part_out, gate_out, up_out, down_out, dctx_out, delta_out, gain_out) = outs
    (ctx, m_full, dh, hid, dgate, dup, w_o, w_d, w_g, w_u, *bufs, ss, rs, wsem) = scratch
    place = Place()
    copies = Copies(ss, rs)
    block, width = tok_ref.shape
    two = 2 * block
    hidden = w_g.shape[1]
    wo_ref, wd_ref, wg_ref, wu_ref, slice_g, slice_u = weight_refs
    load_o = pltpu.make_async_copy(wo_ref, w_o, wsem.at[0])
    load_d = pltpu.make_async_copy(wd_ref, w_d, wsem.at[1])
    load_o.start()
    load_d.start()
    rows4 = slice_g.shape[0]
    at_slot = pl.ds(place.slot * rows4, rows4)
    loads = [
        pltpu.make_async_copy(src, dst, wsem.at[2 + i])
        for i, (src, dst) in enumerate(((wg_ref, w_g), (wu_ref, w_u)))
    ]
    loads_odd = [
        pltpu.make_async_copy(src, dst.at[at_slot], wsem.at[2 + i])
        for i, (src, dst) in enumerate(((slice_g, w_g), (slice_u, w_u)))
    ]

    @pl.when(place.c == 0)
    def _():
        for copy in loads:
            copy.start()

    @pl.when(place.odd)
    def _():
        for copy in loads_odd:
            copy.start()

    ctx[...] = ctx_ref[...].T
    meet((place.beside, place.near, place.over_x, place.over_y))
    fetches = [PlaneFetch(copies, place, w_g), PlaneFetch(copies, place, w_u)]

    @pl.when(place.odd)
    def _():
        for copy in loads_odd:
            copy.wait()

    for fetch in fetches:
        fetch.forward()
    sum_one = GroupSum(copies, bufs, place)
    gather_one = GroupGather(copies, m_full, block, place)
    sum_two = GroupSum(copies, bufs, place)
    gather_two = GroupGather(copies, e_full, block, place)

    def project(k, put):
        rows = slice(k * two, (k + 1) * two)
        tiles(width, 256, lambda cols: put(cols, dot_nn(ctx[rows, :], w_o[:, cols])))

    load_o.wait()
    sum_one.run(project)
    load_d.wait()

    def back_hidden(cols):
        for rows in (slice(0, two), slice(two, 2 * two)):
            dh[rows, cols] = dot_nt(g_full[rows, :], w_d[cols, :]).astype(halves)

    tiles(hidden, 256, back_hidden)
    for fetch in fetches:
        fetch.relay()
    chunk = block // CHUNKS
    for k in range(CHUNKS):
        at = pl.ds(k * chunk, chunk)
        res = tok_ref[at, :].astype(floats) + sum_one.take(k)
        res_out[at, :] = res
        root = lax.rsqrt(jnp.mean(res * res, axis=-1, keepdims=True) + eps_norm)
        m_full[at, :] = (res * root * gain_ref[...]).astype(halves)
        gather_one.put(k)
    sum_one.finish()

    def activate(k):
        rows = slice(k * two, (k + 1) * two)

        def one(cols):
            gate_pre = dot_nn(m_full[rows, :], w_g[:, cols])
            up_pre = dot_nn(m_full[rows, :], w_u[:, cols])
            back = dh[rows, cols].astype(floats)
            sigma = 1.0 / (1.0 + jnp.exp(-gate_pre))
            silu = gate_pre * sigma
            hid[rows, cols] = (silu * up_pre).astype(halves)
            dgate[rows, cols] = (back * up_pre * (sigma + silu * (1.0 - sigma))).astype(halves)
            dup[rows, cols] = (back * silu).astype(halves)

        tiles(hidden, 256, one)

    def partial_out(k):
        rows = slice(k * two, (k + 1) * two)

        def one(cols):
            part_out[rows, cols] = dot_nn(hid[rows, :], w_d[:, cols]).astype(halves)

        tiles(width, 256, one)

    for fetch in fetches:
        fetch.finish()

    @pl.when(place.c == 0)
    def _():
        for copy in loads:
            copy.wait()

    gather_one.wait_here()
    activate(0)
    partial_out(0)
    gather_one.wait_there()
    activate(1)
    gather_one.finish()

    def back_norm(k, put):
        rows = slice(k * two, (k + 1) * two)
        tiles(
            width,
            256,
            lambda cols: put(
                cols, dot_nt(dgate[rows, :], w_g[cols, :]) + dot_nt(dup[rows, :], w_u[cols, :])
            ),
        )

    def outer(left, right, out):
        def one(rows):
            out[rows, :] = lax.dot_general(
                left[:, rows], right[...], (((0,), (0,)), ((), ())), preferred_element_type=floats
            ).astype(halves)

        tiles(width, 256, one)

    sum_two.run(back_norm)
    partial_out(1)
    outer(g_full, hid, down_out)
    outer(m_full, dgate, gate_out)
    gain_out[...] = jnp.zeros_like(gain_out)
    for k in range(CHUNKS):
        at = pl.ds(k * chunk, chunk)
        back = sum_two.take(k)
        res = res_out[at, :]
        root = lax.rsqrt(jnp.mean(res * res, axis=-1, keepdims=True) + eps_norm)
        weighted = back * gain_ref[...]
        slope = jnp.mean(weighted * res, axis=-1, keepdims=True)
        grad = g_full[at, :].astype(floats) + root * weighted - res * (root * root * root * slope)
        gain_out[...] += jnp.sum(back * res * root, axis=0, keepdims=True)
        gres_out[at, :] = grad
        e_full[at, :] = grad.astype(halves)
        gather_two.put(k)
    sum_two.finish()
    outer(m_full, dup, up_out)

    def back_context(k):
        lanes = slice(k * two, (k + 1) * two)
        grad = dot_nt(w_o[...], e_full[lanes, :]).astype(halves)
        dctx_out[:, lanes] = grad
        prod = grad.astype(floats) * ctx_ref[:, lanes].astype(floats)
        for hd in range(delta_out.shape[0]):
            delta_out[hd : hd + 1, lanes] = VSCALE * jnp.sum(
                prod[hd * HEAD_WIDTH : (hd + 1) * HEAD_WIDTH], axis=0, keepdims=True
            )

    gather_two.wait_here()
    back_context(0)
    gather_two.wait_there()
    back_context(1)
    gather_two.finish()
    for fetch in fetches:
        fetch.drain()


def middle(context_t, tokens, gain, grad_full, weights):
    q_cols, group = context_t.shape
    block, width = tokens.shape
    hidden = weights[2].shape[1]
    shape = jax.ShapeDtypeStruct
    out_shape = (
        shape((block, width), floats),
        shape((block, width), floats),
        shape((group, width), halves),
        shape((group, width), halves),
        shape((width, hidden), halves),
        shape((width, hidden), halves),
        shape((width, hidden), halves),
        shape((q_cols, group), halves),
        shape((q_cols // HEAD_WIDTH, group), floats),
        shape((1, width), floats),
    )
    scratch = [
        pltpu.VMEM((group, q_cols), halves),
        pltpu.VMEM((group, width), halves),
        *[pltpu.VMEM((group, hidden), halves)] * 4,
        *[pltpu.VMEM(weight.shape, halves) for weight in weights[:4]],
        *[pltpu.VMEM((block, width), floats)] * 2,
        *[pltpu.VMEM((block, width), halves)] * 6,
        *copy_semaphores(),
        pltpu.SemaphoreType.DMA((4,)),
    ]

    def kernel(*refs):
        mid_kernel(*refs[:4], refs[4:10], refs[10:20], refs[20:])

    return pl.pallas_call(
        kernel,
        out_shape=out_shape,
        in_specs=[VM] * 4 + [HB] * 6,
        out_specs=(VM,) * 10,
        scratch_shapes=scratch,
        compiler_params=pltpu.CompilerParams(
            collective_id=1, has_side_effects=True, vmem_limit_bytes=62 << 20
        ),
        name="middle",
    )(context_t, tokens, gain, grad_full, *weights)


def routes(target):
    pairs = []
    for index in range(32):
        dp, z = divmod(index, 4)
        there = target(dp // 4, dp // 2 % 2, dp % 2, z)
        if there is not None:
            y, x, c, z = there
            pairs.append((index, (y * 4 + x * 2 + c) * 4 + z))
    return pairs


ROUTES = {
    "core": routes(lambda y, x, c, z: (y, x, 1 - c, z)),
    "x": routes(lambda y, x, c, z: (y, 1 - x, c, z)),
    "y": routes(lambda y, x, c, z: (1 - y, x, c, z)),
    "near": routes(lambda y, x, c, z: (y, x, c, z ^ 1)),
    "far": routes(lambda y, x, c, z: (y, x, c, z ^ 2)),
    "cross": routes(lambda y, x, c, z: (y, x, 1 - c, z ^ 2)),
    "odd_far": routes(lambda y, x, c, z: (y, x, c, z ^ 2) if c else None),
    "odd_x": routes(lambda y, x, c, z: (y, 1 - x, c, z) if c else None),
    "odd_y": routes(lambda y, x, c, z: (1 - y, x, c, z) if c else None),
    "odd_xy": routes(lambda y, x, c, z: (1 - y, 1 - x, c, z) if c else None),
    "home": routes(lambda y, x, c, z: (y, x, 0, z ^ 2) if c else (y, x, 1, z)),
    "x_up": routes(lambda y, x, c, z: None if x else (y, 1, c, z)),
    "y_up": routes(lambda y, x, c, z: None if y else (1, x, c, z)),
    "x_down": routes(lambda y, x, c, z: (y, 0, c, z) if x else None),
    "y_down": routes(lambda y, x, c, z: (0, x, c, z) if y else None),
    "relay": routes(lambda y, x, c, z: (1, 0, c, z) if x and y else None),
    "unrelay": routes(lambda y, x, c, z: (1, 1, c, z) if y and not x else None),
}
FAR_BASE = 1 << 24


def send(block, way):
    return lax.ppermute(block, ("dp", "tp"), ROUTES[way])


def scatter_group(here, there):
    rows = here.shape[0] // 2
    there_sum = there[:rows] + send(there[rows:].astype(halves), "core").astype(floats)
    here_sum = here[:rows].astype(floats) + send(here[rows:].astype(halves), "core").astype(floats)
    return here_sum + send(there_sum.astype(halves), "near").astype(floats)


def dot_tt(a, b):
    return lax.dot_general(a, b, (((0,), (1,)), ((), ())), preferred_element_type=floats)


def rope_tables(positions):
    half_width = HEAD_WIDTH // 2
    inverse = 1.0 / rope_base ** (jnp.arange(half_width, dtype=floats) * 2.0 / HEAD_WIDTH)
    angles = inverse[:, None] * positions.astype(floats)[None, :]
    return jnp.cos(angles), jnp.sin(angles)


def turn(linear, cosine, sine):
    shaped = linear.reshape(-1, 2, HEAD_WIDTH // 2, linear.shape[-1])
    one, two = shaped[:, 0], shaped[:, 1]
    turned = jnp.stack([one * cosine - two * sine, two * cosine + one * sine], axis=1)
    return turned.reshape(linear.shape)


def norm_back(vectors, gain, grad):
    root = lax.rsqrt(jnp.mean(vectors * vectors, axis=-1, keepdims=True) + eps_norm)
    weighted = grad * gain
    slope = jnp.mean(weighted * vectors, axis=-1, keepdims=True)
    back = root * weighted - vectors * (root * root * root * slope)
    return back, jnp.sum(grad * vectors * root, axis=0)


def sum_rows_over_plane(grad, x, y, x_first):
    shaped = grad.reshape(2, 2, -1, grad.shape[-1])

    def pick(array, at, axis):
        return lax.dynamic_index_in_dim(array, at, axis, keepdims=False)

    axes = (("x", x, 1), ("y", y, 0)) if x_first else (("y", y, 0), ("x", x, 1))
    (way, at, axis), (way_two, at_two, _) = axes
    come = send(pick(shaped, 1 - at, axis), way)
    half = pick(shaped, at, axis).astype(floats) + come.astype(floats)
    come = send(pick(half, 1 - at_two, 0).astype(halves), way_two)
    return pick(half, at_two, 0) + come.astype(floats)


def sum_rows_home(part, odd):
    rows = part.shape[0] // 2
    first, second = part[:rows], part[rows:]
    one = send(jnp.where(odd, first, second).astype(halves), "home").astype(floats)
    two = send(second.astype(halves), "odd_far").astype(floats)
    return jnp.where(odd, one + two, first + one)


def local_regrouped(
    tokens,
    out_grad,
    segment_ids,
    attn_gain,
    query_weight,
    key_matrix,
    value_matrix,
    output_weight,
    mlp_gain,
    gate_weight,
    up_weight,
    down_weight,
):
    block = tokens.shape[0]
    row_len = 4 * block
    dp, z = lax.axis_index("dp"), lax.axis_index("tp")
    y, x, c = dp // 4, dp // 2 % 2, dp % 2
    j = dp // 2
    odd = c == 1
    pair, side = z // 2, z % 2
    q_cols, kv_cols = query_weight.shape[1], key_matrix.shape[1]
    heads = q_cols // HEAD_WIDTH
    group_width = q_cols // kv_cols
    ff_cols = gate_weight.shape[1]
    gain_attn, gain_mlp = attn_gain.astype(floats), mlp_gain.astype(floats)

    def base(j_of, core, pair_of, side_of):
        return (2 * j_of + core) * row_len + (2 * pair_of + side_of) * block

    bases = [
        base(j, c, pair, side),
        base(j, 1 - c, pair, side),
        base(j, c, pair, 1 - side),
        base(j, 1 - c, pair, 1 - side),
    ]
    counts = [jnp.sum((segment_ids < item).astype(jnp.int32)) for item in range(1, 4)]
    segs = jnp.concatenate([lax.dynamic_slice_in_dim(segment_ids, b, block) for b in bases])
    index = jnp.concatenate([b + jnp.arange(block, dtype=jnp.int32) for b in bases])
    start = jnp.zeros_like(segs)
    for item in range(1, 4):
        start = jnp.where(segs == item, counts[item - 1], start)
    cosine, sine = rope_tables(index - start)
    index_row, start_row = index[None, :], start[None, :]
    starts4 = start.reshape(4, block)

    tokens32 = tokens.astype(floats)
    joined = jnp.concatenate([query_weight, key_matrix, value_matrix], axis=1)
    q_t, pieces, normed_full, grad_full, joined, weight_o, weight_d = first_part(
        tokens, out_grad, gain_attn[None, :], cosine, sine, joined, output_weight, down_weight,
        q_cols, kv_cols,
    )
    slot = 2 * y + x
    rows = gate_weight.shape[0] // 4
    own_slices = [
        lax.dynamic_slice_in_dim(weight, slot * rows, rows) for weight in (gate_weight, up_weight)
    ]
    own_slices, pieces = lax.optimization_barrier((own_slices, pieces))
    slices = [send(part, "odd_far") for part in own_slices]

    piece_bases = []
    for n in range(2):
        side_n = side if n == 0 else 1 - side
        for cross in range(2):
            cores = (c, 1 - c) if cross == 0 else (1 - c, c)
            pair_of = pair if cross == 0 else 1 - pair
            for j_of, present in (
                (j, True),
                (j - 1, x == 1),
                (j - 2, y == 1),
                (j - 1, (y == 1) & (x == 0)),
            ):
                for core in cores:
                    piece_bases.append(
                        jnp.where(present, base(j_of, core, pair_of, side_n), FAR_BASE)
                    )
    total_blocks = len(piece_bases)

    def padded(values):
        values = jnp.stack(values).astype(jnp.int32)
        return jnp.pad(values, (0, total_blocks - values.shape[0]))

    sc = jnp.stack(
        [
            padded(piece_bases),
            padded(bases),
            jnp.pad(starts4[:, 0], (0, total_blocks - 4)),
            jnp.pad(starts4[:, -1], (0, total_blocks - 4)),
        ]
    )
    context_t, log_total = attend_forward(sc, q_t, index_row, start_row, pieces)

    (
        residual, grad_residual, attn_grad_full, part_out, gate_grad, up_grad, down_grad,
        d_context_t, delta, mlp_gain_part,
    ) = middle(
        context_t, tokens, gain_mlp[None, :], grad_full,
        (weight_o, weight_d, gate_weight, up_weight, *slices),
    )
    output = residual + scatter_group(part_out[: 2 * block], part_out[2 * block :])
    gate_sum = sum_rows_home(sum_rows_over_plane(gate_grad, x, y, True), odd)
    up_sum = sum_rows_home(sum_rows_over_plane(up_grad, x, y, False), odd)
    down_sum = sum_rows_home(sum_rows_over_plane(down_grad, x, y, True), odd)

    output_grad = dot_tt(attn_grad_full, context_t).astype(halves)
    output_sum = sum_rows_home(sum_rows_over_plane(output_grad, x, y, False), odd)
    d_query_t, d_pieces = attend_backward(
        sc, q_t, d_context_t, log_total, delta, index_row, start_row, pieces
    )
    d_halves = []
    for n in range(2):
        sums = []
        for cross in range(2):
            own, from_x, from_y, from_relay = (d_pieces[8 * n + 4 * cross + i] for i in range(4))
            back = send(from_relay, "unrelay").astype(floats)
            from_y = (from_y.astype(floats) + back).astype(halves)
            sums.append(
                own.astype(floats)
                + send(from_x, "x_down").astype(floats)
                + send(from_y, "y_down").astype(floats)
            )
        d_halves.append(sums[0] + send(sums[1].astype(halves), "cross").astype(floats))
    d_kv = jnp.concatenate(d_halves, axis=1)
    d_turned = turn(jnp.concatenate([d_query_t, d_kv[:kv_cols]]), cosine, -sine)
    d_linear = jnp.concatenate([d_turned, d_kv[kv_cols:]]).astype(halves)
    here_d = dot_tt(d_linear[:, : 2 * block], joined)
    there_d = dot_tt(d_linear[:, 2 * block :], joined)
    grad_normed = scatter_group(here_d, there_d)
    proj_grad = lax.dot_general(
        normed_full, d_linear, (((0,), (1,)), ((), ())), preferred_element_type=floats
    ).astype(halves)
    proj_sum = sum_rows_home(sum_rows_over_plane(proj_grad, x, y, True), odd)
    grad_tokens_part, attn_gain_part = norm_back(tokens32, gain_attn, grad_normed)
    input_grad = grad_residual + grad_tokens_part

    gains = jnp.stack([attn_gain_part, mlp_gain_part[0]])
    for way in ("core", "x", "y", "near", "far"):
        gains = gains + send(gains, way)
    per = gains.shape[1] // 8
    gains = lax.dynamic_slice_in_dim(gains, dp * per, per, axis=1)
    return (
        output.astype(halves),
        input_grad,
        gains[0],
        proj_sum[:, :q_cols],
        proj_sum[:, q_cols : q_cols + kv_cols],
        proj_sum[:, q_cols + kv_cols :],
        output_sum.T,
        gains[1],
        gate_sum,
        up_sum,
        down_sum.T,
    )


def solution(mesh):
    regroup = mesh.shape["dp"] == 8 and mesh.shape["tp"] == 4
    chosen = local_regrouped if regroup else local
    return jax.shard_map(
        chosen,
        mesh=mesh,
        in_specs=(
            P(("dp", "tp"), None),
            P(("dp", "tp"), None),
            P(),
            P(),
            P(None, "tp"),
            P(None, "tp"),
            P(None, "tp"),
            P("tp", None),
            P(),
            P(None, "tp"),
            P(None, "tp"),
            P("tp", None),
        ),
        out_specs=(
            P(("dp", "tp"), None),
            P(("dp", "tp"), None),
            P("dp"),
            P("dp", "tp"),
            P("dp", "tp"),
            P("dp", "tp"),
            P("tp", "dp"),
            P("dp"),
            P("dp", "tp"),
            P("dp", "tp"),
            P("tp", "dp"),
        ),
        check_vma=False,
    )
```

```python
import functools

import jax
import jax.numpy as jnp
from jax import lax
from jax.experimental import pallas as pl
from jax.experimental.pallas import tpu as pltpu
from jax.sharding import PartitionSpec as P

HEAD_WIDTH = 96
BLK = 256
LOG2E = 1.4426950408889634
SCORE = LOG2E * HEAD_WIDTH ** (-0.5)
VSCALE = 2.0 ** -9
floats = jnp.float32
halves = jnp.bfloat16


def dot_nn(a, b):
    return jnp.dot(a, b, preferred_element_type=floats)


def dot_nt(a, b):
    return lax.dot_general(a, b, (((1,), (1,)), ((), ())), preferred_element_type=floats)


def pair_state(sc, kb, qb):
    key_base = sc[0, kb]
    q_base, least, most = sc[1, qb], sc[2, qb], sc[3, qb]
    needed = (key_base <= q_base + (BLK - 1)) & (key_base + (BLK - 1) >= least)
    whole = (key_base + (BLK - 1) <= q_base) & (key_base >= most)
    return key_base, needed, whole


def allowed_mask(key_base, tok_ref, start_ref, lanes):
    keys = key_base + lax.broadcasted_iota(jnp.int32, (BLK, BLK), 0)
    return (keys <= tok_ref[0:1, lanes]) & (keys >= start_ref[0:1, lanes])


def fwd_kernel(n, width, first, last, sc, q_ref, tok_ref, start_ref, pieces, *refs):
    if not first:
        acc_in, sum_in = refs[:2]
        refs = refs[2:]
    out_acc, out_sum = refs[:2]
    kv, keys_nat, acc, total, q_wide, sem = refs[2:]
    per = width // BLK
    for i in range(n):
        pltpu.make_async_copy(pieces.at[i], kv.at[i], sem.at[i]).start()
    if first:
        acc[...] = jnp.zeros_like(acc)
        total[...] = jnp.zeros_like(total)
    else:
        acc[...] = acc_in[...]
        total[...] = sum_in[...]
    for i in range(n):
        pltpu.make_async_copy(pieces.at[i], kv.at[i], sem.at[i]).wait()
    heads_kv = pieces.shape[1] // (2 * HEAD_WIDTH)
    group = q_ref.shape[0] // (heads_kv * HEAD_WIDTH)
    v_off = heads_kv * HEAD_WIDTH
    places = [
        (h, slice((h * group + g) * HEAD_WIDTH, (h * group + g + 1) * HEAD_WIDTH), slice(qb * BLK, (qb + 1) * BLK),
         slice(h * HEAD_WIDTH, (h + 1) * HEAD_WIDTH), slice((qb * group + g) * BLK, (qb * group + g + 1) * BLK), h * group + g)
        for h in range(heads_kv) for g in range(group) for qb in range(q_ref.shape[1] // BLK)
    ]
    for h, rows, lanes, wrows, wlanes, hd in places:
        q_wide[wrows, wlanes] = q_ref[rows, lanes]

    def key_block(kb, carry):
        piece = kb // per
        klanes = pl.ds(pl.multiple_of((kb % per) * BLK, BLK), BLK)
        for h in range(heads_kv):
            keys_nat[h] = kv[piece, h * HEAD_WIDTH : (h + 1) * HEAD_WIDTH, klanes].T

        def query_block(qb, carry):
            key_base, needed, whole = pair_state(sc, kb, qb)
            lanes = pl.ds(pl.multiple_of(qb * BLK, BLK), BLK)

            def unit(masked):
                wide = pl.ds(pl.multiple_of(qb * (group * BLK), group * BLK), group * BLK)
                if masked:
                    allowed = allowed_mask(key_base, tok_ref, start_ref, lanes)
                    allowed = jnp.concatenate([allowed] * group, axis=1)
                scores = [
                    dot_nn(keys_nat[h], q_wide[h * HEAD_WIDTH : (h + 1) * HEAD_WIDTH, wide])
                    for h in range(heads_kv)
                ]
                weights = [jnp.exp2(s * SCORE) for s in scores]
                if masked:
                    weights = [jnp.where(allowed, w, 0.0) for w in weights]
                sums = [jnp.sum(w, axis=0, keepdims=True) for w in weights]
                parts = [
                    dot_nn(
                        kv[piece, v_off + h * HEAD_WIDTH : v_off + (h + 1) * HEAD_WIDTH, klanes],
                        weights[h].astype(halves),
                    )
                    for h in range(heads_kv)
                ]
                for h in range(heads_kv):
                    total[h : h + 1, wide] += sums[h]
                    acc[h * HEAD_WIDTH : (h + 1) * HEAD_WIDTH, wide] += parts[h]

            pl.when(needed & whole)(lambda: unit(False))
            pl.when(needed & jnp.logical_not(whole))(lambda: unit(True))
            return carry

        return lax.fori_loop(0, q_ref.shape[1] // BLK, query_block, carry)

    lax.fori_loop(0, n * per, key_block, 0)
    if last:
        for h, rows, lanes, wrows, wlanes, hd in places:
            row = total[h : h + 1, wlanes]
            out_acc[rows, lanes] = (acc[wrows, wlanes] * ((1.0 / VSCALE) / row)).astype(halves)
            out_sum[hd : hd + 1, lanes] = jnp.log2(row)
    else:
        out_acc[...] = acc[...]
        out_sum[...] = total[...]


VM = pl.BlockSpec(memory_space=pltpu.VMEM)
SM = pl.BlockSpec(memory_space=pltpu.SMEM)
HB = pl.BlockSpec(memory_space=pl.ANY)


def attend_forward(sc, q_t, tok, start, pieces, state=None, last=True):
    n, width = pieces.shape[0], pieces.shape[2]
    heads = q_t.shape[0] // HEAD_WIDTH
    heads_kv = pieces.shape[1] // (2 * HEAD_WIDTH)
    first = state is None
    tokens = q_t.shape[1]
    out_shape = (
        jax.ShapeDtypeStruct(q_t.shape, halves if last else floats),
        jax.ShapeDtypeStruct((heads, tokens), floats),
    )
    return pl.pallas_call(
        functools.partial(fwd_kernel, n, width, first, last),
        out_shape=out_shape,
        in_specs=[SM, VM, VM, VM] + [HB] + ([] if first else [VM, VM]),
        out_specs=(VM, VM),
        scratch_shapes=[
            pltpu.VMEM(pieces.shape, halves),
            pltpu.VMEM((heads_kv, BLK, HEAD_WIDTH), halves),
            pltpu.VMEM((heads_kv * HEAD_WIDTH, tokens * heads // heads_kv), floats),
            pltpu.VMEM((heads_kv, tokens * heads // heads_kv), floats),
            pltpu.VMEM((heads_kv * HEAD_WIDTH, tokens * heads // heads_kv), halves),
            pltpu.SemaphoreType.DMA((n,)),
        ],
        compiler_params=pltpu.CompilerParams(vmem_limit_bytes=40 << 20),
        name="attend_forward",
    )(sc, q_t, tok, start, pieces, *(() if first else state))


def bwd_kernel(n, width, first, sc, q_ref, do_ref, log_ref, delta_ref, tok_ref, start_ref, pieces, *refs):
    if not first:
        dq_in = refs[0]
        refs = refs[1:]
    dq_out = refs[0]
    dkv_out = refs[1]
    kv, dkv, keys_nat, vals_nat, acc, q_wide, do_wide, log_wide, delta_wide, dq_wide, sem, osem = refs[2:]
    per = width // BLK
    for i in range(n):
        pltpu.make_async_copy(pieces.at[i], kv.at[i], sem.at[i]).start()
    for i in range(n):
        pltpu.make_async_copy(pieces.at[i], kv.at[i], sem.at[i]).wait()
    heads_kv = pieces.shape[1] // (2 * HEAD_WIDTH)
    group = q_ref.shape[0] // (heads_kv * HEAD_WIDTH)
    v_off = heads_kv * HEAD_WIDTH
    places = [
        (h, slice((h * group + g) * HEAD_WIDTH, (h * group + g + 1) * HEAD_WIDTH), slice(qb * BLK, (qb + 1) * BLK),
         slice(h * HEAD_WIDTH, (h + 1) * HEAD_WIDTH), slice((qb * group + g) * BLK, (qb * group + g + 1) * BLK), h * group + g)
        for h in range(heads_kv) for g in range(group) for qb in range(q_ref.shape[1] // BLK)
    ]
    for h, rows, lanes, wrows, wlanes, hd in places:
        q_wide[wrows, wlanes] = q_ref[rows, lanes]
        do_wide[wrows, wlanes] = do_ref[rows, lanes]
        log_wide[h : h + 1, wlanes] = log_ref[hd : hd + 1, lanes]
        delta_wide[h : h + 1, wlanes] = delta_ref[hd : hd + 1, lanes]
        dq_wide[wrows, wlanes] = jnp.zeros((HEAD_WIDTH, BLK), floats) if first else dq_in[rows, lanes]
    out_scale = (1.0 / VSCALE) * HEAD_WIDTH ** (-0.5)

    def key_block(kb, carry):
        piece = kb // per
        klanes = pl.ds(pl.multiple_of((kb % per) * BLK, BLK), BLK)
        for h in range(heads_kv):
            keys_nat[h] = kv[piece, h * HEAD_WIDTH : (h + 1) * HEAD_WIDTH, klanes].T
            vals_nat[h] = kv[piece, v_off + h * HEAD_WIDTH : v_off + (h + 1) * HEAD_WIDTH, klanes].T
        acc[...] = jnp.zeros_like(acc)

        def query_block(qb, carry):
            key_base, needed, whole = pair_state(sc, kb, qb)
            lanes = pl.ds(pl.multiple_of(qb * BLK, BLK), BLK)

            def unit(masked):
                wide = pl.ds(pl.multiple_of(qb * (group * BLK), group * BLK), group * BLK)
                if masked:
                    allowed = allowed_mask(key_base, tok_ref, start_ref, lanes)
                    allowed = jnp.concatenate([allowed] * group, axis=1)
                heads = range(heads_kv)
                krows = [slice(h * HEAD_WIDTH, (h + 1) * HEAD_WIDTH) for h in heads]
                vrows = [slice(v_off + h * HEAD_WIDTH, v_off + (h + 1) * HEAD_WIDTH) for h in heads]
                qt = [q_wide[krows[h], wide] for h in heads]
                dot = [do_wide[krows[h], wide] for h in heads]
                scores = [dot_nn(keys_nat[h], qt[h]) for h in heads]
                dprobs = [dot_nn(vals_nat[h], dot[h]) for h in heads]
                weights = [
                    jnp.exp2(scores[h] * SCORE - log_wide[h : h + 1, wide]) for h in heads
                ]
                if masked:
                    weights = [jnp.where(allowed, w, 0.0) for w in weights]
                ds = [
                    (weights[h] * (dprobs[h] - delta_wide[h : h + 1, wide])).astype(halves)
                    for h in heads
                ]
                dv = [dot_nt(dot[h], weights[h].astype(halves)) for h in heads]
                dk = [dot_nt(qt[h], ds[h]) for h in heads]
                dq = [dot_nn(kv[piece, krows[h], klanes], ds[h]) for h in heads]
                for h in heads:
                    acc[vrows[h], :] += dv[h]
                    acc[krows[h], :] += dk[h]
                    dq_wide[krows[h], wide] += dq[h]

            pl.when(needed & whole)(lambda: unit(False))
            pl.when(needed & jnp.logical_not(whole))(lambda: unit(True))
            return carry

        carry = lax.fori_loop(0, q_ref.shape[1] // BLK, query_block, carry)
        dkv[piece, 0:v_off, klanes] = (acc[0:v_off, :] * out_scale).astype(halves)
        dkv[piece, v_off:, klanes] = acc[v_off:, :].astype(halves)
        return carry

    lax.fori_loop(0, n * per, key_block, 0)
    for i in range(n):
        pltpu.make_async_copy(dkv.at[i], dkv_out.at[i], osem.at[i]).start()
    for h, rows, lanes, wrows, wlanes, hd in places:
        dq_out[rows, lanes] = dq_wide[wrows, wlanes] * out_scale
    for i in range(n):
        pltpu.make_async_copy(dkv.at[i], dkv_out.at[i], osem.at[i]).wait()


def attend_backward(sc, q_t, do_t, log_total, delta, tok, start, pieces):
    n, width = pieces.shape[0], pieces.shape[2]
    heads_kv = pieces.shape[1] // (2 * HEAD_WIDTH)
    wide = q_t.shape[0] // (heads_kv * HEAD_WIDTH) * q_t.shape[1]
    outs = pl.pallas_call(
        functools.partial(bwd_kernel, n, width, True),
        out_shape=(
            jax.ShapeDtypeStruct(q_t.shape, floats),
            jax.ShapeDtypeStruct(pieces.shape, halves),
        ),
        in_specs=[SM] + [VM] * 6 + [HB],
        out_specs=(VM, HB),
        scratch_shapes=[
            pltpu.VMEM(pieces.shape, halves),
            pltpu.VMEM(pieces.shape, halves),
            pltpu.VMEM((heads_kv, BLK, HEAD_WIDTH), halves),
            pltpu.VMEM((heads_kv, BLK, HEAD_WIDTH), halves),
            pltpu.VMEM((pieces.shape[1], BLK), floats),
            pltpu.VMEM((heads_kv * HEAD_WIDTH, wide), halves),
            pltpu.VMEM((heads_kv * HEAD_WIDTH, wide), halves),
            pltpu.VMEM((heads_kv, wide), floats),
            pltpu.VMEM((heads_kv, wide), floats),
            pltpu.VMEM((heads_kv * HEAD_WIDTH, wide), floats),
            pltpu.SemaphoreType.DMA((n,)),
            pltpu.SemaphoreType.DMA((n,)),
        ],
        compiler_params=pltpu.CompilerParams(vmem_limit_bytes=44 << 20),
        name="attend_backward",
    )(sc, q_t, do_t, log_total, delta, tok, start, pieces)
    return outs


eps_norm = 1e-05
rope_base = 100000.0
reach_limit = 8


def shifted(block, axis, distance):
    devices = range(lax.axis_size(axis))
    route = [(i - distance, i) for i in devices if i - distance in devices]
    return lax.ppermute(block, axis, route)


def rms_scale(value_vectors, gain_vec):
    return (
        value_vectors
        * lax.rsqrt(jnp.mean(value_vectors * value_vectors, axis=-1, keepdims=True) + eps_norm)
        * gain_vec
    )


def rotary_turn(value_vectors, token_positions, heads):
    half_width = HEAD_WIDTH // 2
    inverse = 1.0 / rope_base ** (jnp.arange(half_width, dtype=jnp.float32) * 2.0 / HEAD_WIDTH)
    angles = token_positions.astype(jnp.float32)[:, None] * inverse[None, :]
    cosine = jnp.cos(angles)[:, None, :]
    sine_part = jnp.sin(angles)[:, None, :]
    shaped = value_vectors.reshape(value_vectors.shape[0], heads, HEAD_WIDTH)
    first_half = shaped[..., :half_width]
    second = shaped[..., half_width:]
    turned = jnp.concatenate(
        [first_half * cosine - second * sine_part, second * cosine + first_half * sine_part],
        axis=-1,
    )
    return turned.reshape(value_vectors.shape)


def swiglu(gate_pre, up_pre):
    return jax.nn.silu(gate_pre) * up_pre


def contract_rows(left_side, right_side):
    return lax.dot_general(
        left_side, right_side, (((0,), (0,)), ((), ())), preferred_element_type=jnp.float32
    )


def contract_cols(left_side, right_side):
    return lax.dot_general(
        left_side, right_side, (((1,), (1,)), ((), ())), preferred_element_type=jnp.float32
    )


def local(
    tokens,
    out_grad,
    segment_ids,
    attn_gain,
    query_weight,
    key_matrix,
    value_matrix,
    output_weight,
    mlp_gain,
    gate_weight,
    up_weight,
    down_weight,
):
    floats = jnp.float32
    halves = jnp.bfloat16
    shard_rows = tokens.shape[0]
    row_len = shard_rows * lax.axis_size("tp")
    row_index = lax.axis_index("dp")
    reach = min(reach_limit, lax.axis_size("dp") // 2)
    heads_q = query_weight.shape[1] // HEAD_WIDTH
    heads_kv = key_matrix.shape[1] // HEAD_WIDTH
    group_width = heads_q // heads_kv
    q_cols = heads_q * HEAD_WIDTH
    kv_cols = heads_kv * HEAD_WIDTH
    score_scale = HEAD_WIDTH ** (-0.5)
    row_first = row_index * row_len
    seg_row = lax.dynamic_slice_in_dim(segment_ids, row_first, row_len)
    index_row = row_first + jnp.arange(row_len, dtype=jnp.int32)
    every_index = jnp.arange(segment_ids.shape[0], dtype=jnp.int32)
    marks = (segment_ids[1:] != segment_ids[:-1]).astype(jnp.int32)
    starts = jnp.concatenate([jnp.zeros((1,), jnp.int32), marks * every_index[1:]])
    is_at = (starts[None, :] <= index_row[:, None]).astype(jnp.int32)
    token_positions = index_row - jnp.max(is_at * starts[None, :], axis=1)
    tokens32 = tokens.astype(floats)
    gain_attn = attn_gain.astype(floats)
    gain_mlp = mlp_gain.astype(floats)
    normed = rms_scale(tokens32, gain_attn).astype(halves)
    normed_full = lax.all_gather(normed, "tp", axis=0, tiled=True)
    joined = jnp.concatenate([query_weight, key_matrix, value_matrix], axis=1)
    projected = jnp.dot(normed_full, joined, preferred_element_type=floats)
    q_linear = projected[:, :q_cols]
    key_linear_out = projected[:, q_cols : q_cols + kv_cols]
    query_vectors = rotary_turn(q_linear, token_positions, heads_q).astype(halves)
    key_vectors = rotary_turn(key_linear_out, token_positions, heads_kv).astype(halves)
    value_vectors = projected[:, q_cols + kv_cols :].astype(halves)
    query_heads = query_vectors.reshape(row_len, heads_kv, group_width, HEAD_WIDTH)
    held_blocks = [(key_vectors, value_vectors)]
    moving = (key_vectors, value_vectors)
    for step_hop in range(reach):
        moving = shifted((moving[0], moving[1]), "dp", 1)
        held_blocks.append(moving)

    def block_mask(step_hop):
        key_row = row_index - step_hop
        seg_keys = lax.dynamic_slice_in_dim(segment_ids, jnp.maximum(key_row, 0) * row_len, row_len)
        key_index = key_row * row_len + jnp.arange(row_len, dtype=jnp.int32)
        return (seg_keys[None, :] == seg_row[:, None]) & (key_index[None, :] <= index_row[:, None])

    def block_needed(step_hop):
        last_key = jnp.maximum((row_index - step_hop + 1) * row_len - 1, 0)
        return (row_index >= step_hop) & (segment_ids[last_key] == seg_row[0])

    block_masks = [block_mask(step_hop) for step_hop in range(reach + 1)]

    def apply_block(step_hop, update, state_in):
        key_block, value_block = held_blocks[step_hop]
        if step_hop == 0:
            return update(state_in, key_block, value_block, block_masks[0])
        return lax.cond(
            block_needed(step_hop),
            update,
            lambda state_kept, key_skip, value_skip, mask_skip: state_kept,
            state_in,
            key_block,
            value_block,
            block_masks[step_hop],
        )

    def scores(key_block, allowed):
        raw_scores = jnp.einsum(
            "qhgd,khd->hgqk",
            query_heads,
            key_block.reshape(row_len, heads_kv, HEAD_WIDTH),
            preferred_element_type=floats,
        )
        return jnp.where(allowed, raw_scores * score_scale, -jnp.inf)

    def add_online(state_in, key_block, value_block, allowed):
        run_max, run_total, run_sum = state_in
        block_scores = scores(key_block, allowed)
        new_max = jnp.maximum(run_max, jnp.max(block_scores, axis=-1))
        factor = jnp.exp(run_max - new_max)
        weights = jnp.exp(block_scores - new_max[..., None])
        run_total = run_total * factor + jnp.sum(weights, axis=-1)
        run_sum = run_sum * jnp.moveaxis(factor, 2, 0)[..., None] + jnp.einsum(
            "hgqk,khd->qhgd",
            weights.astype(halves),
            value_block.reshape(row_len, heads_kv, HEAD_WIDTH),
            preferred_element_type=floats,
        )
        return (new_max, run_total, run_sum)

    online = (
        jnp.full((heads_kv, group_width, row_len), -jnp.inf, floats),
        jnp.zeros((heads_kv, group_width, row_len), floats),
        jnp.zeros((row_len, heads_kv, group_width, HEAD_WIDTH), floats),
    )
    for step_hop in range(reach + 1):
        online = apply_block(step_hop, add_online, online)
    run_max, run_total, run_sum = online
    log_total = (run_max + jnp.log(run_total))[..., None]
    context_heads = (run_sum / jnp.moveaxis(run_total, 2, 0)[..., None]).astype(halves)
    context = context_heads.reshape(row_len, q_cols)
    residual = tokens32 + lax.psum_scatter(
        jnp.dot(context, output_weight, preferred_element_type=floats).astype(jnp.bfloat16),
        "tp",
        scatter_dimension=0,
        tiled=True,
    ).astype(jnp.float32)
    mlp_normed = rms_scale(residual, gain_mlp).astype(halves)
    mlp_full = lax.all_gather(mlp_normed, "tp", axis=0, tiled=True)
    gate_pre = jnp.dot(mlp_full, gate_weight, preferred_element_type=floats)
    up_pre = jnp.dot(mlp_full, up_weight, preferred_element_type=floats)
    hidden = swiglu(gate_pre, up_pre).astype(halves)
    output = residual + lax.psum_scatter(
        jnp.dot(hidden, down_weight, preferred_element_type=floats).astype(jnp.bfloat16),
        "tp",
        scatter_dimension=0,
        tiled=True,
    ).astype(jnp.float32)
    grad_full = lax.all_gather(out_grad, "tp", axis=0, tiled=True)
    grad_hidden = contract_cols(grad_full, down_weight)
    down_grad = contract_rows(grad_full, hidden)
    silu_back = jax.vjp(swiglu, gate_pre, up_pre)[1]
    grad_gate, grad_up = silu_back(grad_hidden)
    grad_gate = grad_gate.astype(halves)
    grad_up = grad_up.astype(halves)
    gate_grad = contract_rows(mlp_full, grad_gate)
    up_grad = contract_rows(mlp_full, grad_up)
    grad_mlp_normed = lax.psum_scatter(
        (contract_cols(grad_gate, gate_weight) + contract_cols(grad_up, up_weight)).astype(
            jnp.bfloat16
        ),
        "tp",
        scatter_dimension=0,
        tiled=True,
    ).astype(jnp.float32)
    mlp_norm_back = jax.vjp(rms_scale, residual, gain_mlp)[1]
    grad_residual_part, mlp_gain_part = mlp_norm_back(grad_mlp_normed)
    grad_residual = out_grad.astype(floats) + grad_residual_part
    attn_grad_full = lax.all_gather(grad_residual.astype(halves), "tp", axis=0, tiled=True)
    output_grad = contract_rows(attn_grad_full, context)
    grad_context = (
        contract_cols(attn_grad_full, output_weight)
        .astype(halves)
        .reshape(row_len, heads_kv, group_width, HEAD_WIDTH)
    )
    delta_col = jnp.einsum(
        "qhgd,qhgd->hgq", grad_context, context_heads, preferred_element_type=floats
    )[..., None]

    def add_grads(state_in, key_block, value_block, allowed):
        query_acc, key_acc, value_acc = state_in
        probabilities = jnp.exp(scores(key_block, allowed) - log_total)
        grad_probs = jnp.einsum(
            "qhgd,khd->hgqk",
            grad_context,
            value_block.reshape(row_len, heads_kv, HEAD_WIDTH),
            preferred_element_type=floats,
        )
        grad_scores = (probabilities * (grad_probs - delta_col)).astype(halves)
        key_heads = key_block.reshape(row_len, heads_kv, HEAD_WIDTH)
        query_acc = (
            query_acc
            + jnp.einsum("hgqk,khd->qhgd", grad_scores, key_heads, preferred_element_type=floats)
            * score_scale
        )
        key_acc = (
            key_acc
            + jnp.einsum(
                "hgqk,qhgd->khd", grad_scores, query_heads, preferred_element_type=floats
            ).reshape(row_len, kv_cols)
            * score_scale
        )
        value_acc = value_acc + jnp.einsum(
            "hgqk,qhgd->khd",
            probabilities.astype(halves),
            grad_context,
            preferred_element_type=floats,
        ).reshape(row_len, kv_cols)
        return (query_acc, key_acc, value_acc)

    query_acc = jnp.zeros((row_len, heads_kv, group_width, HEAD_WIDTH), floats)
    carried = (jnp.zeros((row_len, kv_cols), floats), jnp.zeros((row_len, kv_cols), floats))
    for step_hop in range(reach, 0, -1):
        query_acc, key_acc, value_acc = apply_block(
            step_hop, add_grads, (query_acc, carried[0], carried[1])
        )
        carried = (
            shifted(key_acc.astype(jnp.bfloat16), "dp", -1).astype(key_acc.dtype),
            shifted(value_acc.astype(jnp.bfloat16), "dp", -1).astype(value_acc.dtype),
        )
    query_acc, key_total, value_total = apply_block(
        0, add_grads, (query_acc, carried[0], carried[1])
    )
    query_back = jax.vjp(lambda linear: rotary_turn(linear, token_positions, heads_q), q_linear)[1]
    key_back = jax.vjp(
        lambda linear: rotary_turn(linear, token_positions, heads_kv), key_linear_out
    )[1]
    grad_q_linear = query_back(query_acc.reshape(row_len, q_cols))[0]
    grad_k_linear = key_back(key_total)[0]
    grads_joined = jnp.concatenate([grad_q_linear, grad_k_linear, value_total], axis=1).astype(
        halves
    )
    proj_grad = contract_rows(normed_full, grads_joined)
    grad_normed = lax.psum_scatter(
        contract_cols(grads_joined, joined).astype(jnp.bfloat16),
        "tp",
        scatter_dimension=0,
        tiled=True,
    ).astype(jnp.float32)
    attn_norm_back = jax.vjp(rms_scale, tokens32, gain_attn)[1]
    grad_tokens_part, attn_gain_part = attn_norm_back(grad_normed)
    input_grad = grad_residual + grad_tokens_part
    def scatter_rows(grad):
        return lax.psum_scatter(
            grad.astype(halves), "dp", scatter_dimension=0, tiled=True
        ).astype(floats)

    mlp_sums = scatter_rows(jnp.concatenate([gate_grad, up_grad, down_grad], axis=1))
    ff_cols = gate_weight.shape[1]
    gate_sum = mlp_sums[:, :ff_cols]
    up_sum = mlp_sums[:, ff_cols : 2 * ff_cols]
    down_sum = mlp_sums[:, 2 * ff_cols :]
    attn_sums = scatter_rows(jnp.concatenate([proj_grad, output_grad], axis=1))
    query_sum = attn_sums[:, :q_cols]
    key_sum = attn_sums[:, q_cols : q_cols + kv_cols]
    value_sum = attn_sums[:, q_cols + kv_cols : q_cols + 2 * kv_cols]
    output_sum = attn_sums[:, q_cols + 2 * kv_cols :]
    attn_gain_sum = lax.psum_scatter(attn_gain_part, "dp", scatter_dimension=0, tiled=True)
    mlp_gain_sum = lax.psum_scatter(mlp_gain_part, "dp", scatter_dimension=0, tiled=True)
    attn_gain_total, mlp_gain_total = lax.psum((attn_gain_sum, mlp_gain_sum), "tp")
    return (
        output.astype(halves),
        input_grad,
        attn_gain_total,
        query_sum,
        key_sum,
        value_sum,
        output_sum.T,
        mlp_gain_total,
        gate_sum,
        up_sum,
        down_sum.T,
    )


MESH = pl.DeviceIdType.MESH


def meet(devices):
    barrier = pltpu.get_barrier_semaphore()
    for device in devices:
        pl.semaphore_signal(barrier, inc=1, device_id=device, device_id_type=MESH)
    pl.semaphore_wait(barrier, len(devices))


def tiles(total, step, body):
    def one(i, carry):
        body(pl.ds(pl.multiple_of(i * step, step), step))
        return carry

    lax.fori_loop(0, total // step, one, 0)


CHUNKS = 4


class GroupSum:
    def __init__(self, copies, bufs, place):
        self.copies, self.bufs, self.place = copies, bufs, place

    def run(self, product):
        part_near, part_own, out_far, out_beside, out_near, in_near, in_own, in_sum = self.bufs

        def put_there(cols, value):
            rows = value.shape[0] // 2
            part_near[:, cols] = value[:rows]
            out_far[:, cols] = value[rows:].astype(halves)

        def put_here(cols, value):
            rows = value.shape[0] // 2
            part_own[:, cols] = value[:rows]
            out_beside[:, cols] = value[rows:].astype(halves)

        product(1, put_there)
        self.far = self.copies.make(out_far, in_near, self.place.beside)
        self.far.start()
        product(0, put_here)
        self.side = self.copies.make(out_beside, in_own, self.place.beside)
        self.side.start()
        self.far.wait_recv()
        rows = part_near.shape[0] // CHUNKS
        self.sums = []
        for k in range(CHUNKS):
            at = pl.ds(k * rows, rows)
            out_near[at, :] = (part_near[at, :] + in_near[at, :].astype(floats)).astype(halves)
            copy = self.copies.make(out_near.at[at], in_sum.at[at], self.place.near)
            copy.start()
            self.sums.append(copy)

    def take(self, k):
        part_near, part_own, out_far, out_beside, out_near, in_near, in_own, in_sum = self.bufs
        if k == 0:
            self.side.wait_recv()
        self.sums[k].wait_recv()
        rows = part_own.shape[0] // CHUNKS
        at = pl.ds(k * rows, rows)
        return part_own[at, :] + in_own[at, :].astype(floats) + in_sum[at, :].astype(floats)

    def finish(self):
        for copy in (self.far, self.side, *self.sums):
            copy.wait_send()


class GroupGather:
    def __init__(self, copies, full, block, place):
        self.copies, self.full, self.block, self.place = copies, full, block, place
        self.sent = []

    def slot(self, n, k):
        rows = self.block // CHUNKS
        return self.full.at[pl.ds(n * self.block + k * rows, rows)]

    def put(self, k):
        for i, (n, device) in enumerate(((2, self.place.near), (1, self.place.beside))):
            copy = self.copies.make(self.slot(0, k), self.slot(n, k), device)
            copy.start()
            self.sent.append((i, copy))

    def wait_here(self):
        for i, copy in self.sent:
            if i == 1:
                copy.wait_recv()

    def wait_there(self):
        relays = []
        k = 0
        for i, copy in self.sent:
            if i == 0:
                copy.wait_recv()
                relay = self.copies.make(self.slot(2, k), self.slot(3, k), self.place.beside)
                relay.start()
                relays.append(relay)
                k += 1
        for relay in relays:
            relay.wait_recv()
        self.sent += [(2, relay) for relay in relays]

    def finish(self):
        for _, copy in self.sent:
            copy.wait_send()


class Copies:
    limit = 96

    def __init__(self, send_sems, recv_sems):
        self.send_sems, self.recv_sems, self.used = send_sems, recv_sems, 0

    def make(self, src, dst, device):
        i = self.used
        self.used += 1
        return pltpu.make_async_remote_copy(
            src_ref=src,
            dst_ref=dst,
            send_sem=self.send_sems.at[i],
            recv_sem=self.recv_sems.at[i],
            device_id=device,
            device_id_type=MESH,
        )


def copy_semaphores():
    return [pltpu.SemaphoreType.DMA((Copies.limit,)), pltpu.SemaphoreType.DMA((Copies.limit,))]


class Place:
    def __init__(self):
        dp, z = lax.axis_index("dp"), lax.axis_index("tp")
        self.dp, self.z = dp, z
        self.c = lax.rem(dp, 2)
        self.x = lax.rem(dp // 2, 2)
        self.y = dp // 4
        far_z = lax.rem(z + 2, 4)
        self.beside = (dp + 1 - 2 * self.c, z)
        self.near = (dp, z + 1 - 2 * lax.rem(z, 2))
        self.far = (dp, far_z)
        self.cross = (self.beside[0], far_z)
        self.over_x = (dp + 2 - 4 * self.x, z)
        self.over_y = (dp + 4 - 8 * self.y, z)
        self.slot = 2 * self.y + self.x
        self.slot_x = 2 * self.y + 1 - self.x
        self.slot_y = 2 - 2 * self.y + self.x
        self.odd = self.c == 1
        self.corner = (self.x == 1) & (self.y == 1)
        self.turn = (self.x == 0) & (self.y == 1)


class PlaneFetch:
    def __init__(self, copies, place, out, own=None):
        self.place, self.out = place, out
        rows = out.shape[0] // 8

        def part(slot, ch):
            return pl.ds(slot * (2 * rows) + ch * rows, rows)

        def remote(slot, ch, device):
            at = part(slot, ch)
            return copies.make(out.at[at], out.at[at], device)

        p = place
        self.hop = None
        if own is not None:
            self.hop = [
                copies.make(own.at[part(p.slot, ch)], out.at[part(p.slot, ch)], p.far)
                for ch in range(2)
            ]
        self.x = [remote(p.slot, ch, p.over_x) for ch in range(2)]
        self.y = [remote(p.slot, ch, p.over_y) for ch in range(2)]
        self.relay_y = remote(p.slot_x, 0, p.over_y)
        self.relay_x = remote(p.slot_y, 1, p.over_x)

    def start(self):
        @pl.when(self.place.odd)
        def _():
            for copy in self.hop:
                copy.start()

    def forward(self):
        @pl.when(self.place.odd)
        def _():
            for ch in range(2):
                if self.hop is not None:
                    self.hop[ch].wait_recv()
                self.x[ch].start()
                self.y[ch].start()

    def relay(self):
        @pl.when(self.place.odd)
        def _():
            self.x[0].wait_recv()
            self.relay_y.start()
            self.y[1].wait_recv()
            self.relay_x.start()

    def finish(self):
        @pl.when(self.place.odd)
        def _():
            self.x[1].wait_recv()
            self.y[0].wait_recv()
            self.relay_y.wait_recv()
            self.relay_x.wait_recv()

    def drain(self):
        @pl.when(self.place.odd)
        def _():
            for copy in (self.hop or []) + self.x + self.y + [self.relay_y, self.relay_x]:
                copy.wait_send()


class Spread:
    def __init__(self, copies, place, source, slots):
        self.place = place
        self.to_x = copies.make(source, slots[1], place.over_x)
        self.to_y = copies.make(source, slots[2], place.over_y)
        self.relayed = copies.make(slots[2], slots[3], place.over_x)

    def start(self):
        pl.when(self.place.x == 0)(self.to_x.start)
        pl.when(self.place.y == 0)(self.to_y.start)

    def relay(self):
        @pl.when(self.place.corner)
        def _():
            self.to_y.wait_recv()
            self.relayed.start()

    def finish(self):
        p = self.place
        pl.when(p.x == 1)(self.to_x.wait_recv)
        pl.when((p.y == 1) & (p.x == 0))(self.to_y.wait_recv)
        pl.when(p.turn)(self.relayed.wait_recv)
        pl.when(p.x == 0)(self.to_x.wait_send)
        pl.when(p.y == 0)(self.to_y.wait_send)
        pl.when(p.corner)(self.relayed.wait_send)


def first_kernel(
    tok_ref, grad_ref, gain_ref, cos_ref, sin_ref, joined_in, wo_in, wd_in,
    q_out, kv_out, n_full, g_full, joined, wo_out, wd_out,
    linear, kv_own, ss, rs, lsem,
):
    place = Place()
    copies = Copies(ss, rs)
    block, width = tok_ref.shape
    two = 2 * block
    q_cols = q_out.shape[0]
    kv_cols = kv_own.shape[1] // 2
    local = [
        pltpu.make_async_copy(src, dst, lsem.at[i])
        for i, (src, dst) in enumerate(((joined_in, joined), (wo_in, wo_out), (wd_in, wd_out)))
    ]

    @pl.when(place.c == 0)
    def _():
        for copy in local:
            copy.start()

    own_grad = pltpu.make_async_copy(grad_ref, g_full.at[pl.ds(0, block)], lsem.at[3])
    own_grad.start()
    meet((place.beside, place.near, place.far, place.cross, place.over_x, place.over_y))

    fetch_joined = PlaneFetch(copies, place, joined, joined_in)
    fetch_o = PlaneFetch(copies, place, wo_out, wo_in)
    fetch_d = PlaneFetch(copies, place, wd_out, wd_in)
    gather = GroupGather(copies, n_full, block, place)
    gather_g = GroupGather(copies, g_full, block, place)
    fetch_joined.start()
    chunk = block // CHUNKS
    for k in range(CHUNKS):
        at = pl.ds(k * chunk, chunk)
        tok = tok_ref[at, :].astype(floats)
        root = lax.rsqrt(jnp.mean(tok * tok, axis=-1, keepdims=True) + eps_norm)
        n_full[at, :] = (tok * root * gain_ref[...]).astype(halves)
        gather.put(k)
    fetch_joined.forward()
    fetch_o.start()
    fetch_d.start()
    fetch_joined.relay()
    gather.wait_here()
    fetch_joined.finish()
    pl.when(place.c == 0)(local[0].wait)

    def project(k):
        rows = slice(k * two, (k + 1) * two)

        def one(cols):
            linear[cols, :] = dot_nn(n_full[rows, :], joined[:, cols]).T

        tiles(joined.shape[1], 256, one)
        half_width = HEAD_WIDTH // 2
        for head in range((q_cols + kv_cols) // HEAD_WIDTH):
            low = slice(head * HEAD_WIDTH, head * HEAD_WIDTH + half_width)
            high = slice(head * HEAD_WIDTH + half_width, (head + 1) * HEAD_WIDTH)
            one_half, two_half = linear[low, :], linear[high, :]
            cosine, sine = cos_ref[:, rows], sin_ref[:, rows]
            first = (one_half * cosine - two_half * sine).astype(halves)
            second = (two_half * cosine + one_half * sine).astype(halves)
            if head * HEAD_WIDTH < q_cols:
                q_out[low, rows] = first
                q_out[high, rows] = second
            else:
                kv_own[k, low.start - q_cols : low.stop - q_cols, :] = first
                kv_own[k, high.start - q_cols : high.stop - q_cols, :] = second
        kv_own[k, kv_cols:, :] = (linear[q_cols + kv_cols :, :].astype(halves) * VSCALE).astype(halves)

    crossings, spreads_a, spreads_b, kept = [], [], [], []

    def share(k):
        slots = [kv_out.at[8 * k + i] for i in range(8)]
        keep = pltpu.make_async_copy(kv_own.at[k], slots[0], lsem.at[4 + k])
        keep.start()
        kept.append(keep)
        crossing = copies.make(kv_own.at[k], slots[4], place.cross)
        crossing.start()
        crossings.append(crossing)
        spread = Spread(copies, place, kv_own.at[k], slots[:4])
        spread.start()
        spreads_a.append(spread)
        spreads_b.append(Spread(copies, place, slots[4], slots[4:]))

    project(0)
    share(0)
    gather.wait_there()
    project(1)
    share(1)
    own_grad.wait()
    for k in range(CHUNKS):
        gather_g.put(k)
    fetch_o.forward()
    fetch_d.forward()
    spreads_a[0].relay()
    spreads_a[1].relay()
    fetch_o.relay()
    fetch_d.relay()
    crossings[0].wait_recv()
    spreads_b[0].start()
    gather_g.wait_there()
    spreads_b[0].relay()
    crossings[1].wait_recv()
    spreads_b[1].start()
    spreads_b[1].relay()
    fetch_o.finish()
    fetch_d.finish()
    gather_g.wait_here()
    for spread in spreads_a + spreads_b:
        spread.finish()
    for copy in kept:
        copy.wait()

    @pl.when(place.c == 0)
    def _():
        for copy in local[1:]:
            copy.wait()

    for copy in crossings:
        copy.wait_send()
    for fetch in (fetch_joined, fetch_o, fetch_d):
        fetch.drain()
    gather.finish()
    gather_g.finish()


def first_part(tokens, out_grad, gain, cosine, sine, joined, weight_o, weight_d, q_cols, kv_cols):
    block, width = tokens.shape
    group = 4 * block
    shape = jax.ShapeDtypeStruct
    out_shape = (
        shape((q_cols, group), halves),
        shape((16, 2 * kv_cols, 2 * block), halves),
        shape((group, width), halves),
        shape((group, width), halves),
        shape(joined.shape, halves),
        shape(weight_o.shape, halves),
        shape(weight_d.shape, halves),
    )
    return pl.pallas_call(
        first_kernel,
        out_shape=out_shape,
        in_specs=[VM] * 5 + [HB] * 3,
        out_specs=(VM, HB, VM, VM, VM, HB, HB),
        scratch_shapes=[
            pltpu.VMEM((joined.shape[1], 2 * block), floats),
            pltpu.VMEM((2, 2 * kv_cols, 2 * block), halves),
            *copy_semaphores(),
            pltpu.SemaphoreType.DMA((6,)),
        ],
        compiler_params=pltpu.CompilerParams(
            collective_id=2, has_side_effects=True, vmem_limit_bytes=40 << 20
        ),
        name="first",
    )(tokens, out_grad, gain, cosine, sine, joined, weight_o, weight_d)


class PlaneSum:
    def __init__(self, copies, place, x_first, bufs, sent=None, come=None):
        self.place, self.bufs, self.x_first = place, bufs, x_first
        half, keep, come_two, home_one, home_two = bufs
        first, second = (place.over_x, place.over_y) if x_first else (place.over_y, place.over_x)
        self.at = place.y if x_first else place.x
        self.one = None if sent is None else copies.make(sent, come, first)
        self.two = copies.make(half, come_two, second)
        rows = home_one.shape[0]
        c = place.c
        home = (c * place.cross[0] + (1 - c) * place.beside[0], c * place.cross[1] + (1 - c) * place.beside[1])
        self.to_home = copies.make(half.at[pl.ds((1 - c) * rows, rows)], home_one, home)
        self.to_far = copies.make(half.at[pl.ds(rows, rows)], home_two, place.far)

    def cross_second(self, kept, come):
        if self.one is not None:
            self.one.wait()
        half, keep, come_two, home_one, home_two = self.bufs
        at = self.at
        half[...] = (kept[1 - at].astype(floats) + come[1 - at].astype(floats)).astype(halves)
        self.two.start()
        keep[...] = (kept[at].astype(floats) + come[at].astype(floats)).astype(halves)

    def go_home(self):
        half, keep, come_two, home_one, home_two = self.bufs
        self.two.wait()
        half[...] = (keep[...].astype(floats) + come_two[...].astype(floats)).astype(halves)
        self.to_home.start()
        pl.when(self.place.odd)(self.to_far.start)

    def finish(self, out):
        half, keep, come_two, home_one, home_two = self.bufs
        rows = home_one.shape[0]
        self.to_home.wait()

        @pl.when(self.place.c == 0)
        def _():
            out[...] = half[:rows, :].astype(floats) + home_one[...].astype(floats)

        @pl.when(self.place.odd)
        def _():
            self.to_far.wait()
            out[...] = home_one[...].astype(floats) + home_two[...].astype(floats)


def plane_buffers(rows, cols):
    full = pltpu.VMEM((rows, cols), halves)
    part = pltpu.VMEM((rows // 2, cols), halves)
    return [full, full, full, part, part]


def outer_blocks(place, x_first, left, right, send_ref, keep_ref, on_sent):
    rows = left.shape[1] // 4
    for kept in (False, True):
        for i in range(2):
            if x_first:
                block = 2 * i + (place.x if kept else 1 - place.x)
            else:
                block = 2 * (place.y if kept else 1 - place.y) + i
            cols = pl.ds(pl.multiple_of(block * rows, 128), rows)
            value = lax.dot_general(
                left[:, cols], right, (((0,), (0,)), ((), ())), preferred_element_type=floats
            ).astype(halves)
            (keep_ref if kept else send_ref)[i] = value
        if not kept:
            on_sent()


def mid_kernel(ctx_ref, tok_ref, gain_ref, g_full, weight_refs, outs, scratch):
    (res_out, gres_out, e_full, part_out, down_keep, down_come, gate_keep, gate_send, up_keep, up_send,
     dctx_out, delta_out, gain_out) = outs
    (ctx, m_full, dh, hid, dgate, dup, w_o, w_d, w_g, w_u, down_send, *bufs, ss, rs, wsem) = scratch
    place = Place()
    copies = Copies(ss, rs)
    block, width = tok_ref.shape
    two = 2 * block
    hidden = w_g.shape[1]
    wo_ref, wd_ref, wg_ref, wu_ref, slice_g, slice_u = weight_refs
    load_o = pltpu.make_async_copy(wo_ref, w_o, wsem.at[0])
    load_d = pltpu.make_async_copy(wd_ref, w_d, wsem.at[1])
    load_o.start()
    load_d.start()
    rows4 = slice_g.shape[0]
    at_slot = pl.ds(place.slot * rows4, rows4)
    loads = [
        pltpu.make_async_copy(src, dst, wsem.at[2 + i])
        for i, (src, dst) in enumerate(((wg_ref, w_g), (wu_ref, w_u)))
    ]
    loads_odd = [
        pltpu.make_async_copy(src, dst.at[at_slot], wsem.at[2 + i])
        for i, (src, dst) in enumerate(((slice_g, w_g), (slice_u, w_u)))
    ]

    @pl.when(place.c == 0)
    def _():
        for copy in loads:
            copy.start()

    @pl.when(place.odd)
    def _():
        for copy in loads_odd:
            copy.start()

    ctx[...] = ctx_ref[...].T
    meet((place.beside, place.near, place.over_x, place.over_y))
    fetches = [PlaneFetch(copies, place, w_g), PlaneFetch(copies, place, w_u)]

    @pl.when(place.odd)
    def _():
        for copy in loads_odd:
            copy.wait()

    for fetch in fetches:
        fetch.forward()
    sum_one = GroupSum(copies, bufs, place)
    gather_one = GroupGather(copies, m_full, block, place)
    sum_two = GroupSum(copies, bufs, place)
    gather_two = GroupGather(copies, e_full, block, place)

    def project(k, put):
        rows = slice(k * two, (k + 1) * two)
        tiles(width, 256, lambda cols: put(cols, dot_nn(ctx[rows, :], w_o[:, cols])))

    load_o.wait()
    sum_one.run(project)
    load_d.wait()

    def back_hidden(cols):
        for rows in (slice(0, two), slice(two, 2 * two)):
            dh[rows, cols] = dot_nt(g_full[rows, :], w_d[cols, :]).astype(halves)

    tiles(hidden, 256, back_hidden)
    for fetch in fetches:
        fetch.relay()
    chunk = block // CHUNKS
    for k in range(CHUNKS):
        at = pl.ds(k * chunk, chunk)
        res = tok_ref[at, :].astype(floats) + sum_one.take(k)
        res_out[at, :] = res
        root = lax.rsqrt(jnp.mean(res * res, axis=-1, keepdims=True) + eps_norm)
        m_full[at, :] = (res * root * gain_ref[...]).astype(halves)
        gather_one.put(k)
    sum_one.finish()

    def activate(k):
        rows = slice(k * two, (k + 1) * two)

        def one(cols):
            gate_pre = dot_nn(m_full[rows, :], w_g[:, cols])
            up_pre = dot_nn(m_full[rows, :], w_u[:, cols])
            back = dh[rows, cols].astype(floats)
            sigma = 1.0 / (1.0 + jnp.exp(-gate_pre))
            silu = gate_pre * sigma
            hid[rows, cols] = (silu * up_pre).astype(halves)
            dgate[rows, cols] = (back * up_pre * (sigma + silu * (1.0 - sigma))).astype(halves)
            dup[rows, cols] = (back * silu).astype(halves)

        tiles(hidden, 256, one)

    def partial_out(k):
        rows = slice(k * two, (k + 1) * two)

        def one(cols):
            part_out[rows, cols] = dot_nn(hid[rows, :], w_d[:, cols]).astype(halves)

        tiles(width, 256, one)

    for fetch in fetches:
        fetch.finish()

    @pl.when(place.c == 0)
    def _():
        for copy in loads:
            copy.wait()

    gather_one.wait_here()
    activate(0)
    partial_out(0)
    gather_one.wait_there()
    activate(1)
    gather_one.finish()

    def back_norm(k, put):
        rows = slice(k * two, (k + 1) * two)
        tiles(
            width,
            256,
            lambda cols: put(
                cols, dot_nt(dgate[rows, :], w_g[cols, :]) + dot_nt(dup[rows, :], w_u[cols, :])
            ),
        )

    sum_two.run(back_norm)
    partial_out(1)
    down_over = copies.make(down_send, down_come, place.over_x)
    outer_blocks(place, True, g_full, hid[...], down_send, down_keep, down_over.start)
    outer_blocks(place, False, m_full, dgate[...], gate_send, gate_keep, lambda: None)
    gain_out[...] = jnp.zeros_like(gain_out)
    for k in range(CHUNKS):
        at = pl.ds(k * chunk, chunk)
        back = sum_two.take(k)
        res = res_out[at, :]
        root = lax.rsqrt(jnp.mean(res * res, axis=-1, keepdims=True) + eps_norm)
        weighted = back * gain_ref[...]
        slope = jnp.mean(weighted * res, axis=-1, keepdims=True)
        grad = g_full[at, :].astype(floats) + root * weighted - res * (root * root * root * slope)
        gain_out[...] += jnp.sum(back * res * root, axis=0, keepdims=True)
        gres_out[at, :] = grad
        e_full[at, :] = grad.astype(halves)
        gather_two.put(k)
    sum_two.finish()
    outer_blocks(place, True, m_full, dup[...], up_send, up_keep, lambda: None)

    def back_context(k):
        lanes = slice(k * two, (k + 1) * two)
        grad = dot_nt(w_o[...], e_full[lanes, :]).astype(halves)
        dctx_out[:, lanes] = grad
        prod = grad.astype(floats) * ctx_ref[:, lanes].astype(floats)
        for hd in range(delta_out.shape[0]):
            delta_out[hd : hd + 1, lanes] = VSCALE * jnp.sum(
                prod[hd * HEAD_WIDTH : (hd + 1) * HEAD_WIDTH], axis=0, keepdims=True
            )

    gather_two.wait_here()
    back_context(0)
    gather_two.wait_there()
    back_context(1)
    gather_two.finish()
    for fetch in fetches:
        fetch.drain()
    down_over.wait()


def middle(context_t, tokens, gain, grad_full, weights):
    q_cols, group = context_t.shape
    block, width = tokens.shape
    hidden = weights[2].shape[1]
    shape = jax.ShapeDtypeStruct
    out_shape = (
        shape((block, width), floats),
        shape((block, width), floats),
        shape((group, width), halves),
        shape((group, width), halves),
        *[shape((2, width // 4, hidden), halves)] * 6,
        shape((q_cols, group), halves),
        shape((q_cols // HEAD_WIDTH, group), floats),
        shape((1, width), floats),
    )
    scratch = [
        pltpu.VMEM((group, q_cols), halves),
        pltpu.VMEM((group, width), halves),
        *[pltpu.VMEM((group, hidden), halves)] * 4,
        *[pltpu.VMEM(weight.shape, halves) for weight in weights[:4]],
        pltpu.VMEM((2, width // 4, hidden), halves),
        *[pltpu.VMEM((block, width), floats)] * 2,
        *[pltpu.VMEM((block, width), halves)] * 6,
        *copy_semaphores(),
        pltpu.SemaphoreType.DMA((4,)),
    ]

    def kernel(*refs):
        mid_kernel(*refs[:4], refs[4:10], refs[10:23], refs[23:])

    return pl.pallas_call(
        kernel,
        out_shape=out_shape,
        in_specs=[VM] * 4 + [HB] * 6,
        out_specs=(VM,) * 13,
        scratch_shapes=scratch,
        compiler_params=pltpu.CompilerParams(
            collective_id=1, has_side_effects=True, vmem_limit_bytes=62 << 20
        ),
        name="middle",
    )(context_t, tokens, gain, grad_full, *weights)


def last_kernel(ins, outs, scratch):
    (dq_ref, dkv_ref, cos_ref, sin_ref, n_ref, joined, tok_ref, gain_ref, gres_ref, e_ref, ctx_ref,
     gain_mlp_ref, *mlp) = ins
    (in_grad, gains_out, gate_out, up_out, down_out, q_out, kv_out, o_out) = outs
    (full, ctx, d_lin, acc_a, acc_b, own, x_in, y_in, rel_in, cross_in, cross_out, kept, come,
     gains, gains_in, *rest) = scratch
    bufs_mlp = [rest[5 * i : 5 * i + 5] for i in range(3)]
    rest = rest[15:]
    bufs_attn = [rest[8 * i : 8 * i + 8] for i in range(3)]
    rest = rest[24:]
    sum_bufs, (ss, rs, lsem) = rest[:8], rest[8:]
    place = Place()
    copies = Copies(ss, rs)
    block, width = tok_ref.shape
    two = 2 * block
    q_cols = dq_ref.shape[0]
    kv_cols = own.shape[1] // 2
    half_width = HEAD_WIDTH // 2

    load_e = pltpu.make_async_copy(e_ref, full, lsem.at[0])
    load_e.start()
    order = (4, 12, 0, 8)
    own_loads = [
        pltpu.make_async_copy(dkv_ref.at[at], own.at[i], lsem.at[1 + i]) for i, at in enumerate(order)
    ]
    y_loads = [
        pltpu.make_async_copy(dkv_ref.at[at + 2], y_in.at[i], lsem.at[5 + i])
        for i, at in enumerate(order)
    ]
    for copy in own_loads:
        copy.start()

    @pl.when(place.corner)
    def _():
        for copy in y_loads:
            copy.start()

    def load_mlp(i):
        return [
            pltpu.make_async_copy(mlp[2 * i], kept, lsem.at[9]),
            pltpu.make_async_copy(mlp[2 * i + 1], come, lsem.at[10]),
        ]

    loads = load_mlp(0)
    for copy in loads:
        copy.start()
    gains[0, 0:1, :] = gain_mlp_ref[...]
    gains[0, 1:2, :] = jnp.zeros_like(gain_mlp_ref)
    meet((place.beside, place.near, place.far, place.cross, place.over_x, place.over_y))

    back_rel = [copies.make(dkv_ref.at[at + 3], rel_in.at[i], place.over_x) for i, at in enumerate(order)]
    back_x = [copies.make(dkv_ref.at[at + 1], x_in.at[i], place.over_x) for i, at in enumerate(order)]
    back_y = [copies.make(dkv_ref.at[at + 2], y_in.at[i], place.over_y) for i, at in enumerate(order)]
    back_sum = [copies.make(y_in.at[i], y_in.at[i], place.over_y) for i in range(4)]
    crossing = [copies.make(cross_out.at[i], cross_in.at[i], place.cross) for i in range(2)]
    for i in range(4):
        pl.when(place.turn)(back_rel[i].start)
        pl.when(place.x == 1)(back_x[i].start)
        pl.when(place.turn)(back_y[i].start)

    def corner_sum(i):
        @pl.when(place.corner)
        def _():
            back_rel[i].wait_recv()
            y_loads[i].wait()
            y_in[i] = (y_in[i].astype(floats) + rel_in[i].astype(floats)).astype(halves)
            back_sum[i].start()

    def home_sum(i, put):
        own_loads[i].wait()
        acc_b[...] = own[i].astype(floats)

        @pl.when(place.x == 0)
        def _():
            back_x[i].wait_recv()
            acc_b[...] += x_in[i].astype(floats)

        @pl.when((place.y == 0) & (place.x == 0))
        def _():
            back_y[i].wait_recv()
            acc_b[...] += y_in[i].astype(floats)

        @pl.when((place.y == 0) & (place.x == 1))
        def _():
            back_sum[i].wait_recv()
            acc_b[...] += y_in[i].astype(floats)

        put()

    sums = []
    for i, x_first in enumerate((True, False, True)):
        sums.append(PlaneSum(copies, place, x_first, bufs_mlp[i]))
    for i in range(3):
        for copy in loads:
            copy.wait()
        sums[i].cross_second(kept, come)
        if i < 2:
            loads = load_mlp(i + 1)
            for copy in loads:
                copy.start()
        if i == 1:
            corner_sum(0)
    ctx[...] = ctx_ref[...].T

    attn_sums = []
    for i, x_first in enumerate((False, True, False)):
        sent, keep, got = bufs_attn[i][:3]
        attn_sums.append(PlaneSum(copies, place, x_first, bufs_attn[i][3:], sent, got))

    def attn_grad(i, left, right):
        sent, keep, got = bufs_attn[i][:3]
        outer_blocks(place, attn_sums[i].x_first, left, right, sent, keep, attn_sums[i].one.start)

    corner_sum(1)
    load_e.wait()
    attn_grad(0, full, ctx[...])
    load_n = pltpu.make_async_copy(n_ref, full, lsem.at[0])
    load_n.start()

    def cross_back(i):
        def put():
            cross_out[i] = acc_b[...].astype(halves)
            crossing[i].start()

        home_sum(i, put)

    def unturn(value, at, first_row):
        low, high = value[:half_width], value[half_width:]
        cosine, sine = cos_ref[:, at], sin_ref[:, at]
        turned = jnp.concatenate([low * cosine + high * sine, high * cosine - low * sine], axis=0)
        d_lin[first_row : first_row + HEAD_WIDTH, at] = turned.astype(halves)

    cross_back(0)
    corner_sum(2)
    everything = slice(0, 2 * two)
    for head in range(q_cols // HEAD_WIDTH):
        unturn(dq_ref[head * HEAD_WIDTH : (head + 1) * HEAD_WIDTH, :], everything, head * HEAD_WIDTH)
    cross_back(1)
    corner_sum(3)
    load_n.wait()
    attn_grad(1, full, d_lin[:q_cols, :].T)
    for plane in sums:
        plane.go_home()

    def second(i):
        sent, keep, got = bufs_attn[i][:3]
        attn_sums[i].cross_second(keep, got)

    second(0)

    def keep_a(k):
        def put():
            acc_a[:, k * two : (k + 1) * two] = acc_b[...]

        home_sum(2 + k, put)

    keep_a(0)
    keep_a(1)
    second(1)
    attn_sums[0].go_home()
    for k in range(2):
        crossing[k].wait_recv()
        lanes = slice(k * two, (k + 1) * two)
        total = acc_a[:, lanes] + cross_in[k].astype(floats)
        for head in range(kv_cols // HEAD_WIDTH):
            rows = slice(head * HEAD_WIDTH, (head + 1) * HEAD_WIDTH)
            unturn(total[rows], lanes, q_cols + head * HEAD_WIDTH)
        d_lin[q_cols + kv_cols :, lanes] = total[kv_cols:].astype(halves)

    group_sum = GroupSum(copies, sum_bufs, place)

    def back_norm(k, put):
        rows = slice(k * two, (k + 1) * two)
        left = d_lin[:, rows].T

        def one(cols):
            value = dot_nt(left, joined[cols, :])
            put(cols, value)
            gains[0, 1:2, cols] += jnp.sum(value * full[rows, cols].astype(floats), axis=0, keepdims=True)

        tiles(width, 256, one)

    group_sum.run(back_norm)
    gains[0, 1:2, :] = gains[0, 1:2, :] / gain_ref[...]
    attn_grad(2, full, d_lin[q_cols:, :].T)
    attn_sums[1].go_home()
    for stage, device in enumerate((place.beside, place.over_x, place.over_y, place.near, place.far)):
        copy = copies.make(gains.at[stage], gains_in.at[stage], device)
        copy.start()
        copy.wait()
        if stage < 4:
            gains[stage + 1] = gains[stage] + gains_in[stage]
        else:
            gains_out[...] = gains[stage] + gains_in[stage]
        if stage == 2:
            second(2)
    for plane, out in zip(sums, (down_out, gate_out, up_out)):
        plane.finish(out)
    attn_sums[2].go_home()
    chunk = block // CHUNKS
    for k in range(CHUNKS):
        at = pl.ds(k * chunk, chunk)
        back = group_sum.take(k)
        tok = tok_ref[at, :].astype(floats)
        root = lax.rsqrt(jnp.mean(tok * tok, axis=-1, keepdims=True) + eps_norm)
        weighted = back * gain_ref[...]
        slope = jnp.mean(weighted * tok, axis=-1, keepdims=True)
        in_grad[at, :] = gres_ref[at, :] + root * weighted - tok * (root * root * root * slope)
    for plane, out in zip(attn_sums, (o_out, q_out, kv_out)):
        plane.finish(out)
    group_sum.finish()
    for i in range(4):
        pl.when(place.turn)(back_rel[i].wait_send)
        pl.when(place.x == 1)(back_x[i].wait_send)
        pl.when(place.turn)(back_y[i].wait_send)
        pl.when(place.corner)(back_sum[i].wait_send)
    for copy in crossing:
        copy.wait_send()


def last_part(d_query_t, d_kv, cosine, sine, normed, joined, tokens, gain, gres, e_full, context_t, gain_mlp, mlp):
    block, width = tokens.shape
    group = 4 * block
    q_cols, kv_all = d_query_t.shape[0], d_kv.shape[1]
    kv_cols = kv_all // 2
    hidden = mlp[0].shape[2]
    per = width // 8
    shape = jax.ShapeDtypeStruct
    out_shape = (
        shape((block, width), floats),
        shape((2, width), floats),
        *[shape((per, hidden), floats)] * 3,
        shape((per, q_cols), floats),
        shape((per, kv_all), floats),
        shape((per, q_cols), floats),
    )
    piece = (kv_all, 2 * block)
    scratch = [
        pltpu.VMEM((group, width), halves),
        pltpu.VMEM((group, q_cols), halves),
        pltpu.VMEM((joined.shape[1], group), halves),
        pltpu.VMEM((kv_all, group), floats),
        pltpu.VMEM(piece, floats),
        *[pltpu.VMEM((4,) + piece, halves)] * 4,
        *[pltpu.VMEM((2,) + piece, halves)] * 2,
        *[pltpu.VMEM((2, width // 4, hidden), halves)] * 2,
        *[pltpu.VMEM((5, 2, width), floats)] * 2,
    ]
    for _ in range(3):
        scratch += plane_buffers(width // 4, hidden)
    for cols in (q_cols, q_cols, kv_all):
        scratch += [pltpu.VMEM((2, width // 4, cols), halves)] * 3 + plane_buffers(width // 4, cols)
    scratch += [
        *[pltpu.VMEM((block, width), floats)] * 2,
        *[pltpu.VMEM((block, width), halves)] * 6,
        *copy_semaphores(),
        pltpu.SemaphoreType.DMA((11,)),
    ]

    def kernel(*refs):
        last_kernel(refs[:18], refs[18:26], refs[26:])

    return pl.pallas_call(
        kernel,
        out_shape=out_shape,
        in_specs=[VM, HB, VM, VM, HB, VM, VM, VM, VM, HB, VM, VM] + [HB] * 6,
        out_specs=(VM,) * 8,
        scratch_shapes=scratch,
        compiler_params=pltpu.CompilerParams(
            collective_id=3, has_side_effects=True, vmem_limit_bytes=63 << 20
        ),
        name="last",
    )(d_query_t, d_kv, cosine, sine, normed, joined, tokens, gain, gres, e_full, context_t, gain_mlp, *mlp)


def routes(target):
    pairs = []
    for index in range(32):
        dp, z = divmod(index, 4)
        there = target(dp // 4, dp // 2 % 2, dp % 2, z)
        if there is not None:
            y, x, c, z = there
            pairs.append((index, (y * 4 + x * 2 + c) * 4 + z))
    return pairs


ROUTES = {
    "core": routes(lambda y, x, c, z: (y, x, 1 - c, z)),
    "x": routes(lambda y, x, c, z: (y, 1 - x, c, z)),
    "y": routes(lambda y, x, c, z: (1 - y, x, c, z)),
    "near": routes(lambda y, x, c, z: (y, x, c, z ^ 1)),
    "far": routes(lambda y, x, c, z: (y, x, c, z ^ 2)),
    "cross": routes(lambda y, x, c, z: (y, x, 1 - c, z ^ 2)),
    "odd_far": routes(lambda y, x, c, z: (y, x, c, z ^ 2) if c else None),
    "odd_x": routes(lambda y, x, c, z: (y, 1 - x, c, z) if c else None),
    "odd_y": routes(lambda y, x, c, z: (1 - y, x, c, z) if c else None),
    "odd_xy": routes(lambda y, x, c, z: (1 - y, 1 - x, c, z) if c else None),
    "home": routes(lambda y, x, c, z: (y, x, 0, z ^ 2) if c else (y, x, 1, z)),
    "x_up": routes(lambda y, x, c, z: None if x else (y, 1, c, z)),
    "y_up": routes(lambda y, x, c, z: None if y else (1, x, c, z)),
    "x_down": routes(lambda y, x, c, z: (y, 0, c, z) if x else None),
    "y_down": routes(lambda y, x, c, z: (0, x, c, z) if y else None),
    "relay": routes(lambda y, x, c, z: (1, 0, c, z) if x and y else None),
    "unrelay": routes(lambda y, x, c, z: (1, 1, c, z) if y and not x else None),
}
FAR_BASE = 1 << 24


def send(block, way):
    return lax.ppermute(block, ("dp", "tp"), ROUTES[way])


def scatter_group(here, there):
    rows = here.shape[0] // 2
    there_sum = there[:rows] + send(there[rows:].astype(halves), "core").astype(floats)
    here_sum = here[:rows].astype(floats) + send(here[rows:].astype(halves), "core").astype(floats)
    return here_sum + send(there_sum.astype(halves), "near").astype(floats)


def rope_tables(positions):
    half_width = HEAD_WIDTH // 2
    inverse = 1.0 / rope_base ** (jnp.arange(half_width, dtype=floats) * 2.0 / HEAD_WIDTH)
    angles = inverse[:, None] * positions.astype(floats)[None, :]
    return jnp.cos(angles), jnp.sin(angles)


def local_regrouped(
    tokens,
    out_grad,
    segment_ids,
    attn_gain,
    query_weight,
    key_matrix,
    value_matrix,
    output_weight,
    mlp_gain,
    gate_weight,
    up_weight,
    down_weight,
):
    block = tokens.shape[0]
    row_len = 4 * block
    dp, z = lax.axis_index("dp"), lax.axis_index("tp")
    y, x, c = dp // 4, dp // 2 % 2, dp % 2
    j = dp // 2
    odd = c == 1
    pair, side = z // 2, z % 2
    q_cols, kv_cols = query_weight.shape[1], key_matrix.shape[1]
    heads = q_cols // HEAD_WIDTH
    group_width = q_cols // kv_cols
    ff_cols = gate_weight.shape[1]
    gain_attn, gain_mlp = attn_gain.astype(floats), mlp_gain.astype(floats)

    def base(j_of, core, pair_of, side_of):
        return (2 * j_of + core) * row_len + (2 * pair_of + side_of) * block

    bases = [
        base(j, c, pair, side),
        base(j, 1 - c, pair, side),
        base(j, c, pair, 1 - side),
        base(j, 1 - c, pair, 1 - side),
    ]
    counts = [jnp.sum((segment_ids < item).astype(jnp.int32)) for item in range(1, 4)]
    segs = jnp.concatenate([lax.dynamic_slice_in_dim(segment_ids, b, block) for b in bases])
    index = jnp.concatenate([b + jnp.arange(block, dtype=jnp.int32) for b in bases])
    start = jnp.zeros_like(segs)
    for item in range(1, 4):
        start = jnp.where(segs == item, counts[item - 1], start)
    cosine, sine = rope_tables(index - start)
    index_row, start_row = index[None, :], start[None, :]
    starts4 = start.reshape(4, block)

    tokens32 = tokens.astype(floats)
    joined = jnp.concatenate([query_weight, key_matrix, value_matrix], axis=1)
    q_t, pieces, normed_full, grad_full, joined, weight_o, weight_d = first_part(
        tokens, out_grad, gain_attn[None, :], cosine, sine, joined, output_weight, down_weight,
        q_cols, kv_cols,
    )
    slot = 2 * y + x
    rows = gate_weight.shape[0] // 4
    own_slices = [
        lax.dynamic_slice_in_dim(weight, slot * rows, rows) for weight in (gate_weight, up_weight)
    ]
    own_slices, pieces = lax.optimization_barrier((own_slices, pieces))
    slices = [send(part, "odd_far") for part in own_slices]

    piece_bases = []
    for n in range(2):
        side_n = side if n == 0 else 1 - side
        for cross in range(2):
            cores = (c, 1 - c) if cross == 0 else (1 - c, c)
            pair_of = pair if cross == 0 else 1 - pair
            for j_of, present in (
                (j, True),
                (j - 1, x == 1),
                (j - 2, y == 1),
                (j - 1, (y == 1) & (x == 0)),
            ):
                for core in cores:
                    piece_bases.append(
                        jnp.where(present, base(j_of, core, pair_of, side_n), FAR_BASE)
                    )
    total_blocks = len(piece_bases)

    def padded(values):
        values = jnp.stack(values).astype(jnp.int32)
        return jnp.pad(values, (0, total_blocks - values.shape[0]))

    sc = jnp.stack(
        [
            padded(piece_bases),
            padded(bases),
            jnp.pad(starts4[:, 0], (0, total_blocks - 4)),
            jnp.pad(starts4[:, -1], (0, total_blocks - 4)),
        ]
    )
    context_t, log_total = attend_forward(sc, q_t, index_row, start_row, pieces)

    (
        residual, grad_residual, attn_grad_full, part_out, down_keep, down_come, gate_keep, gate_send,
        up_keep, up_send,
        d_context_t, delta, mlp_gain_part,
    ) = middle(
        context_t, tokens, gain_mlp[None, :], grad_full,
        (weight_o, weight_d, gate_weight, up_weight, *slices),
    )
    output = residual + scatter_group(part_out[: 2 * block], part_out[2 * block :])
    gate_come = send(gate_send, "y")
    up_come = send(up_send, "x")

    d_query_t, d_pieces = attend_backward(
        sc, q_t, d_context_t, log_total, delta, index_row, start_row, pieces
    )
    input_grad, gains, gate_sum, up_sum, down_sum, query_sum, kv_sum, output_sum = last_part(
        d_query_t, d_pieces, cosine, sine, normed_full, joined, tokens, gain_attn[None, :],
        grad_residual, attn_grad_full, context_t, mlp_gain_part,
        (down_keep, down_come, gate_keep, gate_come, up_keep, up_come),
    )
    per = gains.shape[1] // 8
    gains = lax.dynamic_slice_in_dim(gains, dp * per, per, axis=1)
    return (
        output.astype(halves),
        input_grad,
        gains[1],
        query_sum,
        kv_sum[:, :kv_cols],
        kv_sum[:, kv_cols:],
        output_sum.T,
        gains[0],
        gate_sum,
        up_sum,
        down_sum.T,
    )


def solution(mesh):
    regroup = mesh.shape["dp"] == 8 and mesh.shape["tp"] == 4
    chosen = local_regrouped if regroup else local
    return jax.shard_map(
        chosen,
        mesh=mesh,
        in_specs=(
            P(("dp", "tp"), None),
            P(("dp", "tp"), None),
            P(),
            P(),
            P(None, "tp"),
            P(None, "tp"),
            P(None, "tp"),
            P("tp", None),
            P(),
            P(None, "tp"),
            P(None, "tp"),
            P("tp", None),
        ),
        out_specs=(
            P(("dp", "tp"), None),
            P(("dp", "tp"), None),
            P("dp"),
            P("dp", "tp"),
            P("dp", "tp"),
            P("dp", "tp"),
            P("tp", "dp"),
            P("dp"),
            P("dp", "tp"),
            P("dp", "tp"),
            P("tp", "dp"),
        ),
        check_vma=False,
    )
```

```python
import functools

import jax
import jax.numpy as jnp
from jax import lax
from jax.experimental import pallas as pl
from jax.experimental.pallas import tpu as pltpu
from jax.sharding import PartitionSpec as P

HEAD_WIDTH = 96
BLK = 256
LOG2E = 1.4426950408889634
SCORE = LOG2E * HEAD_WIDTH ** (-0.5)
VSCALE = 2.0 ** -9
FAR_BASE = 1 << 24
floats = jnp.float32
halves = jnp.bfloat16


def dot_nn(a, b):
    return jnp.dot(a, b, preferred_element_type=floats)


def dot_nt(a, b):
    return lax.dot_general(a, b, (((1,), (1,)), ((), ())), preferred_element_type=floats)


def token_base(j, core, pair, side):
    return ((2 * j + core) * 4 + 2 * pair + side) * BLK


def group_bases():
    dp, z = lax.axis_index("dp"), lax.axis_index("tp")
    j, c, pair, side = dp // 2, lax.rem(dp, 2), z // 2, lax.rem(z, 2)
    return [
        token_base(j, core, pair, at) for at in (side, 1 - side) for core in (c, 1 - c)
    ]


def item_start(counts_ref, token):
    start = jnp.zeros_like(token)
    for i in range(3):
        start = jnp.where(token >= counts_ref[i], counts_ref[i], start)
    return start


def group_index():
    lanes = lax.broadcasted_iota(jnp.int32, (1, BLK), 1)
    return jnp.concatenate([lanes + base for base in group_bases()], axis=1)


def fill_places(counts_ref, sc, tok_ref, start_ref):
    dp, z = lax.axis_index("dp"), lax.axis_index("tp")
    j, c, pair, side = dp // 2, lax.rem(dp, 2), z // 2, lax.rem(z, 2)
    x, y = lax.rem(j, 2), j // 2
    kb = 0
    for side_of in (side, 1 - side):
        for cores, pair_of in (((c, 1 - c), pair), ((1 - c, c), 1 - pair)):
            for j_of, present in ((j, None), (j - 1, x), (j - 2, y), (j - 1, y * (1 - x))):
                for core in cores:
                    base = token_base(j_of, core, pair_of, side_of)
                    sc[0, kb] = base if present is None else jnp.where(present == 1, base, FAR_BASE)
                    kb += 1
    for qb, base in enumerate(group_bases()):
        sc[1, qb] = base
        sc[2, qb] = item_start(counts_ref, base)
        sc[3, qb] = item_start(counts_ref, base + (BLK - 1))
    index = group_index()
    tok_ref[...] = index
    start_ref[...] = item_start(counts_ref, index)


def pair_state(sc, kb, qb):
    key_base = sc[0, kb]
    q_base, least, most = sc[1, qb], sc[2, qb], sc[3, qb]
    needed = (key_base <= q_base + (BLK - 1)) & (key_base + (BLK - 1) >= least)
    whole = (key_base + (BLK - 1) <= q_base) & (key_base >= most)
    return key_base, needed, whole


def allowed_mask(key_base, tok_ref, start_ref, lanes):
    keys = key_base + lax.broadcasted_iota(jnp.int32, (BLK, BLK), 0)
    return (keys <= tok_ref[0:1, lanes]) & (keys >= start_ref[0:1, lanes])


def fwd_kernel(n, width, counts, q_ref, pieces, *refs):
    out_acc, out_sum = refs[:2]
    kv, keys_nat, acc, total, q_wide, sc, tok_ref, start_ref, sem = refs[2:]
    per = width // BLK
    for i in range(n):
        pltpu.make_async_copy(pieces.at[i], kv.at[i], sem.at[i]).start()
    acc[...] = jnp.zeros_like(acc)
    total[...] = jnp.zeros_like(total)
    fill_places(counts, sc, tok_ref, start_ref)
    for i in range(n):
        pltpu.make_async_copy(pieces.at[i], kv.at[i], sem.at[i]).wait()
    heads_kv = pieces.shape[1] // (2 * HEAD_WIDTH)
    group = q_ref.shape[0] // (heads_kv * HEAD_WIDTH)
    v_off = heads_kv * HEAD_WIDTH
    places = [
        (h, slice((h * group + g) * HEAD_WIDTH, (h * group + g + 1) * HEAD_WIDTH), slice(qb * BLK, (qb + 1) * BLK),
         slice(h * HEAD_WIDTH, (h + 1) * HEAD_WIDTH), slice((qb * group + g) * BLK, (qb * group + g + 1) * BLK), h * group + g)
        for h in range(heads_kv) for g in range(group) for qb in range(q_ref.shape[1] // BLK)
    ]
    for h, rows, lanes, wrows, wlanes, hd in places:
        q_wide[wrows, wlanes] = q_ref[rows, lanes]

    def key_block(kb, carry):
        piece = kb // per
        klanes = pl.ds(pl.multiple_of((kb % per) * BLK, BLK), BLK)
        for h in range(heads_kv):
            keys_nat[h] = kv[piece, h * HEAD_WIDTH : (h + 1) * HEAD_WIDTH, klanes].T

        def query_block(qb, carry):
            key_base, needed, whole = pair_state(sc, kb, qb)
            lanes = pl.ds(pl.multiple_of(qb * BLK, BLK), BLK)

            def unit(masked):
                wide = pl.ds(pl.multiple_of(qb * (group * BLK), group * BLK), group * BLK)
                if masked:
                    allowed = allowed_mask(key_base, tok_ref, start_ref, lanes)
                    allowed = jnp.concatenate([allowed] * group, axis=1)
                scores = [
                    dot_nn(keys_nat[h], q_wide[h * HEAD_WIDTH : (h + 1) * HEAD_WIDTH, wide])
                    for h in range(heads_kv)
                ]
                weights = [jnp.exp2(s * SCORE) for s in scores]
                if masked:
                    weights = [jnp.where(allowed, w, 0.0) for w in weights]
                sums = [jnp.sum(w, axis=0, keepdims=True) for w in weights]
                parts = [
                    dot_nn(
                        kv[piece, v_off + h * HEAD_WIDTH : v_off + (h + 1) * HEAD_WIDTH, klanes],
                        weights[h].astype(halves),
                    )
                    for h in range(heads_kv)
                ]
                for h in range(heads_kv):
                    total[h : h + 1, wide] += sums[h]
                    acc[h * HEAD_WIDTH : (h + 1) * HEAD_WIDTH, wide] += parts[h]

            pl.when(needed & whole)(lambda: unit(False))
            pl.when(needed & jnp.logical_not(whole))(lambda: unit(True))
            return carry

        return lax.fori_loop(0, q_ref.shape[1] // BLK, query_block, carry)

    lax.fori_loop(0, n * per, key_block, 0)
    for h, rows, lanes, wrows, wlanes, hd in places:
        row = total[h : h + 1, wlanes]
        out_acc[rows, lanes] = (acc[wrows, wlanes] * ((1.0 / VSCALE) / row)).astype(halves)
        out_sum[hd : hd + 1, lanes] = jnp.log2(row)


VM = pl.BlockSpec(memory_space=pltpu.VMEM)
SM = pl.BlockSpec(memory_space=pltpu.SMEM)
HB = pl.BlockSpec(memory_space=pl.ANY)
HM = pl.BlockSpec(memory_space=pltpu.HBM)


def place_scratch(blocks, tokens):
    return [
        pltpu.SMEM((4, blocks), jnp.int32),
        pltpu.VMEM((1, tokens), jnp.int32),
        pltpu.VMEM((1, tokens), jnp.int32),
    ]


def attend_forward(counts, q_t, pieces):
    n, width = pieces.shape[0], pieces.shape[2]
    heads = q_t.shape[0] // HEAD_WIDTH
    heads_kv = pieces.shape[1] // (2 * HEAD_WIDTH)
    tokens = q_t.shape[1]
    wide = tokens * heads // heads_kv
    return pl.pallas_call(
        functools.partial(fwd_kernel, n, width),
        out_shape=(
            jax.ShapeDtypeStruct(q_t.shape, halves),
            jax.ShapeDtypeStruct((heads, tokens), floats),
        ),
        in_specs=[SM, VM, HM],
        out_specs=(VM, VM),
        scratch_shapes=[
            pltpu.VMEM(pieces.shape, halves),
            pltpu.VMEM((heads_kv, BLK, HEAD_WIDTH), halves),
            pltpu.VMEM((heads_kv * HEAD_WIDTH, wide), floats),
            pltpu.VMEM((heads_kv, wide), floats),
            pltpu.VMEM((heads_kv * HEAD_WIDTH, wide), halves),
            *place_scratch(n * width // BLK, tokens),
            pltpu.SemaphoreType.DMA((n,)),
        ],
        compiler_params=pltpu.CompilerParams(vmem_limit_bytes=63 << 20),
        name="attend_forward",
    )(counts, q_t, pieces)


def bwd_kernel(n, width, counts, q_ref, do_ref, log_ref, delta_ref, pieces, *refs):
    dq_out = refs[0]
    dkv_out = refs[1]
    kv, dkv, keys_nat, vals_nat, acc, q_wide, do_wide, log_wide, delta_wide, dq_wide, sc, tok_ref, start_ref, sem, osem = refs[2:]
    per = width // BLK
    for i in range(n):
        pltpu.make_async_copy(pieces.at[i], kv.at[i], sem.at[i]).start()
    fill_places(counts, sc, tok_ref, start_ref)
    for i in range(n):
        pltpu.make_async_copy(pieces.at[i], kv.at[i], sem.at[i]).wait()
    heads_kv = pieces.shape[1] // (2 * HEAD_WIDTH)
    group = q_ref.shape[0] // (heads_kv * HEAD_WIDTH)
    v_off = heads_kv * HEAD_WIDTH
    places = [
        (h, slice((h * group + g) * HEAD_WIDTH, (h * group + g + 1) * HEAD_WIDTH), slice(qb * BLK, (qb + 1) * BLK),
         slice(h * HEAD_WIDTH, (h + 1) * HEAD_WIDTH), slice((qb * group + g) * BLK, (qb * group + g + 1) * BLK), h * group + g)
        for h in range(heads_kv) for g in range(group) for qb in range(q_ref.shape[1] // BLK)
    ]
    for h, rows, lanes, wrows, wlanes, hd in places:
        q_wide[wrows, wlanes] = q_ref[rows, lanes]
        do_wide[wrows, wlanes] = do_ref[rows, lanes]
        log_wide[h : h + 1, wlanes] = log_ref[hd : hd + 1, lanes]
        delta_wide[h : h + 1, wlanes] = delta_ref[hd : hd + 1, lanes]
        dq_wide[wrows, wlanes] = jnp.zeros((HEAD_WIDTH, BLK), floats)
    out_scale = (1.0 / VSCALE) * HEAD_WIDTH ** (-0.5)

    def key_block(kb, carry):
        piece = kb // per
        klanes = pl.ds(pl.multiple_of((kb % per) * BLK, BLK), BLK)
        for h in range(heads_kv):
            keys_nat[h] = kv[piece, h * HEAD_WIDTH : (h + 1) * HEAD_WIDTH, klanes].T
            vals_nat[h] = kv[piece, v_off + h * HEAD_WIDTH : v_off + (h + 1) * HEAD_WIDTH, klanes].T
        acc[...] = jnp.zeros_like(acc)

        def query_block(qb, carry):
            key_base, needed, whole = pair_state(sc, kb, qb)
            lanes = pl.ds(pl.multiple_of(qb * BLK, BLK), BLK)

            def unit(masked):
                wide = pl.ds(pl.multiple_of(qb * (group * BLK), group * BLK), group * BLK)
                if masked:
                    allowed = allowed_mask(key_base, tok_ref, start_ref, lanes)
                    allowed = jnp.concatenate([allowed] * group, axis=1)
                heads = range(heads_kv)
                krows = [slice(h * HEAD_WIDTH, (h + 1) * HEAD_WIDTH) for h in heads]
                vrows = [slice(v_off + h * HEAD_WIDTH, v_off + (h + 1) * HEAD_WIDTH) for h in heads]
                qt = [q_wide[krows[h], wide] for h in heads]
                dot = [do_wide[krows[h], wide] for h in heads]
                scores = [dot_nn(keys_nat[h], qt[h]) for h in heads]
                dprobs = [dot_nn(vals_nat[h], dot[h]) for h in heads]
                weights = [
                    jnp.exp2(scores[h] * SCORE - log_wide[h : h + 1, wide]) for h in heads
                ]
                if masked:
                    weights = [jnp.where(allowed, w, 0.0) for w in weights]
                ds = [
                    (weights[h] * (dprobs[h] - delta_wide[h : h + 1, wide])).astype(halves)
                    for h in heads
                ]
                dv = [dot_nt(dot[h], weights[h].astype(halves)) for h in heads]
                dk = [dot_nt(qt[h], ds[h]) for h in heads]
                dq = [dot_nn(kv[piece, krows[h], klanes], ds[h]) for h in heads]
                for h in heads:
                    acc[vrows[h], :] += dv[h]
                    acc[krows[h], :] += dk[h]
                    dq_wide[krows[h], wide] += dq[h]

            pl.when(needed & whole)(lambda: unit(False))
            pl.when(needed & jnp.logical_not(whole))(lambda: unit(True))
            return carry

        carry = lax.fori_loop(0, q_ref.shape[1] // BLK, query_block, carry)
        dkv[piece, 0:v_off, klanes] = (acc[0:v_off, :] * out_scale).astype(halves)
        dkv[piece, v_off:, klanes] = acc[v_off:, :].astype(halves)
        return carry

    lax.fori_loop(0, n * per, key_block, 0)
    for i in range(n):
        pltpu.make_async_copy(dkv.at[i], dkv_out.at[i], osem.at[i]).start()
    for h, rows, lanes, wrows, wlanes, hd in places:
        dq_out[rows, lanes] = dq_wide[wrows, wlanes] * out_scale
    for i in range(n):
        pltpu.make_async_copy(dkv.at[i], dkv_out.at[i], osem.at[i]).wait()


def attend_backward(counts, q_t, do_t, log_total, delta, pieces):
    n, width = pieces.shape[0], pieces.shape[2]
    heads_kv = pieces.shape[1] // (2 * HEAD_WIDTH)
    wide = q_t.shape[0] // (heads_kv * HEAD_WIDTH) * q_t.shape[1]
    outs = pl.pallas_call(
        functools.partial(bwd_kernel, n, width),
        out_shape=(
            jax.ShapeDtypeStruct(q_t.shape, floats),
            jax.ShapeDtypeStruct(pieces.shape, halves),
        ),
        in_specs=[SM] + [VM] * 4 + [HM],
        out_specs=(VM, HM),
        scratch_shapes=[
            pltpu.VMEM(pieces.shape, halves),
            pltpu.VMEM(pieces.shape, halves),
            pltpu.VMEM((heads_kv, BLK, HEAD_WIDTH), halves),
            pltpu.VMEM((heads_kv, BLK, HEAD_WIDTH), halves),
            pltpu.VMEM((pieces.shape[1], BLK), floats),
            pltpu.VMEM((heads_kv * HEAD_WIDTH, wide), halves),
            pltpu.VMEM((heads_kv * HEAD_WIDTH, wide), halves),
            pltpu.VMEM((heads_kv, wide), floats),
            pltpu.VMEM((heads_kv, wide), floats),
            pltpu.VMEM((heads_kv * HEAD_WIDTH, wide), floats),
            *place_scratch(n * width // BLK, q_t.shape[1]),
            pltpu.SemaphoreType.DMA((n,)),
            pltpu.SemaphoreType.DMA((n,)),
        ],
        compiler_params=pltpu.CompilerParams(vmem_limit_bytes=63 << 20),
        name="attend_backward",
    )(counts, q_t, do_t, log_total, delta, pieces)
    return outs


eps_norm = 1e-05
rope_base = 100000.0
reach_limit = 8


def shifted(block, axis, distance):
    devices = range(lax.axis_size(axis))
    route = [(i - distance, i) for i in devices if i - distance in devices]
    return lax.ppermute(block, axis, route)


def rms_scale(value_vectors, gain_vec):
    return (
        value_vectors
        * lax.rsqrt(jnp.mean(value_vectors * value_vectors, axis=-1, keepdims=True) + eps_norm)
        * gain_vec
    )


def rotary_turn(value_vectors, token_positions, heads):
    half_width = HEAD_WIDTH // 2
    inverse = 1.0 / rope_base ** (jnp.arange(half_width, dtype=jnp.float32) * 2.0 / HEAD_WIDTH)
    angles = token_positions.astype(jnp.float32)[:, None] * inverse[None, :]
    cosine = jnp.cos(angles)[:, None, :]
    sine_part = jnp.sin(angles)[:, None, :]
    shaped = value_vectors.reshape(value_vectors.shape[0], heads, HEAD_WIDTH)
    first_half = shaped[..., :half_width]
    second = shaped[..., half_width:]
    turned = jnp.concatenate(
        [first_half * cosine - second * sine_part, second * cosine + first_half * sine_part],
        axis=-1,
    )
    return turned.reshape(value_vectors.shape)


def swiglu(gate_pre, up_pre):
    return jax.nn.silu(gate_pre) * up_pre


def contract_rows(left_side, right_side):
    return lax.dot_general(
        left_side, right_side, (((0,), (0,)), ((), ())), preferred_element_type=jnp.float32
    )


def contract_cols(left_side, right_side):
    return lax.dot_general(
        left_side, right_side, (((1,), (1,)), ((), ())), preferred_element_type=jnp.float32
    )


def local(
    tokens,
    out_grad,
    segment_ids,
    attn_gain,
    query_weight,
    key_matrix,
    value_matrix,
    output_weight,
    mlp_gain,
    gate_weight,
    up_weight,
    down_weight,
):
    floats = jnp.float32
    halves = jnp.bfloat16
    shard_rows = tokens.shape[0]
    row_len = shard_rows * lax.axis_size("tp")
    row_index = lax.axis_index("dp")
    reach = min(reach_limit, lax.axis_size("dp") // 2)
    heads_q = query_weight.shape[1] // HEAD_WIDTH
    heads_kv = key_matrix.shape[1] // HEAD_WIDTH
    group_width = heads_q // heads_kv
    q_cols = heads_q * HEAD_WIDTH
    kv_cols = heads_kv * HEAD_WIDTH
    score_scale = HEAD_WIDTH ** (-0.5)
    row_first = row_index * row_len
    seg_row = lax.dynamic_slice_in_dim(segment_ids, row_first, row_len)
    index_row = row_first + jnp.arange(row_len, dtype=jnp.int32)
    every_index = jnp.arange(segment_ids.shape[0], dtype=jnp.int32)
    marks = (segment_ids[1:] != segment_ids[:-1]).astype(jnp.int32)
    starts = jnp.concatenate([jnp.zeros((1,), jnp.int32), marks * every_index[1:]])
    is_at = (starts[None, :] <= index_row[:, None]).astype(jnp.int32)
    token_positions = index_row - jnp.max(is_at * starts[None, :], axis=1)
    tokens32 = tokens.astype(floats)
    gain_attn = attn_gain.astype(floats)
    gain_mlp = mlp_gain.astype(floats)
    normed = rms_scale(tokens32, gain_attn).astype(halves)
    normed_full = lax.all_gather(normed, "tp", axis=0, tiled=True)
    joined = jnp.concatenate([query_weight, key_matrix, value_matrix], axis=1)
    projected = jnp.dot(normed_full, joined, preferred_element_type=floats)
    q_linear = projected[:, :q_cols]
    key_linear_out = projected[:, q_cols : q_cols + kv_cols]
    query_vectors = rotary_turn(q_linear, token_positions, heads_q).astype(halves)
    key_vectors = rotary_turn(key_linear_out, token_positions, heads_kv).astype(halves)
    value_vectors = projected[:, q_cols + kv_cols :].astype(halves)
    query_heads = query_vectors.reshape(row_len, heads_kv, group_width, HEAD_WIDTH)
    held_blocks = [(key_vectors, value_vectors)]
    moving = (key_vectors, value_vectors)
    for step_hop in range(reach):
        moving = shifted((moving[0], moving[1]), "dp", 1)
        held_blocks.append(moving)

    def block_mask(step_hop):
        key_row = row_index - step_hop
        seg_keys = lax.dynamic_slice_in_dim(segment_ids, jnp.maximum(key_row, 0) * row_len, row_len)
        key_index = key_row * row_len + jnp.arange(row_len, dtype=jnp.int32)
        return (seg_keys[None, :] == seg_row[:, None]) & (key_index[None, :] <= index_row[:, None])

    def block_needed(step_hop):
        last_key = jnp.maximum((row_index - step_hop + 1) * row_len - 1, 0)
        return (row_index >= step_hop) & (segment_ids[last_key] == seg_row[0])

    block_masks = [block_mask(step_hop) for step_hop in range(reach + 1)]

    def apply_block(step_hop, update, state_in):
        key_block, value_block = held_blocks[step_hop]
        if step_hop == 0:
            return update(state_in, key_block, value_block, block_masks[0])
        return lax.cond(
            block_needed(step_hop),
            update,
            lambda state_kept, key_skip, value_skip, mask_skip: state_kept,
            state_in,
            key_block,
            value_block,
            block_masks[step_hop],
        )

    def scores(key_block, allowed):
        raw_scores = jnp.einsum(
            "qhgd,khd->hgqk",
            query_heads,
            key_block.reshape(row_len, heads_kv, HEAD_WIDTH),
            preferred_element_type=floats,
        )
        return jnp.where(allowed, raw_scores * score_scale, -jnp.inf)

    def add_online(state_in, key_block, value_block, allowed):
        run_max, run_total, run_sum = state_in
        block_scores = scores(key_block, allowed)
        new_max = jnp.maximum(run_max, jnp.max(block_scores, axis=-1))
        factor = jnp.exp(run_max - new_max)
        weights = jnp.exp(block_scores - new_max[..., None])
        run_total = run_total * factor + jnp.sum(weights, axis=-1)
        run_sum = run_sum * jnp.moveaxis(factor, 2, 0)[..., None] + jnp.einsum(
            "hgqk,khd->qhgd",
            weights.astype(halves),
            value_block.reshape(row_len, heads_kv, HEAD_WIDTH),
            preferred_element_type=floats,
        )
        return (new_max, run_total, run_sum)

    online = (
        jnp.full((heads_kv, group_width, row_len), -jnp.inf, floats),
        jnp.zeros((heads_kv, group_width, row_len), floats),
        jnp.zeros((row_len, heads_kv, group_width, HEAD_WIDTH), floats),
    )
    for step_hop in range(reach + 1):
        online = apply_block(step_hop, add_online, online)
    run_max, run_total, run_sum = online
    log_total = (run_max + jnp.log(run_total))[..., None]
    context_heads = (run_sum / jnp.moveaxis(run_total, 2, 0)[..., None]).astype(halves)
    context = context_heads.reshape(row_len, q_cols)
    residual = tokens32 + lax.psum_scatter(
        jnp.dot(context, output_weight, preferred_element_type=floats).astype(jnp.bfloat16),
        "tp",
        scatter_dimension=0,
        tiled=True,
    ).astype(jnp.float32)
    mlp_normed = rms_scale(residual, gain_mlp).astype(halves)
    mlp_full = lax.all_gather(mlp_normed, "tp", axis=0, tiled=True)
    gate_pre = jnp.dot(mlp_full, gate_weight, preferred_element_type=floats)
    up_pre = jnp.dot(mlp_full, up_weight, preferred_element_type=floats)
    hidden = swiglu(gate_pre, up_pre).astype(halves)
    output = residual + lax.psum_scatter(
        jnp.dot(hidden, down_weight, preferred_element_type=floats).astype(jnp.bfloat16),
        "tp",
        scatter_dimension=0,
        tiled=True,
    ).astype(jnp.float32)
    grad_full = lax.all_gather(out_grad, "tp", axis=0, tiled=True)
    grad_hidden = contract_cols(grad_full, down_weight)
    down_grad = contract_rows(grad_full, hidden)
    silu_back = jax.vjp(swiglu, gate_pre, up_pre)[1]
    grad_gate, grad_up = silu_back(grad_hidden)
    grad_gate = grad_gate.astype(halves)
    grad_up = grad_up.astype(halves)
    gate_grad = contract_rows(mlp_full, grad_gate)
    up_grad = contract_rows(mlp_full, grad_up)
    grad_mlp_normed = lax.psum_scatter(
        (contract_cols(grad_gate, gate_weight) + contract_cols(grad_up, up_weight)).astype(
            jnp.bfloat16
        ),
        "tp",
        scatter_dimension=0,
        tiled=True,
    ).astype(jnp.float32)
    mlp_norm_back = jax.vjp(rms_scale, residual, gain_mlp)[1]
    grad_residual_part, mlp_gain_part = mlp_norm_back(grad_mlp_normed)
    grad_residual = out_grad.astype(floats) + grad_residual_part
    attn_grad_full = lax.all_gather(grad_residual.astype(halves), "tp", axis=0, tiled=True)
    output_grad = contract_rows(attn_grad_full, context)
    grad_context = (
        contract_cols(attn_grad_full, output_weight)
        .astype(halves)
        .reshape(row_len, heads_kv, group_width, HEAD_WIDTH)
    )
    delta_col = jnp.einsum(
        "qhgd,qhgd->hgq", grad_context, context_heads, preferred_element_type=floats
    )[..., None]

    def add_grads(state_in, key_block, value_block, allowed):
        query_acc, key_acc, value_acc = state_in
        probabilities = jnp.exp(scores(key_block, allowed) - log_total)
        grad_probs = jnp.einsum(
            "qhgd,khd->hgqk",
            grad_context,
            value_block.reshape(row_len, heads_kv, HEAD_WIDTH),
            preferred_element_type=floats,
        )
        grad_scores = (probabilities * (grad_probs - delta_col)).astype(halves)
        key_heads = key_block.reshape(row_len, heads_kv, HEAD_WIDTH)
        query_acc = (
            query_acc
            + jnp.einsum("hgqk,khd->qhgd", grad_scores, key_heads, preferred_element_type=floats)
            * score_scale
        )
        key_acc = (
            key_acc
            + jnp.einsum(
                "hgqk,qhgd->khd", grad_scores, query_heads, preferred_element_type=floats
            ).reshape(row_len, kv_cols)
            * score_scale
        )
        value_acc = value_acc + jnp.einsum(
            "hgqk,qhgd->khd",
            probabilities.astype(halves),
            grad_context,
            preferred_element_type=floats,
        ).reshape(row_len, kv_cols)
        return (query_acc, key_acc, value_acc)

    query_acc = jnp.zeros((row_len, heads_kv, group_width, HEAD_WIDTH), floats)
    carried = (jnp.zeros((row_len, kv_cols), floats), jnp.zeros((row_len, kv_cols), floats))
    for step_hop in range(reach, 0, -1):
        query_acc, key_acc, value_acc = apply_block(
            step_hop, add_grads, (query_acc, carried[0], carried[1])
        )
        carried = (
            shifted(key_acc.astype(jnp.bfloat16), "dp", -1).astype(key_acc.dtype),
            shifted(value_acc.astype(jnp.bfloat16), "dp", -1).astype(value_acc.dtype),
        )
    query_acc, key_total, value_total = apply_block(
        0, add_grads, (query_acc, carried[0], carried[1])
    )
    query_back = jax.vjp(lambda linear: rotary_turn(linear, token_positions, heads_q), q_linear)[1]
    key_back = jax.vjp(
        lambda linear: rotary_turn(linear, token_positions, heads_kv), key_linear_out
    )[1]
    grad_q_linear = query_back(query_acc.reshape(row_len, q_cols))[0]
    grad_k_linear = key_back(key_total)[0]
    grads_joined = jnp.concatenate([grad_q_linear, grad_k_linear, value_total], axis=1).astype(
        halves
    )
    proj_grad = contract_rows(normed_full, grads_joined)
    grad_normed = lax.psum_scatter(
        contract_cols(grads_joined, joined).astype(jnp.bfloat16),
        "tp",
        scatter_dimension=0,
        tiled=True,
    ).astype(jnp.float32)
    attn_norm_back = jax.vjp(rms_scale, tokens32, gain_attn)[1]
    grad_tokens_part, attn_gain_part = attn_norm_back(grad_normed)
    input_grad = grad_residual + grad_tokens_part
    def scatter_rows(grad):
        return lax.psum_scatter(
            grad.astype(halves), "dp", scatter_dimension=0, tiled=True
        ).astype(floats)

    mlp_sums = scatter_rows(jnp.concatenate([gate_grad, up_grad, down_grad], axis=1))
    ff_cols = gate_weight.shape[1]
    gate_sum = mlp_sums[:, :ff_cols]
    up_sum = mlp_sums[:, ff_cols : 2 * ff_cols]
    down_sum = mlp_sums[:, 2 * ff_cols :]
    attn_sums = scatter_rows(jnp.concatenate([proj_grad, output_grad], axis=1))
    query_sum = attn_sums[:, :q_cols]
    key_sum = attn_sums[:, q_cols : q_cols + kv_cols]
    value_sum = attn_sums[:, q_cols + kv_cols : q_cols + 2 * kv_cols]
    output_sum = attn_sums[:, q_cols + 2 * kv_cols :]
    attn_gain_sum = lax.psum_scatter(attn_gain_part, "dp", scatter_dimension=0, tiled=True)
    mlp_gain_sum = lax.psum_scatter(mlp_gain_part, "dp", scatter_dimension=0, tiled=True)
    attn_gain_total, mlp_gain_total = lax.psum((attn_gain_sum, mlp_gain_sum), "tp")
    return (
        output.astype(halves),
        input_grad,
        attn_gain_total,
        query_sum,
        key_sum,
        value_sum,
        output_sum.T,
        mlp_gain_total,
        gate_sum,
        up_sum,
        down_sum.T,
    )


MESH = pl.DeviceIdType.MESH


def meet(devices):
    barrier = pltpu.get_barrier_semaphore()
    for device in devices:
        pl.semaphore_signal(barrier, inc=1, device_id=device, device_id_type=MESH)
    pl.semaphore_wait(barrier, len(devices))


def tiles(total, step, body):
    def one(i, carry):
        body(pl.ds(pl.multiple_of(i * step, step), step))
        return carry

    lax.fori_loop(0, total // step, one, 0)


CHUNKS = 4


class GroupSum:
    def __init__(self, copies, bufs, place):
        self.copies, self.bufs, self.place = copies, bufs, place

    def run(self, product):
        part_near, part_own, out_far, out_beside, out_near, in_near, in_own, in_sum = self.bufs

        def put_there(cols, value):
            rows = value.shape[0] // 2
            part_near[:, cols] = value[:rows]
            out_far[:, cols] = value[rows:].astype(halves)

        def put_here(cols, value):
            rows = value.shape[0] // 2
            part_own[:, cols] = value[:rows]
            out_beside[:, cols] = value[rows:].astype(halves)

        product(1, put_there)
        self.far = self.copies.make(out_far, in_near, self.place.beside)
        self.far.start()
        product(0, put_here)
        self.side = self.copies.make(out_beside, in_own, self.place.beside)
        self.side.start()
        self.far.wait_recv()
        rows = part_near.shape[0] // CHUNKS
        self.sums = []
        for k in range(CHUNKS):
            at = pl.ds(k * rows, rows)
            out_near[at, :] = (part_near[at, :] + in_near[at, :].astype(floats)).astype(halves)
            copy = self.copies.make(out_near.at[at], in_sum.at[at], self.place.near)
            copy.start()
            self.sums.append(copy)

    def take(self, k):
        part_near, part_own, out_far, out_beside, out_near, in_near, in_own, in_sum = self.bufs
        if k == 0:
            self.side.wait_recv()
        self.sums[k].wait_recv()
        rows = part_own.shape[0] // CHUNKS
        at = pl.ds(k * rows, rows)
        return part_own[at, :] + in_own[at, :].astype(floats) + in_sum[at, :].astype(floats)

    def finish(self):
        for copy in (self.far, self.side, *self.sums):
            copy.wait_send()


class GroupGather:
    def __init__(self, copies, full, block, place):
        self.copies, self.full, self.block, self.place = copies, full, block, place
        self.sent = []

    def slot(self, n, k):
        rows = self.block // CHUNKS
        return self.full.at[pl.ds(n * self.block + k * rows, rows)]

    def put(self, k):
        for i, (n, device) in enumerate(((2, self.place.near), (1, self.place.beside))):
            copy = self.copies.make(self.slot(0, k), self.slot(n, k), device)
            copy.start()
            self.sent.append((i, copy))

    def wait_here(self):
        for i, copy in self.sent:
            if i == 1:
                copy.wait_recv()

    def wait_there(self):
        relays = []
        k = 0
        for i, copy in self.sent:
            if i == 0:
                copy.wait_recv()
                relay = self.copies.make(self.slot(2, k), self.slot(3, k), self.place.beside)
                relay.start()
                relays.append(relay)
                k += 1
        for relay in relays:
            relay.wait_recv()
        self.sent += [(2, relay) for relay in relays]

    def finish(self):
        for _, copy in self.sent:
            copy.wait_send()


class Copies:
    limit = 96

    def __init__(self, send_sems, recv_sems):
        self.send_sems, self.recv_sems, self.used = send_sems, recv_sems, 0

    def make(self, src, dst, device):
        i = self.used
        self.used += 1
        return pltpu.make_async_remote_copy(
            src_ref=src,
            dst_ref=dst,
            send_sem=self.send_sems.at[i],
            recv_sem=self.recv_sems.at[i],
            device_id=device,
            device_id_type=MESH,
        )


def copy_semaphores():
    return [pltpu.SemaphoreType.DMA((Copies.limit,)), pltpu.SemaphoreType.DMA((Copies.limit,))]


class Place:
    def __init__(self):
        dp, z = lax.axis_index("dp"), lax.axis_index("tp")
        self.dp, self.z = dp, z
        self.c = lax.rem(dp, 2)
        self.x = lax.rem(dp // 2, 2)
        self.y = dp // 4
        far_z = lax.rem(z + 2, 4)
        self.beside = (dp + 1 - 2 * self.c, z)
        self.near = (dp, z + 1 - 2 * lax.rem(z, 2))
        self.far = (dp, far_z)
        self.cross = (self.beside[0], far_z)
        self.over_x = (dp + 2 - 4 * self.x, z)
        self.over_y = (dp + 4 - 8 * self.y, z)
        self.slot = 2 * self.y + self.x
        self.slot_x = 2 * self.y + 1 - self.x
        self.slot_y = 2 - 2 * self.y + self.x
        self.odd = self.c == 1
        self.corner = (self.x == 1) & (self.y == 1)
        self.turn = (self.x == 0) & (self.y == 1)


def rope_tables(counts_ref, inverse_ref, cos_ref, sin_ref):
    index = group_index()
    positions = (index - item_start(counts_ref, index)).astype(floats)
    angles = inverse_ref[...] * positions
    cos_ref[...] = jnp.cos(angles)
    sin_ref[...] = jnp.sin(angles)


class PlaneFetch:
    def __init__(self, copies, place, out, own=None, own_slice=None):
        self.place, self.out = place, out
        rows = out.shape[0] // 8

        def part(slot, ch):
            return pl.ds(slot * (2 * rows) + ch * rows, rows)

        def remote(slot, ch, device):
            at = part(slot, ch)
            return copies.make(out.at[at], out.at[at], device)

        p = place
        self.hop = None
        if own is not None:
            self.hop = [
                copies.make(own.at[part(p.slot, ch)], out.at[part(p.slot, ch)], p.far)
                for ch in range(2)
            ]
        if own_slice is not None:
            self.hop = [
                copies.make(own_slice.at[part(0, ch)], out.at[part(p.slot, ch)], p.far)
                for ch in range(2)
            ]
        self.x = [remote(p.slot, ch, p.over_x) for ch in range(2)]
        self.y = [remote(p.slot, ch, p.over_y) for ch in range(2)]
        self.relay_y = remote(p.slot_x, 0, p.over_y)
        self.relay_x = remote(p.slot_y, 1, p.over_x)

    def start(self):
        @pl.when(self.place.odd)
        def _():
            for copy in self.hop:
                copy.start()

    def forward(self):
        @pl.when(self.place.odd)
        def _():
            for ch in range(2):
                if self.hop is not None:
                    self.hop[ch].wait_recv()
                self.x[ch].start()
                self.y[ch].start()

    def relay(self):
        @pl.when(self.place.odd)
        def _():
            self.x[0].wait_recv()
            self.relay_y.start()
            self.y[1].wait_recv()
            self.relay_x.start()

    def finish(self):
        @pl.when(self.place.odd)
        def _():
            self.x[1].wait_recv()
            self.y[0].wait_recv()
            self.relay_y.wait_recv()
            self.relay_x.wait_recv()

    def drain(self):
        @pl.when(self.place.odd)
        def _():
            for copy in (self.hop or []) + self.x + self.y + [self.relay_y, self.relay_x]:
                copy.wait_send()


class Spread:
    def __init__(self, copies, place, source, slots):
        self.place = place
        self.to_x = copies.make(source, slots[1], place.over_x)
        self.to_y = copies.make(source, slots[2], place.over_y)
        self.relayed = copies.make(slots[2], slots[3], place.over_x)

    def start(self):
        pl.when(self.place.x == 0)(self.to_x.start)
        pl.when(self.place.y == 0)(self.to_y.start)

    def relay(self):
        @pl.when(self.place.corner)
        def _():
            self.to_y.wait_recv()
            self.relayed.start()

    def finish(self):
        p = self.place
        pl.when(p.x == 1)(self.to_x.wait_recv)
        pl.when((p.y == 1) & (p.x == 0))(self.to_y.wait_recv)
        pl.when(p.turn)(self.relayed.wait_recv)
        pl.when(p.x == 0)(self.to_x.wait_send)
        pl.when(p.y == 0)(self.to_y.wait_send)
        pl.when(p.corner)(self.relayed.wait_send)


def first_kernel(
    counts, inverse_ref, tok_ref, grad_ref, gain_ref, wq_in, wk_ref, wv_ref, wo_in, wd_in, wg_in, wu_in,
    q_out, kv_out, n_out, g_full, joined_out, wo_out, wd_out, slice_g, slice_u,
    n_full, joined, own_slice, slices, cos_ref, sin_ref, linear, kv_own, ss, rs, lsem,
):
    place = Place()
    copies = Copies(ss, rs)
    block, width = tok_ref.shape
    two = 2 * block
    q_cols = q_out.shape[0]
    kv_cols = kv_own.shape[1] // 2
    q_lanes = pl.ds(0, q_cols)
    slice_rows = pl.ds(place.slot * own_slice.shape[0], own_slice.shape[0])
    load_q = pltpu.make_async_copy(wq_in, joined.at[:, q_lanes], lsem.at[0])
    load_q_odd = pltpu.make_async_copy(
        wq_in.at[slice_rows], own_slice.at[:, q_lanes], lsem.at[0]
    )
    pl.when(place.c == 0)(load_q.start)
    pl.when(place.odd)(load_q_odd.start)
    rows4 = slice_g.shape[0]
    at_slot = pl.ds(place.slot * rows4, rows4)
    slice_loads = [
        pltpu.make_async_copy(src.at[at_slot], slices.at[i], lsem.at[1 + i])
        for i, src in enumerate((wg_in, wu_in))
    ]
    slice_stores = [
        pltpu.make_async_copy(slices.at[i], dst, lsem.at[6 + i])
        for i, dst in enumerate((slice_g, slice_u))
    ]
    for copy in slice_loads:
        copy.start()

    own_grad = pltpu.make_async_copy(grad_ref, g_full.at[pl.ds(0, block)], lsem.at[3])
    own_grad.start()
    meet((place.beside, place.near, place.far, place.cross, place.over_x, place.over_y))

    @pl.when(place.odd)
    def _():
        lanes = pl.ds(pl.multiple_of(place.slot * own_slice.shape[0], 128), own_slice.shape[0])
        own_slice[:, q_cols : q_cols + kv_cols] = wk_ref[:, lanes].T
        own_slice[:, q_cols + kv_cols :] = wv_ref[:, lanes].T
        load_q_odd.wait()

    fetch_joined = PlaneFetch(copies, place, joined, own_slice=own_slice)
    fetch_o = PlaneFetch(copies, place, wo_out, wo_in)
    fetch_d = PlaneFetch(copies, place, wd_out, wd_in)
    gather = GroupGather(copies, n_full, block, place)
    gather_g = GroupGather(copies, g_full, block, place)
    fetch_joined.start()
    chunk = block // CHUNKS
    for k in range(CHUNKS):
        at = pl.ds(k * chunk, chunk)
        tok = tok_ref[at, :].astype(floats)
        root = lax.rsqrt(jnp.mean(tok * tok, axis=-1, keepdims=True) + eps_norm)
        n_full[at, :] = (tok * root * gain_ref[...]).astype(halves)
        gather.put(k)
    fetch_joined.forward()
    fetch_o.start()
    fetch_d.start()
    @pl.when(place.c == 0)
    def _():
        joined[:, q_cols : q_cols + kv_cols] = wk_ref[...].T
        joined[:, q_cols + kv_cols :] = wv_ref[...].T

    rope_tables(counts, inverse_ref, cos_ref, sin_ref)
    for load, store in zip(slice_loads, slice_stores):
        load.wait()
        store.start()
    fetch_joined.relay()
    gather.wait_here()
    fetch_joined.finish()
    pl.when(place.c == 0)(load_q.wait)
    keep_joined = pltpu.make_async_copy(joined, joined_out, lsem.at[8])
    keep_joined.start()

    def project(k):
        rows = slice(k * two, (k + 1) * two)

        def one(cols):
            linear[cols, :] = dot_nn(n_full[rows, :], joined[:, cols]).T

        tiles(joined.shape[1], 256, one)
        half_width = HEAD_WIDTH // 2
        for head in range((q_cols + kv_cols) // HEAD_WIDTH):
            low = slice(head * HEAD_WIDTH, head * HEAD_WIDTH + half_width)
            high = slice(head * HEAD_WIDTH + half_width, (head + 1) * HEAD_WIDTH)
            one_half, two_half = linear[low, :], linear[high, :]
            cosine, sine = cos_ref[:, rows], sin_ref[:, rows]
            first = (one_half * cosine - two_half * sine).astype(halves)
            second = (two_half * cosine + one_half * sine).astype(halves)
            if head * HEAD_WIDTH < q_cols:
                q_out[low, rows] = first
                q_out[high, rows] = second
            else:
                kv_own[k, low.start - q_cols : low.stop - q_cols, :] = first
                kv_own[k, high.start - q_cols : high.stop - q_cols, :] = second
        kv_own[k, kv_cols:, :] = (linear[q_cols + kv_cols :, :].astype(halves) * VSCALE).astype(halves)

    crossings, spreads_a, spreads_b, kept = [], [], [], []

    def share(k):
        slots = [kv_out.at[8 * k + i] for i in range(8)]
        keep = pltpu.make_async_copy(kv_own.at[k], slots[0], lsem.at[4 + k])
        keep.start()
        kept.append(keep)
        crossing = copies.make(kv_own.at[k], slots[4], place.cross)
        crossing.start()
        crossings.append(crossing)
        spread = Spread(copies, place, kv_own.at[k], slots[:4])
        spread.start()
        spreads_a.append(spread)
        spreads_b.append(Spread(copies, place, slots[4], slots[4:]))

    project(0)
    share(0)
    gather.wait_there()
    own_grad.wait()
    for k in range(CHUNKS):
        gather_g.put(k)
    project(1)
    share(1)
    keep_n = pltpu.make_async_copy(n_full, n_out, lsem.at[9])
    keep_n.start()
    fetch_o.forward()
    fetch_d.forward()
    spreads_a[0].relay()
    spreads_a[1].relay()
    crossings[0].wait_recv()
    spreads_b[0].start()
    fetch_o.relay()
    fetch_d.relay()
    gather_g.wait_there()
    spreads_b[0].relay()
    crossings[1].wait_recv()
    spreads_b[1].start()
    spreads_b[1].relay()
    fetch_o.finish()
    fetch_d.finish()
    gather_g.wait_here()
    for spread in spreads_a + spreads_b:
        spread.finish()
    for copy in kept + slice_stores + [keep_joined, keep_n]:
        copy.wait()
    for copy in crossings:
        copy.wait_send()
    for fetch in (fetch_joined, fetch_o, fetch_d):
        fetch.drain()
    gather.finish()
    gather_g.finish()


def first_part(counts, inverse, tokens, out_grad, gain, projections, weights):
    block, width = tokens.shape
    group = 4 * block
    shape = jax.ShapeDtypeStruct
    hidden = weights[2].shape[1]
    part = (width // 4, hidden)
    half_width = HEAD_WIDTH // 2
    q_cols, kv_cols = projections[0].shape[1], projections[1].shape[0]
    joined_cols = q_cols + 2 * kv_cols
    out_shape = (
        shape((q_cols, group), halves),
        shape((16, 2 * kv_cols, 2 * block), halves),
        shape((group, width), halves),
        shape((group, width), halves),
        shape((width, joined_cols), halves),
        shape(weights[0].shape, halves),
        shape(weights[1].shape, halves),
        shape(part, halves),
        shape(part, halves),
    )
    return pl.pallas_call(
        first_kernel,
        out_shape=out_shape,
        in_specs=[SM] + [VM] * 4 + [HB, VM, VM] + [HB] * 4,
        out_specs=(VM, HM, HM, VM, HM, HM, HM, HM, HM),
        scratch_shapes=[
            pltpu.VMEM((group, width), halves),
            pltpu.VMEM((width, joined_cols), halves),
            pltpu.VMEM((width // 4, joined_cols), halves),
            pltpu.VMEM((2,) + part, halves),
            pltpu.VMEM((half_width, group), floats),
            pltpu.VMEM((half_width, group), floats),
            pltpu.VMEM((joined_cols, 2 * block), floats),
            pltpu.VMEM((2, 2 * kv_cols, 2 * block), halves),
            *copy_semaphores(),
            pltpu.SemaphoreType.DMA((10,)),
        ],
        compiler_params=pltpu.CompilerParams(
            collective_id=2, has_side_effects=True, vmem_limit_bytes=63 << 20
        ),
        name="first",
    )(counts, inverse, tokens, out_grad, gain, *projections, *weights)


class PlaneSum:
    def __init__(self, copies, place, x_first, bufs, sent=None, come=None):
        self.place, self.bufs, self.x_first = place, bufs, x_first
        half, keep, come_two, home_one, home_two = bufs
        first, second = (place.over_x, place.over_y) if x_first else (place.over_y, place.over_x)
        self.at = place.y if x_first else place.x
        self.one = None if sent is None else copies.make(sent, come, first)
        self.two = copies.make(half, come_two, second)
        rows = home_one.shape[0]
        c = place.c
        home = (c * place.cross[0] + (1 - c) * place.beside[0], c * place.cross[1] + (1 - c) * place.beside[1])
        self.to_home = copies.make(half.at[pl.ds((1 - c) * rows, rows)], home_one, home)
        self.to_far = copies.make(half.at[pl.ds(rows, rows)], home_two, place.far)

    def cross_second(self, kept, come):
        if self.one is not None:
            self.one.wait()
        half, keep, come_two, home_one, home_two = self.bufs
        at = self.at
        half[...] = (kept[1 - at].astype(floats) + come[1 - at].astype(floats)).astype(halves)
        self.two.start()
        keep[...] = (kept[at].astype(floats) + come[at].astype(floats)).astype(halves)

    def go_home(self):
        half, keep, come_two, home_one, home_two = self.bufs
        self.two.wait()
        half[...] = (keep[...].astype(floats) + come_two[...].astype(floats)).astype(halves)
        self.to_home.start()
        pl.when(self.place.odd)(self.to_far.start)

    def finish(self, out):
        half, keep, come_two, home_one, home_two = self.bufs
        rows = home_one.shape[0]
        self.to_home.wait()

        @pl.when(self.place.c == 0)
        def _():
            out[...] = half[:rows, :].astype(floats) + home_one[...].astype(floats)

        @pl.when(self.place.odd)
        def _():
            self.to_far.wait()
            out[...] = home_one[...].astype(floats) + home_two[...].astype(floats)


def plane_buffers(rows, cols):
    full = pltpu.VMEM((rows, cols), halves)
    part = pltpu.VMEM((rows // 2, cols), halves)
    return [full, full, full, part, part]


def outer_blocks(place, x_first, left, right, send_ref, keep_ref, on_sent):
    rows = left.shape[1] // 4
    for kept in (False, True):
        for i in range(2):
            if x_first:
                block = 2 * i + (place.x if kept else 1 - place.x)
            else:
                block = 2 * (place.y if kept else 1 - place.y) + i
            cols = pl.ds(pl.multiple_of(block * rows, 128), rows)
            value = lax.dot_general(
                left[:, cols], right, (((0,), (0,)), ((), ())), preferred_element_type=floats
            ).astype(halves)
            (keep_ref if kept else send_ref)[i] = value
        if not kept:
            on_sent()


def mid_kernel(ctx_ref, tok_ref, gain_ref, g_full, weight_refs, outs, scratch):
    (res_out, gres_out, e_full, near_out, down_keep, down_come, gate_keep, gate_send, up_keep, up_send,
     dctx_out, delta_out, gain_out) = outs
    (ctx, m_full, dh, hid, dgate, dup, w_o, w_d, w_g, w_u, down_send, part_out, far_in, own_in, *bufs, ss, rs, wsem) = scratch
    place = Place()
    copies = Copies(ss, rs)
    block, width = tok_ref.shape
    two = 2 * block
    hidden = w_g.shape[1]
    wo_ref, wd_ref, wg_ref, wu_ref, wo_got, wd_got, slice_g, slice_u = weight_refs
    first_loads = [
        pltpu.make_async_copy(src, dst, wsem.at[i])
        for i, (src, dst) in enumerate(((wo_ref, w_o), (wd_ref, w_d)))
    ]
    first_loads_odd = [
        pltpu.make_async_copy(src, dst, wsem.at[i])
        for i, (src, dst) in enumerate(((wo_got, w_o), (wd_got, w_d)))
    ]

    def wait_first(i):
        pl.when(place.c == 0)(first_loads[i].wait)
        pl.when(place.odd)(first_loads_odd[i].wait)

    rows4 = slice_g.shape[0]
    at_slot = pl.ds(place.slot * rows4, rows4)
    loads = [
        pltpu.make_async_copy(src, dst, wsem.at[2 + i])
        for i, (src, dst) in enumerate(((wg_ref, w_g), (wu_ref, w_u)))
    ]
    loads_odd = [
        pltpu.make_async_copy(src, dst.at[at_slot], wsem.at[2 + i])
        for i, (src, dst) in enumerate(((slice_g, w_g), (slice_u, w_u)))
    ]

    @pl.when(place.c == 0)
    def _():
        for copy in first_loads + loads:
            copy.start()

    @pl.when(place.odd)
    def _():
        for copy in first_loads_odd + loads_odd:
            copy.start()

    ctx[...] = ctx_ref[...].T
    meet((place.beside, place.near, place.over_x, place.over_y))
    fetches = [PlaneFetch(copies, place, w_g), PlaneFetch(copies, place, w_u)]

    @pl.when(place.odd)
    def _():
        for copy in loads_odd:
            copy.wait()

    for fetch in fetches:
        fetch.forward()
    sum_one = GroupSum(copies, bufs, place)
    gather_one = GroupGather(copies, m_full, block, place)
    sum_two = GroupSum(copies, bufs, place)
    gather_two = GroupGather(copies, e_full, block, place)

    def project(k, put):
        rows = slice(k * two, (k + 1) * two)
        tiles(width, 256, lambda cols: put(cols, dot_nn(ctx[rows, :], w_o[:, cols])))

    wait_first(0)
    sum_one.run(project)
    wait_first(1)

    def back_hidden(cols):
        for rows in (slice(0, two), slice(two, 2 * two)):
            dh[rows, cols] = dot_nt(g_full[rows, :], w_d[cols, :]).astype(halves)

    tiles(hidden, 256, back_hidden)
    for fetch in fetches:
        fetch.relay()
    chunk = block // CHUNKS
    for k in range(CHUNKS):
        at = pl.ds(k * chunk, chunk)
        res = tok_ref[at, :].astype(floats) + sum_one.take(k)
        res_out[at, :] = res
        root = lax.rsqrt(jnp.mean(res * res, axis=-1, keepdims=True) + eps_norm)
        m_full[at, :] = (res * root * gain_ref[...]).astype(halves)
        gather_one.put(k)
    sum_one.finish()

    def activate(k):
        rows = slice(k * two, (k + 1) * two)

        def one(cols):
            gate_pre = dot_nn(m_full[rows, :], w_g[:, cols])
            up_pre = dot_nn(m_full[rows, :], w_u[:, cols])
            back = dh[rows, cols].astype(floats)
            sigma = 1.0 / (1.0 + jnp.exp(-gate_pre))
            silu = gate_pre * sigma
            hid[rows, cols] = (silu * up_pre).astype(halves)
            dgate[rows, cols] = (back * up_pre * (sigma + silu * (1.0 - sigma))).astype(halves)
            dup[rows, cols] = (back * silu).astype(halves)

        tiles(hidden, 256, one)

    def partial_out(k):
        rows = slice(k * two, (k + 1) * two)

        def one(cols):
            part_out[rows, cols] = dot_nn(hid[rows, :], w_d[:, cols]).astype(halves)

        tiles(width, 256, one)

    for fetch in fetches:
        fetch.finish()

    @pl.when(place.c == 0)
    def _():
        for copy in loads:
            copy.wait()

    gather_one.wait_here()
    activate(0)
    partial_out(0)
    gather_one.wait_there()
    activate(1)
    gather_one.finish()

    def back_norm(k, put):
        rows = slice(k * two, (k + 1) * two)
        tiles(
            width,
            256,
            lambda cols: put(
                cols, dot_nt(dgate[rows, :], w_g[cols, :]) + dot_nt(dup[rows, :], w_u[cols, :])
            ),
        )

    sum_two.run(back_norm)
    partial_out(1)
    to_side = [
        copies.make(part_out.at[pl.ds(3 * block, block)], far_in, place.beside),
        copies.make(part_out.at[pl.ds(block, block)], own_in, place.beside),
    ]
    for copy in to_side:
        copy.start()
    down_over = copies.make(down_send, down_come, place.over_x)
    outer_blocks(place, True, g_full, hid[...], down_send, down_keep, down_over.start)
    outer_blocks(place, False, m_full, dgate[...], gate_send, gate_keep, lambda: None)
    gain_out[...] = jnp.zeros_like(gain_out)
    for k in range(CHUNKS):
        at = pl.ds(k * chunk, chunk)
        back = sum_two.take(k)
        res = res_out[at, :]
        root = lax.rsqrt(jnp.mean(res * res, axis=-1, keepdims=True) + eps_norm)
        weighted = back * gain_ref[...]
        slope = jnp.mean(weighted * res, axis=-1, keepdims=True)
        grad = g_full[at, :].astype(floats) + root * weighted - res * (root * root * root * slope)
        gain_out[...] += jnp.sum(back * res * root, axis=0, keepdims=True)
        gres_out[at, :] = grad
        e_full[at, :] = grad.astype(halves)
        gather_two.put(k)
    sum_two.finish()
    outer_blocks(place, True, m_full, dup[...], up_send, up_keep, lambda: None)

    def back_context(k):
        lanes = slice(k * two, (k + 1) * two)
        grad = dot_nt(w_o[...], e_full[lanes, :]).astype(halves)
        dctx_out[:, lanes] = grad
        prod = grad.astype(floats) * ctx_ref[:, lanes].astype(floats)
        for hd in range(delta_out.shape[0]):
            delta_out[hd : hd + 1, lanes] = VSCALE * jnp.sum(
                prod[hd * HEAD_WIDTH : (hd + 1) * HEAD_WIDTH], axis=0, keepdims=True
            )

    for copy in to_side:
        copy.wait()
    for k in range(CHUNKS):
        at = pl.ds(k * chunk, chunk)
        near = pl.ds(two + k * chunk, chunk)
        near_out[at, :] = (part_out[near, :].astype(floats) + far_in[at, :].astype(floats)).astype(halves)
        res_out[at, :] += part_out[at, :].astype(floats) + own_in[at, :].astype(floats)
    gather_two.wait_here()
    back_context(0)
    gather_two.wait_there()
    back_context(1)
    gather_two.finish()
    for fetch in fetches:
        fetch.drain()
    down_over.wait()


def middle(context_t, tokens, gain, grad_full, weights):
    q_cols, group = context_t.shape
    block, width = tokens.shape
    hidden = weights[2].shape[1]
    shape = jax.ShapeDtypeStruct
    out_shape = (
        shape((block, width), floats),
        shape((block, width), floats),
        shape((group, width), halves),
        shape((block, width), halves),
        *[shape((2, width // 4, hidden), halves)] * 6,
        shape((q_cols, group), halves),
        shape((q_cols // HEAD_WIDTH, group), floats),
        shape((1, width), floats),
    )
    scratch = [
        pltpu.VMEM((group, q_cols), halves),
        pltpu.VMEM((group, width), halves),
        *[pltpu.VMEM((group, hidden), halves)] * 4,
        *[pltpu.VMEM(weight.shape, halves) for weight in weights[:4]],
        pltpu.VMEM((2, width // 4, hidden), halves),
        pltpu.VMEM((group, width), halves),
        *[pltpu.VMEM((block, width), halves)] * 2,
        *[pltpu.VMEM((block, width), floats)] * 2,
        *[pltpu.VMEM((block, width), halves)] * 6,
        *copy_semaphores(),
        pltpu.SemaphoreType.DMA((4,)),
    ]

    def kernel(*refs):
        mid_kernel(*refs[:4], refs[4:12], refs[12:25], refs[25:])

    return pl.pallas_call(
        kernel,
        out_shape=out_shape,
        in_specs=[VM] * 4 + [HB] * 8,
        out_specs=(VM,) * 13,
        scratch_shapes=scratch,
        compiler_params=pltpu.CompilerParams(
            collective_id=1, has_side_effects=True, vmem_limit_bytes=63 << 20
        ),
        name="middle",
    )(context_t, tokens, gain, grad_full, *weights)


def last_kernel(ins, outs, scratch):
    (counts, inverse_ref, dq_ref, dkv_ref, n_ref, joined_ref, tok_ref, gain_ref, gres_ref, e_ref, ctx_ref,
     gain_mlp_ref, *mlp) = ins
    (in_grad, gains_out, gate_out, up_out, down_out, q_out, kv_out, o_out) = outs
    (full, ctx, d_lin, acc_a, acc_b, own, x_in, y_in, rel_in, cross_in, cross_out, kept, come,
     gains, gains_in, cos_ref, sin_ref, joined, *rest) = scratch
    bufs_mlp = [rest[5 * i : 5 * i + 5] for i in range(3)]
    rest = rest[15:]
    bufs_attn = [rest[8 * i : 8 * i + 8] for i in range(3)]
    rest = rest[24:]
    sum_bufs, (ss, rs, lsem) = rest[:8], rest[8:]
    place = Place()
    copies = Copies(ss, rs)
    block, width = tok_ref.shape
    two = 2 * block
    q_cols = dq_ref.shape[0]
    kv_cols = own.shape[1] // 2
    half_width = HEAD_WIDTH // 2

    load_e = pltpu.make_async_copy(e_ref, full, lsem.at[0])
    load_e.start()
    load_joined = pltpu.make_async_copy(joined_ref, joined, lsem.at[11])
    load_joined.start()
    order = (4, 12, 0, 8)
    own_loads = [
        pltpu.make_async_copy(dkv_ref.at[at], own.at[i], lsem.at[1 + i]) for i, at in enumerate(order)
    ]
    y_loads = [
        pltpu.make_async_copy(dkv_ref.at[at + 2], y_in.at[i], lsem.at[5 + i])
        for i, at in enumerate(order)
    ]
    for copy in own_loads:
        copy.start()

    @pl.when(place.corner)
    def _():
        for copy in y_loads:
            copy.start()

    def load_mlp(i):
        return [
            pltpu.make_async_copy(mlp[2 * i], kept, lsem.at[9]),
            pltpu.make_async_copy(mlp[2 * i + 1], come, lsem.at[10]),
        ]

    loads = load_mlp(0)
    for copy in loads:
        copy.start()
    gains[0, 0:1, :] = gain_mlp_ref[...]
    gains[0, 1:2, :] = jnp.zeros_like(gain_mlp_ref)
    meet((place.beside, place.near, place.far, place.cross, place.over_x, place.over_y))

    back_rel = [copies.make(dkv_ref.at[at + 3], rel_in.at[i], place.over_x) for i, at in enumerate(order)]
    back_x = [copies.make(dkv_ref.at[at + 1], x_in.at[i], place.over_x) for i, at in enumerate(order)]
    back_y = [copies.make(dkv_ref.at[at + 2], y_in.at[i], place.over_y) for i, at in enumerate(order)]
    back_sum = [copies.make(y_in.at[i], y_in.at[i], place.over_y) for i in range(4)]
    crossing = [copies.make(cross_out.at[i], cross_in.at[i], place.cross) for i in range(2)]
    def start_back(i):
        pl.when(place.turn)(back_rel[i].start)
        pl.when(place.x == 1)(back_x[i].start)
        pl.when(place.turn)(back_y[i].start)

    start_back(0)
    start_back(1)

    def corner_sum(i):
        @pl.when(place.corner)
        def _():
            back_rel[i].wait_recv()
            y_loads[i].wait()
            y_in[i] = (y_in[i].astype(floats) + rel_in[i].astype(floats)).astype(halves)
            back_sum[i].start()

    def home_sum(i, put):
        own_loads[i].wait()
        acc_b[...] = own[i].astype(floats)

        @pl.when(place.x == 0)
        def _():
            back_x[i].wait_recv()
            acc_b[...] += x_in[i].astype(floats)

        @pl.when((place.y == 0) & (place.x == 0))
        def _():
            back_y[i].wait_recv()
            acc_b[...] += y_in[i].astype(floats)

        @pl.when((place.y == 0) & (place.x == 1))
        def _():
            back_sum[i].wait_recv()
            acc_b[...] += y_in[i].astype(floats)

        put()

    sums = []
    for i, x_first in enumerate((True, False, True)):
        sums.append(PlaneSum(copies, place, x_first, bufs_mlp[i]))
    for i in range(3):
        for copy in loads:
            copy.wait()
        sums[i].cross_second(kept, come)
        if i < 2:
            loads = load_mlp(i + 1)
            for copy in loads:
                copy.start()
        if i == 1:
            corner_sum(0)
            start_back(2)
            start_back(3)
    ctx[...] = ctx_ref[...].T
    rope_tables(counts, inverse_ref, cos_ref, sin_ref)

    attn_sums = []
    for i, x_first in enumerate((False, True, False)):
        sent, keep, got = bufs_attn[i][:3]
        attn_sums.append(PlaneSum(copies, place, x_first, bufs_attn[i][3:], sent, got))

    def attn_grad(i, left, right):
        sent, keep, got = bufs_attn[i][:3]
        outer_blocks(place, attn_sums[i].x_first, left, right, sent, keep, attn_sums[i].one.start)

    corner_sum(1)
    load_e.wait()
    attn_grad(0, full, ctx[...])
    load_n = pltpu.make_async_copy(n_ref, full, lsem.at[0])
    load_n.start()

    def cross_back(i):
        def put():
            cross_out[i] = acc_b[...].astype(halves)
            crossing[i].start()

        home_sum(i, put)

    def unturn(value, at, first_row):
        low, high = value[:half_width], value[half_width:]
        cosine, sine = cos_ref[:, at], sin_ref[:, at]
        turned = jnp.concatenate([low * cosine + high * sine, high * cosine - low * sine], axis=0)
        d_lin[first_row : first_row + HEAD_WIDTH, at] = turned.astype(halves)

    cross_back(0)
    corner_sum(2)
    everything = slice(0, 2 * two)
    for head in range(q_cols // HEAD_WIDTH):
        unturn(dq_ref[head * HEAD_WIDTH : (head + 1) * HEAD_WIDTH, :], everything, head * HEAD_WIDTH)
    cross_back(1)
    corner_sum(3)
    load_n.wait()
    attn_grad(1, full, d_lin[:q_cols, :].T)
    for plane in sums:
        plane.go_home()

    def second(i):
        sent, keep, got = bufs_attn[i][:3]
        attn_sums[i].cross_second(keep, got)

    second(0)

    def keep_a(k):
        def put():
            acc_a[:, k * two : (k + 1) * two] = acc_b[...]

        home_sum(2 + k, put)

    keep_a(0)
    keep_a(1)
    second(1)
    attn_sums[0].go_home()
    for k in range(2):
        crossing[k].wait_recv()
        lanes = slice(k * two, (k + 1) * two)
        total = acc_a[:, lanes] + cross_in[k].astype(floats)
        for head in range(kv_cols // HEAD_WIDTH):
            rows = slice(head * HEAD_WIDTH, (head + 1) * HEAD_WIDTH)
            unturn(total[rows], lanes, q_cols + head * HEAD_WIDTH)
        d_lin[q_cols + kv_cols :, lanes] = total[kv_cols:].astype(halves)

    group_sum = GroupSum(copies, sum_bufs, place)
    load_joined.wait()

    def back_norm(k, put):
        rows = slice(k * two, (k + 1) * two)
        left = d_lin[:, rows].T

        def one(cols):
            value = dot_nt(left, joined[cols, :])
            put(cols, value)
            gains[0, 1:2, cols] += jnp.sum(value * full[rows, cols].astype(floats), axis=0, keepdims=True)

        tiles(width, 256, one)

    group_sum.run(back_norm)
    gains[0, 1:2, :] = gains[0, 1:2, :] / gain_ref[...]
    attn_grad(2, full, d_lin[q_cols:, :].T)
    attn_sums[1].go_home()
    for stage, device in enumerate((place.beside, place.over_x, place.over_y, place.near, place.far)):
        copy = copies.make(gains.at[stage], gains_in.at[stage], device)
        copy.start()
        copy.wait()
        if stage < 4:
            gains[stage + 1] = gains[stage] + gains_in[stage]
        else:
            gains_out[...] = gains[stage] + gains_in[stage]
        if stage == 2:
            second(2)
    for plane, out in zip(sums, (down_out, gate_out, up_out)):
        plane.finish(out)
    attn_sums[2].go_home()
    chunk = block // CHUNKS
    for k in range(CHUNKS):
        at = pl.ds(k * chunk, chunk)
        back = group_sum.take(k)
        tok = tok_ref[at, :].astype(floats)
        root = lax.rsqrt(jnp.mean(tok * tok, axis=-1, keepdims=True) + eps_norm)
        weighted = back * gain_ref[...]
        slope = jnp.mean(weighted * tok, axis=-1, keepdims=True)
        in_grad[at, :] = gres_ref[at, :] + root * weighted - tok * (root * root * root * slope)
    for plane, out in zip(attn_sums, (o_out, q_out, kv_out)):
        plane.finish(out)
    group_sum.finish()
    for i in range(4):
        pl.when(place.turn)(back_rel[i].wait_send)
        pl.when(place.x == 1)(back_x[i].wait_send)
        pl.when(place.turn)(back_y[i].wait_send)
        pl.when(place.corner)(back_sum[i].wait_send)
    for copy in crossing:
        copy.wait_send()


def last_part(counts, inverse, d_query_t, d_kv, normed, joined, tokens, gain, gres, e_full, context_t, gain_mlp, mlp):
    block, width = tokens.shape
    group = 4 * block
    q_cols, kv_all = d_query_t.shape[0], d_kv.shape[1]
    kv_cols = kv_all // 2
    hidden = mlp[0].shape[2]
    per = width // 8
    shape = jax.ShapeDtypeStruct
    out_shape = (
        shape((block, width), floats),
        shape((2, width), floats),
        *[shape((per, hidden), floats)] * 3,
        shape((per, q_cols), floats),
        shape((per, kv_all), floats),
        shape((per, q_cols), floats),
    )
    piece = (kv_all, 2 * block)
    scratch = [
        pltpu.VMEM((group, width), halves),
        pltpu.VMEM((group, q_cols), halves),
        pltpu.VMEM((joined.shape[1], group), halves),
        pltpu.VMEM((kv_all, group), floats),
        pltpu.VMEM(piece, floats),
        *[pltpu.VMEM((4,) + piece, halves)] * 4,
        *[pltpu.VMEM((2,) + piece, halves)] * 2,
        *[pltpu.VMEM((2, width // 4, hidden), halves)] * 2,
        *[pltpu.VMEM((5, 2, width), floats)] * 2,
        *[pltpu.VMEM((HEAD_WIDTH // 2, group), floats)] * 2,
        pltpu.VMEM(joined.shape, halves),
    ]
    for _ in range(3):
        scratch += plane_buffers(width // 4, hidden)
    for cols in (q_cols, q_cols, kv_all):
        scratch += [pltpu.VMEM((2, width // 4, cols), halves)] * 3 + plane_buffers(width // 4, cols)
    scratch += [
        *[pltpu.VMEM((block, width), floats)] * 2,
        *[pltpu.VMEM((block, width), halves)] * 6,
        *copy_semaphores(),
        pltpu.SemaphoreType.DMA((12,)),
    ]

    def kernel(*refs):
        last_kernel(refs[:18], refs[18:26], refs[26:])

    return pl.pallas_call(
        kernel,
        out_shape=out_shape,
        in_specs=[SM, VM, VM, HM, HM, HM, VM, VM, VM, HM, VM, VM] + [HM] * 6,
        out_specs=(VM,) * 8,
        scratch_shapes=scratch,
        compiler_params=pltpu.CompilerParams(
            collective_id=3, has_side_effects=True, vmem_limit_bytes=63 << 20
        ),
        name="last",
    )(counts, inverse, d_query_t, d_kv, normed, joined, tokens, gain, gres, e_full, context_t, gain_mlp, *mlp)


def finish_kernel(*refs):
    base, near, kv_sum, *ready = refs[:9]
    output, k_out, v_out, *outs = refs[9:18]
    out_buf, k_buf, v_buf, sem = refs[18:]
    copies = [pltpu.make_async_copy(src, dst, sem.at[i]) for i, (src, dst) in enumerate(zip(ready, outs))]
    for copy in copies:
        copy.start()
    out_buf[...] = (base[...] + near[...].astype(floats)).astype(halves)
    kv_cols = k_buf.shape[1]
    k_buf[...] = kv_sum[:, :kv_cols]
    v_buf[...] = kv_sum[:, kv_cols:]
    more = [
        pltpu.make_async_copy(src, dst, sem.at[len(copies) + i])
        for i, (src, dst) in enumerate(((out_buf, output), (k_buf, k_out), (v_buf, v_out)))
    ]
    for copy in more:
        copy.start()
    for copy in copies + more:
        copy.wait()


def finish(base, near, kv_sum, *ready):
    shape = jax.ShapeDtypeStruct
    rows, cols = kv_sum.shape
    small = (rows, cols // 2)
    return pl.pallas_call(
        finish_kernel,
        out_shape=(
            shape(base.shape, halves),
            shape(small, floats),
            shape(small, floats),
            *[shape(a.shape, a.dtype) for a in ready],
        ),
        in_specs=[VM] * (3 + len(ready)),
        out_specs=(HM,) * (3 + len(ready)),
        scratch_shapes=[
            pltpu.VMEM(base.shape, halves),
            pltpu.VMEM(small, floats),
            pltpu.VMEM(small, floats),
            pltpu.SemaphoreType.DMA((3 + len(ready),)),
        ],
        compiler_params=pltpu.CompilerParams(vmem_limit_bytes=63 << 20),
        name="finish",
    )(base, near, kv_sum, *ready)


def routes(target):
    pairs = []
    for index in range(32):
        dp, z = divmod(index, 4)
        there = target(dp // 4, dp // 2 % 2, dp % 2, z)
        if there is not None:
            y, x, c, z = there
            pairs.append((index, (y * 4 + x * 2 + c) * 4 + z))
    return pairs


ROUTES = {
    "core": routes(lambda y, x, c, z: (y, x, 1 - c, z)),
    "x": routes(lambda y, x, c, z: (y, 1 - x, c, z)),
    "y": routes(lambda y, x, c, z: (1 - y, x, c, z)),
    "near": routes(lambda y, x, c, z: (y, x, c, z ^ 1)),
    "far": routes(lambda y, x, c, z: (y, x, c, z ^ 2)),
    "cross": routes(lambda y, x, c, z: (y, x, 1 - c, z ^ 2)),
    "odd_far": routes(lambda y, x, c, z: (y, x, c, z ^ 2) if c else None),
    "odd_x": routes(lambda y, x, c, z: (y, 1 - x, c, z) if c else None),
    "odd_y": routes(lambda y, x, c, z: (1 - y, x, c, z) if c else None),
    "odd_xy": routes(lambda y, x, c, z: (1 - y, 1 - x, c, z) if c else None),
    "home": routes(lambda y, x, c, z: (y, x, 0, z ^ 2) if c else (y, x, 1, z)),
    "x_up": routes(lambda y, x, c, z: None if x else (y, 1, c, z)),
    "y_up": routes(lambda y, x, c, z: None if y else (1, x, c, z)),
    "x_down": routes(lambda y, x, c, z: (y, 0, c, z) if x else None),
    "y_down": routes(lambda y, x, c, z: (0, x, c, z) if y else None),
    "relay": routes(lambda y, x, c, z: (1, 0, c, z) if x and y else None),
    "unrelay": routes(lambda y, x, c, z: (1, 1, c, z) if y and not x else None),
}


def send(block, way):
    return lax.ppermute(block, ("dp", "tp"), ROUTES[way])


def local_regrouped(
    tokens,
    out_grad,
    segment_ids,
    attn_gain,
    query_weight,
    key_matrix,
    value_matrix,
    output_weight,
    mlp_gain,
    gate_weight,
    up_weight,
    down_weight,
):
    block = tokens.shape[0]
    dp = lax.axis_index("dp")
    half_width = HEAD_WIDTH // 2
    gain_attn, gain_mlp = attn_gain.astype(floats)[None, :], mlp_gain.astype(floats)[None, :]
    counts = jnp.sum(
        (segment_ids[None, :] < jnp.arange(1, 4, dtype=jnp.int32)[:, None]).astype(jnp.int32), axis=1
    )
    inverse = 1.0 / rope_base ** (jnp.arange(half_width, dtype=floats) * 2.0 / HEAD_WIDTH)
    inverse = inverse[:, None]
    q_t, pieces, normed_full, grad_full, joined, weight_o, weight_d, slice_g, slice_u = first_part(
        counts, inverse, tokens, out_grad, gain_attn,
        (query_weight, key_matrix.T, value_matrix.T),
        (output_weight, down_weight, gate_weight, up_weight),
    )
    slices = [send(part, "odd_far") for part in (slice_g, slice_u)]
    context_t, log_total = attend_forward(counts, q_t, pieces)
    (
        out_base, grad_residual, attn_grad_full, out_near, down_keep, down_come, gate_keep, gate_send,
        up_keep, up_send, d_context_t, delta, mlp_gain_part,
    ) = middle(
        context_t, tokens, gain_mlp, grad_full,
        (output_weight, down_weight, gate_weight, up_weight, weight_o, weight_d, *slices),
    )
    gate_come = send(gate_send, "y")
    up_come = send(up_send, "x")
    out_near = send(out_near, "near")
    d_query_t, d_pieces = attend_backward(counts, q_t, d_context_t, log_total, delta, pieces)
    input_grad, gains, gate_sum, up_sum, down_sum, query_sum, kv_sum, output_sum = last_part(
        counts, inverse, d_query_t, d_pieces, normed_full, joined, tokens, gain_attn,
        grad_residual, attn_grad_full, context_t, mlp_gain_part,
        (down_keep, down_come, gate_keep, gate_come, up_keep, up_come),
    )
    per = gains.shape[1] // 8
    gains = lax.dynamic_slice_in_dim(gains, dp * per, per, axis=1)
    output, key_sum, value_sum, input_grad, query_sum, output_sum, gate_sum, up_sum, down_sum = finish(
        out_base, out_near, kv_sum, input_grad, query_sum, output_sum, gate_sum, up_sum, down_sum
    )
    return (
        output,
        input_grad,
        gains[1],
        query_sum,
        key_sum,
        value_sum,
        output_sum.T,
        gains[0],
        gate_sum,
        up_sum,
        down_sum.T,
    )


def solution(mesh):
    regroup = mesh.shape["dp"] == 8 and mesh.shape["tp"] == 4
    chosen = local_regrouped if regroup else local
    return jax.shard_map(
        chosen,
        mesh=mesh,
        in_specs=(
            P(("dp", "tp"), None),
            P(("dp", "tp"), None),
            P(),
            P(),
            P(None, "tp"),
            P(None, "tp"),
            P(None, "tp"),
            P("tp", None),
            P(),
            P(None, "tp"),
            P(None, "tp"),
            P("tp", None),
        ),
        out_specs=(
            P(("dp", "tp"), None),
            P(("dp", "tp"), None),
            P("dp"),
            P("dp", "tp"),
            P("dp", "tp"),
            P("dp", "tp"),
            P("tp", "dp"),
            P("dp"),
            P("dp", "tp"),
            P("dp", "tp"),
            P("tp", "dp"),
        ),
        check_vma=False,
    )
```

```python
import functools

import jax
import jax.numpy as jnp
from jax import lax
from jax.experimental import pallas as pl
from jax.experimental.pallas import tpu as pltpu
from jax.sharding import PartitionSpec as P

HEAD_WIDTH = 96
BLK = 256
LOG2E = 1.4426950408889634
SCORE = LOG2E * HEAD_WIDTH ** (-0.5)
VSCALE = 2.0 ** -9
FAR_BASE = 1 << 24
floats = jnp.float32
halves = jnp.bfloat16


def dot_nn(a, b):
    return jnp.dot(a, b, preferred_element_type=floats)


def dot_nt(a, b):
    return lax.dot_general(a, b, (((1,), (1,)), ((), ())), preferred_element_type=floats)


def token_base(j, core, pair, side):
    return ((2 * j + core) * 4 + 2 * pair + side) * BLK


def group_bases():
    dp, z = lax.axis_index("dp"), lax.axis_index("tp")
    j, c, pair, side = dp // 2, lax.rem(dp, 2), z // 2, lax.rem(z, 2)
    return [
        token_base(j, core, pair, at) for at in (side, 1 - side) for core in (c, 1 - c)
    ]


def item_start(counts_ref, token):
    start = jnp.zeros_like(token)
    for i in range(3):
        start = jnp.where(token >= counts_ref[i], counts_ref[i], start)
    return start


def group_index():
    lanes = lax.broadcasted_iota(jnp.int32, (1, BLK), 1)
    return jnp.concatenate([lanes + base for base in group_bases()], axis=1)


def fill_places(counts_ref, sc, tok_ref, start_ref):
    dp, z = lax.axis_index("dp"), lax.axis_index("tp")
    j, c, pair, side = dp // 2, lax.rem(dp, 2), z // 2, lax.rem(z, 2)
    x, y = lax.rem(j, 2), j // 2
    kb = 0
    for side_of in (side, 1 - side):
        for cores, pair_of in (((c, 1 - c), pair), ((1 - c, c), 1 - pair)):
            for j_of, present in ((j, None), (j - 1, x), (j - 2, y), (j - 1, y * (1 - x))):
                for core in cores:
                    base = token_base(j_of, core, pair_of, side_of)
                    sc[0, kb] = base if present is None else jnp.where(present == 1, base, FAR_BASE)
                    kb += 1
    for qb, base in enumerate(group_bases()):
        sc[1, qb] = base
        sc[2, qb] = item_start(counts_ref, base)
        sc[3, qb] = item_start(counts_ref, base + (BLK - 1))
    index = group_index()
    tok_ref[...] = index
    start_ref[...] = item_start(counts_ref, index)


def pair_state(sc, kb, qb):
    key_base = sc[0, kb]
    q_base, least, most = sc[1, qb], sc[2, qb], sc[3, qb]
    needed = (key_base <= q_base + (BLK - 1)) & (key_base + (BLK - 1) >= least)
    whole = (key_base + (BLK - 1) <= q_base) & (key_base >= most)
    return key_base, needed, whole


def allowed_mask(key_base, tok_ref, start_ref, lanes):
    keys = key_base + lax.broadcasted_iota(jnp.int32, (BLK, BLK), 0)
    return (keys <= tok_ref[0:1, lanes]) & (keys >= start_ref[0:1, lanes])


def fwd_kernel(n, width, counts, q_ref, pieces, *refs):
    out_acc, out_sum = refs[:2]
    kv, keys_nat, acc, total, q_wide, sc, tok_ref, start_ref, sem = refs[2:]
    per = width // BLK
    for i in range(n):
        pltpu.make_async_copy(pieces.at[i], kv.at[i], sem.at[i]).start()
    acc[...] = jnp.zeros_like(acc)
    total[...] = jnp.zeros_like(total)
    fill_places(counts, sc, tok_ref, start_ref)
    for i in range(n):
        pltpu.make_async_copy(pieces.at[i], kv.at[i], sem.at[i]).wait()
    heads_kv = pieces.shape[1] // (2 * HEAD_WIDTH)
    group = q_ref.shape[0] // (heads_kv * HEAD_WIDTH)
    v_off = heads_kv * HEAD_WIDTH
    places = [
        (h, slice((h * group + g) * HEAD_WIDTH, (h * group + g + 1) * HEAD_WIDTH), slice(qb * BLK, (qb + 1) * BLK),
         slice(h * HEAD_WIDTH, (h + 1) * HEAD_WIDTH), slice((qb * group + g) * BLK, (qb * group + g + 1) * BLK), h * group + g)
        for h in range(heads_kv) for g in range(group) for qb in range(q_ref.shape[1] // BLK)
    ]
    for h, rows, lanes, wrows, wlanes, hd in places:
        q_wide[wrows, wlanes] = q_ref[rows, lanes]

    def key_block(kb, carry):
        piece = kb // per
        klanes = pl.ds(pl.multiple_of((kb % per) * BLK, BLK), BLK)
        for h in range(heads_kv):
            keys_nat[h] = kv[piece, h * HEAD_WIDTH : (h + 1) * HEAD_WIDTH, klanes].T

        def query_block(qb, carry):
            key_base, needed, whole = pair_state(sc, kb, qb)
            lanes = pl.ds(pl.multiple_of(qb * BLK, BLK), BLK)

            def unit(masked):
                wide = pl.ds(pl.multiple_of(qb * (group * BLK), group * BLK), group * BLK)
                if masked:
                    allowed = allowed_mask(key_base, tok_ref, start_ref, lanes)
                    allowed = jnp.concatenate([allowed] * group, axis=1)
                scores = [
                    dot_nn(keys_nat[h], q_wide[h * HEAD_WIDTH : (h + 1) * HEAD_WIDTH, wide])
                    for h in range(heads_kv)
                ]
                weights = [jnp.exp2(s * SCORE) for s in scores]
                if masked:
                    weights = [jnp.where(allowed, w, 0.0) for w in weights]
                sums = [jnp.sum(w, axis=0, keepdims=True) for w in weights]
                parts = [
                    dot_nn(
                        kv[piece, v_off + h * HEAD_WIDTH : v_off + (h + 1) * HEAD_WIDTH, klanes],
                        weights[h].astype(halves),
                    )
                    for h in range(heads_kv)
                ]
                for h in range(heads_kv):
                    total[h : h + 1, wide] += sums[h]
                    acc[h * HEAD_WIDTH : (h + 1) * HEAD_WIDTH, wide] += parts[h]

            pl.when(needed & whole)(lambda: unit(False))
            pl.when(needed & jnp.logical_not(whole))(lambda: unit(True))
            return carry

        return lax.fori_loop(0, q_ref.shape[1] // BLK, query_block, carry)

    lax.fori_loop(0, n * per, key_block, 0)
    for h, rows, lanes, wrows, wlanes, hd in places:
        row = total[h : h + 1, wlanes]
        out_acc[rows, lanes] = (acc[wrows, wlanes] * ((1.0 / VSCALE) / row)).astype(halves)
        out_sum[hd : hd + 1, lanes] = jnp.log2(row)


VM = pl.BlockSpec(memory_space=pltpu.VMEM)
SM = pl.BlockSpec(memory_space=pltpu.SMEM)
HB = pl.BlockSpec(memory_space=pl.ANY)
HM = pl.BlockSpec(memory_space=pltpu.HBM)


def place_scratch(blocks, tokens):
    return [
        pltpu.SMEM((4, blocks), jnp.int32),
        pltpu.VMEM((1, tokens), jnp.int32),
        pltpu.VMEM((1, tokens), jnp.int32),
    ]


def attend_forward(counts, q_t, pieces):
    n, width = pieces.shape[0], pieces.shape[2]
    heads = q_t.shape[0] // HEAD_WIDTH
    heads_kv = pieces.shape[1] // (2 * HEAD_WIDTH)
    tokens = q_t.shape[1]
    wide = tokens * heads // heads_kv
    return pl.pallas_call(
        functools.partial(fwd_kernel, n, width),
        out_shape=(
            jax.ShapeDtypeStruct(q_t.shape, halves),
            jax.ShapeDtypeStruct((heads, tokens), floats),
        ),
        in_specs=[SM, VM, HM],
        out_specs=(VM, VM),
        scratch_shapes=[
            pltpu.VMEM(pieces.shape, halves),
            pltpu.VMEM((heads_kv, BLK, HEAD_WIDTH), halves),
            pltpu.VMEM((heads_kv * HEAD_WIDTH, wide), floats),
            pltpu.VMEM((heads_kv, wide), floats),
            pltpu.VMEM((heads_kv * HEAD_WIDTH, wide), halves),
            *place_scratch(n * width // BLK, tokens),
            pltpu.SemaphoreType.DMA((n,)),
        ],
        compiler_params=pltpu.CompilerParams(vmem_limit_bytes=63 << 20),
        name="attend_forward",
    )(counts, q_t, pieces)


def bwd_kernel(n, width, counts, q_ref, do_ref, log_ref, delta_ref, pieces, *refs):
    dq_out = refs[0]
    dkv_out = refs[1]
    kv, dkv, keys_nat, vals_nat, acc, q_wide, do_wide, log_wide, delta_wide, dq_wide, sc, tok_ref, start_ref, sem, osem = refs[2:]
    per = width // BLK
    for i in range(n):
        pltpu.make_async_copy(pieces.at[i], kv.at[i], sem.at[i]).start()
    fill_places(counts, sc, tok_ref, start_ref)
    for i in range(n):
        pltpu.make_async_copy(pieces.at[i], kv.at[i], sem.at[i]).wait()
    heads_kv = pieces.shape[1] // (2 * HEAD_WIDTH)
    group = q_ref.shape[0] // (heads_kv * HEAD_WIDTH)
    v_off = heads_kv * HEAD_WIDTH
    places = [
        (h, slice((h * group + g) * HEAD_WIDTH, (h * group + g + 1) * HEAD_WIDTH), slice(qb * BLK, (qb + 1) * BLK),
         slice(h * HEAD_WIDTH, (h + 1) * HEAD_WIDTH), slice((qb * group + g) * BLK, (qb * group + g + 1) * BLK), h * group + g)
        for h in range(heads_kv) for g in range(group) for qb in range(q_ref.shape[1] // BLK)
    ]
    for h, rows, lanes, wrows, wlanes, hd in places:
        q_wide[wrows, wlanes] = q_ref[rows, lanes]
        do_wide[wrows, wlanes] = do_ref[rows, lanes]
        log_wide[h : h + 1, wlanes] = log_ref[hd : hd + 1, lanes]
        delta_wide[h : h + 1, wlanes] = delta_ref[hd : hd + 1, lanes]
        dq_wide[wrows, wlanes] = jnp.zeros((HEAD_WIDTH, BLK), floats)
    out_scale = (1.0 / VSCALE) * HEAD_WIDTH ** (-0.5)

    def key_block(kb, carry):
        piece = kb // per
        klanes = pl.ds(pl.multiple_of((kb % per) * BLK, BLK), BLK)
        for h in range(heads_kv):
            keys_nat[h] = kv[piece, h * HEAD_WIDTH : (h + 1) * HEAD_WIDTH, klanes].T
            vals_nat[h] = kv[piece, v_off + h * HEAD_WIDTH : v_off + (h + 1) * HEAD_WIDTH, klanes].T
        acc[...] = jnp.zeros_like(acc)

        def query_block(qb, carry):
            key_base, needed, whole = pair_state(sc, kb, qb)
            lanes = pl.ds(pl.multiple_of(qb * BLK, BLK), BLK)

            def unit(masked):
                wide = pl.ds(pl.multiple_of(qb * (group * BLK), group * BLK), group * BLK)
                if masked:
                    allowed = allowed_mask(key_base, tok_ref, start_ref, lanes)
                    allowed = jnp.concatenate([allowed] * group, axis=1)
                heads = range(heads_kv)
                krows = [slice(h * HEAD_WIDTH, (h + 1) * HEAD_WIDTH) for h in heads]
                vrows = [slice(v_off + h * HEAD_WIDTH, v_off + (h + 1) * HEAD_WIDTH) for h in heads]
                qt = [q_wide[krows[h], wide] for h in heads]
                dot = [do_wide[krows[h], wide] for h in heads]
                scores = [dot_nn(keys_nat[h], qt[h]) for h in heads]
                dprobs = [dot_nn(vals_nat[h], dot[h]) for h in heads]
                weights = [
                    jnp.exp2(scores[h] * SCORE - log_wide[h : h + 1, wide]) for h in heads
                ]
                if masked:
                    weights = [jnp.where(allowed, w, 0.0) for w in weights]
                ds = [
                    (weights[h] * (dprobs[h] - delta_wide[h : h + 1, wide])).astype(halves)
                    for h in heads
                ]
                dv = [dot_nt(dot[h], weights[h].astype(halves)) for h in heads]
                dk = [dot_nt(qt[h], ds[h]) for h in heads]
                dq = [dot_nn(kv[piece, krows[h], klanes], ds[h]) for h in heads]
                for h in heads:
                    acc[vrows[h], :] += dv[h]
                    acc[krows[h], :] += dk[h]
                    dq_wide[krows[h], wide] += dq[h]

            pl.when(needed & whole)(lambda: unit(False))
            pl.when(needed & jnp.logical_not(whole))(lambda: unit(True))
            return carry

        carry = lax.fori_loop(0, q_ref.shape[1] // BLK, query_block, carry)
        dkv[piece, 0:v_off, klanes] = (acc[0:v_off, :] * out_scale).astype(halves)
        dkv[piece, v_off:, klanes] = acc[v_off:, :].astype(halves)
        return carry

    lax.fori_loop(0, n * per, key_block, 0)
    for i in range(n):
        pltpu.make_async_copy(dkv.at[i], dkv_out.at[i], osem.at[i]).start()
    for h, rows, lanes, wrows, wlanes, hd in places:
        dq_out[rows, lanes] = dq_wide[wrows, wlanes] * out_scale
    for i in range(n):
        pltpu.make_async_copy(dkv.at[i], dkv_out.at[i], osem.at[i]).wait()


def attend_backward(counts, q_t, do_t, log_total, delta, pieces):
    n, width = pieces.shape[0], pieces.shape[2]
    heads_kv = pieces.shape[1] // (2 * HEAD_WIDTH)
    wide = q_t.shape[0] // (heads_kv * HEAD_WIDTH) * q_t.shape[1]
    outs = pl.pallas_call(
        functools.partial(bwd_kernel, n, width),
        out_shape=(
            jax.ShapeDtypeStruct(q_t.shape, floats),
            jax.ShapeDtypeStruct(pieces.shape, halves),
        ),
        in_specs=[SM] + [VM] * 4 + [HM],
        out_specs=(VM, HM),
        scratch_shapes=[
            pltpu.VMEM(pieces.shape, halves),
            pltpu.VMEM(pieces.shape, halves),
            pltpu.VMEM((heads_kv, BLK, HEAD_WIDTH), halves),
            pltpu.VMEM((heads_kv, BLK, HEAD_WIDTH), halves),
            pltpu.VMEM((pieces.shape[1], BLK), floats),
            pltpu.VMEM((heads_kv * HEAD_WIDTH, wide), halves),
            pltpu.VMEM((heads_kv * HEAD_WIDTH, wide), halves),
            pltpu.VMEM((heads_kv, wide), floats),
            pltpu.VMEM((heads_kv, wide), floats),
            pltpu.VMEM((heads_kv * HEAD_WIDTH, wide), floats),
            *place_scratch(n * width // BLK, q_t.shape[1]),
            pltpu.SemaphoreType.DMA((n,)),
            pltpu.SemaphoreType.DMA((n,)),
        ],
        compiler_params=pltpu.CompilerParams(vmem_limit_bytes=63 << 20),
        name="attend_backward",
    )(counts, q_t, do_t, log_total, delta, pieces)
    return outs


eps_norm = 1e-05
rope_base = 100000.0
reach_limit = 8


def shifted(block, axis, distance):
    devices = range(lax.axis_size(axis))
    route = [(i - distance, i) for i in devices if i - distance in devices]
    return lax.ppermute(block, axis, route)


def rms_scale(value_vectors, gain_vec):
    return (
        value_vectors
        * lax.rsqrt(jnp.mean(value_vectors * value_vectors, axis=-1, keepdims=True) + eps_norm)
        * gain_vec
    )


def rotary_turn(value_vectors, token_positions, heads):
    half_width = HEAD_WIDTH // 2
    inverse = 1.0 / rope_base ** (jnp.arange(half_width, dtype=jnp.float32) * 2.0 / HEAD_WIDTH)
    angles = token_positions.astype(jnp.float32)[:, None] * inverse[None, :]
    cosine = jnp.cos(angles)[:, None, :]
    sine_part = jnp.sin(angles)[:, None, :]
    shaped = value_vectors.reshape(value_vectors.shape[0], heads, HEAD_WIDTH)
    first_half = shaped[..., :half_width]
    second = shaped[..., half_width:]
    turned = jnp.concatenate(
        [first_half * cosine - second * sine_part, second * cosine + first_half * sine_part],
        axis=-1,
    )
    return turned.reshape(value_vectors.shape)


def swiglu(gate_pre, up_pre):
    return jax.nn.silu(gate_pre) * up_pre


def contract_rows(left_side, right_side):
    return lax.dot_general(
        left_side, right_side, (((0,), (0,)), ((), ())), preferred_element_type=jnp.float32
    )


def contract_cols(left_side, right_side):
    return lax.dot_general(
        left_side, right_side, (((1,), (1,)), ((), ())), preferred_element_type=jnp.float32
    )


def local(
    tokens,
    out_grad,
    segment_ids,
    attn_gain,
    query_weight,
    key_matrix,
    value_matrix,
    output_weight,
    mlp_gain,
    gate_weight,
    up_weight,
    down_weight,
):
    floats = jnp.float32
    halves = jnp.bfloat16
    shard_rows = tokens.shape[0]
    row_len = shard_rows * lax.axis_size("tp")
    row_index = lax.axis_index("dp")
    reach = min(reach_limit, lax.axis_size("dp") // 2)
    heads_q = query_weight.shape[1] // HEAD_WIDTH
    heads_kv = key_matrix.shape[1] // HEAD_WIDTH
    group_width = heads_q // heads_kv
    q_cols = heads_q * HEAD_WIDTH
    kv_cols = heads_kv * HEAD_WIDTH
    score_scale = HEAD_WIDTH ** (-0.5)
    row_first = row_index * row_len
    seg_row = lax.dynamic_slice_in_dim(segment_ids, row_first, row_len)
    index_row = row_first + jnp.arange(row_len, dtype=jnp.int32)
    every_index = jnp.arange(segment_ids.shape[0], dtype=jnp.int32)
    marks = (segment_ids[1:] != segment_ids[:-1]).astype(jnp.int32)
    starts = jnp.concatenate([jnp.zeros((1,), jnp.int32), marks * every_index[1:]])
    is_at = (starts[None, :] <= index_row[:, None]).astype(jnp.int32)
    token_positions = index_row - jnp.max(is_at * starts[None, :], axis=1)
    tokens32 = tokens.astype(floats)
    gain_attn = attn_gain.astype(floats)
    gain_mlp = mlp_gain.astype(floats)
    normed = rms_scale(tokens32, gain_attn).astype(halves)
    normed_full = lax.all_gather(normed, "tp", axis=0, tiled=True)
    joined = jnp.concatenate([query_weight, key_matrix, value_matrix], axis=1)
    projected = jnp.dot(normed_full, joined, preferred_element_type=floats)
    q_linear = projected[:, :q_cols]
    key_linear_out = projected[:, q_cols : q_cols + kv_cols]
    query_vectors = rotary_turn(q_linear, token_positions, heads_q).astype(halves)
    key_vectors = rotary_turn(key_linear_out, token_positions, heads_kv).astype(halves)
    value_vectors = projected[:, q_cols + kv_cols :].astype(halves)
    query_heads = query_vectors.reshape(row_len, heads_kv, group_width, HEAD_WIDTH)
    held_blocks = [(key_vectors, value_vectors)]
    moving = (key_vectors, value_vectors)
    for step_hop in range(reach):
        moving = shifted((moving[0], moving[1]), "dp", 1)
        held_blocks.append(moving)

    def block_mask(step_hop):
        key_row = row_index - step_hop
        seg_keys = lax.dynamic_slice_in_dim(segment_ids, jnp.maximum(key_row, 0) * row_len, row_len)
        key_index = key_row * row_len + jnp.arange(row_len, dtype=jnp.int32)
        return (seg_keys[None, :] == seg_row[:, None]) & (key_index[None, :] <= index_row[:, None])

    def block_needed(step_hop):
        last_key = jnp.maximum((row_index - step_hop + 1) * row_len - 1, 0)
        return (row_index >= step_hop) & (segment_ids[last_key] == seg_row[0])

    block_masks = [block_mask(step_hop) for step_hop in range(reach + 1)]

    def apply_block(step_hop, update, state_in):
        key_block, value_block = held_blocks[step_hop]
        if step_hop == 0:
            return update(state_in, key_block, value_block, block_masks[0])
        return lax.cond(
            block_needed(step_hop),
            update,
            lambda state_kept, key_skip, value_skip, mask_skip: state_kept,
            state_in,
            key_block,
            value_block,
            block_masks[step_hop],
        )

    def scores(key_block, allowed):
        raw_scores = jnp.einsum(
            "qhgd,khd->hgqk",
            query_heads,
            key_block.reshape(row_len, heads_kv, HEAD_WIDTH),
            preferred_element_type=floats,
        )
        return jnp.where(allowed, raw_scores * score_scale, -jnp.inf)

    def add_online(state_in, key_block, value_block, allowed):
        run_max, run_total, run_sum = state_in
        block_scores = scores(key_block, allowed)
        new_max = jnp.maximum(run_max, jnp.max(block_scores, axis=-1))
        factor = jnp.exp(run_max - new_max)
        weights = jnp.exp(block_scores - new_max[..., None])
        run_total = run_total * factor + jnp.sum(weights, axis=-1)
        run_sum = run_sum * jnp.moveaxis(factor, 2, 0)[..., None] + jnp.einsum(
            "hgqk,khd->qhgd",
            weights.astype(halves),
            value_block.reshape(row_len, heads_kv, HEAD_WIDTH),
            preferred_element_type=floats,
        )
        return (new_max, run_total, run_sum)

    online = (
        jnp.full((heads_kv, group_width, row_len), -jnp.inf, floats),
        jnp.zeros((heads_kv, group_width, row_len), floats),
        jnp.zeros((row_len, heads_kv, group_width, HEAD_WIDTH), floats),
    )
    for step_hop in range(reach + 1):
        online = apply_block(step_hop, add_online, online)
    run_max, run_total, run_sum = online
    log_total = (run_max + jnp.log(run_total))[..., None]
    context_heads = (run_sum / jnp.moveaxis(run_total, 2, 0)[..., None]).astype(halves)
    context = context_heads.reshape(row_len, q_cols)
    residual = tokens32 + lax.psum_scatter(
        jnp.dot(context, output_weight, preferred_element_type=floats).astype(jnp.bfloat16),
        "tp",
        scatter_dimension=0,
        tiled=True,
    ).astype(jnp.float32)
    mlp_normed = rms_scale(residual, gain_mlp).astype(halves)
    mlp_full = lax.all_gather(mlp_normed, "tp", axis=0, tiled=True)
    gate_pre = jnp.dot(mlp_full, gate_weight, preferred_element_type=floats)
    up_pre = jnp.dot(mlp_full, up_weight, preferred_element_type=floats)
    hidden = swiglu(gate_pre, up_pre).astype(halves)
    output = residual + lax.psum_scatter(
        jnp.dot(hidden, down_weight, preferred_element_type=floats).astype(jnp.bfloat16),
        "tp",
        scatter_dimension=0,
        tiled=True,
    ).astype(jnp.float32)
    grad_full = lax.all_gather(out_grad, "tp", axis=0, tiled=True)
    grad_hidden = contract_cols(grad_full, down_weight)
    down_grad = contract_rows(grad_full, hidden)
    silu_back = jax.vjp(swiglu, gate_pre, up_pre)[1]
    grad_gate, grad_up = silu_back(grad_hidden)
    grad_gate = grad_gate.astype(halves)
    grad_up = grad_up.astype(halves)
    gate_grad = contract_rows(mlp_full, grad_gate)
    up_grad = contract_rows(mlp_full, grad_up)
    grad_mlp_normed = lax.psum_scatter(
        (contract_cols(grad_gate, gate_weight) + contract_cols(grad_up, up_weight)).astype(
            jnp.bfloat16
        ),
        "tp",
        scatter_dimension=0,
        tiled=True,
    ).astype(jnp.float32)
    mlp_norm_back = jax.vjp(rms_scale, residual, gain_mlp)[1]
    grad_residual_part, mlp_gain_part = mlp_norm_back(grad_mlp_normed)
    grad_residual = out_grad.astype(floats) + grad_residual_part
    attn_grad_full = lax.all_gather(grad_residual.astype(halves), "tp", axis=0, tiled=True)
    output_grad = contract_rows(attn_grad_full, context)
    grad_context = (
        contract_cols(attn_grad_full, output_weight)
        .astype(halves)
        .reshape(row_len, heads_kv, group_width, HEAD_WIDTH)
    )
    delta_col = jnp.einsum(
        "qhgd,qhgd->hgq", grad_context, context_heads, preferred_element_type=floats
    )[..., None]

    def add_grads(state_in, key_block, value_block, allowed):
        query_acc, key_acc, value_acc = state_in
        probabilities = jnp.exp(scores(key_block, allowed) - log_total)
        grad_probs = jnp.einsum(
            "qhgd,khd->hgqk",
            grad_context,
            value_block.reshape(row_len, heads_kv, HEAD_WIDTH),
            preferred_element_type=floats,
        )
        grad_scores = (probabilities * (grad_probs - delta_col)).astype(halves)
        key_heads = key_block.reshape(row_len, heads_kv, HEAD_WIDTH)
        query_acc = (
            query_acc
            + jnp.einsum("hgqk,khd->qhgd", grad_scores, key_heads, preferred_element_type=floats)
            * score_scale
        )
        key_acc = (
            key_acc
            + jnp.einsum(
                "hgqk,qhgd->khd", grad_scores, query_heads, preferred_element_type=floats
            ).reshape(row_len, kv_cols)
            * score_scale
        )
        value_acc = value_acc + jnp.einsum(
            "hgqk,qhgd->khd",
            probabilities.astype(halves),
            grad_context,
            preferred_element_type=floats,
        ).reshape(row_len, kv_cols)
        return (query_acc, key_acc, value_acc)

    query_acc = jnp.zeros((row_len, heads_kv, group_width, HEAD_WIDTH), floats)
    carried = (jnp.zeros((row_len, kv_cols), floats), jnp.zeros((row_len, kv_cols), floats))
    for step_hop in range(reach, 0, -1):
        query_acc, key_acc, value_acc = apply_block(
            step_hop, add_grads, (query_acc, carried[0], carried[1])
        )
        carried = (
            shifted(key_acc.astype(jnp.bfloat16), "dp", -1).astype(key_acc.dtype),
            shifted(value_acc.astype(jnp.bfloat16), "dp", -1).astype(value_acc.dtype),
        )
    query_acc, key_total, value_total = apply_block(
        0, add_grads, (query_acc, carried[0], carried[1])
    )
    query_back = jax.vjp(lambda linear: rotary_turn(linear, token_positions, heads_q), q_linear)[1]
    key_back = jax.vjp(
        lambda linear: rotary_turn(linear, token_positions, heads_kv), key_linear_out
    )[1]
    grad_q_linear = query_back(query_acc.reshape(row_len, q_cols))[0]
    grad_k_linear = key_back(key_total)[0]
    grads_joined = jnp.concatenate([grad_q_linear, grad_k_linear, value_total], axis=1).astype(
        halves
    )
    proj_grad = contract_rows(normed_full, grads_joined)
    grad_normed = lax.psum_scatter(
        contract_cols(grads_joined, joined).astype(jnp.bfloat16),
        "tp",
        scatter_dimension=0,
        tiled=True,
    ).astype(jnp.float32)
    attn_norm_back = jax.vjp(rms_scale, tokens32, gain_attn)[1]
    grad_tokens_part, attn_gain_part = attn_norm_back(grad_normed)
    input_grad = grad_residual + grad_tokens_part
    def scatter_rows(grad):
        return lax.psum_scatter(
            grad.astype(halves), "dp", scatter_dimension=0, tiled=True
        ).astype(floats)

    mlp_sums = scatter_rows(jnp.concatenate([gate_grad, up_grad, down_grad], axis=1))
    ff_cols = gate_weight.shape[1]
    gate_sum = mlp_sums[:, :ff_cols]
    up_sum = mlp_sums[:, ff_cols : 2 * ff_cols]
    down_sum = mlp_sums[:, 2 * ff_cols :]
    attn_sums = scatter_rows(jnp.concatenate([proj_grad, output_grad], axis=1))
    query_sum = attn_sums[:, :q_cols]
    key_sum = attn_sums[:, q_cols : q_cols + kv_cols]
    value_sum = attn_sums[:, q_cols + kv_cols : q_cols + 2 * kv_cols]
    output_sum = attn_sums[:, q_cols + 2 * kv_cols :]
    attn_gain_sum = lax.psum_scatter(attn_gain_part, "dp", scatter_dimension=0, tiled=True)
    mlp_gain_sum = lax.psum_scatter(mlp_gain_part, "dp", scatter_dimension=0, tiled=True)
    attn_gain_total, mlp_gain_total = lax.psum((attn_gain_sum, mlp_gain_sum), "tp")
    return (
        output.astype(halves),
        input_grad,
        attn_gain_total,
        query_sum,
        key_sum,
        value_sum,
        output_sum.T,
        mlp_gain_total,
        gate_sum,
        up_sum,
        down_sum.T,
    )


MESH = pl.DeviceIdType.MESH


def meet(devices):
    barrier = pltpu.get_barrier_semaphore()
    for device in devices:
        pl.semaphore_signal(barrier, inc=1, device_id=device, device_id_type=MESH)
    pl.semaphore_wait(barrier, len(devices))


def tiles(total, step, body):
    def one(i, carry):
        body(pl.ds(pl.multiple_of(i * step, step), step))
        return carry

    lax.fori_loop(0, total // step, one, 0)


CHUNKS = 4


class GroupSum:
    def __init__(self, copies, bufs, place):
        self.copies, self.bufs, self.place = copies, bufs, place

        self.far, self.sums = [], []

    def put_there(self, at, cols, value):
        part_near, _, out_far = self.bufs[:3]
        rows = value.shape[0] // 2
        part_near[at, cols] = value[:rows]
        out_far[at, cols] = value[rows:].astype(halves)

    def put_here(self, cols, value):
        _, part_own, _, out_beside = self.bufs[:4]
        rows = value.shape[0] // 2
        part_own[:, cols] = value[:rows]
        out_beside[:, cols] = value[rows:].astype(halves)

    def send_far(self, at):
        _, _, out_far, _, _, in_near = self.bufs[:6]
        copy = self.copies.make(out_far.at[at], in_near.at[at], self.place.beside)
        copy.start()
        self.far.append(copy)

    def send_beside(self):
        _, _, _, out_beside, _, _, in_own = self.bufs[:7]
        self.side = self.copies.make(out_beside, in_own, self.place.beside)
        self.side.start()

    def send_near(self, count):
        part_near, _, _, _, out_near, in_near, _, in_sum = self.bufs
        self.far[-1].wait_recv()
        rows = part_near.shape[0] // CHUNKS
        for _ in range(count):
            at = pl.ds(len(self.sums) * rows, rows)
            out_near[at, :] = (part_near[at, :] + in_near[at, :].astype(floats)).astype(halves)
            copy = self.copies.make(out_near.at[at], in_sum.at[at], self.place.near)
            copy.start()
            self.sums.append(copy)

    def run(self, product):
        everything = pl.ds(0, self.bufs[0].shape[0])
        product(1, lambda cols, value: self.put_there(everything, cols, value))
        self.send_far(everything)
        product(0, self.put_here)
        self.send_beside()
        self.send_near(CHUNKS)

    def take(self, k):
        part_near, part_own, out_far, out_beside, out_near, in_near, in_own, in_sum = self.bufs
        if k == 0:
            self.side.wait_recv()
        self.sums[k].wait_recv()
        rows = part_own.shape[0] // CHUNKS
        at = pl.ds(k * rows, rows)
        return part_own[at, :] + in_own[at, :].astype(floats) + in_sum[at, :].astype(floats)

    def finish(self):
        for copy in (*self.far, self.side, *self.sums):
            copy.wait_send()


class GroupGather:
    def __init__(self, copies, full, block, place):
        self.copies, self.full, self.block, self.place = copies, full, block, place
        self.sent = []

    def slot(self, n, k):
        rows = self.block // CHUNKS
        return self.full.at[pl.ds(n * self.block + k * rows, rows)]

    def put(self, k):
        for i, (n, device) in enumerate(((2, self.place.near), (1, self.place.beside))):
            copy = self.copies.make(self.slot(0, k), self.slot(n, k), device)
            copy.start()
            self.sent.append((i, copy))

    def wait_here(self):
        for i, copy in self.sent:
            if i == 1:
                copy.wait_recv()

    def wait_there(self, part=0, parts=1):
        near = [copy for i, copy in self.sent if i == 0]
        count = CHUNKS // parts
        relays = []
        for k in range(part * count, (part + 1) * count):
            near[k].wait_recv()
            relay = self.copies.make(self.slot(2, k), self.slot(3, k), self.place.beside)
            relay.start()
            relays.append(relay)
        for relay in relays:
            relay.wait_recv()
        self.sent += [(2, relay) for relay in relays]

    def finish(self):
        for _, copy in self.sent:
            copy.wait_send()


class Copies:
    limit = 96

    def __init__(self, send_sems, recv_sems):
        self.send_sems, self.recv_sems, self.used = send_sems, recv_sems, 0

    def make(self, src, dst, device):
        i = self.used
        self.used += 1
        return pltpu.make_async_remote_copy(
            src_ref=src,
            dst_ref=dst,
            send_sem=self.send_sems.at[i],
            recv_sem=self.recv_sems.at[i],
            device_id=device,
            device_id_type=MESH,
        )


def copy_semaphores():
    return [pltpu.SemaphoreType.DMA((Copies.limit,)), pltpu.SemaphoreType.DMA((Copies.limit,))]


class Place:
    def __init__(self):
        dp, z = lax.axis_index("dp"), lax.axis_index("tp")
        self.dp, self.z = dp, z
        self.c = lax.rem(dp, 2)
        self.x = lax.rem(dp // 2, 2)
        self.y = dp // 4
        far_z = lax.rem(z + 2, 4)
        self.beside = (dp + 1 - 2 * self.c, z)
        self.near = (dp, z + 1 - 2 * lax.rem(z, 2))
        self.far = (dp, far_z)
        self.cross = (self.beside[0], far_z)
        self.over_x = (dp + 2 - 4 * self.x, z)
        self.over_y = (dp + 4 - 8 * self.y, z)
        self.slot = 2 * self.y + self.x
        self.slot_x = 2 * self.y + 1 - self.x
        self.slot_y = 2 - 2 * self.y + self.x
        self.odd = self.c == 1
        self.corner = (self.x == 1) & (self.y == 1)
        self.turn = (self.x == 0) & (self.y == 1)


def rope_tables(counts_ref, inverse_ref, cos_ref, sin_ref):
    index = group_index()
    positions = (index - item_start(counts_ref, index)).astype(floats)
    angles = inverse_ref[...] * positions
    cos_ref[...] = jnp.cos(angles)
    sin_ref[...] = jnp.sin(angles)


class PlaneFetch:
    def __init__(self, copies, place, out, own=None, own_slice=None):
        self.place, self.out = place, out
        rows = out.shape[0] // 8

        def part(slot, ch):
            return pl.ds(slot * (2 * rows) + ch * rows, rows)

        def remote(slot, ch, device):
            at = part(slot, ch)
            return copies.make(out.at[at], out.at[at], device)

        p = place
        self.hop = None
        if own is not None:
            self.hop = [
                copies.make(own.at[part(p.slot, ch)], out.at[part(p.slot, ch)], p.far)
                for ch in range(2)
            ]
        if own_slice is not None:
            self.hop = [
                copies.make(own_slice.at[part(0, ch)], out.at[part(p.slot, ch)], p.far)
                for ch in range(2)
            ]
        self.x = [remote(p.slot, ch, p.over_x) for ch in range(2)]
        self.y = [remote(p.slot, ch, p.over_y) for ch in range(2)]
        self.relay_y = remote(p.slot_x, 0, p.over_y)
        self.relay_x = remote(p.slot_y, 1, p.over_x)

    def start(self):
        @pl.when(self.place.odd)
        def _():
            for copy in self.hop:
                copy.start()

    def forward(self):
        @pl.when(self.place.odd)
        def _():
            for ch in range(2):
                if self.hop is not None:
                    self.hop[ch].wait_recv()
                self.x[ch].start()
                self.y[ch].start()

    def relay(self):
        @pl.when(self.place.odd)
        def _():
            self.x[0].wait_recv()
            self.relay_y.start()
            self.y[1].wait_recv()
            self.relay_x.start()

    def finish(self):
        @pl.when(self.place.odd)
        def _():
            self.x[1].wait_recv()
            self.y[0].wait_recv()
            self.relay_y.wait_recv()
            self.relay_x.wait_recv()

    def drain(self):
        @pl.when(self.place.odd)
        def _():
            for copy in (self.hop or []) + self.x + self.y + [self.relay_y, self.relay_x]:
                copy.wait_send()


class Spread:
    def __init__(self, copies, place, source, slots):
        self.place = place
        self.to_x = copies.make(source, slots[1], place.over_x)
        self.to_y = copies.make(source, slots[2], place.over_y)
        self.relayed = copies.make(slots[2], slots[3], place.over_x)

    def start(self):
        pl.when(self.place.x == 0)(self.to_x.start)
        pl.when(self.place.y == 0)(self.to_y.start)

    def relay(self):
        @pl.when(self.place.corner)
        def _():
            self.to_y.wait_recv()
            self.relayed.start()

    def finish(self):
        p = self.place
        pl.when(p.x == 1)(self.to_x.wait_recv)
        pl.when((p.y == 1) & (p.x == 0))(self.to_y.wait_recv)
        pl.when(p.turn)(self.relayed.wait_recv)
        pl.when(p.x == 0)(self.to_x.wait_send)
        pl.when(p.y == 0)(self.to_y.wait_send)
        pl.when(p.corner)(self.relayed.wait_send)


def first_kernel(
    counts, inverse_ref, tok_ref, grad_ref, gain_ref, wq_in, wk_ref, wv_ref, wo_in, wd_in, wg_in, wu_in,
    q_out, kv_out, n_out, g_full, joined_out, wo_out, wd_out, slice_g, slice_u,
    n_full, joined, own_slice, slices, cos_ref, sin_ref, linear, kv_own, ss, rs, lsem,
):
    place = Place()
    copies = Copies(ss, rs)
    block, width = tok_ref.shape
    two = 2 * block
    q_cols = q_out.shape[0]
    kv_cols = kv_own.shape[1] // 2
    q_lanes = pl.ds(0, q_cols)
    slice_rows = pl.ds(place.slot * own_slice.shape[0], own_slice.shape[0])
    load_q = pltpu.make_async_copy(wq_in, joined.at[:, q_lanes], lsem.at[0])
    load_q_odd = pltpu.make_async_copy(
        wq_in.at[slice_rows], own_slice.at[:, q_lanes], lsem.at[0]
    )
    pl.when(place.c == 0)(load_q.start)
    pl.when(place.odd)(load_q_odd.start)
    rows4 = slice_g.shape[0]
    at_slot = pl.ds(place.slot * rows4, rows4)
    slice_loads = [
        pltpu.make_async_copy(src.at[at_slot], slices.at[i], lsem.at[1 + i])
        for i, src in enumerate((wg_in, wu_in))
    ]
    slice_stores = [
        pltpu.make_async_copy(slices.at[i], dst, lsem.at[6 + i])
        for i, dst in enumerate((slice_g, slice_u))
    ]
    for copy in slice_loads:
        copy.start()

    own_grad = pltpu.make_async_copy(grad_ref, g_full.at[pl.ds(0, block)], lsem.at[3])
    own_grad.start()
    meet((place.beside, place.near, place.far, place.cross, place.over_x, place.over_y))

    @pl.when(place.odd)
    def _():
        lanes = pl.ds(pl.multiple_of(place.slot * own_slice.shape[0], 128), own_slice.shape[0])
        own_slice[:, q_cols : q_cols + kv_cols] = wk_ref[:, lanes].T
        own_slice[:, q_cols + kv_cols :] = wv_ref[:, lanes].T
        load_q_odd.wait()

    fetch_joined = PlaneFetch(copies, place, joined, own_slice=own_slice)
    fetch_o = PlaneFetch(copies, place, wo_out, wo_in)
    fetch_d = PlaneFetch(copies, place, wd_out, wd_in)
    gather = GroupGather(copies, n_full, block, place)
    gather_g = GroupGather(copies, g_full, block, place)
    fetch_joined.start()
    chunk = block // CHUNKS
    for k in range(CHUNKS):
        at = pl.ds(k * chunk, chunk)
        tok = tok_ref[at, :].astype(floats)
        root = lax.rsqrt(jnp.mean(tok * tok, axis=-1, keepdims=True) + eps_norm)
        n_full[at, :] = (tok * root * gain_ref[...]).astype(halves)
        gather.put(k)
    fetch_joined.forward()
    fetch_o.start()
    fetch_d.start()
    @pl.when(place.c == 0)
    def _():
        joined[:, q_cols : q_cols + kv_cols] = wk_ref[...].T
        joined[:, q_cols + kv_cols :] = wv_ref[...].T

    rope_tables(counts, inverse_ref, cos_ref, sin_ref)
    for load, store in zip(slice_loads, slice_stores):
        load.wait()
        store.start()
    fetch_joined.relay()
    gather.wait_here()
    fetch_joined.finish()
    pl.when(place.c == 0)(load_q.wait)
    keep_joined = pltpu.make_async_copy(joined, joined_out, lsem.at[8])
    keep_joined.start()

    def project(k):
        rows = slice(k * two, (k + 1) * two)

        def one(cols):
            linear[cols, :] = dot_nn(n_full[rows, :], joined[:, cols]).T

        tiles(joined.shape[1], 256, one)
        half_width = HEAD_WIDTH // 2
        for head in range((q_cols + kv_cols) // HEAD_WIDTH):
            low = slice(head * HEAD_WIDTH, head * HEAD_WIDTH + half_width)
            high = slice(head * HEAD_WIDTH + half_width, (head + 1) * HEAD_WIDTH)
            one_half, two_half = linear[low, :], linear[high, :]
            cosine, sine = cos_ref[:, rows], sin_ref[:, rows]
            first = (one_half * cosine - two_half * sine).astype(halves)
            second = (two_half * cosine + one_half * sine).astype(halves)
            if head * HEAD_WIDTH < q_cols:
                q_out[low, rows] = first
                q_out[high, rows] = second
            else:
                kv_own[k, low.start - q_cols : low.stop - q_cols, :] = first
                kv_own[k, high.start - q_cols : high.stop - q_cols, :] = second
        kv_own[k, kv_cols:, :] = (linear[q_cols + kv_cols :, :].astype(halves) * VSCALE).astype(halves)

    crossings, spreads_a, spreads_b, kept = [], [], [], []

    def share(k):
        slots = [kv_out.at[8 * k + i] for i in range(8)]
        keep = pltpu.make_async_copy(kv_own.at[k], slots[0], lsem.at[4 + k])
        keep.start()
        kept.append(keep)
        crossing = copies.make(kv_own.at[k], slots[4], place.cross)
        crossing.start()
        crossings.append(crossing)
        spread = Spread(copies, place, kv_own.at[k], slots[:4])
        spread.start()
        spreads_a.append(spread)
        spreads_b.append(Spread(copies, place, slots[4], slots[4:]))

    project(0)
    share(0)
    gather.wait_there()
    own_grad.wait()
    for k in range(CHUNKS):
        gather_g.put(k)
    project(1)
    share(1)
    keep_n = pltpu.make_async_copy(n_full, n_out, lsem.at[9])
    keep_n.start()
    fetch_o.forward()
    fetch_d.forward()
    spreads_a[0].relay()
    spreads_a[1].relay()
    crossings[0].wait_recv()
    spreads_b[0].start()
    fetch_o.relay()
    fetch_d.relay()
    gather_g.wait_there()
    spreads_b[0].relay()
    crossings[1].wait_recv()
    spreads_b[1].start()
    spreads_b[1].relay()
    fetch_o.finish()
    fetch_d.finish()
    gather_g.wait_here()
    for spread in spreads_a + spreads_b:
        spread.finish()
    for copy in kept + slice_stores + [keep_joined, keep_n]:
        copy.wait()
    for copy in crossings:
        copy.wait_send()
    for fetch in (fetch_joined, fetch_o, fetch_d):
        fetch.drain()
    gather.finish()
    gather_g.finish()


def first_part(counts, inverse, tokens, out_grad, gain, projections, weights):
    block, width = tokens.shape
    group = 4 * block
    shape = jax.ShapeDtypeStruct
    hidden = weights[2].shape[1]
    part = (width // 4, hidden)
    half_width = HEAD_WIDTH // 2
    q_cols, kv_cols = projections[0].shape[1], projections[1].shape[0]
    joined_cols = q_cols + 2 * kv_cols
    out_shape = (
        shape((q_cols, group), halves),
        shape((16, 2 * kv_cols, 2 * block), halves),
        shape((group, width), halves),
        shape((group, width), halves),
        shape((width, joined_cols), halves),
        shape(weights[0].shape, halves),
        shape(weights[1].shape, halves),
        shape(part, halves),
        shape(part, halves),
    )
    return pl.pallas_call(
        first_kernel,
        out_shape=out_shape,
        in_specs=[SM] + [VM] * 4 + [HB, VM, VM] + [HB] * 4,
        out_specs=(VM, HM, HM, VM, HM, HM, HM, HM, HM),
        scratch_shapes=[
            pltpu.VMEM((group, width), halves),
            pltpu.VMEM((width, joined_cols), halves),
            pltpu.VMEM((width // 4, joined_cols), halves),
            pltpu.VMEM((2,) + part, halves),
            pltpu.VMEM((half_width, group), floats),
            pltpu.VMEM((half_width, group), floats),
            pltpu.VMEM((joined_cols, 2 * block), floats),
            pltpu.VMEM((2, 2 * kv_cols, 2 * block), halves),
            *copy_semaphores(),
            pltpu.SemaphoreType.DMA((10,)),
        ],
        compiler_params=pltpu.CompilerParams(
            collective_id=2, has_side_effects=True, vmem_limit_bytes=63 << 20
        ),
        name="first",
    )(counts, inverse, tokens, out_grad, gain, *projections, *weights)


class PlaneSum:
    def __init__(self, copies, place, x_first, bufs, sent=None, come=None):
        self.place, self.bufs, self.x_first = place, bufs, x_first
        half, keep, come_two, home_one, home_two = bufs
        first, second = (place.over_x, place.over_y) if x_first else (place.over_y, place.over_x)
        self.at = place.y if x_first else place.x
        self.one = None if sent is None else copies.make(sent, come, first)
        self.two = copies.make(half, come_two, second)
        rows = home_one.shape[0]
        c = place.c
        home = (c * place.cross[0] + (1 - c) * place.beside[0], c * place.cross[1] + (1 - c) * place.beside[1])
        self.to_home = copies.make(half.at[pl.ds((1 - c) * rows, rows)], home_one, home)
        self.to_far = copies.make(half.at[pl.ds(rows, rows)], home_two, place.far)

    def cross_second(self, kept, come):
        if self.one is not None:
            self.one.wait()
        half, keep, come_two, home_one, home_two = self.bufs
        at = self.at
        half[...] = (kept[1 - at].astype(floats) + come[1 - at].astype(floats)).astype(halves)
        self.two.start()
        keep[...] = (kept[at].astype(floats) + come[at].astype(floats)).astype(halves)

    def go_home(self, exchanged=True):
        half, keep, come_two, home_one, home_two = self.bufs
        if exchanged:
            self.two.wait()
        half[...] = (keep[...].astype(floats) + come_two[...].astype(floats)).astype(halves)
        self.to_home.start()
        pl.when(self.place.odd)(self.to_far.start)

    def finish(self, out):
        half, keep, come_two, home_one, home_two = self.bufs
        rows = home_one.shape[0]
        self.to_home.wait()

        @pl.when(self.place.c == 0)
        def _():
            out[...] = half[:rows, :].astype(floats) + home_one[...].astype(floats)

        @pl.when(self.place.odd)
        def _():
            self.to_far.wait()
            out[...] = home_one[...].astype(floats) + home_two[...].astype(floats)


def plane_buffers(rows, cols):
    full = pltpu.VMEM((rows, cols), halves)
    part = pltpu.VMEM((rows // 2, cols), halves)
    return [full, full, full, part, part]


def outer_blocks(place, x_first, left, right, send_ref, keep_ref, on_sent):
    rows = left.shape[1] // 4
    for kept in (False, True):
        for i in range(2):
            if x_first:
                block = 2 * i + (place.x if kept else 1 - place.x)
            else:
                block = 2 * (place.y if kept else 1 - place.y) + i
            cols = pl.ds(pl.multiple_of(block * rows, 128), rows)
            value = lax.dot_general(
                left[:, cols], right, (((0,), (0,)), ((), ())), preferred_element_type=floats
            ).astype(halves)
            (keep_ref if kept else send_ref)[i] = value
        if not kept:
            on_sent()


def mid_kernel(ctx_ref, tok_ref, gain_ref, g_full, weight_refs, outs, scratch):
    (res_out, gres_out, e_full, near_out, down_half, down_mine, gate_keep, gate_send, up_keep, up_send,
     dctx_out, delta_out, gain_out) = outs
    (ctx, m_full, dh, hid, dgate, dup, w_o, w_d, w_g, w_u, down_send, down_keep, down_come, part_out, far_in, own_in, *bufs, ss, rs, wsem) = scratch
    place = Place()
    copies = Copies(ss, rs)
    block, width = tok_ref.shape
    two = 2 * block
    hidden = w_g.shape[1]
    wo_ref, wd_ref, wg_ref, wu_ref, wo_got, wd_got, slice_g, slice_u = weight_refs
    first_loads = [
        pltpu.make_async_copy(src, dst, wsem.at[i])
        for i, (src, dst) in enumerate(((wo_ref, w_o), (wd_ref, w_d)))
    ]
    first_loads_odd = [
        pltpu.make_async_copy(src, dst, wsem.at[i])
        for i, (src, dst) in enumerate(((wo_got, w_o), (wd_got, w_d)))
    ]

    def wait_first(i):
        pl.when(place.c == 0)(first_loads[i].wait)
        pl.when(place.odd)(first_loads_odd[i].wait)

    rows4 = slice_g.shape[0]
    at_slot = pl.ds(place.slot * rows4, rows4)
    loads = [
        pltpu.make_async_copy(src, dst, wsem.at[2 + i])
        for i, (src, dst) in enumerate(((wg_ref, w_g), (wu_ref, w_u)))
    ]
    loads_odd = [
        pltpu.make_async_copy(src, dst.at[at_slot], wsem.at[2 + i])
        for i, (src, dst) in enumerate(((slice_g, w_g), (slice_u, w_u)))
    ]

    @pl.when(place.c == 0)
    def _():
        for copy in first_loads + loads:
            copy.start()

    @pl.when(place.odd)
    def _():
        for copy in first_loads_odd + loads_odd:
            copy.start()

    ctx[...] = ctx_ref[...].T
    meet((place.beside, place.near, place.over_x, place.over_y))
    fetches = [PlaneFetch(copies, place, w_g), PlaneFetch(copies, place, w_u)]

    @pl.when(place.odd)
    def _():
        for copy in loads_odd:
            copy.wait()

    for fetch in fetches:
        fetch.forward()
    sum_one = GroupSum(copies, bufs, place)
    gather_one = GroupGather(copies, m_full, block, place)
    sum_two = GroupSum(copies, bufs, place)
    gather_two = GroupGather(copies, e_full, block, place)

    def project(k, put):
        rows = slice(k * two, (k + 1) * two)
        tiles(width, 256, lambda cols: put(cols, dot_nn(ctx[rows, :], w_o[:, cols])))

    wait_first(0)
    sum_one.run(project)
    wait_first(1)

    def back_hidden(cols):
        for rows in (slice(0, two), slice(two, 2 * two)):
            dh[rows, cols] = dot_nt(g_full[rows, :], w_d[cols, :]).astype(halves)

    tiles(hidden, 256, back_hidden)
    chunk = block // CHUNKS
    for k in range(CHUNKS):
        at = pl.ds(k * chunk, chunk)
        res = tok_ref[at, :].astype(floats) + sum_one.take(k)
        res_out[at, :] = res
        root = lax.rsqrt(jnp.mean(res * res, axis=-1, keepdims=True) + eps_norm)
        m_full[at, :] = (res * root * gain_ref[...]).astype(halves)
        gather_one.put(k)
        if k == 1:
            for fetch in fetches:
                fetch.relay()
    sum_one.finish()

    def there(h):
        rows = block // 2
        return [slice(two + h * rows, two + (h + 1) * rows), slice(3 * block + h * rows, 3 * block + (h + 1) * rows)]

    def read(ref, parts):
        values = [ref[rows, :] for rows in parts]
        return values[0] if len(values) == 1 else jnp.concatenate(values, axis=0)

    def write(ref, parts, cols, value):
        rows = value.shape[0] // len(parts)
        for i, part in enumerate(parts):
            ref[part, cols] = value[i * rows : (i + 1) * rows]

    def activate(parts):
        def one(cols):
            left = read(m_full, parts)
            gate_pre = dot_nn(left, w_g[:, cols])
            up_pre = dot_nn(left, w_u[:, cols])
            back = [dh[rows, cols] for rows in parts]
            back = (back[0] if len(back) == 1 else jnp.concatenate(back, axis=0)).astype(floats)
            sigma = 1.0 / (1.0 + jnp.exp(-gate_pre))
            silu = gate_pre * sigma
            write(hid, parts, cols, (silu * up_pre).astype(halves))
            write(dgate, parts, cols, (back * up_pre * (sigma + silu * (1.0 - sigma))).astype(halves))
            write(dup, parts, cols, (back * silu).astype(halves))

        tiles(hidden, 256, one)

    def partial_out(parts):
        def one(cols):
            write(part_out, parts, cols, dot_nn(read(hid, parts), w_d[:, cols]).astype(halves))

        tiles(width, 256, one)

    def back_norm(parts, put):
        def one(cols):
            put(cols, dot_nt(read(dgate, parts), w_g[cols, :]) + dot_nt(read(dup, parts), w_u[cols, :]))

        tiles(width, 256, one)

    for fetch in fetches:
        fetch.finish()

    @pl.when(place.c == 0)
    def _():
        for copy in loads:
            copy.wait()

    here = [slice(0, two)]
    gather_one.wait_here()
    activate(here)
    partial_out(here)
    whole = [slice(two, 2 * two)]
    gather_one.wait_there()
    at = pl.ds(0, block)
    activate(whole)
    back_norm(whole, lambda cols, value: sum_two.put_there(at, cols, value))
    sum_two.send_far(at)
    gather_one.finish()
    back_norm(here, sum_two.put_here)
    sum_two.send_beside()
    sum_two.send_near(CHUNKS)
    partial_out(whole)
    to_side = [
        copies.make(part_out.at[pl.ds(3 * block, block)], far_in, place.beside),
        copies.make(part_out.at[pl.ds(block, block)], own_in, place.beside),
    ]
    for copy in to_side:
        copy.start()
    down_over = copies.make(down_send, down_come, place.over_x)
    outer_blocks(place, True, g_full, hid[...], down_send, down_keep, down_over.start)
    outer_blocks(place, False, m_full, dgate[...], gate_send, gate_keep, lambda: None)
    gain_out[...] = jnp.zeros_like(gain_out)
    for k in range(CHUNKS):
        at = pl.ds(k * chunk, chunk)
        back = sum_two.take(k)
        res = res_out[at, :]
        root = lax.rsqrt(jnp.mean(res * res, axis=-1, keepdims=True) + eps_norm)
        weighted = back * gain_ref[...]
        slope = jnp.mean(weighted * res, axis=-1, keepdims=True)
        grad = g_full[at, :].astype(floats) + root * weighted - res * (root * root * root * slope)
        gain_out[...] += jnp.sum(back * res * root, axis=0, keepdims=True)
        gres_out[at, :] = grad
        e_full[at, :] = grad.astype(halves)
        gather_two.put(k)
    sum_two.finish()
    outer_blocks(place, True, m_full, dup[...], up_send, up_keep, lambda: None)

    def back_context(parts):
        grad = dot_nt(w_o[...], read(e_full, parts)).astype(halves)
        rows = grad.shape[1] // len(parts)
        for i, part in enumerate(parts):
            piece = grad[:, i * rows : (i + 1) * rows]
            dctx_out[:, part] = piece
            prod = piece.astype(floats) * ctx_ref[:, part].astype(floats)
            for hd in range(delta_out.shape[0]):
                delta_out[hd : hd + 1, part] = VSCALE * jnp.sum(
                    prod[hd * HEAD_WIDTH : (hd + 1) * HEAD_WIDTH], axis=0, keepdims=True
                )

    for copy in to_side:
        copy.wait()
    for k in range(CHUNKS):
        at = pl.ds(k * chunk, chunk)
        near = pl.ds(two + k * chunk, chunk)
        near_out[at, :] = (part_out[near, :].astype(floats) + far_in[at, :].astype(floats)).astype(halves)
        res_out[at, :] += part_out[at, :].astype(floats) + own_in[at, :].astype(floats)
    gather_two.wait_here()
    back_context(here)
    gather_two.wait_there(0, 2)
    back_context(there(0))
    down_over.wait()
    at = place.y
    down_half[...] = (down_keep[1 - at].astype(floats) + down_come[1 - at].astype(floats)).astype(halves)
    down_mine[...] = (down_keep[at].astype(floats) + down_come[at].astype(floats)).astype(halves)
    gather_two.wait_there(1, 2)
    back_context(there(1))
    gather_two.finish()
    for fetch in fetches:
        fetch.drain()


def middle(context_t, tokens, gain, grad_full, weights):
    q_cols, group = context_t.shape
    block, width = tokens.shape
    hidden = weights[2].shape[1]
    shape = jax.ShapeDtypeStruct
    out_shape = (
        shape((block, width), floats),
        shape((block, width), floats),
        shape((group, width), halves),
        shape((block, width), halves),
        *[shape((width // 4, hidden), halves)] * 2,
        *[shape((2, width // 4, hidden), halves)] * 4,
        shape((q_cols, group), halves),
        shape((q_cols // HEAD_WIDTH, group), floats),
        shape((1, width), floats),
    )
    scratch = [
        pltpu.VMEM((group, q_cols), halves),
        pltpu.VMEM((group, width), halves),
        *[pltpu.VMEM((group, hidden), halves)] * 4,
        *[pltpu.VMEM(weight.shape, halves) for weight in weights[:4]],
        *[pltpu.VMEM((2, width // 4, hidden), halves)] * 3,
        pltpu.VMEM((group, width), halves),
        *[pltpu.VMEM((block, width), halves)] * 2,
        *[pltpu.VMEM((block, width), floats)] * 2,
        *[pltpu.VMEM((block, width), halves)] * 6,
        *copy_semaphores(),
        pltpu.SemaphoreType.DMA((4,)),
    ]

    def kernel(*refs):
        mid_kernel(*refs[:4], refs[4:12], refs[12:25], refs[25:])

    return pl.pallas_call(
        kernel,
        out_shape=out_shape,
        in_specs=[VM] * 4 + [HB] * 8,
        out_specs=(VM,) * 13,
        scratch_shapes=scratch,
        compiler_params=pltpu.CompilerParams(
            collective_id=1, has_side_effects=True, vmem_limit_bytes=63 << 20
        ),
        name="middle",
    )(context_t, tokens, gain, grad_full, *weights)


def last_kernel(ins, outs, scratch):
    (counts, inverse_ref, dq_ref, dkv_ref, n_ref, joined_ref, tok_ref, gain_ref, gres_ref, e_ref, ctx_ref,
     gain_mlp_ref, *mlp) = ins
    (in_grad, gains_out, gate_out, up_out, down_out, q_out, kv_out, o_out) = outs
    (full, ctx, d_lin, acc_a, acc_b, own, x_in, y_in, rel_in, cross_in, cross_out, kept, come,
     gains, gains_in, cos_ref, sin_ref, joined, *rest) = scratch
    bufs_mlp = [rest[5 * i : 5 * i + 5] for i in range(3)]
    rest = rest[15:]
    bufs_attn = [rest[8 * i : 8 * i + 8] for i in range(3)]
    rest = rest[24:]
    sum_bufs, (ss, rs, lsem) = rest[:8], rest[8:]
    place = Place()
    copies = Copies(ss, rs)
    block, width = tok_ref.shape
    two = 2 * block
    q_cols = dq_ref.shape[0]
    kv_cols = own.shape[1] // 2
    half_width = HEAD_WIDTH // 2

    load_e = pltpu.make_async_copy(e_ref, full, lsem.at[0])
    load_e.start()
    load_joined = pltpu.make_async_copy(joined_ref, joined, lsem.at[11])
    load_joined.start()
    order = (4, 12, 0, 8)
    own_loads = [
        pltpu.make_async_copy(dkv_ref.at[at], own.at[i], lsem.at[1 + i]) for i, at in enumerate(order)
    ]
    y_loads = [
        pltpu.make_async_copy(dkv_ref.at[at + 2], y_in.at[i], lsem.at[5 + i])
        for i, at in enumerate(order)
    ]
    for copy in own_loads:
        copy.start()

    @pl.when(place.corner)
    def _():
        for copy in y_loads:
            copy.start()

    def load_mlp(i):
        return [
            pltpu.make_async_copy(mlp[2 * i], kept, lsem.at[9]),
            pltpu.make_async_copy(mlp[2 * i + 1], come, lsem.at[10]),
        ]

    down_loads = [
        pltpu.make_async_copy(mlp[i], bufs_mlp[0][1 + i], lsem.at[12 + i]) for i in range(2)
    ]
    loads = load_mlp(1)
    for copy in down_loads + loads:
        copy.start()
    gains[0, 0:1, :] = gain_mlp_ref[...]
    gains[0, 1:2, :] = jnp.zeros_like(gain_mlp_ref)
    meet((place.beside, place.near, place.far, place.cross, place.over_x, place.over_y))

    back_rel = [copies.make(dkv_ref.at[at + 3], rel_in.at[i], place.over_x) for i, at in enumerate(order)]
    back_x = [copies.make(dkv_ref.at[at + 1], x_in.at[i], place.over_x) for i, at in enumerate(order)]
    back_y = [copies.make(dkv_ref.at[at + 2], y_in.at[i], place.over_y) for i, at in enumerate(order)]
    back_sum = [copies.make(y_in.at[i], y_in.at[i], place.over_y) for i in range(4)]
    crossing = [copies.make(cross_out.at[i], cross_in.at[i], place.cross) for i in range(2)]
    def start_back(i):
        pl.when(place.turn)(back_rel[i].start)
        pl.when(place.x == 1)(back_x[i].start)
        pl.when(place.turn)(back_y[i].start)

    start_back(0)
    start_back(1)

    def corner_sum(i):
        @pl.when(place.corner)
        def _():
            back_rel[i].wait_recv()
            y_loads[i].wait()
            y_in[i] = (y_in[i].astype(floats) + rel_in[i].astype(floats)).astype(halves)
            back_sum[i].start()

    def home_sum(i, put):
        own_loads[i].wait()
        acc_b[...] = own[i].astype(floats)

        @pl.when(place.x == 0)
        def _():
            back_x[i].wait_recv()
            acc_b[...] += x_in[i].astype(floats)

        @pl.when((place.y == 0) & (place.x == 0))
        def _():
            back_y[i].wait_recv()
            acc_b[...] += y_in[i].astype(floats)

        @pl.when((place.y == 0) & (place.x == 1))
        def _():
            back_sum[i].wait_recv()
            acc_b[...] += y_in[i].astype(floats)

        put()

    sums = []
    for i, x_first in enumerate((True, False, True)):
        sums.append(PlaneSum(copies, place, x_first, bufs_mlp[i]))
    for copy in down_loads:
        copy.wait()
    sums[0].go_home(exchanged=False)
    for i in (1, 2):
        for copy in loads:
            copy.wait()
        sums[i].cross_second(kept, come)
        if i == 1:
            loads = load_mlp(2)
            for copy in loads:
                copy.start()
            corner_sum(0)
            start_back(2)
            start_back(3)
    ctx[...] = ctx_ref[...].T
    rope_tables(counts, inverse_ref, cos_ref, sin_ref)

    attn_sums = []
    for i, x_first in enumerate((False, True, False)):
        sent, keep, got = bufs_attn[i][:3]
        attn_sums.append(PlaneSum(copies, place, x_first, bufs_attn[i][3:], sent, got))

    def attn_grad(i, left, right):
        sent, keep, got = bufs_attn[i][:3]
        outer_blocks(place, attn_sums[i].x_first, left, right, sent, keep, attn_sums[i].one.start)

    corner_sum(1)
    load_e.wait()
    attn_grad(0, full, ctx[...])
    load_n = pltpu.make_async_copy(n_ref, full, lsem.at[0])
    load_n.start()

    def cross_back(i):
        def put():
            cross_out[i] = acc_b[...].astype(halves)
            crossing[i].start()

        home_sum(i, put)

    def unturn(value, at, first_row):
        low, high = value[:half_width], value[half_width:]
        cosine, sine = cos_ref[:, at], sin_ref[:, at]
        turned = jnp.concatenate([low * cosine + high * sine, high * cosine - low * sine], axis=0)
        d_lin[first_row : first_row + HEAD_WIDTH, at] = turned.astype(halves)

    cross_back(0)
    corner_sum(2)
    everything = slice(0, 2 * two)
    for head in range(q_cols // HEAD_WIDTH):
        unturn(dq_ref[head * HEAD_WIDTH : (head + 1) * HEAD_WIDTH, :], everything, head * HEAD_WIDTH)
    cross_back(1)
    corner_sum(3)
    load_n.wait()
    attn_grad(1, full, d_lin[:q_cols, :].T)
    for plane in sums[1:]:
        plane.go_home()

    def second(i):
        sent, keep, got = bufs_attn[i][:3]
        attn_sums[i].cross_second(keep, got)

    second(0)

    def keep_a(k):
        def put():
            acc_a[:, k * two : (k + 1) * two] = acc_b[...]

        home_sum(2 + k, put)

    keep_a(0)
    keep_a(1)
    second(1)
    attn_sums[0].go_home()
    for k in range(2):
        crossing[k].wait_recv()
        lanes = slice(k * two, (k + 1) * two)
        total = acc_a[:, lanes] + cross_in[k].astype(floats)
        for head in range(kv_cols // HEAD_WIDTH):
            rows = slice(head * HEAD_WIDTH, (head + 1) * HEAD_WIDTH)
            unturn(total[rows], lanes, q_cols + head * HEAD_WIDTH)
        d_lin[q_cols + kv_cols :, lanes] = total[kv_cols:].astype(halves)

    group_sum = GroupSum(copies, sum_bufs, place)
    load_joined.wait()

    def back_norm(k, put):
        rows = slice(k * two, (k + 1) * two)
        left = d_lin[:, rows].T

        def one(cols):
            value = dot_nt(left, joined[cols, :])
            put(cols, value)
            gains[0, 1:2, cols] += jnp.sum(value * full[rows, cols].astype(floats), axis=0, keepdims=True)

        tiles(width, 256, one)

    group_sum.run(back_norm)
    gains[0, 1:2, :] = gains[0, 1:2, :] / gain_ref[...]
    attn_grad(2, full, d_lin[q_cols:, :].T)
    attn_sums[1].go_home()
    for stage, device in enumerate((place.beside, place.over_x, place.over_y, place.near, place.far)):
        copy = copies.make(gains.at[stage], gains_in.at[stage], device)
        copy.start()
        copy.wait()
        if stage < 4:
            gains[stage + 1] = gains[stage] + gains_in[stage]
        else:
            gains_out[...] = gains[stage] + gains_in[stage]
        if stage == 2:
            second(2)
    for plane, out in zip(sums, (down_out, gate_out, up_out)):
        plane.finish(out)
    attn_sums[2].go_home()
    chunk = block // CHUNKS
    for k in range(CHUNKS):
        at = pl.ds(k * chunk, chunk)
        back = group_sum.take(k)
        tok = tok_ref[at, :].astype(floats)
        root = lax.rsqrt(jnp.mean(tok * tok, axis=-1, keepdims=True) + eps_norm)
        weighted = back * gain_ref[...]
        slope = jnp.mean(weighted * tok, axis=-1, keepdims=True)
        in_grad[at, :] = gres_ref[at, :] + root * weighted - tok * (root * root * root * slope)
    for plane, out in zip(attn_sums, (o_out, q_out, kv_out)):
        plane.finish(out)
    group_sum.finish()
    for i in range(4):
        pl.when(place.turn)(back_rel[i].wait_send)
        pl.when(place.x == 1)(back_x[i].wait_send)
        pl.when(place.turn)(back_y[i].wait_send)
        pl.when(place.corner)(back_sum[i].wait_send)
    for copy in crossing:
        copy.wait_send()


def last_part(counts, inverse, d_query_t, d_kv, normed, joined, tokens, gain, gres, e_full, context_t, gain_mlp, mlp):
    block, width = tokens.shape
    group = 4 * block
    q_cols, kv_all = d_query_t.shape[0], d_kv.shape[1]
    kv_cols = kv_all // 2
    hidden = mlp[0].shape[1]
    per = width // 8
    shape = jax.ShapeDtypeStruct
    out_shape = (
        shape((block, width), floats),
        shape((2, width), floats),
        *[shape((per, hidden), floats)] * 3,
        shape((per, q_cols), floats),
        shape((per, kv_all), floats),
        shape((per, q_cols), floats),
    )
    piece = (kv_all, 2 * block)
    scratch = [
        pltpu.VMEM((group, width), halves),
        pltpu.VMEM((group, q_cols), halves),
        pltpu.VMEM((joined.shape[1], group), halves),
        pltpu.VMEM((kv_all, group), floats),
        pltpu.VMEM(piece, floats),
        *[pltpu.VMEM((4,) + piece, halves)] * 4,
        *[pltpu.VMEM((2,) + piece, halves)] * 2,
        *[pltpu.VMEM((2, width // 4, hidden), halves)] * 2,
        *[pltpu.VMEM((5, 2, width), floats)] * 2,
        *[pltpu.VMEM((HEAD_WIDTH // 2, group), floats)] * 2,
        pltpu.VMEM(joined.shape, halves),
    ]
    for _ in range(3):
        scratch += plane_buffers(width // 4, hidden)
    for cols in (q_cols, q_cols, kv_all):
        scratch += [pltpu.VMEM((2, width // 4, cols), halves)] * 3 + plane_buffers(width // 4, cols)
    scratch += [
        *[pltpu.VMEM((block, width), floats)] * 2,
        *[pltpu.VMEM((block, width), halves)] * 6,
        *copy_semaphores(),
        pltpu.SemaphoreType.DMA((14,)),
    ]

    def kernel(*refs):
        last_kernel(refs[:18], refs[18:26], refs[26:])

    return pl.pallas_call(
        kernel,
        out_shape=out_shape,
        in_specs=[SM, VM, VM, HM, HM, HM, VM, VM, VM, HM, VM, VM] + [HM] * 6,
        out_specs=(VM,) * 8,
        scratch_shapes=scratch,
        compiler_params=pltpu.CompilerParams(
            collective_id=3, has_side_effects=True, vmem_limit_bytes=63 << 20
        ),
        name="last",
    )(counts, inverse, d_query_t, d_kv, normed, joined, tokens, gain, gres, e_full, context_t, gain_mlp, *mlp)


def finish_kernel(*refs):
    base, near, kv_sum, *ready = refs[:9]
    output, k_out, v_out, *outs = refs[9:18]
    out_buf, k_buf, v_buf, sem = refs[18:]
    copies = [pltpu.make_async_copy(src, dst, sem.at[i]) for i, (src, dst) in enumerate(zip(ready, outs))]
    for copy in copies:
        copy.start()
    out_buf[...] = (base[...] + near[...].astype(floats)).astype(halves)
    kv_cols = k_buf.shape[1]
    k_buf[...] = kv_sum[:, :kv_cols]
    v_buf[...] = kv_sum[:, kv_cols:]
    more = [
        pltpu.make_async_copy(src, dst, sem.at[len(copies) + i])
        for i, (src, dst) in enumerate(((out_buf, output), (k_buf, k_out), (v_buf, v_out)))
    ]
    for copy in more:
        copy.start()
    for copy in copies + more:
        copy.wait()


def finish(base, near, kv_sum, *ready):
    shape = jax.ShapeDtypeStruct
    rows, cols = kv_sum.shape
    small = (rows, cols // 2)
    return pl.pallas_call(
        finish_kernel,
        out_shape=(
            shape(base.shape, halves),
            shape(small, floats),
            shape(small, floats),
            *[shape(a.shape, a.dtype) for a in ready],
        ),
        in_specs=[VM] * (3 + len(ready)),
        out_specs=(HM,) * (3 + len(ready)),
        scratch_shapes=[
            pltpu.VMEM(base.shape, halves),
            pltpu.VMEM(small, floats),
            pltpu.VMEM(small, floats),
            pltpu.SemaphoreType.DMA((3 + len(ready),)),
        ],
        compiler_params=pltpu.CompilerParams(vmem_limit_bytes=63 << 20),
        name="finish",
    )(base, near, kv_sum, *ready)


def routes(target):
    pairs = []
    for index in range(32):
        dp, z = divmod(index, 4)
        there = target(dp // 4, dp // 2 % 2, dp % 2, z)
        if there is not None:
            y, x, c, z = there
            pairs.append((index, (y * 4 + x * 2 + c) * 4 + z))
    return pairs


ROUTES = {
    "core": routes(lambda y, x, c, z: (y, x, 1 - c, z)),
    "x": routes(lambda y, x, c, z: (y, 1 - x, c, z)),
    "y": routes(lambda y, x, c, z: (1 - y, x, c, z)),
    "near": routes(lambda y, x, c, z: (y, x, c, z ^ 1)),
    "far": routes(lambda y, x, c, z: (y, x, c, z ^ 2)),
    "cross": routes(lambda y, x, c, z: (y, x, 1 - c, z ^ 2)),
    "odd_far": routes(lambda y, x, c, z: (y, x, c, z ^ 2) if c else None),
    "odd_x": routes(lambda y, x, c, z: (y, 1 - x, c, z) if c else None),
    "odd_y": routes(lambda y, x, c, z: (1 - y, x, c, z) if c else None),
    "odd_xy": routes(lambda y, x, c, z: (1 - y, 1 - x, c, z) if c else None),
    "home": routes(lambda y, x, c, z: (y, x, 0, z ^ 2) if c else (y, x, 1, z)),
    "x_up": routes(lambda y, x, c, z: None if x else (y, 1, c, z)),
    "y_up": routes(lambda y, x, c, z: None if y else (1, x, c, z)),
    "x_down": routes(lambda y, x, c, z: (y, 0, c, z) if x else None),
    "y_down": routes(lambda y, x, c, z: (0, x, c, z) if y else None),
    "relay": routes(lambda y, x, c, z: (1, 0, c, z) if x and y else None),
    "unrelay": routes(lambda y, x, c, z: (1, 1, c, z) if y and not x else None),
}


def send(block, way):
    return lax.ppermute(block, ("dp", "tp"), ROUTES[way])


def local_regrouped(
    tokens,
    out_grad,
    segment_ids,
    attn_gain,
    query_weight,
    key_matrix,
    value_matrix,
    output_weight,
    mlp_gain,
    gate_weight,
    up_weight,
    down_weight,
):
    block = tokens.shape[0]
    dp = lax.axis_index("dp")
    half_width = HEAD_WIDTH // 2
    gain_attn, gain_mlp = attn_gain.astype(floats)[None, :], mlp_gain.astype(floats)[None, :]
    counts = jnp.sum(
        (segment_ids[None, :] < jnp.arange(1, 4, dtype=jnp.int32)[:, None]).astype(jnp.int32), axis=1
    )
    inverse = 1.0 / rope_base ** (jnp.arange(half_width, dtype=floats) * 2.0 / HEAD_WIDTH)
    inverse = inverse[:, None]
    q_t, pieces, normed_full, grad_full, joined, weight_o, weight_d, slice_g, slice_u = first_part(
        counts, inverse, tokens, out_grad, gain_attn,
        (query_weight, key_matrix.T, value_matrix.T),
        (output_weight, down_weight, gate_weight, up_weight),
    )
    slices = [send(part, "odd_far") for part in (slice_g, slice_u)]
    context_t, log_total = attend_forward(counts, q_t, pieces)
    (
        out_base, grad_residual, attn_grad_full, out_near, down_half, down_mine, gate_keep, gate_send,
        up_keep, up_send, d_context_t, delta, mlp_gain_part,
    ) = middle(
        context_t, tokens, gain_mlp, grad_full,
        (output_weight, down_weight, gate_weight, up_weight, weight_o, weight_d, *slices),
    )
    gate_come = send(gate_send, "y")
    up_come = send(up_send, "x")
    down_come = send(down_half, "y")
    out_near = send(out_near, "near")
    d_query_t, d_pieces = attend_backward(counts, q_t, d_context_t, log_total, delta, pieces)
    input_grad, gains, gate_sum, up_sum, down_sum, query_sum, kv_sum, output_sum = last_part(
        counts, inverse, d_query_t, d_pieces, normed_full, joined, tokens, gain_attn,
        grad_residual, attn_grad_full, context_t, mlp_gain_part,
        (down_mine, down_come, gate_keep, gate_come, up_keep, up_come),
    )
    per = gains.shape[1] // 8
    gains = lax.dynamic_slice_in_dim(gains, dp * per, per, axis=1)
    output, key_sum, value_sum, input_grad, query_sum, output_sum, gate_sum, up_sum, down_sum = finish(
        out_base, out_near, kv_sum, input_grad, query_sum, output_sum, gate_sum, up_sum, down_sum
    )
    return (
        output,
        input_grad,
        gains[1],
        query_sum,
        key_sum,
        value_sum,
        output_sum.T,
        gains[0],
        gate_sum,
        up_sum,
        down_sum.T,
    )


def solution(mesh):
    regroup = mesh.shape["dp"] == 8 and mesh.shape["tp"] == 4
    chosen = local_regrouped if regroup else local
    return jax.shard_map(
        chosen,
        mesh=mesh,
        in_specs=(
            P(("dp", "tp"), None),
            P(("dp", "tp"), None),
            P(),
            P(),
            P(None, "tp"),
            P(None, "tp"),
            P(None, "tp"),
            P("tp", None),
            P(),
            P(None, "tp"),
            P(None, "tp"),
            P("tp", None),
        ),
        out_specs=(
            P(("dp", "tp"), None),
            P(("dp", "tp"), None),
            P("dp"),
            P("dp", "tp"),
            P("dp", "tp"),
            P("dp", "tp"),
            P("tp", "dp"),
            P("dp"),
            P("dp", "tp"),
            P("dp", "tp"),
            P("tp", "dp"),
        ),
        check_vma=False,
    )
```

```python
import functools

import jax
import jax.numpy as jnp
from jax import lax
from jax.experimental import pallas as pl
from jax.experimental.pallas import tpu as pltpu
from jax.sharding import PartitionSpec as P

HEAD_WIDTH = 96
BLK = 256
LOG2E = 1.4426950408889634
SCORE = LOG2E * HEAD_WIDTH ** (-0.5)
VSCALE = 2.0 ** -9
FAR_BASE = 1 << 24
floats = jnp.float32
halves = jnp.bfloat16


def dot_nn(a, b):
    return jnp.dot(a, b, preferred_element_type=floats)


def dot_nt(a, b):
    return lax.dot_general(a, b, (((1,), (1,)), ((), ())), preferred_element_type=floats)


def token_base(j, core, pair, side):
    return ((2 * j + core) * 4 + 2 * pair + side) * BLK


def group_bases():
    dp, z = lax.axis_index("dp"), lax.axis_index("tp")
    j, c, pair, side = dp // 2, lax.rem(dp, 2), z // 2, lax.rem(z, 2)
    return [
        token_base(j, core, pair, at) for at in (side, 1 - side) for core in (c, 1 - c)
    ]


def item_start(counts_ref, token):
    start = jnp.zeros_like(token)
    for i in range(3):
        start = jnp.where(token >= counts_ref[i], counts_ref[i], start)
    return start


def group_index():
    lanes = lax.broadcasted_iota(jnp.int32, (1, BLK), 1)
    return jnp.concatenate([lanes + base for base in group_bases()], axis=1)


def fill_places(counts_ref, sc, tok_ref, start_ref):
    dp, z = lax.axis_index("dp"), lax.axis_index("tp")
    j, c, pair, side = dp // 2, lax.rem(dp, 2), z // 2, lax.rem(z, 2)
    x, y = lax.rem(j, 2), j // 2
    kb = 0
    for side_of in (side, 1 - side):
        for cores, pair_of in (((c, 1 - c), pair), ((1 - c, c), 1 - pair)):
            for j_of, present in ((j, None), (j - 1, x), (j - 2, y), (j - 1, y * (1 - x))):
                for core in cores:
                    base = token_base(j_of, core, pair_of, side_of)
                    sc[0, kb] = base if present is None else jnp.where(present == 1, base, FAR_BASE)
                    kb += 1
    for qb, base in enumerate(group_bases()):
        sc[1, qb] = base
        sc[2, qb] = item_start(counts_ref, base)
        sc[3, qb] = item_start(counts_ref, base + (BLK - 1))
    index = group_index()
    tok_ref[...] = index
    start_ref[...] = item_start(counts_ref, index)


def pair_state(sc, kb, qb):
    key_base = sc[0, kb]
    q_base, least, most = sc[1, qb], sc[2, qb], sc[3, qb]
    needed = (key_base <= q_base + (BLK - 1)) & (key_base + (BLK - 1) >= least)
    whole = (key_base + (BLK - 1) <= q_base) & (key_base >= most)
    return key_base, needed, whole


def allowed_mask(key_bases, tok_ref, start_ref, lanes):
    masks = []
    for key_base in key_bases:
        keys = key_base + lax.broadcasted_iota(jnp.int32, (BLK, BLK), 0)
        masks.append((keys <= tok_ref[0:1, lanes]) & (keys >= start_ref[0:1, lanes]))
    return masks[0] if len(masks) == 1 else jnp.concatenate(masks, axis=0)


def piece_used(sc, piece, blocks):
    used = False
    for kb in range(2):
        for qb in range(blocks):
            used = used | pair_state(sc, 2 * piece + kb, qb)[1]
    return used


def for_piece(sc, piece, qb, unit):
    one_base, one, one_whole = pair_state(sc, 2 * piece, qb)
    two_base, two, two_whole = pair_state(sc, 2 * piece + 1, qb)
    both, free = one & two, one_whole & two_whole
    bases = (one_base, two_base)
    pl.when(both & free)(lambda: unit((0, 1), bases, False))
    pl.when(both & jnp.logical_not(free))(lambda: unit((0, 1), bases, True))
    pl.when(one & jnp.logical_not(two))(lambda: unit((0,), bases[:1], True))
    pl.when(two & jnp.logical_not(one))(lambda: unit((1,), bases[1:], True))


def fwd_kernel(n, width, counts, q_ref, pieces, *refs):
    out_acc, out_sum = refs[:2]
    kv, keys_nat, acc, total, q_wide, sc, tok_ref, start_ref, sem = refs[2:]
    for i in range(n):
        pltpu.make_async_copy(pieces.at[i], kv.at[i], sem.at[i]).start()
    acc[...] = jnp.zeros_like(acc)
    total[...] = jnp.zeros_like(total)
    fill_places(counts, sc, tok_ref, start_ref)
    heads_kv = pieces.shape[1] // (2 * HEAD_WIDTH)
    group = q_ref.shape[0] // (heads_kv * HEAD_WIDTH)
    v_off = heads_kv * HEAD_WIDTH
    places = [
        (h, slice((h * group + g) * HEAD_WIDTH, (h * group + g + 1) * HEAD_WIDTH), slice(qb * BLK, (qb + 1) * BLK),
         slice(h * HEAD_WIDTH, (h + 1) * HEAD_WIDTH), slice((qb * group + g) * BLK, (qb * group + g + 1) * BLK), h * group + g)
        for h in range(heads_kv) for g in range(group) for qb in range(q_ref.shape[1] // BLK)
    ]
    for h, rows, lanes, wrows, wlanes, hd in places:
        q_wide[wrows, wlanes] = q_ref[rows, lanes]

    def key_piece(piece, carry):
        pltpu.make_async_copy(pieces.at[piece], kv.at[piece], sem.at[piece]).wait()
        def query_block(qb, carry):
            lanes = pl.ds(pl.multiple_of(qb * BLK, BLK), BLK)
            wide = pl.ds(pl.multiple_of(qb * (group * BLK), group * BLK), group * BLK)

            def unit(subs, bases, masked):
                keys = slice(subs[0] * BLK, (subs[-1] + 1) * BLK)
                if masked:
                    allowed = allowed_mask(bases, tok_ref, start_ref, lanes)
                    allowed = jnp.concatenate([allowed] * group, axis=1)
                scores = [
                    dot_nn(keys_nat[h, keys], q_wide[h * HEAD_WIDTH : (h + 1) * HEAD_WIDTH, wide])
                    for h in range(heads_kv)
                ]
                weights = [jnp.exp2(s * SCORE) for s in scores]
                if masked:
                    weights = [jnp.where(allowed, w, 0.0) for w in weights]
                sums = [jnp.sum(w, axis=0, keepdims=True) for w in weights]
                parts = [
                    dot_nn(
                        kv[piece, v_off + h * HEAD_WIDTH : v_off + (h + 1) * HEAD_WIDTH, keys],
                        weights[h].astype(halves),
                    )
                    for h in range(heads_kv)
                ]
                for h in range(heads_kv):
                    total[h : h + 1, wide] += sums[h]
                    acc[h * HEAD_WIDTH : (h + 1) * HEAD_WIDTH, wide] += parts[h]

            for_piece(sc, piece, qb, unit)
            return carry

        @pl.when(piece_used(sc, piece, q_ref.shape[1] // BLK))
        def _():
            for h in range(heads_kv):
                keys_nat[h] = kv[piece, h * HEAD_WIDTH : (h + 1) * HEAD_WIDTH, :].T
            lax.fori_loop(0, q_ref.shape[1] // BLK, query_block, 0)

        return carry

    lax.fori_loop(0, n, key_piece, 0)
    for h, rows, lanes, wrows, wlanes, hd in places:
        row = total[h : h + 1, wlanes]
        out_acc[rows, lanes] = (acc[wrows, wlanes] * ((1.0 / VSCALE) / row)).astype(halves)
        out_sum[hd : hd + 1, lanes] = jnp.log2(row)


VM = pl.BlockSpec(memory_space=pltpu.VMEM)
SM = pl.BlockSpec(memory_space=pltpu.SMEM)
HB = pl.BlockSpec(memory_space=pl.ANY)
HM = pl.BlockSpec(memory_space=pltpu.HBM)


def place_scratch(blocks, tokens):
    return [
        pltpu.SMEM((4, blocks), jnp.int32),
        pltpu.VMEM((1, tokens), jnp.int32),
        pltpu.VMEM((1, tokens), jnp.int32),
    ]


def attend_forward(counts, q_t, pieces):
    n, width = pieces.shape[0], pieces.shape[2]
    heads = q_t.shape[0] // HEAD_WIDTH
    heads_kv = pieces.shape[1] // (2 * HEAD_WIDTH)
    tokens = q_t.shape[1]
    wide = tokens * heads // heads_kv
    return pl.pallas_call(
        functools.partial(fwd_kernel, n, width),
        out_shape=(
            jax.ShapeDtypeStruct(q_t.shape, halves),
            jax.ShapeDtypeStruct((heads, tokens), floats),
        ),
        in_specs=[SM, VM, HM],
        out_specs=(VM, VM),
        scratch_shapes=[
            pltpu.VMEM(pieces.shape, halves),
            pltpu.VMEM((heads_kv, width, HEAD_WIDTH), halves),
            pltpu.VMEM((heads_kv * HEAD_WIDTH, wide), floats),
            pltpu.VMEM((heads_kv, wide), floats),
            pltpu.VMEM((heads_kv * HEAD_WIDTH, wide), halves),
            *place_scratch(n * width // BLK, tokens),
            pltpu.SemaphoreType.DMA((n,)),
        ],
        compiler_params=pltpu.CompilerParams(vmem_limit_bytes=63 << 20),
        name="attend_forward",
    )(counts, q_t, pieces)


def bwd_kernel(n, width, counts, q_ref, do_ref, log_ref, delta_ref, pieces, *refs):
    dq_out = refs[0]
    dkv_out = refs[1]
    kv, dkv, keys_nat, vals_nat, acc, q_wide, do_wide, log_wide, delta_wide, dq_wide, sc, tok_ref, start_ref, sem, osem = refs[2:]
    for i in range(n):
        pltpu.make_async_copy(pieces.at[i], kv.at[i], sem.at[i]).start()
    fill_places(counts, sc, tok_ref, start_ref)
    heads_kv = pieces.shape[1] // (2 * HEAD_WIDTH)
    group = q_ref.shape[0] // (heads_kv * HEAD_WIDTH)
    v_off = heads_kv * HEAD_WIDTH
    places = [
        (h, slice((h * group + g) * HEAD_WIDTH, (h * group + g + 1) * HEAD_WIDTH), slice(qb * BLK, (qb + 1) * BLK),
         slice(h * HEAD_WIDTH, (h + 1) * HEAD_WIDTH), slice((qb * group + g) * BLK, (qb * group + g + 1) * BLK), h * group + g)
        for h in range(heads_kv) for g in range(group) for qb in range(q_ref.shape[1] // BLK)
    ]
    for h, rows, lanes, wrows, wlanes, hd in places:
        q_wide[wrows, wlanes] = q_ref[rows, lanes]
        do_wide[wrows, wlanes] = do_ref[rows, lanes]
        log_wide[h : h + 1, wlanes] = log_ref[hd : hd + 1, lanes]
        delta_wide[h : h + 1, wlanes] = delta_ref[hd : hd + 1, lanes]
        dq_wide[wrows, wlanes] = jnp.zeros((HEAD_WIDTH, BLK), floats)
    out_scale = (1.0 / VSCALE) * HEAD_WIDTH ** (-0.5)

    def key_piece(piece, carry):
        pltpu.make_async_copy(pieces.at[piece], kv.at[piece], sem.at[piece]).wait()
        def query_block(qb, carry):
            lanes = pl.ds(pl.multiple_of(qb * BLK, BLK), BLK)
            wide = pl.ds(pl.multiple_of(qb * (group * BLK), group * BLK), group * BLK)

            def unit(subs, bases, masked):
                keys = slice(subs[0] * BLK, (subs[-1] + 1) * BLK)
                if masked:
                    allowed = allowed_mask(bases, tok_ref, start_ref, lanes)
                    allowed = jnp.concatenate([allowed] * group, axis=1)
                heads = range(heads_kv)
                krows = [slice(h * HEAD_WIDTH, (h + 1) * HEAD_WIDTH) for h in heads]
                vrows = [slice(v_off + h * HEAD_WIDTH, v_off + (h + 1) * HEAD_WIDTH) for h in heads]
                qt = [q_wide[krows[h], wide] for h in heads]
                dot = [do_wide[krows[h], wide] for h in heads]
                scores = [dot_nn(keys_nat[h, keys], qt[h]) for h in heads]
                dprobs = [dot_nn(vals_nat[h, keys], dot[h]) for h in heads]
                weights = [
                    jnp.exp2(scores[h] * SCORE - log_wide[h : h + 1, wide]) for h in heads
                ]
                if masked:
                    weights = [jnp.where(allowed, w, 0.0) for w in weights]
                ds = [
                    (weights[h] * (dprobs[h] - delta_wide[h : h + 1, wide])).astype(halves)
                    for h in heads
                ]
                dv = [dot_nt(dot[h], weights[h].astype(halves)) for h in heads]
                dk = [dot_nt(qt[h], ds[h]) for h in heads]
                dq = [dot_nn(kv[piece, krows[h], keys], ds[h]) for h in heads]
                for h in heads:
                    acc[vrows[h], keys] += dv[h]
                    acc[krows[h], keys] += dk[h]
                    dq_wide[krows[h], wide] += dq[h]

            for_piece(sc, piece, qb, unit)
            return carry

        used = piece_used(sc, piece, q_ref.shape[1] // BLK)

        @pl.when(used)
        def _():
            for h in range(heads_kv):
                rows = slice(h * HEAD_WIDTH, (h + 1) * HEAD_WIDTH)
                vals = slice(v_off + h * HEAD_WIDTH, v_off + (h + 1) * HEAD_WIDTH)
                keys_nat[h] = kv[piece, rows, :].T
                vals_nat[h] = kv[piece, vals, :].T
            acc[...] = jnp.zeros_like(acc)
            lax.fori_loop(0, q_ref.shape[1] // BLK, query_block, 0)
            dkv[piece, 0:v_off, :] = (acc[0:v_off, :] * out_scale).astype(halves)
            dkv[piece, v_off:, :] = acc[v_off:, :].astype(halves)

        @pl.when(jnp.logical_not(used))
        def _():
            dkv[piece] = jnp.zeros(dkv.shape[1:], halves)

        pltpu.make_async_copy(dkv.at[piece], dkv_out.at[piece], osem.at[piece]).start()
        return carry

    lax.fori_loop(0, n, key_piece, 0)
    for h, rows, lanes, wrows, wlanes, hd in places:
        dq_out[rows, lanes] = dq_wide[wrows, wlanes] * out_scale
    for i in range(n):
        pltpu.make_async_copy(dkv.at[i], dkv_out.at[i], osem.at[i]).wait()


def attend_backward(counts, q_t, do_t, log_total, delta, pieces):
    n, width = pieces.shape[0], pieces.shape[2]
    heads_kv = pieces.shape[1] // (2 * HEAD_WIDTH)
    wide = q_t.shape[0] // (heads_kv * HEAD_WIDTH) * q_t.shape[1]
    outs = pl.pallas_call(
        functools.partial(bwd_kernel, n, width),
        out_shape=(
            jax.ShapeDtypeStruct(q_t.shape, floats),
            jax.ShapeDtypeStruct(pieces.shape, halves),
        ),
        in_specs=[SM] + [VM] * 4 + [HM],
        out_specs=(VM, HM),
        scratch_shapes=[
            pltpu.VMEM(pieces.shape, halves),
            pltpu.VMEM(pieces.shape, halves),
            pltpu.VMEM((heads_kv, width, HEAD_WIDTH), halves),
            pltpu.VMEM((heads_kv, width, HEAD_WIDTH), halves),
            pltpu.VMEM(pieces.shape[1:], floats),
            pltpu.VMEM((heads_kv * HEAD_WIDTH, wide), halves),
            pltpu.VMEM((heads_kv * HEAD_WIDTH, wide), halves),
            pltpu.VMEM((heads_kv, wide), floats),
            pltpu.VMEM((heads_kv, wide), floats),
            pltpu.VMEM((heads_kv * HEAD_WIDTH, wide), floats),
            *place_scratch(n * width // BLK, q_t.shape[1]),
            pltpu.SemaphoreType.DMA((n,)),
            pltpu.SemaphoreType.DMA((n,)),
        ],
        compiler_params=pltpu.CompilerParams(vmem_limit_bytes=63 << 20),
        name="attend_backward",
    )(counts, q_t, do_t, log_total, delta, pieces)
    return outs


eps_norm = 1e-05
rope_base = 100000.0
reach_limit = 8


def shifted(block, axis, distance):
    devices = range(lax.axis_size(axis))
    route = [(i - distance, i) for i in devices if i - distance in devices]
    return lax.ppermute(block, axis, route)


def rms_scale(value_vectors, gain_vec):
    return (
        value_vectors
        * lax.rsqrt(jnp.mean(value_vectors * value_vectors, axis=-1, keepdims=True) + eps_norm)
        * gain_vec
    )


def rotary_turn(value_vectors, token_positions, heads):
    half_width = HEAD_WIDTH // 2
    inverse = 1.0 / rope_base ** (jnp.arange(half_width, dtype=jnp.float32) * 2.0 / HEAD_WIDTH)
    angles = token_positions.astype(jnp.float32)[:, None] * inverse[None, :]
    cosine = jnp.cos(angles)[:, None, :]
    sine_part = jnp.sin(angles)[:, None, :]
    shaped = value_vectors.reshape(value_vectors.shape[0], heads, HEAD_WIDTH)
    first_half = shaped[..., :half_width]
    second = shaped[..., half_width:]
    turned = jnp.concatenate(
        [first_half * cosine - second * sine_part, second * cosine + first_half * sine_part],
        axis=-1,
    )
    return turned.reshape(value_vectors.shape)


def swiglu(gate_pre, up_pre):
    return jax.nn.silu(gate_pre) * up_pre


def contract_rows(left_side, right_side):
    return lax.dot_general(
        left_side, right_side, (((0,), (0,)), ((), ())), preferred_element_type=jnp.float32
    )


def contract_cols(left_side, right_side):
    return lax.dot_general(
        left_side, right_side, (((1,), (1,)), ((), ())), preferred_element_type=jnp.float32
    )


def local(
    tokens,
    out_grad,
    segment_ids,
    attn_gain,
    query_weight,
    key_matrix,
    value_matrix,
    output_weight,
    mlp_gain,
    gate_weight,
    up_weight,
    down_weight,
):
    floats = jnp.float32
    halves = jnp.bfloat16
    shard_rows = tokens.shape[0]
    row_len = shard_rows * lax.axis_size("tp")
    row_index = lax.axis_index("dp")
    reach = min(reach_limit, lax.axis_size("dp") // 2)
    heads_q = query_weight.shape[1] // HEAD_WIDTH
    heads_kv = key_matrix.shape[1] // HEAD_WIDTH
    group_width = heads_q // heads_kv
    q_cols = heads_q * HEAD_WIDTH
    kv_cols = heads_kv * HEAD_WIDTH
    score_scale = HEAD_WIDTH ** (-0.5)
    row_first = row_index * row_len
    seg_row = lax.dynamic_slice_in_dim(segment_ids, row_first, row_len)
    index_row = row_first + jnp.arange(row_len, dtype=jnp.int32)
    every_index = jnp.arange(segment_ids.shape[0], dtype=jnp.int32)
    marks = (segment_ids[1:] != segment_ids[:-1]).astype(jnp.int32)
    starts = jnp.concatenate([jnp.zeros((1,), jnp.int32), marks * every_index[1:]])
    is_at = (starts[None, :] <= index_row[:, None]).astype(jnp.int32)
    token_positions = index_row - jnp.max(is_at * starts[None, :], axis=1)
    tokens32 = tokens.astype(floats)
    gain_attn = attn_gain.astype(floats)
    gain_mlp = mlp_gain.astype(floats)
    normed = rms_scale(tokens32, gain_attn).astype(halves)
    normed_full = lax.all_gather(normed, "tp", axis=0, tiled=True)
    joined = jnp.concatenate([query_weight, key_matrix, value_matrix], axis=1)
    projected = jnp.dot(normed_full, joined, preferred_element_type=floats)
    q_linear = projected[:, :q_cols]
    key_linear_out = projected[:, q_cols : q_cols + kv_cols]
    query_vectors = rotary_turn(q_linear, token_positions, heads_q).astype(halves)
    key_vectors = rotary_turn(key_linear_out, token_positions, heads_kv).astype(halves)
    value_vectors = projected[:, q_cols + kv_cols :].astype(halves)
    query_heads = query_vectors.reshape(row_len, heads_kv, group_width, HEAD_WIDTH)
    held_blocks = [(key_vectors, value_vectors)]
    moving = (key_vectors, value_vectors)
    for step_hop in range(reach):
        moving = shifted((moving[0], moving[1]), "dp", 1)
        held_blocks.append(moving)

    def block_mask(step_hop):
        key_row = row_index - step_hop
        seg_keys = lax.dynamic_slice_in_dim(segment_ids, jnp.maximum(key_row, 0) * row_len, row_len)
        key_index = key_row * row_len + jnp.arange(row_len, dtype=jnp.int32)
        return (seg_keys[None, :] == seg_row[:, None]) & (key_index[None, :] <= index_row[:, None])

    def block_needed(step_hop):
        last_key = jnp.maximum((row_index - step_hop + 1) * row_len - 1, 0)
        return (row_index >= step_hop) & (segment_ids[last_key] == seg_row[0])

    block_masks = [block_mask(step_hop) for step_hop in range(reach + 1)]

    def apply_block(step_hop, update, state_in):
        key_block, value_block = held_blocks[step_hop]
        if step_hop == 0:
            return update(state_in, key_block, value_block, block_masks[0])
        return lax.cond(
            block_needed(step_hop),
            update,
            lambda state_kept, key_skip, value_skip, mask_skip: state_kept,
            state_in,
            key_block,
            value_block,
            block_masks[step_hop],
        )

    def scores(key_block, allowed):
        raw_scores = jnp.einsum(
            "qhgd,khd->hgqk",
            query_heads,
            key_block.reshape(row_len, heads_kv, HEAD_WIDTH),
            preferred_element_type=floats,
        )
        return jnp.where(allowed, raw_scores * score_scale, -jnp.inf)

    def add_online(state_in, key_block, value_block, allowed):
        run_max, run_total, run_sum = state_in
        block_scores = scores(key_block, allowed)
        new_max = jnp.maximum(run_max, jnp.max(block_scores, axis=-1))
        factor = jnp.exp(run_max - new_max)
        weights = jnp.exp(block_scores - new_max[..., None])
        run_total = run_total * factor + jnp.sum(weights, axis=-1)
        run_sum = run_sum * jnp.moveaxis(factor, 2, 0)[..., None] + jnp.einsum(
            "hgqk,khd->qhgd",
            weights.astype(halves),
            value_block.reshape(row_len, heads_kv, HEAD_WIDTH),
            preferred_element_type=floats,
        )
        return (new_max, run_total, run_sum)

    online = (
        jnp.full((heads_kv, group_width, row_len), -jnp.inf, floats),
        jnp.zeros((heads_kv, group_width, row_len), floats),
        jnp.zeros((row_len, heads_kv, group_width, HEAD_WIDTH), floats),
    )
    for step_hop in range(reach + 1):
        online = apply_block(step_hop, add_online, online)
    run_max, run_total, run_sum = online
    log_total = (run_max + jnp.log(run_total))[..., None]
    context_heads = (run_sum / jnp.moveaxis(run_total, 2, 0)[..., None]).astype(halves)
    context = context_heads.reshape(row_len, q_cols)
    residual = tokens32 + lax.psum_scatter(
        jnp.dot(context, output_weight, preferred_element_type=floats).astype(jnp.bfloat16),
        "tp",
        scatter_dimension=0,
        tiled=True,
    ).astype(jnp.float32)
    mlp_normed = rms_scale(residual, gain_mlp).astype(halves)
    mlp_full = lax.all_gather(mlp_normed, "tp", axis=0, tiled=True)
    gate_pre = jnp.dot(mlp_full, gate_weight, preferred_element_type=floats)
    up_pre = jnp.dot(mlp_full, up_weight, preferred_element_type=floats)
    hidden = swiglu(gate_pre, up_pre).astype(halves)
    output = residual + lax.psum_scatter(
        jnp.dot(hidden, down_weight, preferred_element_type=floats).astype(jnp.bfloat16),
        "tp",
        scatter_dimension=0,
        tiled=True,
    ).astype(jnp.float32)
    grad_full = lax.all_gather(out_grad, "tp", axis=0, tiled=True)
    grad_hidden = contract_cols(grad_full, down_weight)
    down_grad = contract_rows(grad_full, hidden)
    silu_back = jax.vjp(swiglu, gate_pre, up_pre)[1]
    grad_gate, grad_up = silu_back(grad_hidden)
    grad_gate = grad_gate.astype(halves)
    grad_up = grad_up.astype(halves)
    gate_grad = contract_rows(mlp_full, grad_gate)
    up_grad = contract_rows(mlp_full, grad_up)
    grad_mlp_normed = lax.psum_scatter(
        (contract_cols(grad_gate, gate_weight) + contract_cols(grad_up, up_weight)).astype(
            jnp.bfloat16
        ),
        "tp",
        scatter_dimension=0,
        tiled=True,
    ).astype(jnp.float32)
    mlp_norm_back = jax.vjp(rms_scale, residual, gain_mlp)[1]
    grad_residual_part, mlp_gain_part = mlp_norm_back(grad_mlp_normed)
    grad_residual = out_grad.astype(floats) + grad_residual_part
    attn_grad_full = lax.all_gather(grad_residual.astype(halves), "tp", axis=0, tiled=True)
    output_grad = contract_rows(attn_grad_full, context)
    grad_context = (
        contract_cols(attn_grad_full, output_weight)
        .astype(halves)
        .reshape(row_len, heads_kv, group_width, HEAD_WIDTH)
    )
    delta_col = jnp.einsum(
        "qhgd,qhgd->hgq", grad_context, context_heads, preferred_element_type=floats
    )[..., None]

    def add_grads(state_in, key_block, value_block, allowed):
        query_acc, key_acc, value_acc = state_in
        probabilities = jnp.exp(scores(key_block, allowed) - log_total)
        grad_probs = jnp.einsum(
            "qhgd,khd->hgqk",
            grad_context,
            value_block.reshape(row_len, heads_kv, HEAD_WIDTH),
            preferred_element_type=floats,
        )
        grad_scores = (probabilities * (grad_probs - delta_col)).astype(halves)
        key_heads = key_block.reshape(row_len, heads_kv, HEAD_WIDTH)
        query_acc = (
            query_acc
            + jnp.einsum("hgqk,khd->qhgd", grad_scores, key_heads, preferred_element_type=floats)
            * score_scale
        )
        key_acc = (
            key_acc
            + jnp.einsum(
                "hgqk,qhgd->khd", grad_scores, query_heads, preferred_element_type=floats
            ).reshape(row_len, kv_cols)
            * score_scale
        )
        value_acc = value_acc + jnp.einsum(
            "hgqk,qhgd->khd",
            probabilities.astype(halves),
            grad_context,
            preferred_element_type=floats,
        ).reshape(row_len, kv_cols)
        return (query_acc, key_acc, value_acc)

    query_acc = jnp.zeros((row_len, heads_kv, group_width, HEAD_WIDTH), floats)
    carried = (jnp.zeros((row_len, kv_cols), floats), jnp.zeros((row_len, kv_cols), floats))
    for step_hop in range(reach, 0, -1):
        query_acc, key_acc, value_acc = apply_block(
            step_hop, add_grads, (query_acc, carried[0], carried[1])
        )
        carried = (
            shifted(key_acc.astype(jnp.bfloat16), "dp", -1).astype(key_acc.dtype),
            shifted(value_acc.astype(jnp.bfloat16), "dp", -1).astype(value_acc.dtype),
        )
    query_acc, key_total, value_total = apply_block(
        0, add_grads, (query_acc, carried[0], carried[1])
    )
    query_back = jax.vjp(lambda linear: rotary_turn(linear, token_positions, heads_q), q_linear)[1]
    key_back = jax.vjp(
        lambda linear: rotary_turn(linear, token_positions, heads_kv), key_linear_out
    )[1]
    grad_q_linear = query_back(query_acc.reshape(row_len, q_cols))[0]
    grad_k_linear = key_back(key_total)[0]
    grads_joined = jnp.concatenate([grad_q_linear, grad_k_linear, value_total], axis=1).astype(
        halves
    )
    proj_grad = contract_rows(normed_full, grads_joined)
    grad_normed = lax.psum_scatter(
        contract_cols(grads_joined, joined).astype(jnp.bfloat16),
        "tp",
        scatter_dimension=0,
        tiled=True,
    ).astype(jnp.float32)
    attn_norm_back = jax.vjp(rms_scale, tokens32, gain_attn)[1]
    grad_tokens_part, attn_gain_part = attn_norm_back(grad_normed)
    input_grad = grad_residual + grad_tokens_part
    def scatter_rows(grad):
        return lax.psum_scatter(
            grad.astype(halves), "dp", scatter_dimension=0, tiled=True
        ).astype(floats)

    mlp_sums = scatter_rows(jnp.concatenate([gate_grad, up_grad, down_grad], axis=1))
    ff_cols = gate_weight.shape[1]
    gate_sum = mlp_sums[:, :ff_cols]
    up_sum = mlp_sums[:, ff_cols : 2 * ff_cols]
    down_sum = mlp_sums[:, 2 * ff_cols :]
    attn_sums = scatter_rows(jnp.concatenate([proj_grad, output_grad], axis=1))
    query_sum = attn_sums[:, :q_cols]
    key_sum = attn_sums[:, q_cols : q_cols + kv_cols]
    value_sum = attn_sums[:, q_cols + kv_cols : q_cols + 2 * kv_cols]
    output_sum = attn_sums[:, q_cols + 2 * kv_cols :]
    attn_gain_sum = lax.psum_scatter(attn_gain_part, "dp", scatter_dimension=0, tiled=True)
    mlp_gain_sum = lax.psum_scatter(mlp_gain_part, "dp", scatter_dimension=0, tiled=True)
    attn_gain_total, mlp_gain_total = lax.psum((attn_gain_sum, mlp_gain_sum), "tp")
    return (
        output.astype(halves),
        input_grad,
        attn_gain_total,
        query_sum,
        key_sum,
        value_sum,
        output_sum.T,
        mlp_gain_total,
        gate_sum,
        up_sum,
        down_sum.T,
    )


MESH = pl.DeviceIdType.MESH


def meet(devices):
    barrier = pltpu.get_barrier_semaphore()
    for device in devices:
        pl.semaphore_signal(barrier, inc=1, device_id=device, device_id_type=MESH)
    pl.semaphore_wait(barrier, len(devices))


def tiles(total, step, body):
    def one(i, carry):
        body(pl.ds(pl.multiple_of(i * step, step), step))
        return carry

    lax.fori_loop(0, total // step, one, 0)


CHUNKS = 4


class GroupSum:
    def __init__(self, copies, bufs, place):
        self.copies, self.bufs, self.place = copies, bufs, place

        self.far, self.sums = [], []

    def put_there(self, at, cols, value):
        part_near, _, out_far = self.bufs[:3]
        rows = value.shape[0] // 2
        part_near[at, cols] = value[:rows]
        out_far[at, cols] = value[rows:].astype(halves)

    def put_here(self, cols, value):
        _, part_own, _, out_beside = self.bufs[:4]
        rows = value.shape[0] // 2
        part_own[:, cols] = value[:rows]
        out_beside[:, cols] = value[rows:].astype(halves)

    def send_far(self, at):
        _, _, out_far, _, _, in_near = self.bufs[:6]
        copy = self.copies.make(out_far.at[at], in_near.at[at], self.place.beside)
        copy.start()
        self.far.append(copy)

    def send_beside(self):
        _, _, _, out_beside, _, _, in_own = self.bufs[:7]
        self.side = self.copies.make(out_beside, in_own, self.place.beside)
        self.side.start()

    def send_near(self, count):
        part_near, _, _, _, out_near, in_near, _, in_sum = self.bufs
        self.far[-1].wait_recv()
        rows = part_near.shape[0] // CHUNKS
        for _ in range(count):
            at = pl.ds(len(self.sums) * rows, rows)
            out_near[at, :] = (part_near[at, :] + in_near[at, :].astype(floats)).astype(halves)
            copy = self.copies.make(out_near.at[at], in_sum.at[at], self.place.near)
            copy.start()
            self.sums.append(copy)

    def run(self, product):
        everything = pl.ds(0, self.bufs[0].shape[0])
        product(1, lambda cols, value: self.put_there(everything, cols, value))
        self.send_far(everything)
        product(0, self.put_here)
        self.send_beside()
        self.send_near(CHUNKS)

    def take(self, k):
        part_near, part_own, out_far, out_beside, out_near, in_near, in_own, in_sum = self.bufs
        if k == 0:
            self.side.wait_recv()
        self.sums[k].wait_recv()
        rows = part_own.shape[0] // CHUNKS
        at = pl.ds(k * rows, rows)
        return part_own[at, :] + in_own[at, :].astype(floats) + in_sum[at, :].astype(floats)

    def finish(self):
        for copy in (*self.far, self.side, *self.sums):
            copy.wait_send()


class GroupGather:
    def __init__(self, copies, full, block, place):
        self.copies, self.full, self.block, self.place = copies, full, block, place
        self.sent = []

    def slot(self, n, k):
        rows = self.block // CHUNKS
        return self.full.at[pl.ds(n * self.block + k * rows, rows)]

    def put(self, k):
        for i, (n, device) in enumerate(((2, self.place.near), (1, self.place.beside))):
            copy = self.copies.make(self.slot(0, k), self.slot(n, k), device)
            copy.start()
            self.sent.append((i, copy))

    def wait_here(self):
        for i, copy in self.sent:
            if i == 1:
                copy.wait_recv()

    def wait_there(self, part=0, parts=1):
        near = [copy for i, copy in self.sent if i == 0]
        count = CHUNKS // parts
        relays = []
        for k in range(part * count, (part + 1) * count):
            near[k].wait_recv()
            relay = self.copies.make(self.slot(2, k), self.slot(3, k), self.place.beside)
            relay.start()
            relays.append(relay)
        for relay in relays:
            relay.wait_recv()
        self.sent += [(2, relay) for relay in relays]

    def finish(self):
        for _, copy in self.sent:
            copy.wait_send()


class Copies:
    limit = 96

    def __init__(self, send_sems, recv_sems):
        self.send_sems, self.recv_sems, self.used = send_sems, recv_sems, 0

    def make(self, src, dst, device):
        i = self.used
        self.used += 1
        return pltpu.make_async_remote_copy(
            src_ref=src,
            dst_ref=dst,
            send_sem=self.send_sems.at[i],
            recv_sem=self.recv_sems.at[i],
            device_id=device,
            device_id_type=MESH,
        )


def copy_semaphores():
    return [pltpu.SemaphoreType.DMA((Copies.limit,)), pltpu.SemaphoreType.DMA((Copies.limit,))]


class Place:
    def __init__(self):
        dp, z = lax.axis_index("dp"), lax.axis_index("tp")
        self.dp, self.z = dp, z
        self.c = lax.rem(dp, 2)
        self.x = lax.rem(dp // 2, 2)
        self.y = dp // 4
        far_z = lax.rem(z + 2, 4)
        self.beside = (dp + 1 - 2 * self.c, z)
        self.near = (dp, z + 1 - 2 * lax.rem(z, 2))
        self.far = (dp, far_z)
        self.cross = (self.beside[0], far_z)
        self.over_x = (dp + 2 - 4 * self.x, z)
        self.over_y = (dp + 4 - 8 * self.y, z)
        self.slot = 2 * self.y + self.x
        self.slot_x = 2 * self.y + 1 - self.x
        self.slot_y = 2 - 2 * self.y + self.x
        self.odd = self.c == 1
        self.corner = (self.x == 1) & (self.y == 1)
        self.turn = (self.x == 0) & (self.y == 1)


def rope_tables(counts_ref, inverse_ref, cos_ref, sin_ref):
    index = group_index()
    positions = (index - item_start(counts_ref, index)).astype(floats)
    angles = inverse_ref[...] * positions
    cos_ref[...] = jnp.cos(angles)
    sin_ref[...] = jnp.sin(angles)


class PlaneFetch:
    def __init__(self, copies, place, out, own=None, own_slice=None):
        self.place, self.out = place, out
        rows = out.shape[0] // 8

        def part(slot, ch):
            return pl.ds(slot * (2 * rows) + ch * rows, rows)

        def remote(slot, ch, device):
            at = part(slot, ch)
            return copies.make(out.at[at], out.at[at], device)

        p = place
        self.hop = None
        if own is not None:
            self.hop = [
                copies.make(own.at[part(p.slot, ch)], out.at[part(p.slot, ch)], p.far)
                for ch in range(2)
            ]
        if own_slice is not None:
            self.hop = [
                copies.make(own_slice.at[part(0, ch)], out.at[part(p.slot, ch)], p.far)
                for ch in range(2)
            ]
        self.x = [remote(p.slot, ch, p.over_x) for ch in range(2)]
        self.y = [remote(p.slot, ch, p.over_y) for ch in range(2)]
        self.relay_y = remote(p.slot_x, 0, p.over_y)
        self.relay_x = remote(p.slot_y, 1, p.over_x)

    def start(self):
        @pl.when(self.place.odd)
        def _():
            for copy in self.hop:
                copy.start()

    def forward(self):
        @pl.when(self.place.odd)
        def _():
            for ch in range(2):
                if self.hop is not None:
                    self.hop[ch].wait_recv()
                self.x[ch].start()
                self.y[ch].start()

    def relay(self):
        @pl.when(self.place.odd)
        def _():
            self.x[0].wait_recv()
            self.relay_y.start()
            self.y[1].wait_recv()
            self.relay_x.start()

    def finish(self):
        @pl.when(self.place.odd)
        def _():
            self.x[1].wait_recv()
            self.y[0].wait_recv()
            self.relay_y.wait_recv()
            self.relay_x.wait_recv()

    def drain(self):
        @pl.when(self.place.odd)
        def _():
            for copy in (self.hop or []) + self.x + self.y + [self.relay_y, self.relay_x]:
                copy.wait_send()


class Spread:
    def __init__(self, copies, place, source, slots):
        self.place = place
        self.to_x = copies.make(source, slots[1], place.over_x)
        self.to_y = copies.make(source, slots[2], place.over_y)
        self.relayed = copies.make(slots[2], slots[3], place.over_x)

    def start(self):
        pl.when(self.place.x == 0)(self.to_x.start)
        pl.when(self.place.y == 0)(self.to_y.start)

    def relay(self):
        @pl.when(self.place.corner)
        def _():
            self.to_y.wait_recv()
            self.relayed.start()

    def finish(self):
        p = self.place
        pl.when(p.x == 1)(self.to_x.wait_recv)
        pl.when((p.y == 1) & (p.x == 0))(self.to_y.wait_recv)
        pl.when(p.turn)(self.relayed.wait_recv)
        pl.when(p.x == 0)(self.to_x.wait_send)
        pl.when(p.y == 0)(self.to_y.wait_send)
        pl.when(p.corner)(self.relayed.wait_send)


def first_kernel(
    counts, inverse_ref, tok_ref, grad_ref, gain_ref, wq_in, wk_ref, wv_ref, wo_in, wd_in, wg_in, wu_in,
    q_out, kv_out, n_out, g_full, joined_out, wo_out, wd_out, slice_g, slice_u,
    n_full, joined, own_slice, slices, cos_ref, sin_ref, linear, kv_own, ss, rs, lsem,
):
    place = Place()
    copies = Copies(ss, rs)
    block, width = tok_ref.shape
    two = 2 * block
    q_cols = q_out.shape[0]
    kv_cols = kv_own.shape[1] // 2
    q_lanes = pl.ds(0, q_cols)
    slice_rows = pl.ds(place.slot * own_slice.shape[0], own_slice.shape[0])
    load_q = pltpu.make_async_copy(wq_in, joined.at[:, q_lanes], lsem.at[0])
    load_q_odd = pltpu.make_async_copy(
        wq_in.at[slice_rows], own_slice.at[:, q_lanes], lsem.at[0]
    )
    pl.when(place.c == 0)(load_q.start)
    pl.when(place.odd)(load_q_odd.start)
    rows4 = slice_g.shape[0]
    at_slot = pl.ds(place.slot * rows4, rows4)
    slice_loads = [
        pltpu.make_async_copy(src.at[at_slot], slices.at[i], lsem.at[1 + i])
        for i, src in enumerate((wg_in, wu_in))
    ]
    slice_stores = [
        pltpu.make_async_copy(slices.at[i], dst, lsem.at[6 + i])
        for i, dst in enumerate((slice_g, slice_u))
    ]
    for copy in slice_loads:
        copy.start()

    own_grad = pltpu.make_async_copy(grad_ref, g_full.at[pl.ds(0, block)], lsem.at[3])
    own_grad.start()
    meet((place.beside, place.near, place.far, place.cross, place.over_x, place.over_y))

    @pl.when(place.odd)
    def _():
        lanes = pl.ds(pl.multiple_of(place.slot * own_slice.shape[0], 128), own_slice.shape[0])
        own_slice[:, q_cols : q_cols + kv_cols] = wk_ref[:, lanes].T
        own_slice[:, q_cols + kv_cols :] = wv_ref[:, lanes].T
        load_q_odd.wait()

    fetch_joined = PlaneFetch(copies, place, joined, own_slice=own_slice)
    fetch_o = PlaneFetch(copies, place, wo_out, wo_in)
    fetch_d = PlaneFetch(copies, place, wd_out, wd_in)
    gather = GroupGather(copies, n_full, block, place)
    gather_g = GroupGather(copies, g_full, block, place)
    fetch_joined.start()
    chunk = block // CHUNKS
    for k in range(CHUNKS):
        at = pl.ds(k * chunk, chunk)
        tok = tok_ref[at, :].astype(floats)
        root = lax.rsqrt(jnp.mean(tok * tok, axis=-1, keepdims=True) + eps_norm)
        n_full[at, :] = (tok * root * gain_ref[...]).astype(halves)
        gather.put(k)
    fetch_joined.forward()
    fetch_o.start()
    fetch_d.start()
    @pl.when(place.c == 0)
    def _():
        joined[:, q_cols : q_cols + kv_cols] = wk_ref[...].T
        joined[:, q_cols + kv_cols :] = wv_ref[...].T

    rope_tables(counts, inverse_ref, cos_ref, sin_ref)
    for load, store in zip(slice_loads, slice_stores):
        load.wait()
        store.start()
    fetch_joined.relay()
    gather.wait_here()
    fetch_joined.finish()
    pl.when(place.c == 0)(load_q.wait)
    keep_joined = pltpu.make_async_copy(joined, joined_out, lsem.at[8])
    keep_joined.start()

    def project(k):
        rows = slice(k * two, (k + 1) * two)

        def one(cols):
            linear[cols, :] = dot_nn(n_full[rows, :], joined[:, cols]).T

        tiles(joined.shape[1], 256, one)
        half_width = HEAD_WIDTH // 2
        for head in range((q_cols + kv_cols) // HEAD_WIDTH):
            low = slice(head * HEAD_WIDTH, head * HEAD_WIDTH + half_width)
            high = slice(head * HEAD_WIDTH + half_width, (head + 1) * HEAD_WIDTH)
            one_half, two_half = linear[low, :], linear[high, :]
            cosine, sine = cos_ref[:, rows], sin_ref[:, rows]
            first = (one_half * cosine - two_half * sine).astype(halves)
            second = (two_half * cosine + one_half * sine).astype(halves)
            if head * HEAD_WIDTH < q_cols:
                q_out[low, rows] = first
                q_out[high, rows] = second
            else:
                kv_own[k, low.start - q_cols : low.stop - q_cols, :] = first
                kv_own[k, high.start - q_cols : high.stop - q_cols, :] = second
        kv_own[k, kv_cols:, :] = (linear[q_cols + kv_cols :, :].astype(halves) * VSCALE).astype(halves)

    crossings, spreads_a, spreads_b, kept = [], [], [], []

    def share(k):
        slots = [kv_out.at[8 * k + i] for i in range(8)]
        keep = pltpu.make_async_copy(kv_own.at[k], slots[0], lsem.at[4 + k])
        keep.start()
        kept.append(keep)
        crossing = copies.make(kv_own.at[k], slots[4], place.cross)
        crossing.start()
        crossings.append(crossing)
        spread = Spread(copies, place, kv_own.at[k], slots[:4])
        spread.start()
        spreads_a.append(spread)
        spreads_b.append(Spread(copies, place, slots[4], slots[4:]))

    project(0)
    share(0)
    gather.wait_there()
    own_grad.wait()
    for k in range(CHUNKS):
        gather_g.put(k)
    project(1)
    share(1)
    keep_n = pltpu.make_async_copy(n_full, n_out, lsem.at[9])
    keep_n.start()
    fetch_o.forward()
    fetch_d.forward()
    spreads_a[0].relay()
    spreads_a[1].relay()
    crossings[0].wait_recv()
    spreads_b[0].start()
    fetch_o.relay()
    fetch_d.relay()
    gather_g.wait_there()
    spreads_b[0].relay()
    crossings[1].wait_recv()
    spreads_b[1].start()
    spreads_b[1].relay()
    fetch_o.finish()
    fetch_d.finish()
    gather_g.wait_here()
    for spread in spreads_a + spreads_b:
        spread.finish()
    for copy in kept + slice_stores + [keep_joined, keep_n]:
        copy.wait()
    for copy in crossings:
        copy.wait_send()
    for fetch in (fetch_joined, fetch_o, fetch_d):
        fetch.drain()
    gather.finish()
    gather_g.finish()


def first_part(counts, inverse, tokens, out_grad, gain, projections, weights):
    block, width = tokens.shape
    group = 4 * block
    shape = jax.ShapeDtypeStruct
    hidden = weights[2].shape[1]
    part = (width // 4, hidden)
    half_width = HEAD_WIDTH // 2
    q_cols, kv_cols = projections[0].shape[1], projections[1].shape[0]
    joined_cols = q_cols + 2 * kv_cols
    out_shape = (
        shape((q_cols, group), halves),
        shape((16, 2 * kv_cols, 2 * block), halves),
        shape((group, width), halves),
        shape((group, width), halves),
        shape((width, joined_cols), halves),
        shape(weights[0].shape, halves),
        shape(weights[1].shape, halves),
        shape(part, halves),
        shape(part, halves),
    )
    return pl.pallas_call(
        first_kernel,
        out_shape=out_shape,
        in_specs=[SM] + [VM] * 4 + [HB, VM, VM] + [HB] * 4,
        out_specs=(VM, HM, HM, VM, HM, HM, HM, HM, HM),
        scratch_shapes=[
            pltpu.VMEM((group, width), halves),
            pltpu.VMEM((width, joined_cols), halves),
            pltpu.VMEM((width // 4, joined_cols), halves),
            pltpu.VMEM((2,) + part, halves),
            pltpu.VMEM((half_width, group), floats),
            pltpu.VMEM((half_width, group), floats),
            pltpu.VMEM((joined_cols, 2 * block), floats),
            pltpu.VMEM((2, 2 * kv_cols, 2 * block), halves),
            *copy_semaphores(),
            pltpu.SemaphoreType.DMA((10,)),
        ],
        compiler_params=pltpu.CompilerParams(
            collective_id=2, has_side_effects=True, vmem_limit_bytes=63 << 20
        ),
        name="first",
    )(counts, inverse, tokens, out_grad, gain, *projections, *weights)


class PlaneSum:
    def __init__(self, copies, place, x_first, bufs, sent=None, come=None):
        self.place, self.bufs, self.x_first = place, bufs, x_first
        half, keep, come_two, home_one, home_two = bufs
        first, second = (place.over_x, place.over_y) if x_first else (place.over_y, place.over_x)
        self.at = place.y if x_first else place.x
        self.one = None if sent is None else copies.make(sent, come, first)
        self.two = copies.make(half, come_two, second)
        rows = home_one.shape[0]
        c = place.c
        home = (c * place.cross[0] + (1 - c) * place.beside[0], c * place.cross[1] + (1 - c) * place.beside[1])
        self.to_home = copies.make(half.at[pl.ds((1 - c) * rows, rows)], home_one, home)
        self.to_far = copies.make(half.at[pl.ds(rows, rows)], home_two, place.far)

    def cross_second(self, kept, come):
        if self.one is not None:
            self.one.wait()
        half, keep, come_two, home_one, home_two = self.bufs
        at = self.at
        half[...] = (kept[1 - at].astype(floats) + come[1 - at].astype(floats)).astype(halves)
        self.two.start()
        keep[...] = (kept[at].astype(floats) + come[at].astype(floats)).astype(halves)

    def go_home(self, exchanged=True):
        half, keep, come_two, home_one, home_two = self.bufs
        if exchanged:
            self.two.wait()
        half[...] = (keep[...].astype(floats) + come_two[...].astype(floats)).astype(halves)
        self.to_home.start()
        pl.when(self.place.odd)(self.to_far.start)

    def finish(self, out):
        half, keep, come_two, home_one, home_two = self.bufs
        rows = home_one.shape[0]
        self.to_home.wait()

        @pl.when(self.place.c == 0)
        def _():
            out[...] = half[:rows, :].astype(floats) + home_one[...].astype(floats)

        @pl.when(self.place.odd)
        def _():
            self.to_far.wait()
            out[...] = home_one[...].astype(floats) + home_two[...].astype(floats)


def plane_buffers(rows, cols):
    full = pltpu.VMEM((rows, cols), halves)
    part = pltpu.VMEM((rows // 2, cols), halves)
    return [full, full, full, part, part]


def outer_blocks(place, x_first, left, right, send_ref, keep_ref, on_sent):
    rows = left.shape[1] // 4
    for kept in (False, True):
        for i in range(2):
            if x_first:
                block = 2 * i + (place.x if kept else 1 - place.x)
            else:
                block = 2 * (place.y if kept else 1 - place.y) + i
            cols = pl.ds(pl.multiple_of(block * rows, 128), rows)
            value = lax.dot_general(
                left[:, cols], right, (((0,), (0,)), ((), ())), preferred_element_type=floats
            ).astype(halves)
            (keep_ref if kept else send_ref)[i] = value
        if not kept:
            on_sent()


def mid_kernel(ctx_ref, tok_ref, gain_ref, g_full, weight_refs, outs, scratch):
    (res_out, gres_out, e_full, near_out, down_half, down_mine, gate_keep, gate_send, up_keep, up_send,
     dctx_out, delta_out, gain_out) = outs
    (ctx, m_full, dh, hid, dgate, dup, w_o, w_d, w_g, w_u, down_send, down_keep, down_come, part_out, far_in, own_in, *bufs, ss, rs, wsem) = scratch
    place = Place()
    copies = Copies(ss, rs)
    block, width = tok_ref.shape
    two = 2 * block
    hidden = w_g.shape[1]
    wo_ref, wd_ref, wg_ref, wu_ref, wo_got, wd_got, slice_g, slice_u = weight_refs
    first_loads = [
        pltpu.make_async_copy(src, dst, wsem.at[i])
        for i, (src, dst) in enumerate(((wo_ref, w_o), (wd_ref, w_d)))
    ]
    first_loads_odd = [
        pltpu.make_async_copy(src, dst, wsem.at[i])
        for i, (src, dst) in enumerate(((wo_got, w_o), (wd_got, w_d)))
    ]

    def wait_first(i):
        pl.when(place.c == 0)(first_loads[i].wait)
        pl.when(place.odd)(first_loads_odd[i].wait)

    rows4 = slice_g.shape[0]
    at_slot = pl.ds(place.slot * rows4, rows4)
    loads = [
        pltpu.make_async_copy(src, dst, wsem.at[2 + i])
        for i, (src, dst) in enumerate(((wg_ref, w_g), (wu_ref, w_u)))
    ]
    loads_odd = [
        pltpu.make_async_copy(src, dst.at[at_slot], wsem.at[2 + i])
        for i, (src, dst) in enumerate(((slice_g, w_g), (slice_u, w_u)))
    ]

    @pl.when(place.c == 0)
    def _():
        for copy in first_loads + loads:
            copy.start()

    @pl.when(place.odd)
    def _():
        for copy in first_loads_odd + loads_odd:
            copy.start()

    ctx[...] = ctx_ref[...].T
    meet((place.beside, place.near, place.over_x, place.over_y))
    fetches = [PlaneFetch(copies, place, w_g), PlaneFetch(copies, place, w_u)]

    @pl.when(place.odd)
    def _():
        for copy in loads_odd:
            copy.wait()

    for fetch in fetches:
        fetch.forward()
    sum_one = GroupSum(copies, bufs, place)
    gather_one = GroupGather(copies, m_full, block, place)
    sum_two = GroupSum(copies, bufs, place)
    gather_two = GroupGather(copies, e_full, block, place)

    def project(k, put):
        rows = slice(k * two, (k + 1) * two)
        tiles(width, 256, lambda cols: put(cols, dot_nn(ctx[rows, :], w_o[:, cols])))

    wait_first(0)
    sum_one.run(project)
    wait_first(1)

    def back_hidden(cols):
        for rows in (slice(0, two), slice(two, 2 * two)):
            dh[rows, cols] = dot_nt(g_full[rows, :], w_d[cols, :]).astype(halves)

    tiles(hidden, 256, back_hidden)
    chunk = block // CHUNKS
    for k in range(CHUNKS):
        at = pl.ds(k * chunk, chunk)
        res = tok_ref[at, :].astype(floats) + sum_one.take(k)
        res_out[at, :] = res
        root = lax.rsqrt(jnp.mean(res * res, axis=-1, keepdims=True) + eps_norm)
        m_full[at, :] = (res * root * gain_ref[...]).astype(halves)
        gather_one.put(k)
        if k == 1:
            for fetch in fetches:
                fetch.relay()
    sum_one.finish()

    def there(h):
        rows = block // 2
        return [slice(two + h * rows, two + (h + 1) * rows), slice(3 * block + h * rows, 3 * block + (h + 1) * rows)]

    def read(ref, parts):
        values = [ref[rows, :] for rows in parts]
        return values[0] if len(values) == 1 else jnp.concatenate(values, axis=0)

    def write(ref, parts, cols, value):
        rows = value.shape[0] // len(parts)
        for i, part in enumerate(parts):
            ref[part, cols] = value[i * rows : (i + 1) * rows]

    def activate(parts):
        def one(cols):
            left = read(m_full, parts)
            gate_pre = dot_nn(left, w_g[:, cols])
            up_pre = dot_nn(left, w_u[:, cols])
            back = [dh[rows, cols] for rows in parts]
            back = (back[0] if len(back) == 1 else jnp.concatenate(back, axis=0)).astype(floats)
            sigma = 1.0 / (1.0 + jnp.exp(-gate_pre))
            silu = gate_pre * sigma
            write(hid, parts, cols, (silu * up_pre).astype(halves))
            write(dgate, parts, cols, (back * up_pre * (sigma + silu * (1.0 - sigma))).astype(halves))
            write(dup, parts, cols, (back * silu).astype(halves))

        tiles(hidden, 256, one)

    def partial_out(parts):
        def one(cols):
            write(part_out, parts, cols, dot_nn(read(hid, parts), w_d[:, cols]).astype(halves))

        tiles(width, 256, one)

    def back_norm(parts, put):
        def one(cols):
            put(cols, dot_nt(read(dgate, parts), w_g[cols, :]) + dot_nt(read(dup, parts), w_u[cols, :]))

        tiles(width, 256, one)

    for fetch in fetches:
        fetch.finish()

    @pl.when(place.c == 0)
    def _():
        for copy in loads:
            copy.wait()

    here = [slice(0, two)]
    gather_one.wait_here()
    activate(here)
    partial_out(here)
    whole = [slice(two, 2 * two)]
    gather_one.wait_there()
    at = pl.ds(0, block)
    activate(whole)
    back_norm(whole, lambda cols, value: sum_two.put_there(at, cols, value))
    sum_two.send_far(at)
    gather_one.finish()
    back_norm(here, sum_two.put_here)
    sum_two.send_beside()
    sum_two.send_near(CHUNKS)
    partial_out(whole)
    to_side = [
        copies.make(part_out.at[pl.ds(3 * block, block)], far_in, place.beside),
        copies.make(part_out.at[pl.ds(block, block)], own_in, place.beside),
    ]
    for copy in to_side:
        copy.start()
    down_over = copies.make(down_send, down_come, place.over_x)
    outer_blocks(place, True, g_full, hid[...], down_send, down_keep, down_over.start)
    outer_blocks(place, False, m_full, dgate[...], gate_send, gate_keep, lambda: None)
    gain_out[...] = jnp.zeros_like(gain_out)
    for k in range(CHUNKS):
        at = pl.ds(k * chunk, chunk)
        back = sum_two.take(k)
        res = res_out[at, :]
        root = lax.rsqrt(jnp.mean(res * res, axis=-1, keepdims=True) + eps_norm)
        weighted = back * gain_ref[...]
        slope = jnp.mean(weighted * res, axis=-1, keepdims=True)
        grad = g_full[at, :].astype(floats) + root * weighted - res * (root * root * root * slope)
        gain_out[...] += jnp.sum(back * res * root, axis=0, keepdims=True)
        gres_out[at, :] = grad
        e_full[at, :] = grad.astype(halves)
        gather_two.put(k)
    sum_two.finish()
    outer_blocks(place, True, m_full, dup[...], up_send, up_keep, lambda: None)

    def back_context(parts):
        grad = dot_nt(w_o[...], read(e_full, parts)).astype(halves)
        rows = grad.shape[1] // len(parts)
        for i, part in enumerate(parts):
            piece = grad[:, i * rows : (i + 1) * rows]
            dctx_out[:, part] = piece
            prod = piece.astype(floats) * ctx_ref[:, part].astype(floats)
            for hd in range(delta_out.shape[0]):
                delta_out[hd : hd + 1, part] = VSCALE * jnp.sum(
                    prod[hd * HEAD_WIDTH : (hd + 1) * HEAD_WIDTH], axis=0, keepdims=True
                )

    for copy in to_side:
        copy.wait()
    for k in range(CHUNKS):
        at = pl.ds(k * chunk, chunk)
        near = pl.ds(two + k * chunk, chunk)
        near_out[at, :] = (part_out[near, :].astype(floats) + far_in[at, :].astype(floats)).astype(halves)
        res_out[at, :] += part_out[at, :].astype(floats) + own_in[at, :].astype(floats)
    gather_two.wait_here()
    back_context(here)
    gather_two.wait_there(0, 2)
    back_context(there(0))
    down_over.wait()
    at = place.y
    down_half[...] = (down_keep[1 - at].astype(floats) + down_come[1 - at].astype(floats)).astype(halves)
    down_mine[...] = (down_keep[at].astype(floats) + down_come[at].astype(floats)).astype(halves)
    gather_two.wait_there(1, 2)
    back_context(there(1))
    gather_two.finish()
    for fetch in fetches:
        fetch.drain()


def middle(context_t, tokens, gain, grad_full, weights):
    q_cols, group = context_t.shape
    block, width = tokens.shape
    hidden = weights[2].shape[1]
    shape = jax.ShapeDtypeStruct
    out_shape = (
        shape((block, width), floats),
        shape((block, width), floats),
        shape((group, width), halves),
        shape((block, width), halves),
        *[shape((width // 4, hidden), halves)] * 2,
        *[shape((2, width // 4, hidden), halves)] * 4,
        shape((q_cols, group), halves),
        shape((q_cols // HEAD_WIDTH, group), floats),
        shape((1, width), floats),
    )
    scratch = [
        pltpu.VMEM((group, q_cols), halves),
        pltpu.VMEM((group, width), halves),
        *[pltpu.VMEM((group, hidden), halves)] * 4,
        *[pltpu.VMEM(weight.shape, halves) for weight in weights[:4]],
        *[pltpu.VMEM((2, width // 4, hidden), halves)] * 3,
        pltpu.VMEM((group, width), halves),
        *[pltpu.VMEM((block, width), halves)] * 2,
        *[pltpu.VMEM((block, width), floats)] * 2,
        *[pltpu.VMEM((block, width), halves)] * 6,
        *copy_semaphores(),
        pltpu.SemaphoreType.DMA((4,)),
    ]

    def kernel(*refs):
        mid_kernel(*refs[:4], refs[4:12], refs[12:25], refs[25:])

    return pl.pallas_call(
        kernel,
        out_shape=out_shape,
        in_specs=[VM] * 4 + [HB] * 8,
        out_specs=(VM,) * 13,
        scratch_shapes=scratch,
        compiler_params=pltpu.CompilerParams(
            collective_id=1, has_side_effects=True, vmem_limit_bytes=63 << 20
        ),
        name="middle",
    )(context_t, tokens, gain, grad_full, *weights)


def last_kernel(ins, outs, scratch):
    (counts, inverse_ref, dq_ref, dkv_ref, n_ref, joined_ref, tok_ref, gain_ref, gres_ref, e_ref, ctx_ref,
     gain_mlp_ref, *mlp) = ins
    (in_grad, gains_out, gate_out, up_out, down_out, q_out, kv_out, o_out) = outs
    (full, ctx, d_lin, acc_a, acc_b, own, x_in, y_in, rel_in, cross_in, cross_out, kept, come,
     gains, gains_in, cos_ref, sin_ref, joined, *rest) = scratch
    bufs_mlp = [rest[5 * i : 5 * i + 5] for i in range(3)]
    rest = rest[15:]
    bufs_attn = [rest[8 * i : 8 * i + 8] for i in range(3)]
    rest = rest[24:]
    sum_bufs, (ss, rs, lsem) = rest[:8], rest[8:]
    place = Place()
    copies = Copies(ss, rs)
    block, width = tok_ref.shape
    two = 2 * block
    q_cols = dq_ref.shape[0]
    kv_cols = own.shape[1] // 2
    half_width = HEAD_WIDTH // 2

    load_e = pltpu.make_async_copy(e_ref, full, lsem.at[0])
    load_e.start()
    load_joined = pltpu.make_async_copy(joined_ref, joined, lsem.at[11])
    load_joined.start()
    order = (4, 12, 0, 8)
    own_loads = [
        pltpu.make_async_copy(dkv_ref.at[at], own.at[i], lsem.at[1 + i]) for i, at in enumerate(order)
    ]
    y_loads = [
        pltpu.make_async_copy(dkv_ref.at[at + 2], y_in.at[i], lsem.at[5 + i])
        for i, at in enumerate(order)
    ]
    for copy in own_loads:
        copy.start()

    @pl.when(place.corner)
    def _():
        for copy in y_loads:
            copy.start()

    def load_mlp(i):
        return [
            pltpu.make_async_copy(mlp[2 * i], kept, lsem.at[9]),
            pltpu.make_async_copy(mlp[2 * i + 1], come, lsem.at[10]),
        ]

    down_loads = [
        pltpu.make_async_copy(mlp[i], bufs_mlp[0][1 + i], lsem.at[12 + i]) for i in range(2)
    ]
    loads = load_mlp(1)
    for copy in down_loads + loads:
        copy.start()
    gains[0, 0:1, :] = gain_mlp_ref[...]
    gains[0, 1:2, :] = jnp.zeros_like(gain_mlp_ref)
    meet((place.beside, place.near, place.far, place.cross, place.over_x, place.over_y))

    back_rel = [copies.make(dkv_ref.at[at + 3], rel_in.at[i], place.over_x) for i, at in enumerate(order)]
    back_x = [copies.make(dkv_ref.at[at + 1], x_in.at[i], place.over_x) for i, at in enumerate(order)]
    back_y = [copies.make(dkv_ref.at[at + 2], y_in.at[i], place.over_y) for i, at in enumerate(order)]
    back_sum = [copies.make(y_in.at[i], y_in.at[i], place.over_y) for i in range(4)]
    crossing = [copies.make(cross_out.at[i], cross_in.at[i], place.cross) for i in range(2)]
    def start_back(i):
        pl.when(place.turn)(back_rel[i].start)
        pl.when(place.x == 1)(back_x[i].start)
        pl.when(place.turn)(back_y[i].start)

    start_back(0)
    start_back(1)

    def corner_sum(i):
        @pl.when(place.corner)
        def _():
            back_rel[i].wait_recv()
            y_loads[i].wait()
            y_in[i] = (y_in[i].astype(floats) + rel_in[i].astype(floats)).astype(halves)
            back_sum[i].start()

    def home_sum(i, put):
        own_loads[i].wait()
        acc_b[...] = own[i].astype(floats)

        @pl.when(place.x == 0)
        def _():
            back_x[i].wait_recv()
            acc_b[...] += x_in[i].astype(floats)

        @pl.when((place.y == 0) & (place.x == 0))
        def _():
            back_y[i].wait_recv()
            acc_b[...] += y_in[i].astype(floats)

        @pl.when((place.y == 0) & (place.x == 1))
        def _():
            back_sum[i].wait_recv()
            acc_b[...] += y_in[i].astype(floats)

        put()

    sums = []
    for i, x_first in enumerate((True, False, True)):
        sums.append(PlaneSum(copies, place, x_first, bufs_mlp[i]))
    for copy in down_loads:
        copy.wait()
    sums[0].go_home(exchanged=False)
    for i in (1, 2):
        for copy in loads:
            copy.wait()
        sums[i].cross_second(kept, come)
        if i == 1:
            loads = load_mlp(2)
            for copy in loads:
                copy.start()
            corner_sum(0)
            start_back(2)
            start_back(3)
    ctx[...] = ctx_ref[...].T
    rope_tables(counts, inverse_ref, cos_ref, sin_ref)

    attn_sums = []
    for i, x_first in enumerate((False, True, False)):
        sent, keep, got = bufs_attn[i][:3]
        attn_sums.append(PlaneSum(copies, place, x_first, bufs_attn[i][3:], sent, got))

    def attn_grad(i, left, right):
        sent, keep, got = bufs_attn[i][:3]
        outer_blocks(place, attn_sums[i].x_first, left, right, sent, keep, attn_sums[i].one.start)

    corner_sum(1)
    load_e.wait()
    attn_grad(0, full, ctx[...])
    load_n = pltpu.make_async_copy(n_ref, full, lsem.at[0])
    load_n.start()

    def cross_back(i):
        def put():
            cross_out[i] = acc_b[...].astype(halves)
            crossing[i].start()

        home_sum(i, put)

    def unturn(value, at, first_row):
        low, high = value[:half_width], value[half_width:]
        cosine, sine = cos_ref[:, at], sin_ref[:, at]
        turned = jnp.concatenate([low * cosine + high * sine, high * cosine - low * sine], axis=0)
        d_lin[first_row : first_row + HEAD_WIDTH, at] = turned.astype(halves)

    cross_back(0)
    corner_sum(2)
    everything = slice(0, 2 * two)
    for head in range(q_cols // HEAD_WIDTH):
        unturn(dq_ref[head * HEAD_WIDTH : (head + 1) * HEAD_WIDTH, :], everything, head * HEAD_WIDTH)
    cross_back(1)
    corner_sum(3)
    load_n.wait()
    attn_grad(1, full, d_lin[:q_cols, :].T)
    for plane in sums[1:]:
        plane.go_home()

    def second(i):
        sent, keep, got = bufs_attn[i][:3]
        attn_sums[i].cross_second(keep, got)

    second(0)

    def keep_a(k):
        def put():
            acc_a[:, k * two : (k + 1) * two] = acc_b[...]

        home_sum(2 + k, put)

    keep_a(0)
    keep_a(1)
    second(1)
    attn_sums[0].go_home()
    for k in range(2):
        crossing[k].wait_recv()
        lanes = slice(k * two, (k + 1) * two)
        total = acc_a[:, lanes] + cross_in[k].astype(floats)
        for head in range(kv_cols // HEAD_WIDTH):
            rows = slice(head * HEAD_WIDTH, (head + 1) * HEAD_WIDTH)
            unturn(total[rows], lanes, q_cols + head * HEAD_WIDTH)
        d_lin[q_cols + kv_cols :, lanes] = total[kv_cols:].astype(halves)

    group_sum = GroupSum(copies, sum_bufs, place)
    load_joined.wait()

    def back_norm(k, put):
        rows = slice(k * two, (k + 1) * two)
        left = d_lin[:, rows].T

        def one(cols):
            value = dot_nt(left, joined[cols, :])
            put(cols, value)
            gains[0, 1:2, cols] += jnp.sum(value * full[rows, cols].astype(floats), axis=0, keepdims=True)

        tiles(width, 256, one)

    group_sum.run(back_norm)
    gains[0, 1:2, :] = gains[0, 1:2, :] / gain_ref[...]
    attn_grad(2, full, d_lin[q_cols:, :].T)
    attn_sums[1].go_home()
    for stage, device in enumerate((place.beside, place.over_x, place.over_y, place.near, place.far)):
        copy = copies.make(gains.at[stage], gains_in.at[stage], device)
        copy.start()
        copy.wait()
        if stage < 4:
            gains[stage + 1] = gains[stage] + gains_in[stage]
        else:
            gains_out[...] = gains[stage] + gains_in[stage]
        if stage == 2:
            second(2)
    for plane, out in zip(sums, (down_out, gate_out, up_out)):
        plane.finish(out)
    attn_sums[2].go_home()
    chunk = block // CHUNKS
    for k in range(CHUNKS):
        at = pl.ds(k * chunk, chunk)
        back = group_sum.take(k)
        tok = tok_ref[at, :].astype(floats)
        root = lax.rsqrt(jnp.mean(tok * tok, axis=-1, keepdims=True) + eps_norm)
        weighted = back * gain_ref[...]
        slope = jnp.mean(weighted * tok, axis=-1, keepdims=True)
        in_grad[at, :] = gres_ref[at, :] + root * weighted - tok * (root * root * root * slope)
    for plane, out in zip(attn_sums, (o_out, q_out, kv_out)):
        plane.finish(out)
    group_sum.finish()
    for i in range(4):
        pl.when(place.turn)(back_rel[i].wait_send)
        pl.when(place.x == 1)(back_x[i].wait_send)
        pl.when(place.turn)(back_y[i].wait_send)
        pl.when(place.corner)(back_sum[i].wait_send)
    for copy in crossing:
        copy.wait_send()


def last_part(counts, inverse, d_query_t, d_kv, normed, joined, tokens, gain, gres, e_full, context_t, gain_mlp, mlp):
    block, width = tokens.shape
    group = 4 * block
    q_cols, kv_all = d_query_t.shape[0], d_kv.shape[1]
    kv_cols = kv_all // 2
    hidden = mlp[0].shape[1]
    per = width // 8
    shape = jax.ShapeDtypeStruct
    out_shape = (
        shape((block, width), floats),
        shape((2, width), floats),
        *[shape((per, hidden), floats)] * 3,
        shape((per, q_cols), floats),
        shape((per, kv_all), floats),
        shape((per, q_cols), floats),
    )
    piece = (kv_all, 2 * block)
    scratch = [
        pltpu.VMEM((group, width), halves),
        pltpu.VMEM((group, q_cols), halves),
        pltpu.VMEM((joined.shape[1], group), halves),
        pltpu.VMEM((kv_all, group), floats),
        pltpu.VMEM(piece, floats),
        *[pltpu.VMEM((4,) + piece, halves)] * 4,
        *[pltpu.VMEM((2,) + piece, halves)] * 2,
        *[pltpu.VMEM((2, width // 4, hidden), halves)] * 2,
        *[pltpu.VMEM((5, 2, width), floats)] * 2,
        *[pltpu.VMEM((HEAD_WIDTH // 2, group), floats)] * 2,
        pltpu.VMEM(joined.shape, halves),
    ]
    for _ in range(3):
        scratch += plane_buffers(width // 4, hidden)
    for cols in (q_cols, q_cols, kv_all):
        scratch += [pltpu.VMEM((2, width // 4, cols), halves)] * 3 + plane_buffers(width // 4, cols)
    scratch += [
        *[pltpu.VMEM((block, width), floats)] * 2,
        *[pltpu.VMEM((block, width), halves)] * 6,
        *copy_semaphores(),
        pltpu.SemaphoreType.DMA((14,)),
    ]

    def kernel(*refs):
        last_kernel(refs[:18], refs[18:26], refs[26:])

    return pl.pallas_call(
        kernel,
        out_shape=out_shape,
        in_specs=[SM, VM, VM, HM, HM, HM, VM, VM, VM, HM, VM, VM] + [HM] * 6,
        out_specs=(VM,) * 8,
        scratch_shapes=scratch,
        compiler_params=pltpu.CompilerParams(
            collective_id=3, has_side_effects=True, vmem_limit_bytes=63 << 20
        ),
        name="last",
    )(counts, inverse, d_query_t, d_kv, normed, joined, tokens, gain, gres, e_full, context_t, gain_mlp, *mlp)


def finish_kernel(*refs):
    base, near, kv_sum, *ready = refs[:9]
    output, k_out, v_out, *outs = refs[9:18]
    out_buf, k_buf, v_buf, sem = refs[18:]
    copies = [pltpu.make_async_copy(src, dst, sem.at[i]) for i, (src, dst) in enumerate(zip(ready, outs))]
    for copy in copies:
        copy.start()
    out_buf[...] = (base[...] + near[...].astype(floats)).astype(halves)
    kv_cols = k_buf.shape[1]
    k_buf[...] = kv_sum[:, :kv_cols]
    v_buf[...] = kv_sum[:, kv_cols:]
    more = [
        pltpu.make_async_copy(src, dst, sem.at[len(copies) + i])
        for i, (src, dst) in enumerate(((out_buf, output), (k_buf, k_out), (v_buf, v_out)))
    ]
    for copy in more:
        copy.start()
    for copy in copies + more:
        copy.wait()


def finish(base, near, kv_sum, *ready):
    shape = jax.ShapeDtypeStruct
    rows, cols = kv_sum.shape
    small = (rows, cols // 2)
    return pl.pallas_call(
        finish_kernel,
        out_shape=(
            shape(base.shape, halves),
            shape(small, floats),
            shape(small, floats),
            *[shape(a.shape, a.dtype) for a in ready],
        ),
        in_specs=[VM] * (3 + len(ready)),
        out_specs=(HM,) * (3 + len(ready)),
        scratch_shapes=[
            pltpu.VMEM(base.shape, halves),
            pltpu.VMEM(small, floats),
            pltpu.VMEM(small, floats),
            pltpu.SemaphoreType.DMA((3 + len(ready),)),
        ],
        compiler_params=pltpu.CompilerParams(vmem_limit_bytes=63 << 20),
        name="finish",
    )(base, near, kv_sum, *ready)


def routes(target):
    pairs = []
    for index in range(32):
        dp, z = divmod(index, 4)
        there = target(dp // 4, dp // 2 % 2, dp % 2, z)
        if there is not None:
            y, x, c, z = there
            pairs.append((index, (y * 4 + x * 2 + c) * 4 + z))
    return pairs


ROUTES = {
    "core": routes(lambda y, x, c, z: (y, x, 1 - c, z)),
    "x": routes(lambda y, x, c, z: (y, 1 - x, c, z)),
    "y": routes(lambda y, x, c, z: (1 - y, x, c, z)),
    "near": routes(lambda y, x, c, z: (y, x, c, z ^ 1)),
    "far": routes(lambda y, x, c, z: (y, x, c, z ^ 2)),
    "cross": routes(lambda y, x, c, z: (y, x, 1 - c, z ^ 2)),
    "odd_far": routes(lambda y, x, c, z: (y, x, c, z ^ 2) if c else None),
    "odd_x": routes(lambda y, x, c, z: (y, 1 - x, c, z) if c else None),
    "odd_y": routes(lambda y, x, c, z: (1 - y, x, c, z) if c else None),
    "odd_xy": routes(lambda y, x, c, z: (1 - y, 1 - x, c, z) if c else None),
    "home": routes(lambda y, x, c, z: (y, x, 0, z ^ 2) if c else (y, x, 1, z)),
    "x_up": routes(lambda y, x, c, z: None if x else (y, 1, c, z)),
    "y_up": routes(lambda y, x, c, z: None if y else (1, x, c, z)),
    "x_down": routes(lambda y, x, c, z: (y, 0, c, z) if x else None),
    "y_down": routes(lambda y, x, c, z: (0, x, c, z) if y else None),
    "relay": routes(lambda y, x, c, z: (1, 0, c, z) if x and y else None),
    "unrelay": routes(lambda y, x, c, z: (1, 1, c, z) if y and not x else None),
}


def send(block, way):
    return lax.ppermute(block, ("dp", "tp"), ROUTES[way])


def local_regrouped(
    tokens,
    out_grad,
    segment_ids,
    attn_gain,
    query_weight,
    key_matrix,
    value_matrix,
    output_weight,
    mlp_gain,
    gate_weight,
    up_weight,
    down_weight,
):
    block = tokens.shape[0]
    dp = lax.axis_index("dp")
    half_width = HEAD_WIDTH // 2
    gain_attn, gain_mlp = attn_gain.astype(floats)[None, :], mlp_gain.astype(floats)[None, :]
    counts = jnp.sum(
        (segment_ids[None, :] < jnp.arange(1, 4, dtype=jnp.int32)[:, None]).astype(jnp.int32), axis=1
    )
    inverse = 1.0 / rope_base ** (jnp.arange(half_width, dtype=floats) * 2.0 / HEAD_WIDTH)
    inverse = inverse[:, None]
    q_t, pieces, normed_full, grad_full, joined, weight_o, weight_d, slice_g, slice_u = first_part(
        counts, inverse, tokens, out_grad, gain_attn,
        (query_weight, key_matrix.T, value_matrix.T),
        (output_weight, down_weight, gate_weight, up_weight),
    )
    slices = [send(part, "odd_far") for part in (slice_g, slice_u)]
    context_t, log_total = attend_forward(counts, q_t, pieces)
    (
        out_base, grad_residual, attn_grad_full, out_near, down_half, down_mine, gate_keep, gate_send,
        up_keep, up_send, d_context_t, delta, mlp_gain_part,
    ) = middle(
        context_t, tokens, gain_mlp, grad_full,
        (output_weight, down_weight, gate_weight, up_weight, weight_o, weight_d, *slices),
    )
    gate_come = send(gate_send, "y")
    up_come = send(up_send, "x")
    down_come = send(down_half, "y")
    out_near = send(out_near, "near")
    d_query_t, d_pieces = attend_backward(counts, q_t, d_context_t, log_total, delta, pieces)
    input_grad, gains, gate_sum, up_sum, down_sum, query_sum, kv_sum, output_sum = last_part(
        counts, inverse, d_query_t, d_pieces, normed_full, joined, tokens, gain_attn,
        grad_residual, attn_grad_full, context_t, mlp_gain_part,
        (down_mine, down_come, gate_keep, gate_come, up_keep, up_come),
    )
    per = gains.shape[1] // 8
    gains = lax.dynamic_slice_in_dim(gains, dp * per, per, axis=1)
    output, key_sum, value_sum, input_grad, query_sum, output_sum, gate_sum, up_sum, down_sum = finish(
        out_base, out_near, kv_sum, input_grad, query_sum, output_sum, gate_sum, up_sum, down_sum
    )
    return (
        output,
        input_grad,
        gains[1],
        query_sum,
        key_sum,
        value_sum,
        output_sum.T,
        gains[0],
        gate_sum,
        up_sum,
        down_sum.T,
    )


def solution(mesh):
    regroup = mesh.shape["dp"] == 8 and mesh.shape["tp"] == 4
    chosen = local_regrouped if regroup else local
    return jax.shard_map(
        chosen,
        mesh=mesh,
        in_specs=(
            P(("dp", "tp"), None),
            P(("dp", "tp"), None),
            P(),
            P(),
            P(None, "tp"),
            P(None, "tp"),
            P(None, "tp"),
            P("tp", None),
            P(),
            P(None, "tp"),
            P(None, "tp"),
            P("tp", None),
        ),
        out_specs=(
            P(("dp", "tp"), None),
            P(("dp", "tp"), None),
            P("dp"),
            P("dp", "tp"),
            P("dp", "tp"),
            P("dp", "tp"),
            P("tp", "dp"),
            P("dp"),
            P("dp", "tp"),
            P("dp", "tp"),
            P("tp", "dp"),
        ),
        check_vma=False,
    )
```

```python
import functools

import jax
import jax.numpy as jnp
from jax import lax
from jax.experimental import pallas as pl
from jax.experimental.pallas import tpu as pltpu
from jax.sharding import PartitionSpec as P

HEAD_WIDTH = 96
BLK = 256
LOG2E = 1.4426950408889634
SCORE = LOG2E * HEAD_WIDTH ** (-0.5)
VSCALE = 2.0 ** -9
FAR_BASE = 1 << 24
floats = jnp.float32
halves = jnp.bfloat16


def dot_nn(a, b):
    return jnp.dot(a, b, preferred_element_type=floats)


def dot_nt(a, b):
    return lax.dot_general(a, b, (((1,), (1,)), ((), ())), preferred_element_type=floats)


def token_base(j, core, pair, side):
    return ((2 * j + core) * 4 + 2 * pair + side) * BLK


def group_bases():
    dp, z = lax.axis_index("dp"), lax.axis_index("tp")
    j, c, pair, side = dp // 2, lax.rem(dp, 2), z // 2, lax.rem(z, 2)
    return [
        token_base(j, core, pair, at) for at in (side, 1 - side) for core in (c, 1 - c)
    ]


def item_start(counts_ref, token):
    start = jnp.zeros_like(token)
    for i in range(3):
        start = jnp.where(token >= counts_ref[i], counts_ref[i], start)
    return start


def group_index():
    lanes = lax.broadcasted_iota(jnp.int32, (1, BLK), 1)
    return jnp.concatenate([lanes + base for base in group_bases()], axis=1)


def fill_places(counts_ref, sc, tok_ref, start_ref):
    dp, z = lax.axis_index("dp"), lax.axis_index("tp")
    j, c, pair, side = dp // 2, lax.rem(dp, 2), z // 2, lax.rem(z, 2)
    x, y = lax.rem(j, 2), j // 2
    kb = 0
    for side_of in (side, 1 - side):
        for cores, pair_of in (((c, 1 - c), pair), ((1 - c, c), 1 - pair)):
            for j_of, present in ((j, None), (j - 1, x), (j - 2, y), (j - 1, y * (1 - x))):
                for core in cores:
                    base = token_base(j_of, core, pair_of, side_of)
                    sc[0, kb] = base if present is None else jnp.where(present == 1, base, FAR_BASE)
                    kb += 1
    for qb, base in enumerate(group_bases()):
        sc[1, qb] = base
        sc[2, qb] = item_start(counts_ref, base)
        sc[3, qb] = item_start(counts_ref, base + (BLK - 1))
    index = group_index()
    tok_ref[...] = index
    start_ref[...] = item_start(counts_ref, index)


def pair_state(sc, kb, qb):
    key_base = sc[0, kb]
    q_base, least, most = sc[1, qb], sc[2, qb], sc[3, qb]
    needed = (key_base <= q_base + (BLK - 1)) & (key_base + (BLK - 1) >= least)
    whole = (key_base + (BLK - 1) <= q_base) & (key_base >= most)
    return key_base, needed, whole


def allowed_mask(key_bases, tok_ref, start_ref, lanes):
    masks = []
    for key_base in key_bases:
        keys = key_base + lax.broadcasted_iota(jnp.int32, (BLK, BLK), 0)
        masks.append((keys <= tok_ref[0:1, lanes]) & (keys >= start_ref[0:1, lanes]))
    return masks[0] if len(masks) == 1 else jnp.concatenate(masks, axis=0)


def piece_used(sc, piece, blocks):
    used = False
    for kb in range(2):
        for qb in range(blocks):
            used = used | pair_state(sc, 2 * piece + kb, qb)[1]
    return used


def for_piece(sc, piece, qb, unit):
    one_base, one, one_whole = pair_state(sc, 2 * piece, qb)
    two_base, two, two_whole = pair_state(sc, 2 * piece + 1, qb)
    both, free = one & two, one_whole & two_whole
    bases = (one_base, two_base)
    pl.when(both & free)(lambda: unit((0, 1), bases, False))
    pl.when(both & jnp.logical_not(free))(lambda: unit((0, 1), bases, True))
    pl.when(one & jnp.logical_not(two))(lambda: unit((0,), bases[:1], True))
    pl.when(two & jnp.logical_not(one))(lambda: unit((1,), bases[1:], True))


def fwd_kernel(n, width, counts, q_ref, pieces, *refs):
    out_acc, out_sum = refs[:2]
    kv, keys_nat, acc, total, q_wide, sc, tok_ref, start_ref, sem = refs[2:]
    for i in range(n):
        pltpu.make_async_copy(pieces.at[i], kv.at[i], sem.at[i]).start()
    acc[...] = jnp.zeros_like(acc)
    total[...] = jnp.zeros_like(total)
    fill_places(counts, sc, tok_ref, start_ref)
    heads_kv = pieces.shape[1] // (2 * HEAD_WIDTH)
    group = q_ref.shape[0] // (heads_kv * HEAD_WIDTH)
    v_off = heads_kv * HEAD_WIDTH
    places = [
        (h, slice((h * group + g) * HEAD_WIDTH, (h * group + g + 1) * HEAD_WIDTH), slice(qb * BLK, (qb + 1) * BLK),
         slice(h * HEAD_WIDTH, (h + 1) * HEAD_WIDTH), slice((qb * group + g) * BLK, (qb * group + g + 1) * BLK), h * group + g)
        for h in range(heads_kv) for g in range(group) for qb in range(q_ref.shape[1] // BLK)
    ]
    for h, rows, lanes, wrows, wlanes, hd in places:
        q_wide[wrows, wlanes] = q_ref[rows, lanes]

    def key_piece(piece, carry):
        pltpu.make_async_copy(pieces.at[piece], kv.at[piece], sem.at[piece]).wait()
        def query_block(qb, carry):
            lanes = pl.ds(pl.multiple_of(qb * BLK, BLK), BLK)
            wide = pl.ds(pl.multiple_of(qb * (group * BLK), group * BLK), group * BLK)

            def unit(subs, bases, masked):
                keys = slice(subs[0] * BLK, (subs[-1] + 1) * BLK)
                if masked:
                    allowed = allowed_mask(bases, tok_ref, start_ref, lanes)
                    allowed = jnp.concatenate([allowed] * group, axis=1)
                scores = [
                    dot_nn(keys_nat[h, keys], q_wide[h * HEAD_WIDTH : (h + 1) * HEAD_WIDTH, wide])
                    for h in range(heads_kv)
                ]
                weights = [jnp.exp2(s * SCORE) for s in scores]
                if masked:
                    weights = [jnp.where(allowed, w, 0.0) for w in weights]
                sums = [jnp.sum(w, axis=0, keepdims=True) for w in weights]
                parts = [
                    dot_nn(
                        kv[piece, v_off + h * HEAD_WIDTH : v_off + (h + 1) * HEAD_WIDTH, keys],
                        weights[h].astype(halves),
                    )
                    for h in range(heads_kv)
                ]
                for h in range(heads_kv):
                    total[h : h + 1, wide] += sums[h]
                    acc[h * HEAD_WIDTH : (h + 1) * HEAD_WIDTH, wide] += parts[h]

            for_piece(sc, piece, qb, unit)
            return carry

        @pl.when(piece_used(sc, piece, q_ref.shape[1] // BLK))
        def _():
            for h in range(heads_kv):
                keys_nat[h] = kv[piece, h * HEAD_WIDTH : (h + 1) * HEAD_WIDTH, :].T
            lax.fori_loop(0, q_ref.shape[1] // BLK, query_block, 0)

        return carry

    lax.fori_loop(0, n, key_piece, 0)
    for h, rows, lanes, wrows, wlanes, hd in places:
        row = total[h : h + 1, wlanes]
        out_acc[rows, lanes] = (acc[wrows, wlanes] * ((1.0 / VSCALE) / row)).astype(halves)
        out_sum[hd : hd + 1, lanes] = jnp.log2(row)


VM = pl.BlockSpec(memory_space=pltpu.VMEM)
SM = pl.BlockSpec(memory_space=pltpu.SMEM)
HB = pl.BlockSpec(memory_space=pl.ANY)
HM = pl.BlockSpec(memory_space=pltpu.HBM)


def place_scratch(blocks, tokens):
    return [
        pltpu.SMEM((4, blocks), jnp.int32),
        pltpu.VMEM((1, tokens), jnp.int32),
        pltpu.VMEM((1, tokens), jnp.int32),
    ]


def attend_forward(counts, q_t, pieces):
    n, width = pieces.shape[0], pieces.shape[2]
    heads = q_t.shape[0] // HEAD_WIDTH
    heads_kv = pieces.shape[1] // (2 * HEAD_WIDTH)
    tokens = q_t.shape[1]
    wide = tokens * heads // heads_kv
    return pl.pallas_call(
        functools.partial(fwd_kernel, n, width),
        out_shape=(
            jax.ShapeDtypeStruct(q_t.shape, halves),
            jax.ShapeDtypeStruct((heads, tokens), floats),
        ),
        in_specs=[SM, VM, HM],
        out_specs=(VM, VM),
        scratch_shapes=[
            pltpu.VMEM(pieces.shape, halves),
            pltpu.VMEM((heads_kv, width, HEAD_WIDTH), halves),
            pltpu.VMEM((heads_kv * HEAD_WIDTH, wide), floats),
            pltpu.VMEM((heads_kv, wide), floats),
            pltpu.VMEM((heads_kv * HEAD_WIDTH, wide), halves),
            *place_scratch(n * width // BLK, tokens),
            pltpu.SemaphoreType.DMA((n,)),
        ],
        compiler_params=pltpu.CompilerParams(vmem_limit_bytes=63 << 20),
        name="attend_forward",
    )(counts, q_t, pieces)


def bwd_kernel(n, width, counts, q_ref, do_ref, log_ref, delta_ref, pieces, *refs):
    dq_out = refs[0]
    dkv_out = refs[1]
    kv, dkv, keys_nat, vals_nat, acc, q_wide, do_wide, log_wide, delta_wide, dq_wide, sc, tok_ref, start_ref, sem, osem = refs[2:]
    for i in range(n):
        pltpu.make_async_copy(pieces.at[i], kv.at[i], sem.at[i]).start()
    fill_places(counts, sc, tok_ref, start_ref)
    heads_kv = pieces.shape[1] // (2 * HEAD_WIDTH)
    group = q_ref.shape[0] // (heads_kv * HEAD_WIDTH)
    v_off = heads_kv * HEAD_WIDTH
    places = [
        (h, slice((h * group + g) * HEAD_WIDTH, (h * group + g + 1) * HEAD_WIDTH), slice(qb * BLK, (qb + 1) * BLK),
         slice(h * HEAD_WIDTH, (h + 1) * HEAD_WIDTH), slice((qb * group + g) * BLK, (qb * group + g + 1) * BLK), h * group + g)
        for h in range(heads_kv) for g in range(group) for qb in range(q_ref.shape[1] // BLK)
    ]
    for h, rows, lanes, wrows, wlanes, hd in places:
        q_wide[wrows, wlanes] = q_ref[rows, lanes]
        do_wide[wrows, wlanes] = do_ref[rows, lanes]
        log_wide[h : h + 1, wlanes] = log_ref[hd : hd + 1, lanes]
        delta_wide[h : h + 1, wlanes] = delta_ref[hd : hd + 1, lanes]
        dq_wide[wrows, wlanes] = jnp.zeros((HEAD_WIDTH, BLK), floats)
    out_scale = (1.0 / VSCALE) * HEAD_WIDTH ** (-0.5)

    def key_piece(piece, carry):
        pltpu.make_async_copy(pieces.at[piece], kv.at[piece], sem.at[piece]).wait()
        def query_block(qb, carry):
            lanes = pl.ds(pl.multiple_of(qb * BLK, BLK), BLK)
            wide = pl.ds(pl.multiple_of(qb * (group * BLK), group * BLK), group * BLK)

            def unit(subs, bases, masked):
                keys = slice(subs[0] * BLK, (subs[-1] + 1) * BLK)
                if masked:
                    allowed = allowed_mask(bases, tok_ref, start_ref, lanes)
                    allowed = jnp.concatenate([allowed] * group, axis=1)
                heads = range(heads_kv)
                krows = [slice(h * HEAD_WIDTH, (h + 1) * HEAD_WIDTH) for h in heads]
                vrows = [slice(v_off + h * HEAD_WIDTH, v_off + (h + 1) * HEAD_WIDTH) for h in heads]
                qt = [q_wide[krows[h], wide] for h in heads]
                dot = [do_wide[krows[h], wide] for h in heads]
                scores = [dot_nn(keys_nat[h, keys], qt[h]) for h in heads]
                dprobs = [dot_nn(vals_nat[h, keys], dot[h]) for h in heads]
                weights = [
                    jnp.exp2(scores[h] * SCORE - log_wide[h : h + 1, wide]) for h in heads
                ]
                if masked:
                    weights = [jnp.where(allowed, w, 0.0) for w in weights]
                ds = [
                    (weights[h] * (dprobs[h] - delta_wide[h : h + 1, wide])).astype(halves)
                    for h in heads
                ]
                dv = [dot_nt(dot[h], weights[h].astype(halves)) for h in heads]
                dk = [dot_nt(qt[h], ds[h]) for h in heads]
                dq = [dot_nn(kv[piece, krows[h], keys], ds[h]) for h in heads]
                for h in heads:
                    acc[vrows[h], keys] += dv[h]
                    acc[krows[h], keys] += dk[h]
                    dq_wide[krows[h], wide] += dq[h]

            for_piece(sc, piece, qb, unit)
            return carry

        used = piece_used(sc, piece, q_ref.shape[1] // BLK)

        @pl.when(used)
        def _():
            for h in range(heads_kv):
                rows = slice(h * HEAD_WIDTH, (h + 1) * HEAD_WIDTH)
                vals = slice(v_off + h * HEAD_WIDTH, v_off + (h + 1) * HEAD_WIDTH)
                keys_nat[h] = kv[piece, rows, :].T
                vals_nat[h] = kv[piece, vals, :].T
            acc[...] = jnp.zeros_like(acc)
            lax.fori_loop(0, q_ref.shape[1] // BLK, query_block, 0)
            dkv[piece, 0:v_off, :] = (acc[0:v_off, :] * out_scale).astype(halves)
            dkv[piece, v_off:, :] = acc[v_off:, :].astype(halves)

        @pl.when(jnp.logical_not(used))
        def _():
            dkv[piece] = jnp.zeros(dkv.shape[1:], halves)

        pltpu.make_async_copy(dkv.at[piece], dkv_out.at[piece], osem.at[piece]).start()
        return carry

    lax.fori_loop(0, n, key_piece, 0)
    for h, rows, lanes, wrows, wlanes, hd in places:
        dq_out[rows, lanes] = dq_wide[wrows, wlanes] * out_scale
    for i in range(n):
        pltpu.make_async_copy(dkv.at[i], dkv_out.at[i], osem.at[i]).wait()


def attend_backward(counts, q_t, do_t, log_total, delta, pieces):
    n, width = pieces.shape[0], pieces.shape[2]
    heads_kv = pieces.shape[1] // (2 * HEAD_WIDTH)
    wide = q_t.shape[0] // (heads_kv * HEAD_WIDTH) * q_t.shape[1]
    outs = pl.pallas_call(
        functools.partial(bwd_kernel, n, width),
        out_shape=(
            jax.ShapeDtypeStruct(q_t.shape, floats),
            jax.ShapeDtypeStruct(pieces.shape, halves),
        ),
        in_specs=[SM] + [VM] * 4 + [HM],
        out_specs=(VM, HM),
        scratch_shapes=[
            pltpu.VMEM(pieces.shape, halves),
            pltpu.VMEM(pieces.shape, halves),
            pltpu.VMEM((heads_kv, width, HEAD_WIDTH), halves),
            pltpu.VMEM((heads_kv, width, HEAD_WIDTH), halves),
            pltpu.VMEM(pieces.shape[1:], floats),
            pltpu.VMEM((heads_kv * HEAD_WIDTH, wide), halves),
            pltpu.VMEM((heads_kv * HEAD_WIDTH, wide), halves),
            pltpu.VMEM((heads_kv, wide), floats),
            pltpu.VMEM((heads_kv, wide), floats),
            pltpu.VMEM((heads_kv * HEAD_WIDTH, wide), floats),
            *place_scratch(n * width // BLK, q_t.shape[1]),
            pltpu.SemaphoreType.DMA((n,)),
            pltpu.SemaphoreType.DMA((n,)),
        ],
        compiler_params=pltpu.CompilerParams(vmem_limit_bytes=63 << 20),
        name="attend_backward",
    )(counts, q_t, do_t, log_total, delta, pieces)
    return outs


eps_norm = 1e-05
rope_base = 100000.0
reach_limit = 8


def shifted(block, axis, distance):
    devices = range(lax.axis_size(axis))
    route = [(i - distance, i) for i in devices if i - distance in devices]
    return lax.ppermute(block, axis, route)


def rms_scale(value_vectors, gain_vec):
    return (
        value_vectors
        * lax.rsqrt(jnp.mean(value_vectors * value_vectors, axis=-1, keepdims=True) + eps_norm)
        * gain_vec
    )


def rotary_turn(value_vectors, token_positions, heads):
    half_width = HEAD_WIDTH // 2
    inverse = 1.0 / rope_base ** (jnp.arange(half_width, dtype=jnp.float32) * 2.0 / HEAD_WIDTH)
    angles = token_positions.astype(jnp.float32)[:, None] * inverse[None, :]
    cosine = jnp.cos(angles)[:, None, :]
    sine_part = jnp.sin(angles)[:, None, :]
    shaped = value_vectors.reshape(value_vectors.shape[0], heads, HEAD_WIDTH)
    first_half = shaped[..., :half_width]
    second = shaped[..., half_width:]
    turned = jnp.concatenate(
        [first_half * cosine - second * sine_part, second * cosine + first_half * sine_part],
        axis=-1,
    )
    return turned.reshape(value_vectors.shape)


def swiglu(gate_pre, up_pre):
    return jax.nn.silu(gate_pre) * up_pre


def contract_rows(left_side, right_side):
    return lax.dot_general(
        left_side, right_side, (((0,), (0,)), ((), ())), preferred_element_type=jnp.float32
    )


def contract_cols(left_side, right_side):
    return lax.dot_general(
        left_side, right_side, (((1,), (1,)), ((), ())), preferred_element_type=jnp.float32
    )


def local(
    tokens,
    out_grad,
    segment_ids,
    attn_gain,
    query_weight,
    key_matrix,
    value_matrix,
    output_weight,
    mlp_gain,
    gate_weight,
    up_weight,
    down_weight,
):
    floats = jnp.float32
    halves = jnp.bfloat16
    shard_rows = tokens.shape[0]
    row_len = shard_rows * lax.axis_size("tp")
    row_index = lax.axis_index("dp")
    reach = min(reach_limit, lax.axis_size("dp") // 2)
    heads_q = query_weight.shape[1] // HEAD_WIDTH
    heads_kv = key_matrix.shape[1] // HEAD_WIDTH
    group_width = heads_q // heads_kv
    q_cols = heads_q * HEAD_WIDTH
    kv_cols = heads_kv * HEAD_WIDTH
    score_scale = HEAD_WIDTH ** (-0.5)
    row_first = row_index * row_len
    seg_row = lax.dynamic_slice_in_dim(segment_ids, row_first, row_len)
    index_row = row_first + jnp.arange(row_len, dtype=jnp.int32)
    every_index = jnp.arange(segment_ids.shape[0], dtype=jnp.int32)
    marks = (segment_ids[1:] != segment_ids[:-1]).astype(jnp.int32)
    starts = jnp.concatenate([jnp.zeros((1,), jnp.int32), marks * every_index[1:]])
    is_at = (starts[None, :] <= index_row[:, None]).astype(jnp.int32)
    token_positions = index_row - jnp.max(is_at * starts[None, :], axis=1)
    tokens32 = tokens.astype(floats)
    gain_attn = attn_gain.astype(floats)
    gain_mlp = mlp_gain.astype(floats)
    normed = rms_scale(tokens32, gain_attn).astype(halves)
    normed_full = lax.all_gather(normed, "tp", axis=0, tiled=True)
    joined = jnp.concatenate([query_weight, key_matrix, value_matrix], axis=1)
    projected = jnp.dot(normed_full, joined, preferred_element_type=floats)
    q_linear = projected[:, :q_cols]
    key_linear_out = projected[:, q_cols : q_cols + kv_cols]
    query_vectors = rotary_turn(q_linear, token_positions, heads_q).astype(halves)
    key_vectors = rotary_turn(key_linear_out, token_positions, heads_kv).astype(halves)
    value_vectors = projected[:, q_cols + kv_cols :].astype(halves)
    query_heads = query_vectors.reshape(row_len, heads_kv, group_width, HEAD_WIDTH)
    held_blocks = [(key_vectors, value_vectors)]
    moving = (key_vectors, value_vectors)
    for step_hop in range(reach):
        moving = shifted((moving[0], moving[1]), "dp", 1)
        held_blocks.append(moving)

    def block_mask(step_hop):
        key_row = row_index - step_hop
        seg_keys = lax.dynamic_slice_in_dim(segment_ids, jnp.maximum(key_row, 0) * row_len, row_len)
        key_index = key_row * row_len + jnp.arange(row_len, dtype=jnp.int32)
        return (seg_keys[None, :] == seg_row[:, None]) & (key_index[None, :] <= index_row[:, None])

    def block_needed(step_hop):
        last_key = jnp.maximum((row_index - step_hop + 1) * row_len - 1, 0)
        return (row_index >= step_hop) & (segment_ids[last_key] == seg_row[0])

    block_masks = [block_mask(step_hop) for step_hop in range(reach + 1)]

    def apply_block(step_hop, update, state_in):
        key_block, value_block = held_blocks[step_hop]
        if step_hop == 0:
            return update(state_in, key_block, value_block, block_masks[0])
        return lax.cond(
            block_needed(step_hop),
            update,
            lambda state_kept, key_skip, value_skip, mask_skip: state_kept,
            state_in,
            key_block,
            value_block,
            block_masks[step_hop],
        )

    def scores(key_block, allowed):
        raw_scores = jnp.einsum(
            "qhgd,khd->hgqk",
            query_heads,
            key_block.reshape(row_len, heads_kv, HEAD_WIDTH),
            preferred_element_type=floats,
        )
        return jnp.where(allowed, raw_scores * score_scale, -jnp.inf)

    def add_online(state_in, key_block, value_block, allowed):
        run_max, run_total, run_sum = state_in
        block_scores = scores(key_block, allowed)
        new_max = jnp.maximum(run_max, jnp.max(block_scores, axis=-1))
        factor = jnp.exp(run_max - new_max)
        weights = jnp.exp(block_scores - new_max[..., None])
        run_total = run_total * factor + jnp.sum(weights, axis=-1)
        run_sum = run_sum * jnp.moveaxis(factor, 2, 0)[..., None] + jnp.einsum(
            "hgqk,khd->qhgd",
            weights.astype(halves),
            value_block.reshape(row_len, heads_kv, HEAD_WIDTH),
            preferred_element_type=floats,
        )
        return (new_max, run_total, run_sum)

    online = (
        jnp.full((heads_kv, group_width, row_len), -jnp.inf, floats),
        jnp.zeros((heads_kv, group_width, row_len), floats),
        jnp.zeros((row_len, heads_kv, group_width, HEAD_WIDTH), floats),
    )
    for step_hop in range(reach + 1):
        online = apply_block(step_hop, add_online, online)
    run_max, run_total, run_sum = online
    log_total = (run_max + jnp.log(run_total))[..., None]
    context_heads = (run_sum / jnp.moveaxis(run_total, 2, 0)[..., None]).astype(halves)
    context = context_heads.reshape(row_len, q_cols)
    residual = tokens32 + lax.psum_scatter(
        jnp.dot(context, output_weight, preferred_element_type=floats).astype(jnp.bfloat16),
        "tp",
        scatter_dimension=0,
        tiled=True,
    ).astype(jnp.float32)
    mlp_normed = rms_scale(residual, gain_mlp).astype(halves)
    mlp_full = lax.all_gather(mlp_normed, "tp", axis=0, tiled=True)
    gate_pre = jnp.dot(mlp_full, gate_weight, preferred_element_type=floats)
    up_pre = jnp.dot(mlp_full, up_weight, preferred_element_type=floats)
    hidden = swiglu(gate_pre, up_pre).astype(halves)
    output = residual + lax.psum_scatter(
        jnp.dot(hidden, down_weight, preferred_element_type=floats).astype(jnp.bfloat16),
        "tp",
        scatter_dimension=0,
        tiled=True,
    ).astype(jnp.float32)
    grad_full = lax.all_gather(out_grad, "tp", axis=0, tiled=True)
    grad_hidden = contract_cols(grad_full, down_weight)
    down_grad = contract_rows(grad_full, hidden)
    silu_back = jax.vjp(swiglu, gate_pre, up_pre)[1]
    grad_gate, grad_up = silu_back(grad_hidden)
    grad_gate = grad_gate.astype(halves)
    grad_up = grad_up.astype(halves)
    gate_grad = contract_rows(mlp_full, grad_gate)
    up_grad = contract_rows(mlp_full, grad_up)
    grad_mlp_normed = lax.psum_scatter(
        (contract_cols(grad_gate, gate_weight) + contract_cols(grad_up, up_weight)).astype(
            jnp.bfloat16
        ),
        "tp",
        scatter_dimension=0,
        tiled=True,
    ).astype(jnp.float32)
    mlp_norm_back = jax.vjp(rms_scale, residual, gain_mlp)[1]
    grad_residual_part, mlp_gain_part = mlp_norm_back(grad_mlp_normed)
    grad_residual = out_grad.astype(floats) + grad_residual_part
    attn_grad_full = lax.all_gather(grad_residual.astype(halves), "tp", axis=0, tiled=True)
    output_grad = contract_rows(attn_grad_full, context)
    grad_context = (
        contract_cols(attn_grad_full, output_weight)
        .astype(halves)
        .reshape(row_len, heads_kv, group_width, HEAD_WIDTH)
    )
    delta_col = jnp.einsum(
        "qhgd,qhgd->hgq", grad_context, context_heads, preferred_element_type=floats
    )[..., None]

    def add_grads(state_in, key_block, value_block, allowed):
        query_acc, key_acc, value_acc = state_in
        probabilities = jnp.exp(scores(key_block, allowed) - log_total)
        grad_probs = jnp.einsum(
            "qhgd,khd->hgqk",
            grad_context,
            value_block.reshape(row_len, heads_kv, HEAD_WIDTH),
            preferred_element_type=floats,
        )
        grad_scores = (probabilities * (grad_probs - delta_col)).astype(halves)
        key_heads = key_block.reshape(row_len, heads_kv, HEAD_WIDTH)
        query_acc = (
            query_acc
            + jnp.einsum("hgqk,khd->qhgd", grad_scores, key_heads, preferred_element_type=floats)
            * score_scale
        )
        key_acc = (
            key_acc
            + jnp.einsum(
                "hgqk,qhgd->khd", grad_scores, query_heads, preferred_element_type=floats
            ).reshape(row_len, kv_cols)
            * score_scale
        )
        value_acc = value_acc + jnp.einsum(
            "hgqk,qhgd->khd",
            probabilities.astype(halves),
            grad_context,
            preferred_element_type=floats,
        ).reshape(row_len, kv_cols)
        return (query_acc, key_acc, value_acc)

    query_acc = jnp.zeros((row_len, heads_kv, group_width, HEAD_WIDTH), floats)
    carried = (jnp.zeros((row_len, kv_cols), floats), jnp.zeros((row_len, kv_cols), floats))
    for step_hop in range(reach, 0, -1):
        query_acc, key_acc, value_acc = apply_block(
            step_hop, add_grads, (query_acc, carried[0], carried[1])
        )
        carried = (
            shifted(key_acc.astype(jnp.bfloat16), "dp", -1).astype(key_acc.dtype),
            shifted(value_acc.astype(jnp.bfloat16), "dp", -1).astype(value_acc.dtype),
        )
    query_acc, key_total, value_total = apply_block(
        0, add_grads, (query_acc, carried[0], carried[1])
    )
    query_back = jax.vjp(lambda linear: rotary_turn(linear, token_positions, heads_q), q_linear)[1]
    key_back = jax.vjp(
        lambda linear: rotary_turn(linear, token_positions, heads_kv), key_linear_out
    )[1]
    grad_q_linear = query_back(query_acc.reshape(row_len, q_cols))[0]
    grad_k_linear = key_back(key_total)[0]
    grads_joined = jnp.concatenate([grad_q_linear, grad_k_linear, value_total], axis=1).astype(
        halves
    )
    proj_grad = contract_rows(normed_full, grads_joined)
    grad_normed = lax.psum_scatter(
        contract_cols(grads_joined, joined).astype(jnp.bfloat16),
        "tp",
        scatter_dimension=0,
        tiled=True,
    ).astype(jnp.float32)
    attn_norm_back = jax.vjp(rms_scale, tokens32, gain_attn)[1]
    grad_tokens_part, attn_gain_part = attn_norm_back(grad_normed)
    input_grad = grad_residual + grad_tokens_part
    def scatter_rows(grad):
        return lax.psum_scatter(
            grad.astype(halves), "dp", scatter_dimension=0, tiled=True
        ).astype(floats)

    mlp_sums = scatter_rows(jnp.concatenate([gate_grad, up_grad, down_grad], axis=1))
    ff_cols = gate_weight.shape[1]
    gate_sum = mlp_sums[:, :ff_cols]
    up_sum = mlp_sums[:, ff_cols : 2 * ff_cols]
    down_sum = mlp_sums[:, 2 * ff_cols :]
    attn_sums = scatter_rows(jnp.concatenate([proj_grad, output_grad], axis=1))
    query_sum = attn_sums[:, :q_cols]
    key_sum = attn_sums[:, q_cols : q_cols + kv_cols]
    value_sum = attn_sums[:, q_cols + kv_cols : q_cols + 2 * kv_cols]
    output_sum = attn_sums[:, q_cols + 2 * kv_cols :]
    attn_gain_sum = lax.psum_scatter(attn_gain_part, "dp", scatter_dimension=0, tiled=True)
    mlp_gain_sum = lax.psum_scatter(mlp_gain_part, "dp", scatter_dimension=0, tiled=True)
    attn_gain_total, mlp_gain_total = lax.psum((attn_gain_sum, mlp_gain_sum), "tp")
    return (
        output.astype(halves),
        input_grad,
        attn_gain_total,
        query_sum,
        key_sum,
        value_sum,
        output_sum.T,
        mlp_gain_total,
        gate_sum,
        up_sum,
        down_sum.T,
    )


MESH = pl.DeviceIdType.MESH


def meet(devices):
    barrier = pltpu.get_barrier_semaphore()
    for device in devices:
        pl.semaphore_signal(barrier, inc=1, device_id=device, device_id_type=MESH)
    pl.semaphore_wait(barrier, len(devices))


def tiles(total, step, body):
    def one(i, carry):
        body(pl.ds(pl.multiple_of(i * step, step), step))
        return carry

    lax.fori_loop(0, total // step, one, 0)


CHUNKS = 4


class GroupSum:
    def __init__(self, copies, bufs, place):
        self.copies, self.bufs, self.place = copies, bufs, place

        self.far, self.sums = [], []

    def put_there(self, at, cols, value):
        part_near, _, out_far = self.bufs[:3]
        rows = value.shape[0] // 2
        part_near[at, cols] = value[:rows]
        out_far[at, cols] = value[rows:].astype(halves)

    def put_here(self, cols, value):
        _, part_own, _, out_beside = self.bufs[:4]
        rows = value.shape[0] // 2
        part_own[:, cols] = value[:rows]
        out_beside[:, cols] = value[rows:].astype(halves)

    def send_far(self, at):
        _, _, out_far, _, _, in_near = self.bufs[:6]
        copy = self.copies.make(out_far.at[at], in_near.at[at], self.place.beside)
        copy.start()
        self.far.append(copy)

    def send_beside(self):
        _, _, _, out_beside, _, _, in_own = self.bufs[:7]
        self.side = self.copies.make(out_beside, in_own, self.place.beside)
        self.side.start()

    def send_near(self, count):
        part_near, _, _, _, out_near, in_near, _, in_sum = self.bufs
        self.far[-1].wait_recv()
        rows = part_near.shape[0] // CHUNKS
        for _ in range(count):
            at = pl.ds(len(self.sums) * rows, rows)
            out_near[at, :] = (part_near[at, :] + in_near[at, :].astype(floats)).astype(halves)
            copy = self.copies.make(out_near.at[at], in_sum.at[at], self.place.near)
            copy.start()
            self.sums.append(copy)

    def run(self, product):
        everything = pl.ds(0, self.bufs[0].shape[0])
        product(1, lambda cols, value: self.put_there(everything, cols, value))
        self.send_far(everything)
        product(0, self.put_here)
        self.send_beside()
        self.send_near(CHUNKS)

    def take(self, k):
        part_near, part_own, out_far, out_beside, out_near, in_near, in_own, in_sum = self.bufs
        if k == 0:
            self.side.wait_recv()
        self.sums[k].wait_recv()
        rows = part_own.shape[0] // CHUNKS
        at = pl.ds(k * rows, rows)
        return part_own[at, :] + in_own[at, :].astype(floats) + in_sum[at, :].astype(floats)

    def finish(self):
        for copy in (*self.far, self.side, *self.sums):
            copy.wait_send()


class GroupGather:
    def __init__(self, copies, full, block, place):
        self.copies, self.full, self.block, self.place = copies, full, block, place
        self.sent = []

    def slot(self, n, k):
        rows = self.block // CHUNKS
        return self.full.at[pl.ds(n * self.block + k * rows, rows)]

    def put(self, k):
        for i, (n, device) in enumerate(((2, self.place.near), (1, self.place.beside))):
            copy = self.copies.make(self.slot(0, k), self.slot(n, k), device)
            copy.start()
            self.sent.append((i, copy))

    def wait_here(self):
        for i, copy in self.sent:
            if i == 1:
                copy.wait_recv()

    def wait_there(self, part=0, parts=1):
        near = [copy for i, copy in self.sent if i == 0]
        count = CHUNKS // parts
        relays = []
        for k in range(part * count, (part + 1) * count):
            near[k].wait_recv()
            relay = self.copies.make(self.slot(2, k), self.slot(3, k), self.place.beside)
            relay.start()
            relays.append(relay)
        for relay in relays:
            relay.wait_recv()
        self.sent += [(2, relay) for relay in relays]

    def finish(self):
        for _, copy in self.sent:
            copy.wait_send()


class Copies:
    limit = 96

    def __init__(self, send_sems, recv_sems):
        self.send_sems, self.recv_sems, self.used = send_sems, recv_sems, 0

    def make(self, src, dst, device):
        i = self.used
        self.used += 1
        return pltpu.make_async_remote_copy(
            src_ref=src,
            dst_ref=dst,
            send_sem=self.send_sems.at[i],
            recv_sem=self.recv_sems.at[i],
            device_id=device,
            device_id_type=MESH,
        )


def copy_semaphores():
    return [pltpu.SemaphoreType.DMA((Copies.limit,)), pltpu.SemaphoreType.DMA((Copies.limit,))]


class Place:
    def __init__(self):
        dp, z = lax.axis_index("dp"), lax.axis_index("tp")
        self.dp, self.z = dp, z
        self.c = lax.rem(dp, 2)
        self.x = lax.rem(dp // 2, 2)
        self.y = dp // 4
        far_z = lax.rem(z + 2, 4)
        self.beside = (dp + 1 - 2 * self.c, z)
        self.near = (dp, z + 1 - 2 * lax.rem(z, 2))
        self.far = (dp, far_z)
        self.cross = (self.beside[0], far_z)
        self.over_x = (dp + 2 - 4 * self.x, z)
        self.over_y = (dp + 4 - 8 * self.y, z)
        self.slot = 2 * self.y + self.x
        self.slot_x = 2 * self.y + 1 - self.x
        self.slot_y = 2 - 2 * self.y + self.x
        self.odd = self.c == 1
        self.corner = (self.x == 1) & (self.y == 1)
        self.turn = (self.x == 0) & (self.y == 1)


def rope_tables(counts_ref, inverse_ref, cos_ref, sin_ref):
    index = group_index()
    positions = (index - item_start(counts_ref, index)).astype(floats)
    angles = inverse_ref[...] * positions
    cos_ref[...] = jnp.cos(angles)
    sin_ref[...] = jnp.sin(angles)


class PlaneFetch:
    def __init__(self, copies, place, out, own=None, own_slice=None):
        self.place, self.out = place, out
        rows = out.shape[0] // 8

        def part(slot, ch):
            return pl.ds(slot * (2 * rows) + ch * rows, rows)

        def remote(slot, ch, device):
            at = part(slot, ch)
            return copies.make(out.at[at], out.at[at], device)

        p = place
        self.hop = None
        if own is not None:
            self.hop = [
                copies.make(own.at[part(p.slot, ch)], out.at[part(p.slot, ch)], p.far)
                for ch in range(2)
            ]
        if own_slice is not None:
            self.hop = [
                copies.make(own_slice.at[part(0, ch)], out.at[part(p.slot, ch)], p.far)
                for ch in range(2)
            ]
        self.x = [remote(p.slot, ch, p.over_x) for ch in range(2)]
        self.y = [remote(p.slot, ch, p.over_y) for ch in range(2)]
        self.relay_y = remote(p.slot_x, 0, p.over_y)
        self.relay_x = remote(p.slot_y, 1, p.over_x)

    def start(self):
        @pl.when(self.place.odd)
        def _():
            for copy in self.hop:
                copy.start()

    def forward(self):
        @pl.when(self.place.odd)
        def _():
            for ch in range(2):
                if self.hop is not None:
                    self.hop[ch].wait_recv()
                self.x[ch].start()
                self.y[ch].start()

    def relay(self):
        @pl.when(self.place.odd)
        def _():
            self.x[0].wait_recv()
            self.relay_y.start()
            self.y[1].wait_recv()
            self.relay_x.start()

    def finish(self):
        @pl.when(self.place.odd)
        def _():
            self.x[1].wait_recv()
            self.y[0].wait_recv()
            self.relay_y.wait_recv()
            self.relay_x.wait_recv()

    def drain(self):
        @pl.when(self.place.odd)
        def _():
            for copy in (self.hop or []) + self.x + self.y + [self.relay_y, self.relay_x]:
                copy.wait_send()


class Spread:
    def __init__(self, copies, place, source, slots):
        self.place = place
        self.to_x = copies.make(source, slots[1], place.over_x)
        self.to_y = copies.make(source, slots[2], place.over_y)
        self.relayed = copies.make(slots[2], slots[3], place.over_x)

    def start(self):
        pl.when(self.place.x == 0)(self.to_x.start)
        pl.when(self.place.y == 0)(self.to_y.start)

    def relay(self):
        @pl.when(self.place.corner)
        def _():
            self.to_y.wait_recv()
            self.relayed.start()

    def finish(self):
        p = self.place
        pl.when(p.x == 1)(self.to_x.wait_recv)
        pl.when((p.y == 1) & (p.x == 0))(self.to_y.wait_recv)
        pl.when(p.turn)(self.relayed.wait_recv)
        pl.when(p.x == 0)(self.to_x.wait_send)
        pl.when(p.y == 0)(self.to_y.wait_send)
        pl.when(p.corner)(self.relayed.wait_send)


def first_kernel(
    counts, inverse_ref, tok_ref, grad_ref, gain_ref, wq_in, wk_ref, wv_ref, wo_in, wd_in, wg_in, wu_in,
    q_out, kv_out, n_out, g_full, joined_out, wo_out, wd_out, slice_g, slice_u,
    n_full, joined, own_slice, slices, cos_ref, sin_ref, linear, kv_own, ss, rs, lsem,
):
    place = Place()
    copies = Copies(ss, rs)
    block, width = tok_ref.shape
    two = 2 * block
    q_cols = q_out.shape[0]
    kv_cols = kv_own.shape[1] // 2
    q_lanes = pl.ds(0, q_cols)
    slice_rows = pl.ds(place.slot * own_slice.shape[0], own_slice.shape[0])
    load_q = pltpu.make_async_copy(wq_in, joined.at[:, q_lanes], lsem.at[0])
    load_q_odd = pltpu.make_async_copy(
        wq_in.at[slice_rows], own_slice.at[:, q_lanes], lsem.at[0]
    )
    pl.when(place.c == 0)(load_q.start)
    pl.when(place.odd)(load_q_odd.start)
    rows4 = slice_g.shape[0]
    at_slot = pl.ds(place.slot * rows4, rows4)
    slice_loads = [
        pltpu.make_async_copy(src.at[at_slot], slices.at[i], lsem.at[1 + i])
        for i, src in enumerate((wg_in, wu_in))
    ]
    slice_stores = [
        pltpu.make_async_copy(slices.at[i], dst, lsem.at[6 + i])
        for i, dst in enumerate((slice_g, slice_u))
    ]
    for copy in slice_loads:
        copy.start()

    own_grad = pltpu.make_async_copy(grad_ref, g_full.at[pl.ds(0, block)], lsem.at[3])
    own_grad.start()
    meet((place.beside, place.near, place.far, place.cross, place.over_x, place.over_y))

    @pl.when(place.odd)
    def _():
        lanes = pl.ds(pl.multiple_of(place.slot * own_slice.shape[0], 128), own_slice.shape[0])
        own_slice[:, q_cols : q_cols + kv_cols] = wk_ref[:, lanes].T
        own_slice[:, q_cols + kv_cols :] = wv_ref[:, lanes].T
        load_q_odd.wait()

    fetch_joined = PlaneFetch(copies, place, joined, own_slice=own_slice)
    fetch_o = PlaneFetch(copies, place, wo_out, wo_in)
    fetch_d = PlaneFetch(copies, place, wd_out, wd_in)
    gather = GroupGather(copies, n_full, block, place)
    gather_g = GroupGather(copies, g_full, block, place)
    fetch_joined.start()
    chunk = block // CHUNKS
    for k in range(CHUNKS):
        at = pl.ds(k * chunk, chunk)
        tok = tok_ref[at, :].astype(floats)
        root = lax.rsqrt(jnp.mean(tok * tok, axis=-1, keepdims=True) + eps_norm)
        n_full[at, :] = (tok * root * gain_ref[...]).astype(halves)
        gather.put(k)
    fetch_joined.forward()
    fetch_o.start()
    fetch_d.start()
    @pl.when(place.c == 0)
    def _():
        joined[:, q_cols : q_cols + kv_cols] = wk_ref[...].T
        joined[:, q_cols + kv_cols :] = wv_ref[...].T

    rope_tables(counts, inverse_ref, cos_ref, sin_ref)
    for load, store in zip(slice_loads, slice_stores):
        load.wait()
        store.start()
    fetch_joined.relay()
    gather.wait_here()
    fetch_joined.finish()
    pl.when(place.c == 0)(load_q.wait)
    keep_joined = pltpu.make_async_copy(joined, joined_out, lsem.at[8])
    keep_joined.start()

    def project(k):
        rows = slice(k * two, (k + 1) * two)

        def one(cols):
            linear[cols, :] = dot_nn(n_full[rows, :], joined[:, cols]).T

        tiles(joined.shape[1], 256, one)
        half_width = HEAD_WIDTH // 2
        for head in range((q_cols + kv_cols) // HEAD_WIDTH):
            low = slice(head * HEAD_WIDTH, head * HEAD_WIDTH + half_width)
            high = slice(head * HEAD_WIDTH + half_width, (head + 1) * HEAD_WIDTH)
            one_half, two_half = linear[low, :], linear[high, :]
            cosine, sine = cos_ref[:, rows], sin_ref[:, rows]
            first = (one_half * cosine - two_half * sine).astype(halves)
            second = (two_half * cosine + one_half * sine).astype(halves)
            if head * HEAD_WIDTH < q_cols:
                q_out[low, rows] = first
                q_out[high, rows] = second
            else:
                kv_own[k, low.start - q_cols : low.stop - q_cols, :] = first
                kv_own[k, high.start - q_cols : high.stop - q_cols, :] = second
        kv_own[k, kv_cols:, :] = (linear[q_cols + kv_cols :, :].astype(halves) * VSCALE).astype(halves)

    crossings, spreads_a, spreads_b, kept = [], [], [], []

    def share(k):
        slots = [kv_out.at[8 * k + i] for i in range(8)]
        keep = pltpu.make_async_copy(kv_own.at[k], slots[0], lsem.at[4 + k])
        keep.start()
        kept.append(keep)
        crossing = copies.make(kv_own.at[k], slots[4], place.cross)
        crossing.start()
        crossings.append(crossing)
        spread = Spread(copies, place, kv_own.at[k], slots[:4])
        spread.start()
        spreads_a.append(spread)
        spreads_b.append(Spread(copies, place, slots[4], slots[4:]))

    project(0)
    share(0)
    gather.wait_there()
    own_grad.wait()
    for k in range(CHUNKS):
        gather_g.put(k)
    project(1)
    share(1)
    keep_n = pltpu.make_async_copy(n_full, n_out, lsem.at[9])
    keep_n.start()
    fetch_o.forward()
    fetch_d.forward()
    spreads_a[0].relay()
    spreads_a[1].relay()
    crossings[0].wait_recv()
    spreads_b[0].start()
    fetch_o.relay()
    fetch_d.relay()
    gather_g.wait_there()
    spreads_b[0].relay()
    crossings[1].wait_recv()
    spreads_b[1].start()
    spreads_b[1].relay()
    fetch_o.finish()
    fetch_d.finish()
    gather_g.wait_here()
    for spread in spreads_a + spreads_b:
        spread.finish()
    for copy in kept + slice_stores + [keep_joined, keep_n]:
        copy.wait()
    for copy in crossings:
        copy.wait_send()
    for fetch in (fetch_joined, fetch_o, fetch_d):
        fetch.drain()
    gather.finish()
    gather_g.finish()


def first_part(counts, inverse, tokens, out_grad, gain, projections, weights):
    block, width = tokens.shape
    group = 4 * block
    shape = jax.ShapeDtypeStruct
    hidden = weights[2].shape[1]
    part = (width // 4, hidden)
    half_width = HEAD_WIDTH // 2
    q_cols, kv_cols = projections[0].shape[1], projections[1].shape[0]
    joined_cols = q_cols + 2 * kv_cols
    out_shape = (
        shape((q_cols, group), halves),
        shape((16, 2 * kv_cols, 2 * block), halves),
        shape((group, width), halves),
        shape((group, width), halves),
        shape((width, joined_cols), halves),
        shape(weights[0].shape, halves),
        shape(weights[1].shape, halves),
        shape(part, halves),
        shape(part, halves),
    )
    return pl.pallas_call(
        first_kernel,
        out_shape=out_shape,
        in_specs=[SM] + [VM] * 4 + [HB, VM, VM] + [HB] * 4,
        out_specs=(VM, HM, HM, VM, HM, HM, HM, HM, HM),
        scratch_shapes=[
            pltpu.VMEM((group, width), halves),
            pltpu.VMEM((width, joined_cols), halves),
            pltpu.VMEM((width // 4, joined_cols), halves),
            pltpu.VMEM((2,) + part, halves),
            pltpu.VMEM((half_width, group), floats),
            pltpu.VMEM((half_width, group), floats),
            pltpu.VMEM((joined_cols, 2 * block), floats),
            pltpu.VMEM((2, 2 * kv_cols, 2 * block), halves),
            *copy_semaphores(),
            pltpu.SemaphoreType.DMA((10,)),
        ],
        compiler_params=pltpu.CompilerParams(
            collective_id=2, has_side_effects=True, vmem_limit_bytes=63 << 20
        ),
        name="first",
    )(counts, inverse, tokens, out_grad, gain, *projections, *weights)


class PlaneSum:
    def __init__(self, copies, place, x_first, bufs, sent=None, come=None):
        self.place, self.bufs, self.x_first = place, bufs, x_first
        half, keep, come_two, home_one, home_two = bufs
        first, second = (place.over_x, place.over_y) if x_first else (place.over_y, place.over_x)
        self.at = place.y if x_first else place.x
        self.one = None if sent is None else copies.make(sent, come, first)
        self.two = copies.make(half, come_two, second)
        rows = home_one.shape[0]
        c = place.c
        home = (c * place.cross[0] + (1 - c) * place.beside[0], c * place.cross[1] + (1 - c) * place.beside[1])
        self.to_home = copies.make(half.at[pl.ds((1 - c) * rows, rows)], home_one, home)
        self.to_far = copies.make(half.at[pl.ds(rows, rows)], home_two, place.far)

    def cross_second(self, kept, come):
        if self.one is not None:
            self.one.wait()
        half, keep, come_two, home_one, home_two = self.bufs
        at = self.at
        half[...] = (kept[1 - at].astype(floats) + come[1 - at].astype(floats)).astype(halves)
        self.two.start()
        keep[...] = (kept[at].astype(floats) + come[at].astype(floats)).astype(halves)

    def go_home(self, exchanged=True):
        half, keep, come_two, home_one, home_two = self.bufs
        if exchanged:
            self.two.wait()
        half[...] = (keep[...].astype(floats) + come_two[...].astype(floats)).astype(halves)
        self.to_home.start()
        pl.when(self.place.odd)(self.to_far.start)

    def finish(self, out):
        half, keep, come_two, home_one, home_two = self.bufs
        rows = home_one.shape[0]
        self.to_home.wait()

        @pl.when(self.place.c == 0)
        def _():
            out[...] = half[:rows, :].astype(floats) + home_one[...].astype(floats)

        @pl.when(self.place.odd)
        def _():
            self.to_far.wait()
            out[...] = home_one[...].astype(floats) + home_two[...].astype(floats)


def plane_buffers(rows, cols):
    full = pltpu.VMEM((rows, cols), halves)
    part = pltpu.VMEM((rows // 2, cols), halves)
    return [full, full, full, part, part]


class RowBlocks:
    def __init__(self, ref, rows):
        self.ref, self.rows = ref, rows

    def at(self, i):
        return pl.ds(pl.multiple_of(i * self.rows, 128), self.rows)

    def __getitem__(self, i):
        return self.ref[self.at(i), :]

    def __setitem__(self, i, value):
        self.ref[self.at(i), :] = value


def outer_blocks(place, x_first, left, right, send_ref, keep_ref, on_sent):
    rows = left.shape[1] // 4
    for kept in (False, True):
        for i in range(2):
            if x_first:
                block = 2 * i + (place.x if kept else 1 - place.x)
            else:
                block = 2 * (place.y if kept else 1 - place.y) + i
            cols = pl.ds(pl.multiple_of(block * rows, 128), rows)
            value = lax.dot_general(
                left[:, cols], right, (((0,), (0,)), ((), ())), preferred_element_type=floats
            ).astype(halves)
            (keep_ref if kept else send_ref)[i] = value
        if not kept:
            on_sent()


def mid_kernel(ctx_ref, tok_ref, gain_ref, g_full, weight_refs, outs, scratch):
    (res_out, gres_out, e_full, near_out, down_half, down_mine, gate_half, gate_mine, up_keep, up_send,
     dctx_out, delta_out, gain_out) = outs
    (ctx, m_full, dh, hid, dgate, dup, w_o, w_d, w_g, w_u, down_send, down_keep, down_come, gate_send, gate_come, part_out, far_in, own_in, *bufs, ss, rs, wsem) = scratch
    place = Place()
    copies = Copies(ss, rs)
    block, width = tok_ref.shape
    two = 2 * block
    hidden = w_g.shape[1]
    wo_ref, wd_ref, wg_ref, wu_ref, wo_got, wd_got, slice_g, slice_u = weight_refs
    first_loads = [
        pltpu.make_async_copy(src, dst, wsem.at[i])
        for i, (src, dst) in enumerate(((wo_ref, w_o), (wd_ref, w_d)))
    ]
    first_loads_odd = [
        pltpu.make_async_copy(src, dst, wsem.at[i])
        for i, (src, dst) in enumerate(((wo_got, w_o), (wd_got, w_d)))
    ]

    def wait_first(i):
        pl.when(place.c == 0)(first_loads[i].wait)
        pl.when(place.odd)(first_loads_odd[i].wait)

    rows4 = slice_g.shape[0]
    at_slot = pl.ds(place.slot * rows4, rows4)
    loads = [
        pltpu.make_async_copy(src, dst, wsem.at[2 + i])
        for i, (src, dst) in enumerate(((wg_ref, w_g), (wu_ref, w_u)))
    ]
    loads_odd = [
        pltpu.make_async_copy(src, dst.at[at_slot], wsem.at[2 + i])
        for i, (src, dst) in enumerate(((slice_g, w_g), (slice_u, w_u)))
    ]

    @pl.when(place.c == 0)
    def _():
        for copy in first_loads + loads:
            copy.start()

    @pl.when(place.odd)
    def _():
        for copy in first_loads_odd + loads_odd:
            copy.start()

    ctx[...] = ctx_ref[...].T
    meet((place.beside, place.near, place.over_x, place.over_y))
    fetches = [PlaneFetch(copies, place, w_g), PlaneFetch(copies, place, w_u)]

    @pl.when(place.odd)
    def _():
        for copy in loads_odd:
            copy.wait()

    for fetch in fetches:
        fetch.forward()
    sum_one = GroupSum(copies, bufs, place)
    gather_one = GroupGather(copies, m_full, block, place)
    sum_two = GroupSum(copies, bufs, place)
    gather_two = GroupGather(copies, e_full, block, place)

    def project(k, put):
        rows = slice(k * two, (k + 1) * two)
        tiles(width, 256, lambda cols: put(cols, dot_nn(ctx[rows, :], w_o[:, cols])))

    wait_first(0)
    sum_one.run(project)
    wait_first(1)

    def back_hidden(cols):
        for rows in (slice(0, two), slice(two, 2 * two)):
            dh[rows, cols] = dot_nt(g_full[rows, :], w_d[cols, :]).astype(halves)

    tiles(hidden, 256, back_hidden)
    chunk = block // CHUNKS
    for k in range(CHUNKS):
        at = pl.ds(k * chunk, chunk)
        res = tok_ref[at, :].astype(floats) + sum_one.take(k)
        res_out[at, :] = res
        root = lax.rsqrt(jnp.mean(res * res, axis=-1, keepdims=True) + eps_norm)
        m_full[at, :] = (res * root * gain_ref[...]).astype(halves)
        gather_one.put(k)
        if k == 1:
            for fetch in fetches:
                fetch.relay()
    sum_one.finish()

    def there(h):
        rows = block // 2
        return [slice(two + h * rows, two + (h + 1) * rows), slice(3 * block + h * rows, 3 * block + (h + 1) * rows)]

    def read(ref, parts):
        values = [ref[rows, :] for rows in parts]
        return values[0] if len(values) == 1 else jnp.concatenate(values, axis=0)

    def write(ref, parts, cols, value):
        rows = value.shape[0] // len(parts)
        for i, part in enumerate(parts):
            ref[part, cols] = value[i * rows : (i + 1) * rows]

    def activate(parts):
        def one(cols):
            left = read(m_full, parts)
            gate_pre = dot_nn(left, w_g[:, cols])
            up_pre = dot_nn(left, w_u[:, cols])
            back = [dh[rows, cols] for rows in parts]
            back = (back[0] if len(back) == 1 else jnp.concatenate(back, axis=0)).astype(floats)
            sigma = 1.0 / (1.0 + jnp.exp(-gate_pre))
            silu = gate_pre * sigma
            write(hid, parts, cols, (silu * up_pre).astype(halves))
            write(dgate, parts, cols, (back * up_pre * (sigma + silu * (1.0 - sigma))).astype(halves))
            write(dup, parts, cols, (back * silu).astype(halves))

        tiles(hidden, 256, one)

    def partial_out(parts):
        def one(cols):
            write(part_out, parts, cols, dot_nn(read(hid, parts), w_d[:, cols]).astype(halves))

        tiles(width, 256, one)

    def back_norm(parts, put):
        def one(cols):
            put(cols, dot_nt(read(dgate, parts), w_g[cols, :]) + dot_nt(read(dup, parts), w_u[cols, :]))

        tiles(width, 256, one)

    for fetch in fetches:
        fetch.finish()

    @pl.when(place.c == 0)
    def _():
        for copy in loads:
            copy.wait()

    here = [slice(0, two)]
    gather_one.wait_here()
    activate(here)
    partial_out(here)
    whole = [slice(two, 2 * two)]
    gather_one.wait_there()
    at = pl.ds(0, block)
    activate(whole)
    back_norm(whole, lambda cols, value: sum_two.put_there(at, cols, value))
    sum_two.send_far(at)
    gather_one.finish()
    back_norm(here, sum_two.put_here)
    sum_two.send_beside()
    sum_two.send_near(CHUNKS)
    partial_out(whole)
    to_side = [
        copies.make(part_out.at[pl.ds(3 * block, block)], far_in, place.beside),
        copies.make(part_out.at[pl.ds(block, block)], own_in, place.beside),
    ]
    for copy in to_side:
        copy.start()
    down_over = copies.make(down_send, down_come, place.over_x)
    outer_blocks(place, True, g_full, hid[...], down_send, down_keep, down_over.start)
    gate_keep = RowBlocks(dh, width // 4)
    gate_over = copies.make(gate_send, gate_come, place.over_y)
    outer_blocks(place, False, m_full, dgate[...], gate_send, gate_keep, gate_over.start)
    gain_out[...] = jnp.zeros_like(gain_out)
    for k in range(CHUNKS):
        at = pl.ds(k * chunk, chunk)
        back = sum_two.take(k)
        res = res_out[at, :]
        root = lax.rsqrt(jnp.mean(res * res, axis=-1, keepdims=True) + eps_norm)
        weighted = back * gain_ref[...]
        slope = jnp.mean(weighted * res, axis=-1, keepdims=True)
        grad = g_full[at, :].astype(floats) + root * weighted - res * (root * root * root * slope)
        gain_out[...] += jnp.sum(back * res * root, axis=0, keepdims=True)
        gres_out[at, :] = grad
        e_full[at, :] = grad.astype(halves)
        gather_two.put(k)
    sum_two.finish()
    outer_blocks(place, True, m_full, dup[...], up_send, up_keep, lambda: None)

    def back_context(parts):
        grad = dot_nt(w_o[...], read(e_full, parts)).astype(halves)
        rows = grad.shape[1] // len(parts)
        for i, part in enumerate(parts):
            piece = grad[:, i * rows : (i + 1) * rows]
            dctx_out[:, part] = piece
            prod = piece.astype(floats) * ctx_ref[:, part].astype(floats)
            for hd in range(delta_out.shape[0]):
                delta_out[hd : hd + 1, part] = VSCALE * jnp.sum(
                    prod[hd * HEAD_WIDTH : (hd + 1) * HEAD_WIDTH], axis=0, keepdims=True
                )

    for copy in to_side:
        copy.wait()
    for k in range(CHUNKS):
        at = pl.ds(k * chunk, chunk)
        near = pl.ds(two + k * chunk, chunk)
        near_out[at, :] = (part_out[near, :].astype(floats) + far_in[at, :].astype(floats)).astype(halves)
        res_out[at, :] += part_out[at, :].astype(floats) + own_in[at, :].astype(floats)
    gather_two.wait_here()
    back_context(here)
    gather_two.wait_there(0, 2)
    back_context(there(0))
    down_over.wait()
    at = place.y
    down_half[...] = (down_keep[1 - at].astype(floats) + down_come[1 - at].astype(floats)).astype(halves)
    down_mine[...] = (down_keep[at].astype(floats) + down_come[at].astype(floats)).astype(halves)
    gather_two.wait_there(1, 2)
    back_context(there(1))
    gather_two.finish()
    for fetch in fetches:
        fetch.drain()
    gate_over.wait()
    at = place.x
    gate_half[...] = (gate_keep[1 - at].astype(floats) + gate_come[1 - at].astype(floats)).astype(halves)
    gate_mine[...] = (gate_keep[at].astype(floats) + gate_come[at].astype(floats)).astype(halves)


def middle(context_t, tokens, gain, grad_full, weights):
    q_cols, group = context_t.shape
    block, width = tokens.shape
    hidden = weights[2].shape[1]
    shape = jax.ShapeDtypeStruct
    out_shape = (
        shape((block, width), floats),
        shape((block, width), floats),
        shape((group, width), halves),
        shape((block, width), halves),
        *[shape((width // 4, hidden), halves)] * 4,
        *[shape((2, width // 4, hidden), halves)] * 2,
        shape((q_cols, group), halves),
        shape((q_cols // HEAD_WIDTH, group), floats),
        shape((1, width), floats),
    )
    scratch = [
        pltpu.VMEM((group, q_cols), halves),
        pltpu.VMEM((group, width), halves),
        *[pltpu.VMEM((group, hidden), halves)] * 4,
        *[pltpu.VMEM(weight.shape, halves) for weight in weights[:4]],
        *[pltpu.VMEM((2, width // 4, hidden), halves)] * 5,
        pltpu.VMEM((group, width), halves),
        *[pltpu.VMEM((block, width), halves)] * 2,
        *[pltpu.VMEM((block, width), floats)] * 2,
        *[pltpu.VMEM((block, width), halves)] * 6,
        *copy_semaphores(),
        pltpu.SemaphoreType.DMA((4,)),
    ]

    def kernel(*refs):
        mid_kernel(*refs[:4], refs[4:12], refs[12:25], refs[25:])

    return pl.pallas_call(
        kernel,
        out_shape=out_shape,
        in_specs=[VM] * 4 + [HB] * 8,
        out_specs=(VM,) * 13,
        scratch_shapes=scratch,
        compiler_params=pltpu.CompilerParams(
            collective_id=1, has_side_effects=True, vmem_limit_bytes=63 << 20
        ),
        name="middle",
    )(context_t, tokens, gain, grad_full, *weights)


def last_kernel(ins, outs, scratch):
    (counts, inverse_ref, dq_ref, dkv_ref, n_ref, joined_ref, tok_ref, gain_ref, gres_ref, e_ref, ctx_ref,
     gain_mlp_ref, *mlp) = ins
    (in_grad, gains_out, gate_out, up_out, down_out, q_out, kv_out, o_out) = outs
    (full, ctx, d_lin, acc_a, acc_b, own, x_in, y_in, rel_in, cross_in, cross_out, kept, come,
     gains, gains_in, cos_ref, sin_ref, joined, *rest) = scratch
    bufs_mlp = [rest[5 * i : 5 * i + 5] for i in range(3)]
    rest = rest[15:]
    bufs_attn = [rest[8 * i : 8 * i + 8] for i in range(3)]
    rest = rest[24:]
    sum_bufs, (ss, rs, lsem) = rest[:8], rest[8:]
    place = Place()
    copies = Copies(ss, rs)
    block, width = tok_ref.shape
    two = 2 * block
    q_cols = dq_ref.shape[0]
    kv_cols = own.shape[1] // 2
    half_width = HEAD_WIDTH // 2

    load_e = pltpu.make_async_copy(e_ref, full, lsem.at[0])
    load_e.start()
    load_joined = pltpu.make_async_copy(joined_ref, joined, lsem.at[11])
    load_joined.start()
    order = (4, 12, 0, 8)
    own_loads = [
        pltpu.make_async_copy(dkv_ref.at[at], own.at[i], lsem.at[1 + i]) for i, at in enumerate(order)
    ]
    y_loads = [
        pltpu.make_async_copy(dkv_ref.at[at + 2], y_in.at[i], lsem.at[5 + i])
        for i, at in enumerate(order)
    ]
    for copy in own_loads:
        copy.start()

    @pl.when(place.corner)
    def _():
        for copy in y_loads:
            copy.start()

    def load_mlp(i):
        return [
            pltpu.make_async_copy(mlp[2 * i], kept, lsem.at[9]),
            pltpu.make_async_copy(mlp[2 * i + 1], come, lsem.at[10]),
        ]

    down_loads = [
        pltpu.make_async_copy(mlp[i], bufs_mlp[0][1 + i], lsem.at[12 + i]) for i in range(2)
    ]
    gate_loads = [
        pltpu.make_async_copy(mlp[2 + i], bufs_mlp[1][1 + i], lsem.at[14 + i]) for i in range(2)
    ]
    loads = load_mlp(2)
    for copy in down_loads + gate_loads + loads:
        copy.start()
    gains[0, 0:1, :] = gain_mlp_ref[...]
    gains[0, 1:2, :] = jnp.zeros_like(gain_mlp_ref)
    meet((place.beside, place.near, place.far, place.cross, place.over_x, place.over_y))

    back_rel = [copies.make(dkv_ref.at[at + 3], rel_in.at[i], place.over_x) for i, at in enumerate(order)]
    back_x = [copies.make(dkv_ref.at[at + 1], x_in.at[i], place.over_x) for i, at in enumerate(order)]
    back_y = [copies.make(dkv_ref.at[at + 2], y_in.at[i], place.over_y) for i, at in enumerate(order)]
    back_sum = [copies.make(y_in.at[i], y_in.at[i], place.over_y) for i in range(4)]
    crossing = [copies.make(cross_out.at[i], cross_in.at[i], place.cross) for i in range(2)]
    def start_back(i):
        pl.when(place.turn)(back_rel[i].start)
        pl.when(place.x == 1)(back_x[i].start)
        pl.when(place.turn)(back_y[i].start)

    start_back(0)
    start_back(1)

    def corner_sum(i):
        @pl.when(place.corner)
        def _():
            back_rel[i].wait_recv()
            y_loads[i].wait()
            y_in[i] = (y_in[i].astype(floats) + rel_in[i].astype(floats)).astype(halves)
            back_sum[i].start()

    def home_sum(i, put):
        own_loads[i].wait()
        acc_b[...] = own[i].astype(floats)

        @pl.when(place.x == 0)
        def _():
            back_x[i].wait_recv()
            acc_b[...] += x_in[i].astype(floats)

        @pl.when((place.y == 0) & (place.x == 0))
        def _():
            back_y[i].wait_recv()
            acc_b[...] += y_in[i].astype(floats)

        @pl.when((place.y == 0) & (place.x == 1))
        def _():
            back_sum[i].wait_recv()
            acc_b[...] += y_in[i].astype(floats)

        put()

    sums = []
    for i, x_first in enumerate((True, False, True)):
        sums.append(PlaneSum(copies, place, x_first, bufs_mlp[i]))
    for copy in down_loads:
        copy.wait()
    sums[0].go_home(exchanged=False)
    corner_sum(0)
    for copy in loads:
        copy.wait()
    sums[2].cross_second(kept, come)
    start_back(2)
    start_back(3)
    ctx[...] = ctx_ref[...].T
    rope_tables(counts, inverse_ref, cos_ref, sin_ref)

    attn_sums = []
    for i, x_first in enumerate((False, True, False)):
        sent, keep, got = bufs_attn[i][:3]
        attn_sums.append(PlaneSum(copies, place, x_first, bufs_attn[i][3:], sent, got))

    def attn_grad(i, left, right):
        sent, keep, got = bufs_attn[i][:3]
        outer_blocks(place, attn_sums[i].x_first, left, right, sent, keep, attn_sums[i].one.start)

    corner_sum(1)
    load_e.wait()
    attn_grad(0, full, ctx[...])
    load_n = pltpu.make_async_copy(n_ref, full, lsem.at[0])
    load_n.start()

    def cross_back(i):
        def put():
            cross_out[i] = acc_b[...].astype(halves)
            crossing[i].start()

        home_sum(i, put)

    def unturn(value, at, first_row):
        low, high = value[:half_width], value[half_width:]
        cosine, sine = cos_ref[:, at], sin_ref[:, at]
        turned = jnp.concatenate([low * cosine + high * sine, high * cosine - low * sine], axis=0)
        d_lin[first_row : first_row + HEAD_WIDTH, at] = turned.astype(halves)

    cross_back(0)
    corner_sum(2)
    everything = slice(0, 2 * two)
    for head in range(q_cols // HEAD_WIDTH):
        unturn(dq_ref[head * HEAD_WIDTH : (head + 1) * HEAD_WIDTH, :], everything, head * HEAD_WIDTH)
    cross_back(1)
    corner_sum(3)
    load_n.wait()
    attn_grad(1, full, d_lin[:q_cols, :].T)
    for copy in gate_loads:
        copy.wait()
    sums[1].go_home(exchanged=False)
    sums[2].go_home()

    def second(i):
        sent, keep, got = bufs_attn[i][:3]
        attn_sums[i].cross_second(keep, got)

    second(0)

    def keep_a(k):
        def put():
            acc_a[:, k * two : (k + 1) * two] = acc_b[...]

        home_sum(2 + k, put)

    keep_a(0)
    keep_a(1)
    second(1)
    attn_sums[0].go_home()
    for k in range(2):
        crossing[k].wait_recv()
        lanes = slice(k * two, (k + 1) * two)
        total = acc_a[:, lanes] + cross_in[k].astype(floats)
        for head in range(kv_cols // HEAD_WIDTH):
            rows = slice(head * HEAD_WIDTH, (head + 1) * HEAD_WIDTH)
            unturn(total[rows], lanes, q_cols + head * HEAD_WIDTH)
        d_lin[q_cols + kv_cols :, lanes] = total[kv_cols:].astype(halves)

    group_sum = GroupSum(copies, sum_bufs, place)
    load_joined.wait()

    def back_norm(k, put):
        rows = slice(k * two, (k + 1) * two)
        left = d_lin[:, rows].T

        def one(cols):
            value = dot_nt(left, joined[cols, :])
            put(cols, value)
            gains[0, 1:2, cols] += jnp.sum(value * full[rows, cols].astype(floats), axis=0, keepdims=True)

        tiles(width, 256, one)

    group_sum.run(back_norm)
    gains[0, 1:2, :] = gains[0, 1:2, :] / gain_ref[...]
    attn_grad(2, full, d_lin[q_cols:, :].T)
    attn_sums[1].go_home()
    for stage, device in enumerate((place.beside, place.over_x, place.over_y, place.near, place.far)):
        copy = copies.make(gains.at[stage], gains_in.at[stage], device)
        copy.start()
        copy.wait()
        if stage < 4:
            gains[stage + 1] = gains[stage] + gains_in[stage]
        else:
            gains_out[...] = gains[stage] + gains_in[stage]
        if stage == 2:
            second(2)
    for plane, out in zip(sums, (down_out, gate_out, up_out)):
        plane.finish(out)
    attn_sums[2].go_home()
    chunk = block // CHUNKS
    for k in range(CHUNKS):
        at = pl.ds(k * chunk, chunk)
        back = group_sum.take(k)
        tok = tok_ref[at, :].astype(floats)
        root = lax.rsqrt(jnp.mean(tok * tok, axis=-1, keepdims=True) + eps_norm)
        weighted = back * gain_ref[...]
        slope = jnp.mean(weighted * tok, axis=-1, keepdims=True)
        in_grad[at, :] = gres_ref[at, :] + root * weighted - tok * (root * root * root * slope)
    for plane, out in zip(attn_sums, (o_out, q_out, kv_out)):
        plane.finish(out)
    group_sum.finish()
    for i in range(4):
        pl.when(place.turn)(back_rel[i].wait_send)
        pl.when(place.x == 1)(back_x[i].wait_send)
        pl.when(place.turn)(back_y[i].wait_send)
        pl.when(place.corner)(back_sum[i].wait_send)
    for copy in crossing:
        copy.wait_send()


def last_part(counts, inverse, d_query_t, d_kv, normed, joined, tokens, gain, gres, e_full, context_t, gain_mlp, mlp):
    block, width = tokens.shape
    group = 4 * block
    q_cols, kv_all = d_query_t.shape[0], d_kv.shape[1]
    kv_cols = kv_all // 2
    hidden = mlp[0].shape[1]
    per = width // 8
    shape = jax.ShapeDtypeStruct
    out_shape = (
        shape((block, width), floats),
        shape((2, width), floats),
        *[shape((per, hidden), floats)] * 3,
        shape((per, q_cols), floats),
        shape((per, kv_all), floats),
        shape((per, q_cols), floats),
    )
    piece = (kv_all, 2 * block)
    scratch = [
        pltpu.VMEM((group, width), halves),
        pltpu.VMEM((group, q_cols), halves),
        pltpu.VMEM((joined.shape[1], group), halves),
        pltpu.VMEM((kv_all, group), floats),
        pltpu.VMEM(piece, floats),
        *[pltpu.VMEM((4,) + piece, halves)] * 4,
        *[pltpu.VMEM((2,) + piece, halves)] * 2,
        *[pltpu.VMEM((2, width // 4, hidden), halves)] * 2,
        *[pltpu.VMEM((5, 2, width), floats)] * 2,
        *[pltpu.VMEM((HEAD_WIDTH // 2, group), floats)] * 2,
        pltpu.VMEM(joined.shape, halves),
    ]
    for _ in range(3):
        scratch += plane_buffers(width // 4, hidden)
    for cols in (q_cols, q_cols, kv_all):
        scratch += [pltpu.VMEM((2, width // 4, cols), halves)] * 3 + plane_buffers(width // 4, cols)
    scratch += [
        *[pltpu.VMEM((block, width), floats)] * 2,
        *[pltpu.VMEM((block, width), halves)] * 6,
        *copy_semaphores(),
        pltpu.SemaphoreType.DMA((16,)),
    ]

    def kernel(*refs):
        last_kernel(refs[:18], refs[18:26], refs[26:])

    return pl.pallas_call(
        kernel,
        out_shape=out_shape,
        in_specs=[SM, VM, VM, HM, HM, HM, VM, VM, VM, HM, VM, VM] + [HM] * 6,
        out_specs=(VM,) * 8,
        scratch_shapes=scratch,
        compiler_params=pltpu.CompilerParams(
            collective_id=3, has_side_effects=True, vmem_limit_bytes=63 << 20
        ),
        name="last",
    )(counts, inverse, d_query_t, d_kv, normed, joined, tokens, gain, gres, e_full, context_t, gain_mlp, *mlp)


def finish_kernel(*refs):
    base, near, kv_sum, *ready = refs[:9]
    output, k_out, v_out, *outs = refs[9:18]
    out_buf, k_buf, v_buf, sem = refs[18:]
    copies = [pltpu.make_async_copy(src, dst, sem.at[i]) for i, (src, dst) in enumerate(zip(ready, outs))]
    for copy in copies:
        copy.start()
    out_buf[...] = (base[...] + near[...].astype(floats)).astype(halves)
    kv_cols = k_buf.shape[1]
    k_buf[...] = kv_sum[:, :kv_cols]
    v_buf[...] = kv_sum[:, kv_cols:]
    more = [
        pltpu.make_async_copy(src, dst, sem.at[len(copies) + i])
        for i, (src, dst) in enumerate(((out_buf, output), (k_buf, k_out), (v_buf, v_out)))
    ]
    for copy in more:
        copy.start()
    for copy in copies + more:
        copy.wait()


def finish(base, near, kv_sum, *ready):
    shape = jax.ShapeDtypeStruct
    rows, cols = kv_sum.shape
    small = (rows, cols // 2)
    return pl.pallas_call(
        finish_kernel,
        out_shape=(
            shape(base.shape, halves),
            shape(small, floats),
            shape(small, floats),
            *[shape(a.shape, a.dtype) for a in ready],
        ),
        in_specs=[VM] * (3 + len(ready)),
        out_specs=(HM,) * (3 + len(ready)),
        scratch_shapes=[
            pltpu.VMEM(base.shape, halves),
            pltpu.VMEM(small, floats),
            pltpu.VMEM(small, floats),
            pltpu.SemaphoreType.DMA((3 + len(ready),)),
        ],
        compiler_params=pltpu.CompilerParams(vmem_limit_bytes=63 << 20),
        name="finish",
    )(base, near, kv_sum, *ready)


def routes(target):
    pairs = []
    for index in range(32):
        dp, z = divmod(index, 4)
        there = target(dp // 4, dp // 2 % 2, dp % 2, z)
        if there is not None:
            y, x, c, z = there
            pairs.append((index, (y * 4 + x * 2 + c) * 4 + z))
    return pairs


ROUTES = {
    "core": routes(lambda y, x, c, z: (y, x, 1 - c, z)),
    "x": routes(lambda y, x, c, z: (y, 1 - x, c, z)),
    "y": routes(lambda y, x, c, z: (1 - y, x, c, z)),
    "near": routes(lambda y, x, c, z: (y, x, c, z ^ 1)),
    "far": routes(lambda y, x, c, z: (y, x, c, z ^ 2)),
    "cross": routes(lambda y, x, c, z: (y, x, 1 - c, z ^ 2)),
    "odd_far": routes(lambda y, x, c, z: (y, x, c, z ^ 2) if c else None),
    "odd_x": routes(lambda y, x, c, z: (y, 1 - x, c, z) if c else None),
    "odd_y": routes(lambda y, x, c, z: (1 - y, x, c, z) if c else None),
    "odd_xy": routes(lambda y, x, c, z: (1 - y, 1 - x, c, z) if c else None),
    "home": routes(lambda y, x, c, z: (y, x, 0, z ^ 2) if c else (y, x, 1, z)),
    "x_up": routes(lambda y, x, c, z: None if x else (y, 1, c, z)),
    "y_up": routes(lambda y, x, c, z: None if y else (1, x, c, z)),
    "x_down": routes(lambda y, x, c, z: (y, 0, c, z) if x else None),
    "y_down": routes(lambda y, x, c, z: (0, x, c, z) if y else None),
    "relay": routes(lambda y, x, c, z: (1, 0, c, z) if x and y else None),
    "unrelay": routes(lambda y, x, c, z: (1, 1, c, z) if y and not x else None),
}


def send(block, way):
    return lax.ppermute(block, ("dp", "tp"), ROUTES[way])


def local_regrouped(
    tokens,
    out_grad,
    segment_ids,
    attn_gain,
    query_weight,
    key_matrix,
    value_matrix,
    output_weight,
    mlp_gain,
    gate_weight,
    up_weight,
    down_weight,
):
    block = tokens.shape[0]
    dp = lax.axis_index("dp")
    half_width = HEAD_WIDTH // 2
    gain_attn, gain_mlp = attn_gain.astype(floats)[None, :], mlp_gain.astype(floats)[None, :]
    counts = jnp.sum(
        (segment_ids[None, :] < jnp.arange(1, 4, dtype=jnp.int32)[:, None]).astype(jnp.int32), axis=1
    )
    inverse = 1.0 / rope_base ** (jnp.arange(half_width, dtype=floats) * 2.0 / HEAD_WIDTH)
    inverse = inverse[:, None]
    q_t, pieces, normed_full, grad_full, joined, weight_o, weight_d, slice_g, slice_u = first_part(
        counts, inverse, tokens, out_grad, gain_attn,
        (query_weight, key_matrix.T, value_matrix.T),
        (output_weight, down_weight, gate_weight, up_weight),
    )
    slices = [send(part, "odd_far") for part in (slice_g, slice_u)]
    context_t, log_total = attend_forward(counts, q_t, pieces)
    (
        out_base, grad_residual, attn_grad_full, out_near, down_half, down_mine, gate_half, gate_mine,
        up_keep, up_send, d_context_t, delta, mlp_gain_part,
    ) = middle(
        context_t, tokens, gain_mlp, grad_full,
        (output_weight, down_weight, gate_weight, up_weight, weight_o, weight_d, *slices),
    )
    gate_come = send(gate_half, "x")
    up_come = send(up_send, "x")
    down_come = send(down_half, "y")
    out_near = send(out_near, "near")
    d_query_t, d_pieces = attend_backward(counts, q_t, d_context_t, log_total, delta, pieces)
    input_grad, gains, gate_sum, up_sum, down_sum, query_sum, kv_sum, output_sum = last_part(
        counts, inverse, d_query_t, d_pieces, normed_full, joined, tokens, gain_attn,
        grad_residual, attn_grad_full, context_t, mlp_gain_part,
        (down_mine, down_come, gate_mine, gate_come, up_keep, up_come),
    )
    per = gains.shape[1] // 8
    gains = lax.dynamic_slice_in_dim(gains, dp * per, per, axis=1)
    output, key_sum, value_sum, input_grad, query_sum, output_sum, gate_sum, up_sum, down_sum = finish(
        out_base, out_near, kv_sum, input_grad, query_sum, output_sum, gate_sum, up_sum, down_sum
    )
    return (
        output,
        input_grad,
        gains[1],
        query_sum,
        key_sum,
        value_sum,
        output_sum.T,
        gains[0],
        gate_sum,
        up_sum,
        down_sum.T,
    )


def solution(mesh):
    regroup = mesh.shape["dp"] == 8 and mesh.shape["tp"] == 4
    chosen = local_regrouped if regroup else local
    return jax.shard_map(
        chosen,
        mesh=mesh,
        in_specs=(
            P(("dp", "tp"), None),
            P(("dp", "tp"), None),
            P(),
            P(),
            P(None, "tp"),
            P(None, "tp"),
            P(None, "tp"),
            P("tp", None),
            P(),
            P(None, "tp"),
            P(None, "tp"),
            P("tp", None),
        ),
        out_specs=(
            P(("dp", "tp"), None),
            P(("dp", "tp"), None),
            P("dp"),
            P("dp", "tp"),
            P("dp", "tp"),
            P("dp", "tp"),
            P("tp", "dp"),
            P("dp"),
            P("dp", "tp"),
            P("dp", "tp"),
            P("tp", "dp"),
        ),
        check_vma=False,
    )
```

```python
import functools

import jax
import jax.numpy as jnp
from jax import lax
from jax.experimental import pallas as pl
from jax.experimental.pallas import tpu as pltpu
from jax.sharding import PartitionSpec as P

HEAD_WIDTH = 96
BLK = 256
LOG2E = 1.4426950408889634
SCORE = LOG2E * HEAD_WIDTH ** (-0.5)
VSCALE = 2.0 ** -9
FAR_BASE = 1 << 24
floats = jnp.float32
halves = jnp.bfloat16


def dot_nn(a, b):
    return jnp.dot(a, b, preferred_element_type=floats)


def dot_nt(a, b):
    return lax.dot_general(a, b, (((1,), (1,)), ((), ())), preferred_element_type=floats)


def token_base(j, core, pair, side):
    return ((2 * j + core) * 4 + 2 * pair + side) * BLK


def group_bases():
    dp, z = lax.axis_index("dp"), lax.axis_index("tp")
    j, c, pair, side = dp // 2, lax.rem(dp, 2), z // 2, lax.rem(z, 2)
    return [
        token_base(j, core, pair, at) for at in (side, 1 - side) for core in (c, 1 - c)
    ]


def item_start(counts_ref, token):
    start = jnp.zeros_like(token)
    for i in range(3):
        start = jnp.where(token >= counts_ref[i], counts_ref[i], start)
    return start


def group_index():
    lanes = lax.broadcasted_iota(jnp.int32, (1, BLK), 1)
    return jnp.concatenate([lanes + base for base in group_bases()], axis=1)


def fill_places(counts_ref, sc, tok_ref, start_ref):
    dp, z = lax.axis_index("dp"), lax.axis_index("tp")
    j, c, pair, side = dp // 2, lax.rem(dp, 2), z // 2, lax.rem(z, 2)
    x, y = lax.rem(j, 2), j // 2
    kb = 0
    for side_of in (side, 1 - side):
        for cores, pair_of in (((c, 1 - c), pair), ((1 - c, c), 1 - pair)):
            for j_of, present in ((j, None), (j - 1, x), (j - 2, y), (j - 1, y * (1 - x))):
                for core in cores:
                    base = token_base(j_of, core, pair_of, side_of)
                    sc[0, kb] = base if present is None else jnp.where(present == 1, base, FAR_BASE)
                    kb += 1
    for qb, base in enumerate(group_bases()):
        sc[1, qb] = base
        sc[2, qb] = item_start(counts_ref, base)
        sc[3, qb] = item_start(counts_ref, base + (BLK - 1))
    index = group_index()
    tok_ref[...] = index
    start_ref[...] = item_start(counts_ref, index)


def pair_state(sc, kb, qb):
    key_base = sc[0, kb]
    q_base, least, most = sc[1, qb], sc[2, qb], sc[3, qb]
    needed = (key_base <= q_base + (BLK - 1)) & (key_base + (BLK - 1) >= least)
    whole = (key_base + (BLK - 1) <= q_base) & (key_base >= most)
    return key_base, needed, whole


def allowed_mask(key_bases, tok_ref, start_ref, lanes):
    masks = []
    for key_base in key_bases:
        keys = key_base + lax.broadcasted_iota(jnp.int32, (BLK, BLK), 0)
        masks.append((keys <= tok_ref[0:1, lanes]) & (keys >= start_ref[0:1, lanes]))
    return masks[0] if len(masks) == 1 else jnp.concatenate(masks, axis=0)


def piece_used(sc, piece, blocks):
    used = False
    for kb in range(2):
        for qb in range(blocks):
            used = used | pair_state(sc, 2 * piece + kb, qb)[1]
    return used


def for_piece(sc, piece, qb, unit):
    one_base, one, one_whole = pair_state(sc, 2 * piece, qb)
    two_base, two, two_whole = pair_state(sc, 2 * piece + 1, qb)
    both, free = one & two, one_whole & two_whole
    bases = (one_base, two_base)
    pl.when(both & free)(lambda: unit((0, 1), bases, False))
    pl.when(both & jnp.logical_not(free))(lambda: unit((0, 1), bases, True))
    pl.when(one & jnp.logical_not(two))(lambda: unit((0,), bases[:1], True))
    pl.when(two & jnp.logical_not(one))(lambda: unit((1,), bases[1:], True))


def fwd_kernel(n, width, counts, q_ref, pieces, *refs):
    out_acc, out_sum = refs[:2]
    kv, keys_nat, acc, total, q_wide, sc, tok_ref, start_ref, sem = refs[2:]
    for i in range(n):
        pltpu.make_async_copy(pieces.at[i], kv.at[i], sem.at[i]).start()
    acc[...] = jnp.zeros_like(acc)
    total[...] = jnp.zeros_like(total)
    fill_places(counts, sc, tok_ref, start_ref)
    heads_kv = pieces.shape[1] // (2 * HEAD_WIDTH)
    group = q_ref.shape[0] // (heads_kv * HEAD_WIDTH)
    v_off = heads_kv * HEAD_WIDTH
    places = [
        (h, slice((h * group + g) * HEAD_WIDTH, (h * group + g + 1) * HEAD_WIDTH), slice(qb * BLK, (qb + 1) * BLK),
         slice(h * HEAD_WIDTH, (h + 1) * HEAD_WIDTH), slice((qb * group + g) * BLK, (qb * group + g + 1) * BLK), h * group + g)
        for h in range(heads_kv) for g in range(group) for qb in range(q_ref.shape[1] // BLK)
    ]
    for h, rows, lanes, wrows, wlanes, hd in places:
        q_wide[wrows, wlanes] = q_ref[rows, lanes]

    def key_piece(piece, carry):
        pltpu.make_async_copy(pieces.at[piece], kv.at[piece], sem.at[piece]).wait()
        def query_block(qb, carry):
            lanes = pl.ds(pl.multiple_of(qb * BLK, BLK), BLK)
            wide = pl.ds(pl.multiple_of(qb * (group * BLK), group * BLK), group * BLK)

            def unit(subs, bases, masked):
                keys = slice(subs[0] * BLK, (subs[-1] + 1) * BLK)
                if masked:
                    allowed = allowed_mask(bases, tok_ref, start_ref, lanes)
                    allowed = jnp.concatenate([allowed] * group, axis=1)
                scores = [
                    dot_nn(keys_nat[h, keys], q_wide[h * HEAD_WIDTH : (h + 1) * HEAD_WIDTH, wide])
                    for h in range(heads_kv)
                ]
                weights = [jnp.exp2(s * SCORE) for s in scores]
                if masked:
                    weights = [jnp.where(allowed, w, 0.0) for w in weights]
                sums = [jnp.sum(w, axis=0, keepdims=True) for w in weights]
                parts = [
                    dot_nn(
                        kv[piece, v_off + h * HEAD_WIDTH : v_off + (h + 1) * HEAD_WIDTH, keys],
                        weights[h].astype(halves),
                    )
                    for h in range(heads_kv)
                ]
                for h in range(heads_kv):
                    total[h : h + 1, wide] += sums[h]
                    acc[h * HEAD_WIDTH : (h + 1) * HEAD_WIDTH, wide] += parts[h]

            for_piece(sc, piece, qb, unit)
            return carry

        @pl.when(piece_used(sc, piece, q_ref.shape[1] // BLK))
        def _():
            for h in range(heads_kv):
                keys_nat[h] = kv[piece, h * HEAD_WIDTH : (h + 1) * HEAD_WIDTH, :].T
            lax.fori_loop(0, q_ref.shape[1] // BLK, query_block, 0)

        return carry

    lax.fori_loop(0, n, key_piece, 0)
    for h, rows, lanes, wrows, wlanes, hd in places:
        row = total[h : h + 1, wlanes]
        out_acc[rows, lanes] = (acc[wrows, wlanes] * ((1.0 / VSCALE) / row)).astype(halves)
        out_sum[hd : hd + 1, lanes] = jnp.log2(row)


VM = pl.BlockSpec(memory_space=pltpu.VMEM)
SM = pl.BlockSpec(memory_space=pltpu.SMEM)
HB = pl.BlockSpec(memory_space=pl.ANY)
HM = pl.BlockSpec(memory_space=pltpu.HBM)


def place_scratch(blocks, tokens):
    return [
        pltpu.SMEM((4, blocks), jnp.int32),
        pltpu.VMEM((1, tokens), jnp.int32),
        pltpu.VMEM((1, tokens), jnp.int32),
    ]


def attend_forward(counts, q_t, pieces):
    n, width = pieces.shape[0], pieces.shape[2]
    heads = q_t.shape[0] // HEAD_WIDTH
    heads_kv = pieces.shape[1] // (2 * HEAD_WIDTH)
    tokens = q_t.shape[1]
    wide = tokens * heads // heads_kv
    return pl.pallas_call(
        functools.partial(fwd_kernel, n, width),
        out_shape=(
            jax.ShapeDtypeStruct(q_t.shape, halves),
            jax.ShapeDtypeStruct((heads, tokens), floats),
        ),
        in_specs=[SM, VM, HM],
        out_specs=(VM, VM),
        scratch_shapes=[
            pltpu.VMEM(pieces.shape, halves),
            pltpu.VMEM((heads_kv, width, HEAD_WIDTH), halves),
            pltpu.VMEM((heads_kv * HEAD_WIDTH, wide), floats),
            pltpu.VMEM((heads_kv, wide), floats),
            pltpu.VMEM((heads_kv * HEAD_WIDTH, wide), halves),
            *place_scratch(n * width // BLK, tokens),
            pltpu.SemaphoreType.DMA((n,)),
        ],
        compiler_params=pltpu.CompilerParams(vmem_limit_bytes=63 << 20),
        name="attend_forward",
    )(counts, q_t, pieces)


def bwd_kernel(n, width, counts, q_ref, do_ref, log_ref, delta_ref, pieces, *refs):
    dq_out = refs[0]
    dkv_out = refs[1]
    kv, dkv, keys_nat, vals_nat, acc, q_wide, do_wide, log_wide, delta_wide, dq_wide, sc, tok_ref, start_ref, sem, osem = refs[2:]
    for i in range(n):
        pltpu.make_async_copy(pieces.at[i], kv.at[i], sem.at[i]).start()
    fill_places(counts, sc, tok_ref, start_ref)
    heads_kv = pieces.shape[1] // (2 * HEAD_WIDTH)
    group = q_ref.shape[0] // (heads_kv * HEAD_WIDTH)
    v_off = heads_kv * HEAD_WIDTH
    places = [
        (h, slice((h * group + g) * HEAD_WIDTH, (h * group + g + 1) * HEAD_WIDTH), slice(qb * BLK, (qb + 1) * BLK),
         slice(h * HEAD_WIDTH, (h + 1) * HEAD_WIDTH), slice((qb * group + g) * BLK, (qb * group + g + 1) * BLK), h * group + g)
        for h in range(heads_kv) for g in range(group) for qb in range(q_ref.shape[1] // BLK)
    ]
    for h, rows, lanes, wrows, wlanes, hd in places:
        q_wide[wrows, wlanes] = q_ref[rows, lanes]
        do_wide[wrows, wlanes] = do_ref[rows, lanes]
        log_wide[h : h + 1, wlanes] = log_ref[hd : hd + 1, lanes]
        delta_wide[h : h + 1, wlanes] = delta_ref[hd : hd + 1, lanes]
        dq_wide[wrows, wlanes] = jnp.zeros((HEAD_WIDTH, BLK), floats)
    out_scale = (1.0 / VSCALE) * HEAD_WIDTH ** (-0.5)

    def key_piece(piece, carry):
        pltpu.make_async_copy(pieces.at[piece], kv.at[piece], sem.at[piece]).wait()
        def query_block(qb, carry):
            lanes = pl.ds(pl.multiple_of(qb * BLK, BLK), BLK)
            wide = pl.ds(pl.multiple_of(qb * (group * BLK), group * BLK), group * BLK)

            def unit(subs, bases, masked):
                keys = slice(subs[0] * BLK, (subs[-1] + 1) * BLK)
                if masked:
                    allowed = allowed_mask(bases, tok_ref, start_ref, lanes)
                    allowed = jnp.concatenate([allowed] * group, axis=1)
                heads = range(heads_kv)
                krows = [slice(h * HEAD_WIDTH, (h + 1) * HEAD_WIDTH) for h in heads]
                vrows = [slice(v_off + h * HEAD_WIDTH, v_off + (h + 1) * HEAD_WIDTH) for h in heads]
                qt = [q_wide[krows[h], wide] for h in heads]
                dot = [do_wide[krows[h], wide] for h in heads]
                scores = [dot_nn(keys_nat[h, keys], qt[h]) for h in heads]
                dprobs = [dot_nn(vals_nat[h, keys], dot[h]) for h in heads]
                weights = [
                    jnp.exp2(scores[h] * SCORE - log_wide[h : h + 1, wide]) for h in heads
                ]
                if masked:
                    weights = [jnp.where(allowed, w, 0.0) for w in weights]
                ds = [
                    (weights[h] * (dprobs[h] - delta_wide[h : h + 1, wide])).astype(halves)
                    for h in heads
                ]
                dv = [dot_nt(dot[h], weights[h].astype(halves)) for h in heads]
                dk = [dot_nt(qt[h], ds[h]) for h in heads]
                dq = [dot_nn(kv[piece, krows[h], keys], ds[h]) for h in heads]
                for h in heads:
                    acc[vrows[h], keys] += dv[h]
                    acc[krows[h], keys] += dk[h]
                    dq_wide[krows[h], wide] += dq[h]

            for_piece(sc, piece, qb, unit)
            return carry

        used = piece_used(sc, piece, q_ref.shape[1] // BLK)

        @pl.when(used)
        def _():
            for h in range(heads_kv):
                rows = slice(h * HEAD_WIDTH, (h + 1) * HEAD_WIDTH)
                vals = slice(v_off + h * HEAD_WIDTH, v_off + (h + 1) * HEAD_WIDTH)
                keys_nat[h] = kv[piece, rows, :].T
                vals_nat[h] = kv[piece, vals, :].T
            acc[...] = jnp.zeros_like(acc)
            lax.fori_loop(0, q_ref.shape[1] // BLK, query_block, 0)
            dkv[piece, 0:v_off, :] = (acc[0:v_off, :] * out_scale).astype(halves)
            dkv[piece, v_off:, :] = acc[v_off:, :].astype(halves)

        @pl.when(jnp.logical_not(used))
        def _():
            dkv[piece] = jnp.zeros(dkv.shape[1:], halves)

        pltpu.make_async_copy(dkv.at[piece], dkv_out.at[piece], osem.at[piece]).start()
        return carry

    lax.fori_loop(0, n, key_piece, 0)
    for h, rows, lanes, wrows, wlanes, hd in places:
        dq_out[rows, lanes] = dq_wide[wrows, wlanes] * out_scale
    for i in range(n):
        pltpu.make_async_copy(dkv.at[i], dkv_out.at[i], osem.at[i]).wait()


def attend_backward(counts, q_t, do_t, log_total, delta, pieces):
    n, width = pieces.shape[0], pieces.shape[2]
    heads_kv = pieces.shape[1] // (2 * HEAD_WIDTH)
    wide = q_t.shape[0] // (heads_kv * HEAD_WIDTH) * q_t.shape[1]
    outs = pl.pallas_call(
        functools.partial(bwd_kernel, n, width),
        out_shape=(
            jax.ShapeDtypeStruct(q_t.shape, floats),
            jax.ShapeDtypeStruct(pieces.shape, halves),
        ),
        in_specs=[SM] + [VM] * 4 + [HM],
        out_specs=(VM, HM),
        scratch_shapes=[
            pltpu.VMEM(pieces.shape, halves),
            pltpu.VMEM(pieces.shape, halves),
            pltpu.VMEM((heads_kv, width, HEAD_WIDTH), halves),
            pltpu.VMEM((heads_kv, width, HEAD_WIDTH), halves),
            pltpu.VMEM(pieces.shape[1:], floats),
            pltpu.VMEM((heads_kv * HEAD_WIDTH, wide), halves),
            pltpu.VMEM((heads_kv * HEAD_WIDTH, wide), halves),
            pltpu.VMEM((heads_kv, wide), floats),
            pltpu.VMEM((heads_kv, wide), floats),
            pltpu.VMEM((heads_kv * HEAD_WIDTH, wide), floats),
            *place_scratch(n * width // BLK, q_t.shape[1]),
            pltpu.SemaphoreType.DMA((n,)),
            pltpu.SemaphoreType.DMA((n,)),
        ],
        compiler_params=pltpu.CompilerParams(vmem_limit_bytes=63 << 20),
        name="attend_backward",
    )(counts, q_t, do_t, log_total, delta, pieces)
    return outs


eps_norm = 1e-05
rope_base = 100000.0
reach_limit = 8


def shifted(block, axis, distance):
    devices = range(lax.axis_size(axis))
    route = [(i - distance, i) for i in devices if i - distance in devices]
    return lax.ppermute(block, axis, route)


def rms_scale(value_vectors, gain_vec):
    return (
        value_vectors
        * lax.rsqrt(jnp.mean(value_vectors * value_vectors, axis=-1, keepdims=True) + eps_norm)
        * gain_vec
    )


def rotary_turn(value_vectors, token_positions, heads):
    half_width = HEAD_WIDTH // 2
    inverse = 1.0 / rope_base ** (jnp.arange(half_width, dtype=jnp.float32) * 2.0 / HEAD_WIDTH)
    angles = token_positions.astype(jnp.float32)[:, None] * inverse[None, :]
    cosine = jnp.cos(angles)[:, None, :]
    sine_part = jnp.sin(angles)[:, None, :]
    shaped = value_vectors.reshape(value_vectors.shape[0], heads, HEAD_WIDTH)
    first_half = shaped[..., :half_width]
    second = shaped[..., half_width:]
    turned = jnp.concatenate(
        [first_half * cosine - second * sine_part, second * cosine + first_half * sine_part],
        axis=-1,
    )
    return turned.reshape(value_vectors.shape)


def swiglu(gate_pre, up_pre):
    return jax.nn.silu(gate_pre) * up_pre


def contract_rows(left_side, right_side):
    return lax.dot_general(
        left_side, right_side, (((0,), (0,)), ((), ())), preferred_element_type=jnp.float32
    )


def contract_cols(left_side, right_side):
    return lax.dot_general(
        left_side, right_side, (((1,), (1,)), ((), ())), preferred_element_type=jnp.float32
    )


def local(
    tokens,
    out_grad,
    segment_ids,
    attn_gain,
    query_weight,
    key_matrix,
    value_matrix,
    output_weight,
    mlp_gain,
    gate_weight,
    up_weight,
    down_weight,
):
    floats = jnp.float32
    halves = jnp.bfloat16
    shard_rows = tokens.shape[0]
    row_len = shard_rows * lax.axis_size("tp")
    row_index = lax.axis_index("dp")
    reach = min(reach_limit, lax.axis_size("dp") // 2)
    heads_q = query_weight.shape[1] // HEAD_WIDTH
    heads_kv = key_matrix.shape[1] // HEAD_WIDTH
    group_width = heads_q // heads_kv
    q_cols = heads_q * HEAD_WIDTH
    kv_cols = heads_kv * HEAD_WIDTH
    score_scale = HEAD_WIDTH ** (-0.5)
    row_first = row_index * row_len
    seg_row = lax.dynamic_slice_in_dim(segment_ids, row_first, row_len)
    index_row = row_first + jnp.arange(row_len, dtype=jnp.int32)
    every_index = jnp.arange(segment_ids.shape[0], dtype=jnp.int32)
    marks = (segment_ids[1:] != segment_ids[:-1]).astype(jnp.int32)
    starts = jnp.concatenate([jnp.zeros((1,), jnp.int32), marks * every_index[1:]])
    is_at = (starts[None, :] <= index_row[:, None]).astype(jnp.int32)
    token_positions = index_row - jnp.max(is_at * starts[None, :], axis=1)
    tokens32 = tokens.astype(floats)
    gain_attn = attn_gain.astype(floats)
    gain_mlp = mlp_gain.astype(floats)
    normed = rms_scale(tokens32, gain_attn).astype(halves)
    normed_full = lax.all_gather(normed, "tp", axis=0, tiled=True)
    joined = jnp.concatenate([query_weight, key_matrix, value_matrix], axis=1)
    projected = jnp.dot(normed_full, joined, preferred_element_type=floats)
    q_linear = projected[:, :q_cols]
    key_linear_out = projected[:, q_cols : q_cols + kv_cols]
    query_vectors = rotary_turn(q_linear, token_positions, heads_q).astype(halves)
    key_vectors = rotary_turn(key_linear_out, token_positions, heads_kv).astype(halves)
    value_vectors = projected[:, q_cols + kv_cols :].astype(halves)
    query_heads = query_vectors.reshape(row_len, heads_kv, group_width, HEAD_WIDTH)
    held_blocks = [(key_vectors, value_vectors)]
    moving = (key_vectors, value_vectors)
    for step_hop in range(reach):
        moving = shifted((moving[0], moving[1]), "dp", 1)
        held_blocks.append(moving)

    def block_mask(step_hop):
        key_row = row_index - step_hop
        seg_keys = lax.dynamic_slice_in_dim(segment_ids, jnp.maximum(key_row, 0) * row_len, row_len)
        key_index = key_row * row_len + jnp.arange(row_len, dtype=jnp.int32)
        return (seg_keys[None, :] == seg_row[:, None]) & (key_index[None, :] <= index_row[:, None])

    def block_needed(step_hop):
        last_key = jnp.maximum((row_index - step_hop + 1) * row_len - 1, 0)
        return (row_index >= step_hop) & (segment_ids[last_key] == seg_row[0])

    block_masks = [block_mask(step_hop) for step_hop in range(reach + 1)]

    def apply_block(step_hop, update, state_in):
        key_block, value_block = held_blocks[step_hop]
        if step_hop == 0:
            return update(state_in, key_block, value_block, block_masks[0])
        return lax.cond(
            block_needed(step_hop),
            update,
            lambda state_kept, key_skip, value_skip, mask_skip: state_kept,
            state_in,
            key_block,
            value_block,
            block_masks[step_hop],
        )

    def scores(key_block, allowed):
        raw_scores = jnp.einsum(
            "qhgd,khd->hgqk",
            query_heads,
            key_block.reshape(row_len, heads_kv, HEAD_WIDTH),
            preferred_element_type=floats,
        )
        return jnp.where(allowed, raw_scores * score_scale, -jnp.inf)

    def add_online(state_in, key_block, value_block, allowed):
        run_max, run_total, run_sum = state_in
        block_scores = scores(key_block, allowed)
        new_max = jnp.maximum(run_max, jnp.max(block_scores, axis=-1))
        factor = jnp.exp(run_max - new_max)
        weights = jnp.exp(block_scores - new_max[..., None])
        run_total = run_total * factor + jnp.sum(weights, axis=-1)
        run_sum = run_sum * jnp.moveaxis(factor, 2, 0)[..., None] + jnp.einsum(
            "hgqk,khd->qhgd",
            weights.astype(halves),
            value_block.reshape(row_len, heads_kv, HEAD_WIDTH),
            preferred_element_type=floats,
        )
        return (new_max, run_total, run_sum)

    online = (
        jnp.full((heads_kv, group_width, row_len), -jnp.inf, floats),
        jnp.zeros((heads_kv, group_width, row_len), floats),
        jnp.zeros((row_len, heads_kv, group_width, HEAD_WIDTH), floats),
    )
    for step_hop in range(reach + 1):
        online = apply_block(step_hop, add_online, online)
    run_max, run_total, run_sum = online
    log_total = (run_max + jnp.log(run_total))[..., None]
    context_heads = (run_sum / jnp.moveaxis(run_total, 2, 0)[..., None]).astype(halves)
    context = context_heads.reshape(row_len, q_cols)
    residual = tokens32 + lax.psum_scatter(
        jnp.dot(context, output_weight, preferred_element_type=floats).astype(jnp.bfloat16),
        "tp",
        scatter_dimension=0,
        tiled=True,
    ).astype(jnp.float32)
    mlp_normed = rms_scale(residual, gain_mlp).astype(halves)
    mlp_full = lax.all_gather(mlp_normed, "tp", axis=0, tiled=True)
    gate_pre = jnp.dot(mlp_full, gate_weight, preferred_element_type=floats)
    up_pre = jnp.dot(mlp_full, up_weight, preferred_element_type=floats)
    hidden = swiglu(gate_pre, up_pre).astype(halves)
    output = residual + lax.psum_scatter(
        jnp.dot(hidden, down_weight, preferred_element_type=floats).astype(jnp.bfloat16),
        "tp",
        scatter_dimension=0,
        tiled=True,
    ).astype(jnp.float32)
    grad_full = lax.all_gather(out_grad, "tp", axis=0, tiled=True)
    grad_hidden = contract_cols(grad_full, down_weight)
    down_grad = contract_rows(grad_full, hidden)
    silu_back = jax.vjp(swiglu, gate_pre, up_pre)[1]
    grad_gate, grad_up = silu_back(grad_hidden)
    grad_gate = grad_gate.astype(halves)
    grad_up = grad_up.astype(halves)
    gate_grad = contract_rows(mlp_full, grad_gate)
    up_grad = contract_rows(mlp_full, grad_up)
    grad_mlp_normed = lax.psum_scatter(
        (contract_cols(grad_gate, gate_weight) + contract_cols(grad_up, up_weight)).astype(
            jnp.bfloat16
        ),
        "tp",
        scatter_dimension=0,
        tiled=True,
    ).astype(jnp.float32)
    mlp_norm_back = jax.vjp(rms_scale, residual, gain_mlp)[1]
    grad_residual_part, mlp_gain_part = mlp_norm_back(grad_mlp_normed)
    grad_residual = out_grad.astype(floats) + grad_residual_part
    attn_grad_full = lax.all_gather(grad_residual.astype(halves), "tp", axis=0, tiled=True)
    output_grad = contract_rows(attn_grad_full, context)
    grad_context = (
        contract_cols(attn_grad_full, output_weight)
        .astype(halves)
        .reshape(row_len, heads_kv, group_width, HEAD_WIDTH)
    )
    delta_col = jnp.einsum(
        "qhgd,qhgd->hgq", grad_context, context_heads, preferred_element_type=floats
    )[..., None]

    def add_grads(state_in, key_block, value_block, allowed):
        query_acc, key_acc, value_acc = state_in
        probabilities = jnp.exp(scores(key_block, allowed) - log_total)
        grad_probs = jnp.einsum(
            "qhgd,khd->hgqk",
            grad_context,
            value_block.reshape(row_len, heads_kv, HEAD_WIDTH),
            preferred_element_type=floats,
        )
        grad_scores = (probabilities * (grad_probs - delta_col)).astype(halves)
        key_heads = key_block.reshape(row_len, heads_kv, HEAD_WIDTH)
        query_acc = (
            query_acc
            + jnp.einsum("hgqk,khd->qhgd", grad_scores, key_heads, preferred_element_type=floats)
            * score_scale
        )
        key_acc = (
            key_acc
            + jnp.einsum(
                "hgqk,qhgd->khd", grad_scores, query_heads, preferred_element_type=floats
            ).reshape(row_len, kv_cols)
            * score_scale
        )
        value_acc = value_acc + jnp.einsum(
            "hgqk,qhgd->khd",
            probabilities.astype(halves),
            grad_context,
            preferred_element_type=floats,
        ).reshape(row_len, kv_cols)
        return (query_acc, key_acc, value_acc)

    query_acc = jnp.zeros((row_len, heads_kv, group_width, HEAD_WIDTH), floats)
    carried = (jnp.zeros((row_len, kv_cols), floats), jnp.zeros((row_len, kv_cols), floats))
    for step_hop in range(reach, 0, -1):
        query_acc, key_acc, value_acc = apply_block(
            step_hop, add_grads, (query_acc, carried[0], carried[1])
        )
        carried = (
            shifted(key_acc.astype(jnp.bfloat16), "dp", -1).astype(key_acc.dtype),
            shifted(value_acc.astype(jnp.bfloat16), "dp", -1).astype(value_acc.dtype),
        )
    query_acc, key_total, value_total = apply_block(
        0, add_grads, (query_acc, carried[0], carried[1])
    )
    query_back = jax.vjp(lambda linear: rotary_turn(linear, token_positions, heads_q), q_linear)[1]
    key_back = jax.vjp(
        lambda linear: rotary_turn(linear, token_positions, heads_kv), key_linear_out
    )[1]
    grad_q_linear = query_back(query_acc.reshape(row_len, q_cols))[0]
    grad_k_linear = key_back(key_total)[0]
    grads_joined = jnp.concatenate([grad_q_linear, grad_k_linear, value_total], axis=1).astype(
        halves
    )
    proj_grad = contract_rows(normed_full, grads_joined)
    grad_normed = lax.psum_scatter(
        contract_cols(grads_joined, joined).astype(jnp.bfloat16),
        "tp",
        scatter_dimension=0,
        tiled=True,
    ).astype(jnp.float32)
    attn_norm_back = jax.vjp(rms_scale, tokens32, gain_attn)[1]
    grad_tokens_part, attn_gain_part = attn_norm_back(grad_normed)
    input_grad = grad_residual + grad_tokens_part
    def scatter_rows(grad):
        return lax.psum_scatter(
            grad.astype(halves), "dp", scatter_dimension=0, tiled=True
        ).astype(floats)

    mlp_sums = scatter_rows(jnp.concatenate([gate_grad, up_grad, down_grad], axis=1))
    ff_cols = gate_weight.shape[1]
    gate_sum = mlp_sums[:, :ff_cols]
    up_sum = mlp_sums[:, ff_cols : 2 * ff_cols]
    down_sum = mlp_sums[:, 2 * ff_cols :]
    attn_sums = scatter_rows(jnp.concatenate([proj_grad, output_grad], axis=1))
    query_sum = attn_sums[:, :q_cols]
    key_sum = attn_sums[:, q_cols : q_cols + kv_cols]
    value_sum = attn_sums[:, q_cols + kv_cols : q_cols + 2 * kv_cols]
    output_sum = attn_sums[:, q_cols + 2 * kv_cols :]
    attn_gain_sum = lax.psum_scatter(attn_gain_part, "dp", scatter_dimension=0, tiled=True)
    mlp_gain_sum = lax.psum_scatter(mlp_gain_part, "dp", scatter_dimension=0, tiled=True)
    attn_gain_total, mlp_gain_total = lax.psum((attn_gain_sum, mlp_gain_sum), "tp")
    return (
        output.astype(halves),
        input_grad,
        attn_gain_total,
        query_sum,
        key_sum,
        value_sum,
        output_sum.T,
        mlp_gain_total,
        gate_sum,
        up_sum,
        down_sum.T,
    )


MESH = pl.DeviceIdType.MESH


def meet(devices):
    barrier = pltpu.get_barrier_semaphore()
    for device in devices:
        pl.semaphore_signal(barrier, inc=1, device_id=device, device_id_type=MESH)
    pl.semaphore_wait(barrier, len(devices))


def tiles(total, step, body):
    def one(i, carry):
        body(pl.ds(pl.multiple_of(i * step, step), step))
        return carry

    lax.fori_loop(0, total // step, one, 0)


CHUNKS = 4


class GroupSum:
    def __init__(self, copies, bufs, place):
        self.copies, self.bufs, self.place = copies, bufs, place

        self.far, self.sums = [], []

    def put_there(self, at, cols, value):
        part_near, _, out_far = self.bufs[:3]
        rows = value.shape[0] // 2
        part_near[at, cols] = value[:rows]
        out_far[at, cols] = value[rows:].astype(halves)

    def put_here(self, cols, value):
        _, part_own, _, out_beside = self.bufs[:4]
        rows = value.shape[0] // 2
        part_own[:, cols] = value[:rows]
        out_beside[:, cols] = value[rows:].astype(halves)

    def send_far(self, at):
        _, _, out_far, _, _, in_near = self.bufs[:6]
        copy = self.copies.make(out_far.at[at], in_near.at[at], self.place.beside)
        copy.start()
        self.far.append(copy)

    def send_beside(self):
        _, _, _, out_beside, _, _, in_own = self.bufs[:7]
        self.side = self.copies.make(out_beside, in_own, self.place.beside)
        self.side.start()

    def send_near(self, count):
        part_near, _, _, _, out_near, in_near, _, in_sum = self.bufs
        self.far[-1].wait_recv()
        rows = part_near.shape[0] // CHUNKS
        for _ in range(count):
            at = pl.ds(len(self.sums) * rows, rows)
            out_near[at, :] = (part_near[at, :] + in_near[at, :].astype(floats)).astype(halves)
            copy = self.copies.make(out_near.at[at], in_sum.at[at], self.place.near)
            copy.start()
            self.sums.append(copy)

    def run(self, product):
        everything = pl.ds(0, self.bufs[0].shape[0])
        product(1, lambda cols, value: self.put_there(everything, cols, value))
        self.send_far(everything)
        product(0, self.put_here)
        self.send_beside()
        self.send_near(CHUNKS)

    def take(self, k):
        part_near, part_own, out_far, out_beside, out_near, in_near, in_own, in_sum = self.bufs
        if k == 0:
            self.side.wait_recv()
        self.sums[k].wait_recv()
        rows = part_own.shape[0] // CHUNKS
        at = pl.ds(k * rows, rows)
        return part_own[at, :] + in_own[at, :].astype(floats) + in_sum[at, :].astype(floats)

    def finish(self):
        for copy in (*self.far, self.side, *self.sums):
            copy.wait_send()


class GroupGather:
    def __init__(self, copies, full, block, place):
        self.copies, self.full, self.block, self.place = copies, full, block, place
        self.sent = []

    def slot(self, n, k):
        rows = self.block // CHUNKS
        return self.full.at[pl.ds(n * self.block + k * rows, rows)]

    def put(self, k):
        for i, (n, device) in enumerate(((2, self.place.near), (1, self.place.beside))):
            copy = self.copies.make(self.slot(0, k), self.slot(n, k), device)
            copy.start()
            self.sent.append((i, copy))

    def wait_here(self):
        for i, copy in self.sent:
            if i == 1:
                copy.wait_recv()

    def wait_there(self, part=0, parts=1):
        near = [copy for i, copy in self.sent if i == 0]
        count = CHUNKS // parts
        relays = []
        for k in range(part * count, (part + 1) * count):
            near[k].wait_recv()
            relay = self.copies.make(self.slot(2, k), self.slot(3, k), self.place.beside)
            relay.start()
            relays.append(relay)
        for relay in relays:
            relay.wait_recv()
        self.sent += [(2, relay) for relay in relays]

    def finish(self):
        for _, copy in self.sent:
            copy.wait_send()


class Copies:
    limit = 96

    def __init__(self, send_sems, recv_sems):
        self.send_sems, self.recv_sems, self.used = send_sems, recv_sems, 0

    def make(self, src, dst, device):
        i = self.used
        self.used += 1
        return pltpu.make_async_remote_copy(
            src_ref=src,
            dst_ref=dst,
            send_sem=self.send_sems.at[i],
            recv_sem=self.recv_sems.at[i],
            device_id=device,
            device_id_type=MESH,
        )


def copy_semaphores():
    return [pltpu.SemaphoreType.DMA((Copies.limit,)), pltpu.SemaphoreType.DMA((Copies.limit,))]


class Place:
    def __init__(self):
        dp, z = lax.axis_index("dp"), lax.axis_index("tp")
        self.dp, self.z = dp, z
        self.c = lax.rem(dp, 2)
        self.x = lax.rem(dp // 2, 2)
        self.y = dp // 4
        far_z = lax.rem(z + 2, 4)
        self.beside = (dp + 1 - 2 * self.c, z)
        self.near = (dp, z + 1 - 2 * lax.rem(z, 2))
        self.far = (dp, far_z)
        self.cross = (self.beside[0], far_z)
        self.over_x = (dp + 2 - 4 * self.x, z)
        self.over_y = (dp + 4 - 8 * self.y, z)
        self.slot = 2 * self.y + self.x
        self.slot_x = 2 * self.y + 1 - self.x
        self.slot_y = 2 - 2 * self.y + self.x
        self.odd = self.c == 1
        self.corner = (self.x == 1) & (self.y == 1)
        self.turn = (self.x == 0) & (self.y == 1)


def rope_tables(counts_ref, inverse_ref, cos_ref, sin_ref):
    index = group_index()
    positions = (index - item_start(counts_ref, index)).astype(floats)
    angles = inverse_ref[...] * positions
    cos_ref[...] = jnp.cos(angles)
    sin_ref[...] = jnp.sin(angles)


class PlaneFetch:
    def __init__(self, copies, place, out, own=None, own_slice=None):
        self.place, self.out = place, out
        rows = out.shape[0] // 8

        def part(slot, ch):
            return pl.ds(slot * (2 * rows) + ch * rows, rows)

        def remote(slot, ch, device):
            at = part(slot, ch)
            return copies.make(out.at[at], out.at[at], device)

        p = place
        self.hop = None
        if own is not None:
            self.hop = [
                copies.make(own.at[part(p.slot, ch)], out.at[part(p.slot, ch)], p.far)
                for ch in range(2)
            ]
        if own_slice is not None:
            self.hop = [
                copies.make(own_slice.at[part(0, ch)], out.at[part(p.slot, ch)], p.far)
                for ch in range(2)
            ]
        self.x = [remote(p.slot, ch, p.over_x) for ch in range(2)]
        self.y = [remote(p.slot, ch, p.over_y) for ch in range(2)]
        self.relay_y = remote(p.slot_x, 0, p.over_y)
        self.relay_x = remote(p.slot_y, 1, p.over_x)

    def start(self):
        @pl.when(self.place.odd)
        def _():
            for copy in self.hop:
                copy.start()

    def forward(self):
        @pl.when(self.place.odd)
        def _():
            for ch in range(2):
                if self.hop is not None:
                    self.hop[ch].wait_recv()
                self.x[ch].start()
                self.y[ch].start()

    def relay(self):
        @pl.when(self.place.odd)
        def _():
            self.x[0].wait_recv()
            self.relay_y.start()
            self.y[1].wait_recv()
            self.relay_x.start()

    def finish(self):
        @pl.when(self.place.odd)
        def _():
            self.x[1].wait_recv()
            self.y[0].wait_recv()
            self.relay_y.wait_recv()
            self.relay_x.wait_recv()

    def drain(self):
        @pl.when(self.place.odd)
        def _():
            for copy in (self.hop or []) + self.x + self.y + [self.relay_y, self.relay_x]:
                copy.wait_send()


class Spread:
    def __init__(self, copies, place, source, slots):
        self.place = place
        self.to_x = copies.make(source, slots[1], place.over_x)
        self.to_y = copies.make(source, slots[2], place.over_y)
        self.relayed = copies.make(slots[2], slots[3], place.over_x)

    def start(self):
        pl.when(self.place.x == 0)(self.to_x.start)
        pl.when(self.place.y == 0)(self.to_y.start)

    def relay(self):
        @pl.when(self.place.corner)
        def _():
            self.to_y.wait_recv()
            self.relayed.start()

    def finish(self):
        p = self.place
        pl.when(p.x == 1)(self.to_x.wait_recv)
        pl.when((p.y == 1) & (p.x == 0))(self.to_y.wait_recv)
        pl.when(p.turn)(self.relayed.wait_recv)
        pl.when(p.x == 0)(self.to_x.wait_send)
        pl.when(p.y == 0)(self.to_y.wait_send)
        pl.when(p.corner)(self.relayed.wait_send)


def first_kernel(
    counts, inverse_ref, tok_ref, grad_ref, gain_ref, wq_in, wk_ref, wv_ref, wo_in, wd_in, wg_in, wu_in,
    q_out, kv_out, n_out, g_full, joined_out, wo_out, wd_out, slice_g, slice_u,
    n_full, joined, own_slice, slices, cos_ref, sin_ref, linear, kv_own, ss, rs, lsem,
):
    place = Place()
    copies = Copies(ss, rs)
    block, width = tok_ref.shape
    two = 2 * block
    q_cols = q_out.shape[0]
    kv_cols = kv_own.shape[1] // 2
    q_lanes = pl.ds(0, q_cols)
    slice_rows = pl.ds(place.slot * own_slice.shape[0], own_slice.shape[0])
    load_q = pltpu.make_async_copy(wq_in, joined.at[:, q_lanes], lsem.at[0])
    load_q_odd = pltpu.make_async_copy(
        wq_in.at[slice_rows], own_slice.at[:, q_lanes], lsem.at[0]
    )
    pl.when(place.c == 0)(load_q.start)
    pl.when(place.odd)(load_q_odd.start)
    rows4 = slice_g.shape[0]
    at_slot = pl.ds(place.slot * rows4, rows4)
    slice_loads = [
        pltpu.make_async_copy(src.at[at_slot], slices.at[i], lsem.at[1 + i])
        for i, src in enumerate((wg_in, wu_in))
    ]
    slice_stores = [
        pltpu.make_async_copy(slices.at[i], dst, lsem.at[6 + i])
        for i, dst in enumerate((slice_g, slice_u))
    ]
    for copy in slice_loads:
        copy.start()

    own_grad = pltpu.make_async_copy(grad_ref, g_full.at[pl.ds(0, block)], lsem.at[3])
    own_grad.start()
    meet((place.beside, place.near, place.far, place.cross, place.over_x, place.over_y))

    @pl.when(place.odd)
    def _():
        lanes = pl.ds(pl.multiple_of(place.slot * own_slice.shape[0], 128), own_slice.shape[0])
        own_slice[:, q_cols : q_cols + kv_cols] = wk_ref[:, lanes].T
        own_slice[:, q_cols + kv_cols :] = wv_ref[:, lanes].T
        load_q_odd.wait()

    fetch_joined = PlaneFetch(copies, place, joined, own_slice=own_slice)
    fetch_o = PlaneFetch(copies, place, wo_out, wo_in)
    fetch_d = PlaneFetch(copies, place, wd_out, wd_in)
    gather = GroupGather(copies, n_full, block, place)
    gather_g = GroupGather(copies, g_full, block, place)
    fetch_joined.start()
    chunk = block // CHUNKS
    for k in range(CHUNKS):
        at = pl.ds(k * chunk, chunk)
        tok = tok_ref[at, :].astype(floats)
        root = lax.rsqrt(jnp.mean(tok * tok, axis=-1, keepdims=True) + eps_norm)
        n_full[at, :] = (tok * root * gain_ref[...]).astype(halves)
        gather.put(k)
    fetch_joined.forward()
    fetch_o.start()
    fetch_d.start()
    @pl.when(place.c == 0)
    def _():
        joined[:, q_cols : q_cols + kv_cols] = wk_ref[...].T
        joined[:, q_cols + kv_cols :] = wv_ref[...].T

    rope_tables(counts, inverse_ref, cos_ref, sin_ref)
    for load, store in zip(slice_loads, slice_stores):
        load.wait()
        store.start()
    fetch_joined.relay()
    gather.wait_here()
    fetch_joined.finish()
    pl.when(place.c == 0)(load_q.wait)
    keep_joined = pltpu.make_async_copy(joined, joined_out, lsem.at[8])
    keep_joined.start()

    def project(k):
        rows = slice(k * two, (k + 1) * two)

        def one(cols):
            linear[cols, :] = dot_nn(n_full[rows, :], joined[:, cols]).T

        tiles(joined.shape[1], 256, one)
        half_width = HEAD_WIDTH // 2
        for head in range((q_cols + kv_cols) // HEAD_WIDTH):
            low = slice(head * HEAD_WIDTH, head * HEAD_WIDTH + half_width)
            high = slice(head * HEAD_WIDTH + half_width, (head + 1) * HEAD_WIDTH)
            one_half, two_half = linear[low, :], linear[high, :]
            cosine, sine = cos_ref[:, rows], sin_ref[:, rows]
            first = (one_half * cosine - two_half * sine).astype(halves)
            second = (two_half * cosine + one_half * sine).astype(halves)
            if head * HEAD_WIDTH < q_cols:
                q_out[low, rows] = first
                q_out[high, rows] = second
            else:
                kv_own[k, low.start - q_cols : low.stop - q_cols, :] = first
                kv_own[k, high.start - q_cols : high.stop - q_cols, :] = second
        kv_own[k, kv_cols:, :] = (linear[q_cols + kv_cols :, :].astype(halves) * VSCALE).astype(halves)

    crossings, spreads_a, spreads_b, kept = [], [], [], []

    def share(k):
        slots = [kv_out.at[8 * k + i] for i in range(8)]
        keep = pltpu.make_async_copy(kv_own.at[k], slots[0], lsem.at[4 + k])
        keep.start()
        kept.append(keep)
        crossing = copies.make(kv_own.at[k], slots[4], place.cross)
        crossing.start()
        crossings.append(crossing)
        spread = Spread(copies, place, kv_own.at[k], slots[:4])
        spread.start()
        spreads_a.append(spread)
        spreads_b.append(Spread(copies, place, slots[4], slots[4:]))

    project(0)
    share(0)
    gather.wait_there()
    own_grad.wait()
    for k in range(CHUNKS):
        gather_g.put(k)
    project(1)
    share(1)
    keep_n = pltpu.make_async_copy(n_full, n_out, lsem.at[9])
    keep_n.start()
    fetch_o.forward()
    fetch_d.forward()
    spreads_a[0].relay()
    spreads_a[1].relay()
    crossings[0].wait_recv()
    spreads_b[0].start()
    fetch_o.relay()
    fetch_d.relay()
    gather_g.wait_there()
    spreads_b[0].relay()
    crossings[1].wait_recv()
    spreads_b[1].start()
    spreads_b[1].relay()
    fetch_o.finish()
    fetch_d.finish()
    gather_g.wait_here()
    for spread in spreads_a + spreads_b:
        spread.finish()
    for copy in kept + slice_stores + [keep_joined, keep_n]:
        copy.wait()
    for copy in crossings:
        copy.wait_send()
    for fetch in (fetch_joined, fetch_o, fetch_d):
        fetch.drain()
    gather.finish()
    gather_g.finish()


def first_part(counts, inverse, tokens, out_grad, gain, projections, weights):
    block, width = tokens.shape
    group = 4 * block
    shape = jax.ShapeDtypeStruct
    hidden = weights[2].shape[1]
    part = (width // 4, hidden)
    half_width = HEAD_WIDTH // 2
    q_cols, kv_cols = projections[0].shape[1], projections[1].shape[0]
    joined_cols = q_cols + 2 * kv_cols
    out_shape = (
        shape((q_cols, group), halves),
        shape((16, 2 * kv_cols, 2 * block), halves),
        shape((group, width), halves),
        shape((group, width), halves),
        shape((width, joined_cols), halves),
        shape(weights[0].shape, halves),
        shape(weights[1].shape, halves),
        shape(part, halves),
        shape(part, halves),
    )
    return pl.pallas_call(
        first_kernel,
        out_shape=out_shape,
        in_specs=[SM] + [VM] * 4 + [HB, VM, VM] + [HB] * 4,
        out_specs=(VM, HM, HM, VM, HM, HM, HM, HM, HM),
        scratch_shapes=[
            pltpu.VMEM((group, width), halves),
            pltpu.VMEM((width, joined_cols), halves),
            pltpu.VMEM((width // 4, joined_cols), halves),
            pltpu.VMEM((2,) + part, halves),
            pltpu.VMEM((half_width, group), floats),
            pltpu.VMEM((half_width, group), floats),
            pltpu.VMEM((joined_cols, 2 * block), floats),
            pltpu.VMEM((2, 2 * kv_cols, 2 * block), halves),
            *copy_semaphores(),
            pltpu.SemaphoreType.DMA((10,)),
        ],
        compiler_params=pltpu.CompilerParams(
            collective_id=2, has_side_effects=True, vmem_limit_bytes=63 << 20
        ),
        name="first",
    )(counts, inverse, tokens, out_grad, gain, *projections, *weights)


class PlaneSum:
    def __init__(self, copies, place, x_first, bufs, sent=None, come=None):
        self.place, self.bufs, self.x_first = place, bufs, x_first
        half, keep, come_two, home_one, home_two = bufs
        first, second = (place.over_x, place.over_y) if x_first else (place.over_y, place.over_x)
        self.at = place.y if x_first else place.x
        self.one = None if sent is None else copies.make(sent, come, first)
        self.two = copies.make(half, come_two, second)
        rows = home_one.shape[0]
        c = place.c
        home = (c * place.cross[0] + (1 - c) * place.beside[0], c * place.cross[1] + (1 - c) * place.beside[1])
        self.to_home = copies.make(half.at[pl.ds((1 - c) * rows, rows)], home_one, home)
        self.to_far = copies.make(half.at[pl.ds(rows, rows)], home_two, place.far)

    def cross_second(self, kept, come):
        if self.one is not None:
            self.one.wait()
        half, keep, come_two, home_one, home_two = self.bufs
        at = self.at
        half[...] = (kept[1 - at].astype(floats) + come[1 - at].astype(floats)).astype(halves)
        self.two.start()
        keep[...] = (kept[at].astype(floats) + come[at].astype(floats)).astype(halves)

    def go_home(self, exchanged=True):
        half, keep, come_two, home_one, home_two = self.bufs
        if exchanged:
            self.two.wait()
        half[...] = (keep[...].astype(floats) + come_two[...].astype(floats)).astype(halves)
        self.to_home.start()
        pl.when(self.place.odd)(self.to_far.start)

    def finish(self, out):
        half, keep, come_two, home_one, home_two = self.bufs
        rows = home_one.shape[0]
        self.to_home.wait()

        @pl.when(self.place.c == 0)
        def _():
            out[...] = half[:rows, :].astype(floats) + home_one[...].astype(floats)

        @pl.when(self.place.odd)
        def _():
            self.to_far.wait()
            out[...] = home_one[...].astype(floats) + home_two[...].astype(floats)


def plane_buffers(rows, cols):
    full = pltpu.VMEM((rows, cols), halves)
    part = pltpu.VMEM((rows // 2, cols), halves)
    return [full, full, full, part, part]


class RowBlocks:
    def __init__(self, ref, rows):
        self.ref, self.rows = ref, rows

    def at(self, i):
        return pl.ds(pl.multiple_of(i * self.rows, 128), self.rows)

    def __getitem__(self, i):
        return self.ref[self.at(i), :]

    def __setitem__(self, i, value):
        self.ref[self.at(i), :] = value


def outer_blocks(place, x_first, left, right, send_ref, keep_ref, on_sent):
    rows = left.shape[1] // 4
    for kept in (False, True):
        for i in range(2):
            if x_first:
                block = 2 * i + (place.x if kept else 1 - place.x)
            else:
                block = 2 * (place.y if kept else 1 - place.y) + i
            cols = pl.ds(pl.multiple_of(block * rows, 128), rows)
            value = lax.dot_general(
                left[:, cols], right, (((0,), (0,)), ((), ())), preferred_element_type=floats
            ).astype(halves)
            (keep_ref if kept else send_ref)[i] = value
        if not kept:
            on_sent()


def mid_kernel(ctx_ref, tok_ref, gain_ref, g_full, weight_refs, outs, scratch):
    (res_out, gres_out, e_full, near_out, down_half, down_mine, gate_half, gate_mine, up_keep, up_send,
     dctx_out, delta_out, gain_out) = outs
    (ctx, m_full, dh, hid, dgate, dup, w_o, w_d, w_g, w_u, down_send, down_keep, down_come, gate_send, gate_come, part_out, far_in, own_in, *bufs, ss, rs, wsem) = scratch
    place = Place()
    copies = Copies(ss, rs)
    block, width = tok_ref.shape
    two = 2 * block
    hidden = w_g.shape[1]
    wo_ref, wd_ref, wg_ref, wu_ref, wo_got, wd_got, slice_g, slice_u = weight_refs
    first_loads = [
        pltpu.make_async_copy(src, dst, wsem.at[i])
        for i, (src, dst) in enumerate(((wo_ref, w_o), (wd_ref, w_d)))
    ]
    first_loads_odd = [
        pltpu.make_async_copy(src, dst, wsem.at[i])
        for i, (src, dst) in enumerate(((wo_got, w_o), (wd_got, w_d)))
    ]

    def wait_first(i):
        pl.when(place.c == 0)(first_loads[i].wait)
        pl.when(place.odd)(first_loads_odd[i].wait)

    rows4 = slice_g.shape[0]
    at_slot = pl.ds(place.slot * rows4, rows4)
    loads = [
        pltpu.make_async_copy(src, dst, wsem.at[2 + i])
        for i, (src, dst) in enumerate(((wg_ref, w_g), (wu_ref, w_u)))
    ]
    loads_odd = [
        pltpu.make_async_copy(src, dst.at[at_slot], wsem.at[2 + i])
        for i, (src, dst) in enumerate(((slice_g, w_g), (slice_u, w_u)))
    ]

    @pl.when(place.c == 0)
    def _():
        for copy in first_loads + loads:
            copy.start()

    @pl.when(place.odd)
    def _():
        for copy in first_loads_odd + loads_odd:
            copy.start()

    ctx[...] = ctx_ref[...].T
    meet((place.beside, place.near, place.over_x, place.over_y))
    fetches = [PlaneFetch(copies, place, w_g), PlaneFetch(copies, place, w_u)]

    @pl.when(place.odd)
    def _():
        for copy in loads_odd:
            copy.wait()

    for fetch in fetches:
        fetch.forward()
    sum_one = GroupSum(copies, bufs, place)
    gather_one = GroupGather(copies, m_full, block, place)
    sum_two = GroupSum(copies, bufs, place)
    gather_two = GroupGather(copies, e_full, block, place)

    def project(k, put):
        rows = slice(k * two, (k + 1) * two)
        tiles(width, 256, lambda cols: put(cols, dot_nn(ctx[rows, :], w_o[:, cols])))

    wait_first(0)
    sum_one.run(project)
    wait_first(1)

    def back_hidden(cols):
        for rows in (slice(0, two), slice(two, 2 * two)):
            dh[rows, cols] = dot_nt(g_full[rows, :], w_d[cols, :]).astype(halves)

    tiles(hidden, 256, back_hidden)
    chunk = block // CHUNKS
    for k in range(CHUNKS):
        at = pl.ds(k * chunk, chunk)
        res = tok_ref[at, :].astype(floats) + sum_one.take(k)
        res_out[at, :] = res
        root = lax.rsqrt(jnp.mean(res * res, axis=-1, keepdims=True) + eps_norm)
        m_full[at, :] = (res * root * gain_ref[...]).astype(halves)
        gather_one.put(k)
        if k == 1:
            for fetch in fetches:
                fetch.relay()
    sum_one.finish()

    def there(h):
        rows = block // 2
        return [slice(two + h * rows, two + (h + 1) * rows), slice(3 * block + h * rows, 3 * block + (h + 1) * rows)]

    def read(ref, parts):
        values = [ref[rows, :] for rows in parts]
        return values[0] if len(values) == 1 else jnp.concatenate(values, axis=0)

    def write(ref, parts, cols, value):
        rows = value.shape[0] // len(parts)
        for i, part in enumerate(parts):
            ref[part, cols] = value[i * rows : (i + 1) * rows]

    def activate(parts):
        def one(cols):
            left = read(m_full, parts)
            gate_pre = dot_nn(left, w_g[:, cols])
            up_pre = dot_nn(left, w_u[:, cols])
            back = [dh[rows, cols] for rows in parts]
            back = (back[0] if len(back) == 1 else jnp.concatenate(back, axis=0)).astype(floats)
            sigma = 1.0 / (1.0 + jnp.exp(-gate_pre))
            silu = gate_pre * sigma
            write(hid, parts, cols, (silu * up_pre).astype(halves))
            write(dgate, parts, cols, (back * up_pre * (sigma + silu * (1.0 - sigma))).astype(halves))
            write(dup, parts, cols, (back * silu).astype(halves))

        tiles(hidden, 256, one)

    def partial_out(parts):
        def one(cols):
            write(part_out, parts, cols, dot_nn(read(hid, parts), w_d[:, cols]).astype(halves))

        tiles(width, 256, one)

    def back_norm(parts, put):
        def one(cols):
            put(cols, dot_nt(read(dgate, parts), w_g[cols, :]) + dot_nt(read(dup, parts), w_u[cols, :]))

        tiles(width, 256, one)

    for fetch in fetches:
        fetch.finish()

    @pl.when(place.c == 0)
    def _():
        for copy in loads:
            copy.wait()

    here = [slice(0, two)]
    gather_one.wait_here()
    activate(here)
    partial_out(here)
    whole = [slice(two, 2 * two)]
    gather_one.wait_there()
    at = pl.ds(0, block)
    activate(whole)
    back_norm(whole, lambda cols, value: sum_two.put_there(at, cols, value))
    sum_two.send_far(at)
    gather_one.finish()
    back_norm(here, sum_two.put_here)
    sum_two.send_beside()
    sum_two.send_near(CHUNKS)
    partial_out(whole)
    to_side = [
        copies.make(part_out.at[pl.ds(3 * block, block)], far_in, place.beside),
        copies.make(part_out.at[pl.ds(block, block)], own_in, place.beside),
    ]
    for copy in to_side:
        copy.start()
    down_over = copies.make(down_send, down_come, place.over_x)
    outer_blocks(place, True, g_full, hid[...], down_send, down_keep, down_over.start)
    gate_keep = RowBlocks(dh, width // 4)
    gate_over = copies.make(gate_send, gate_come, place.over_y)
    outer_blocks(place, False, m_full, dgate[...], gate_send, gate_keep, gate_over.start)
    gain_out[...] = jnp.zeros_like(gain_out)
    for k in range(CHUNKS):
        at = pl.ds(k * chunk, chunk)
        back = sum_two.take(k)
        res = res_out[at, :]
        root = lax.rsqrt(jnp.mean(res * res, axis=-1, keepdims=True) + eps_norm)
        weighted = back * gain_ref[...]
        slope = jnp.mean(weighted * res, axis=-1, keepdims=True)
        grad = g_full[at, :].astype(floats) + root * weighted - res * (root * root * root * slope)
        gain_out[...] += jnp.sum(back * res * root, axis=0, keepdims=True)
        gres_out[at, :] = grad
        e_full[at, :] = grad.astype(halves)
        gather_two.put(k)
    sum_two.finish()
    outer_blocks(place, True, m_full, dup[...], up_send, up_keep, lambda: None)

    def back_context(parts):
        grad = dot_nt(w_o[...], read(e_full, parts)).astype(halves)
        rows = grad.shape[1] // len(parts)
        for i, part in enumerate(parts):
            piece = grad[:, i * rows : (i + 1) * rows]
            dctx_out[:, part] = piece
            prod = piece.astype(floats) * ctx_ref[:, part].astype(floats)
            for hd in range(delta_out.shape[0]):
                delta_out[hd : hd + 1, part] = VSCALE * jnp.sum(
                    prod[hd * HEAD_WIDTH : (hd + 1) * HEAD_WIDTH], axis=0, keepdims=True
                )

    for copy in to_side:
        copy.wait()
    for k in range(CHUNKS):
        at = pl.ds(k * chunk, chunk)
        near = pl.ds(two + k * chunk, chunk)
        near_out[at, :] = (part_out[near, :].astype(floats) + far_in[at, :].astype(floats)).astype(halves)
        res_out[at, :] += part_out[at, :].astype(floats) + own_in[at, :].astype(floats)
    gather_two.wait_here()
    back_context(here)
    gather_two.wait_there(0, 2)
    back_context(there(0))
    down_over.wait()
    at = place.y
    down_half[...] = (down_keep[1 - at].astype(floats) + down_come[1 - at].astype(floats)).astype(halves)
    down_mine[...] = (down_keep[at].astype(floats) + down_come[at].astype(floats)).astype(halves)
    gather_two.wait_there(1, 2)
    back_context(there(1))
    gather_two.finish()
    for fetch in fetches:
        fetch.drain()
    gate_over.wait()
    at = place.x
    gate_half[...] = (gate_keep[1 - at].astype(floats) + gate_come[1 - at].astype(floats)).astype(halves)
    gate_mine[...] = (gate_keep[at].astype(floats) + gate_come[at].astype(floats)).astype(halves)


def middle(context_t, tokens, gain, grad_full, weights):
    q_cols, group = context_t.shape
    block, width = tokens.shape
    hidden = weights[2].shape[1]
    shape = jax.ShapeDtypeStruct
    out_shape = (
        shape((block, width), floats),
        shape((block, width), floats),
        shape((group, width), halves),
        shape((block, width), halves),
        *[shape((width // 4, hidden), halves)] * 4,
        *[shape((2, width // 4, hidden), halves)] * 2,
        shape((q_cols, group), halves),
        shape((q_cols // HEAD_WIDTH, group), floats),
        shape((1, width), floats),
    )
    scratch = [
        pltpu.VMEM((group, q_cols), halves),
        pltpu.VMEM((group, width), halves),
        *[pltpu.VMEM((group, hidden), halves)] * 4,
        *[pltpu.VMEM(weight.shape, halves) for weight in weights[:4]],
        *[pltpu.VMEM((2, width // 4, hidden), halves)] * 5,
        pltpu.VMEM((group, width), halves),
        *[pltpu.VMEM((block, width), halves)] * 2,
        *[pltpu.VMEM((block, width), floats)] * 2,
        *[pltpu.VMEM((block, width), halves)] * 6,
        *copy_semaphores(),
        pltpu.SemaphoreType.DMA((4,)),
    ]

    def kernel(*refs):
        mid_kernel(*refs[:4], refs[4:12], refs[12:25], refs[25:])

    return pl.pallas_call(
        kernel,
        out_shape=out_shape,
        in_specs=[VM] * 4 + [HB] * 8,
        out_specs=(VM,) * 13,
        scratch_shapes=scratch,
        compiler_params=pltpu.CompilerParams(
            collective_id=1, has_side_effects=True, vmem_limit_bytes=63 << 20
        ),
        name="middle",
    )(context_t, tokens, gain, grad_full, *weights)


def last_kernel(ins, outs, scratch):
    (counts, inverse_ref, dq_ref, dkv_ref, n_ref, joined_ref, tok_ref, gain_ref, gres_ref, e_ref, ctx_ref,
     gain_mlp_ref, *mlp) = ins
    (in_grad, gains_out, gate_out, up_out, down_out, q_out, kv_out, o_out) = outs
    (full, ctx, d_lin, acc_a, acc_b, own, x_in, y_in, rel_in, cross_in, cross_out, kept, come,
     gains, gains_in, cos_ref, sin_ref, joined, *rest) = scratch
    bufs_mlp = [rest[5 * i : 5 * i + 5] for i in range(3)]
    rest = rest[15:]
    bufs_attn = [rest[8 * i : 8 * i + 8] for i in range(3)]
    rest = rest[24:]
    sum_bufs, (ss, rs, lsem) = rest[:8], rest[8:]
    place = Place()
    copies = Copies(ss, rs)
    block, width = tok_ref.shape
    two = 2 * block
    q_cols = dq_ref.shape[0]
    kv_cols = own.shape[1] // 2
    half_width = HEAD_WIDTH // 2

    load_e = pltpu.make_async_copy(e_ref, full, lsem.at[0])
    load_e.start()
    load_joined = pltpu.make_async_copy(joined_ref, joined, lsem.at[11])
    load_joined.start()
    order = (4, 12, 0, 8)
    own_loads = [
        pltpu.make_async_copy(dkv_ref.at[at], own.at[i], lsem.at[1 + i]) for i, at in enumerate(order)
    ]
    y_loads = [
        pltpu.make_async_copy(dkv_ref.at[at + 2], y_in.at[i], lsem.at[5 + i])
        for i, at in enumerate(order)
    ]
    for copy in own_loads:
        copy.start()

    @pl.when(place.corner)
    def _():
        for copy in y_loads:
            copy.start()

    def load_mlp(i):
        return [
            pltpu.make_async_copy(mlp[2 * i], kept, lsem.at[9]),
            pltpu.make_async_copy(mlp[2 * i + 1], come, lsem.at[10]),
        ]

    down_loads = [
        pltpu.make_async_copy(mlp[i], bufs_mlp[0][1 + i], lsem.at[12 + i]) for i in range(2)
    ]
    gate_loads = [
        pltpu.make_async_copy(mlp[2 + i], bufs_mlp[1][1 + i], lsem.at[14 + i]) for i in range(2)
    ]
    loads = load_mlp(2)
    for copy in down_loads + gate_loads + loads:
        copy.start()
    gains[0, 0:1, :] = gain_mlp_ref[...]
    gains[0, 1:2, :] = jnp.zeros_like(gain_mlp_ref)
    meet((place.beside, place.near, place.far, place.cross, place.over_x, place.over_y))

    back_rel = [copies.make(dkv_ref.at[at + 3], rel_in.at[i], place.over_x) for i, at in enumerate(order)]
    back_x = [copies.make(dkv_ref.at[at + 1], x_in.at[i], place.over_x) for i, at in enumerate(order)]
    back_y = [copies.make(dkv_ref.at[at + 2], y_in.at[i], place.over_y) for i, at in enumerate(order)]
    back_sum = [copies.make(y_in.at[i], y_in.at[i], place.over_y) for i in range(4)]
    crossing = [copies.make(cross_out.at[i], cross_in.at[i], place.cross) for i in range(2)]
    def start_back(i):
        pl.when(place.turn)(back_rel[i].start)
        pl.when(place.x == 1)(back_x[i].start)
        pl.when(place.turn)(back_y[i].start)

    start_back(0)
    start_back(1)

    def corner_sum(i):
        @pl.when(place.corner)
        def _():
            back_rel[i].wait_recv()
            y_loads[i].wait()
            y_in[i] = (y_in[i].astype(floats) + rel_in[i].astype(floats)).astype(halves)
            back_sum[i].start()

    def home_sum(i, put):
        own_loads[i].wait()
        acc_b[...] = own[i].astype(floats)

        @pl.when(place.x == 0)
        def _():
            back_x[i].wait_recv()
            acc_b[...] += x_in[i].astype(floats)

        @pl.when((place.y == 0) & (place.x == 0))
        def _():
            back_y[i].wait_recv()
            acc_b[...] += y_in[i].astype(floats)

        @pl.when((place.y == 0) & (place.x == 1))
        def _():
            back_sum[i].wait_recv()
            acc_b[...] += y_in[i].astype(floats)

        put()

    sums = []
    for i, x_first in enumerate((True, False, True)):
        sums.append(PlaneSum(copies, place, x_first, bufs_mlp[i]))
    for copy in down_loads:
        copy.wait()
    sums[0].go_home(exchanged=False)
    corner_sum(0)
    for copy in loads:
        copy.wait()
    sums[2].cross_second(kept, come)
    start_back(2)
    start_back(3)
    ctx[...] = ctx_ref[...].T
    rope_tables(counts, inverse_ref, cos_ref, sin_ref)

    attn_sums = []
    for i, x_first in enumerate((False, True, False)):
        sent, keep, got = bufs_attn[i][:3]
        attn_sums.append(PlaneSum(copies, place, x_first, bufs_attn[i][3:], sent, got))

    def attn_grad(i, left, right):
        sent, keep, got = bufs_attn[i][:3]
        outer_blocks(place, attn_sums[i].x_first, left, right, sent, keep, attn_sums[i].one.start)

    corner_sum(1)
    load_e.wait()
    attn_grad(0, full, ctx[...])
    load_n = pltpu.make_async_copy(n_ref, full, lsem.at[0])
    load_n.start()

    def cross_back(i):
        def put():
            cross_out[i] = acc_b[...].astype(halves)
            crossing[i].start()

        home_sum(i, put)

    def unturn(value, at, first_row):
        low, high = value[:half_width], value[half_width:]
        cosine, sine = cos_ref[:, at], sin_ref[:, at]
        turned = jnp.concatenate([low * cosine + high * sine, high * cosine - low * sine], axis=0)
        d_lin[first_row : first_row + HEAD_WIDTH, at] = turned.astype(halves)

    cross_back(0)
    corner_sum(2)
    everything = slice(0, 2 * two)
    for head in range(q_cols // HEAD_WIDTH):
        unturn(dq_ref[head * HEAD_WIDTH : (head + 1) * HEAD_WIDTH, :], everything, head * HEAD_WIDTH)
    cross_back(1)
    corner_sum(3)
    load_n.wait()
    attn_grad(1, full, d_lin[:q_cols, :].T)
    for copy in gate_loads:
        copy.wait()
    sums[1].go_home(exchanged=False)
    sums[2].go_home()

    def second(i):
        sent, keep, got = bufs_attn[i][:3]
        attn_sums[i].cross_second(keep, got)

    second(0)

    def keep_a(k):
        def put():
            acc_a[:, k * two : (k + 1) * two] = acc_b[...]

        home_sum(2 + k, put)

    keep_a(0)
    keep_a(1)
    second(1)
    attn_sums[0].go_home()
    for k in range(2):
        crossing[k].wait_recv()
        lanes = slice(k * two, (k + 1) * two)
        total = acc_a[:, lanes] + cross_in[k].astype(floats)
        for head in range(kv_cols // HEAD_WIDTH):
            rows = slice(head * HEAD_WIDTH, (head + 1) * HEAD_WIDTH)
            unturn(total[rows], lanes, q_cols + head * HEAD_WIDTH)
        d_lin[q_cols + kv_cols :, lanes] = total[kv_cols:].astype(halves)

    group_sum = GroupSum(copies, sum_bufs, place)
    load_joined.wait()

    def back_norm(k, put):
        rows = slice(k * two, (k + 1) * two)
        left = d_lin[:, rows].T

        def one(cols):
            value = dot_nt(left, joined[cols, :])
            put(cols, value)
            gains[0, 1:2, cols] += jnp.sum(value * full[rows, cols].astype(floats), axis=0, keepdims=True)

        tiles(width, 256, one)

    group_sum.run(back_norm)
    gains[0, 1:2, :] = gains[0, 1:2, :] / gain_ref[...]
    attn_grad(2, full, d_lin[q_cols:, :].T)
    attn_sums[1].go_home()
    for stage, device in enumerate((place.beside, place.over_x, place.over_y, place.near, place.far)):
        copy = copies.make(gains.at[stage], gains_in.at[stage], device)
        copy.start()
        copy.wait()
        if stage < 4:
            gains[stage + 1] = gains[stage] + gains_in[stage]
        else:
            gains_out[...] = gains[stage] + gains_in[stage]
        if stage == 2:
            second(2)
    for plane, out in zip(sums, (down_out, gate_out, up_out)):
        plane.finish(out)
    attn_sums[2].go_home()
    chunk = block // CHUNKS
    for k in range(CHUNKS):
        at = pl.ds(k * chunk, chunk)
        back = group_sum.take(k)
        tok = tok_ref[at, :].astype(floats)
        root = lax.rsqrt(jnp.mean(tok * tok, axis=-1, keepdims=True) + eps_norm)
        weighted = back * gain_ref[...]
        slope = jnp.mean(weighted * tok, axis=-1, keepdims=True)
        in_grad[at, :] = gres_ref[at, :] + root * weighted - tok * (root * root * root * slope)
    for plane, out in zip(attn_sums, (o_out, q_out, kv_out)):
        plane.finish(out)
    group_sum.finish()
    for i in range(4):
        pl.when(place.turn)(back_rel[i].wait_send)
        pl.when(place.x == 1)(back_x[i].wait_send)
        pl.when(place.turn)(back_y[i].wait_send)
        pl.when(place.corner)(back_sum[i].wait_send)
    for copy in crossing:
        copy.wait_send()


def last_part(counts, inverse, d_query_t, d_kv, normed, joined, tokens, gain, gres, e_full, context_t, gain_mlp, mlp):
    block, width = tokens.shape
    group = 4 * block
    q_cols, kv_all = d_query_t.shape[0], d_kv.shape[1]
    kv_cols = kv_all // 2
    hidden = mlp[0].shape[1]
    per = width // 8
    shape = jax.ShapeDtypeStruct
    out_shape = (
        shape((block, width), floats),
        shape((2, width), floats),
        *[shape((per, hidden), floats)] * 3,
        shape((per, q_cols), floats),
        shape((per, kv_all), floats),
        shape((per, q_cols), floats),
    )
    piece = (kv_all, 2 * block)
    scratch = [
        pltpu.VMEM((group, width), halves),
        pltpu.VMEM((group, q_cols), halves),
        pltpu.VMEM((joined.shape[1], group), halves),
        pltpu.VMEM((kv_all, group), floats),
        pltpu.VMEM(piece, floats),
        *[pltpu.VMEM((4,) + piece, halves)] * 4,
        *[pltpu.VMEM((2,) + piece, halves)] * 2,
        *[pltpu.VMEM((2, width // 4, hidden), halves)] * 2,
        *[pltpu.VMEM((5, 2, width), floats)] * 2,
        *[pltpu.VMEM((HEAD_WIDTH // 2, group), floats)] * 2,
        pltpu.VMEM(joined.shape, halves),
    ]
    for _ in range(3):
        scratch += plane_buffers(width // 4, hidden)
    for cols in (q_cols, q_cols, kv_all):
        scratch += [pltpu.VMEM((2, width // 4, cols), halves)] * 3 + plane_buffers(width // 4, cols)
    scratch += [
        *[pltpu.VMEM((block, width), floats)] * 2,
        *[pltpu.VMEM((block, width), halves)] * 6,
        *copy_semaphores(),
        pltpu.SemaphoreType.DMA((16,)),
    ]

    def kernel(*refs):
        last_kernel(refs[:18], refs[18:26], refs[26:])

    return pl.pallas_call(
        kernel,
        out_shape=out_shape,
        in_specs=[SM, VM, VM, HM, HM, HM, VM, VM, VM, HM, VM, VM] + [HM] * 6,
        out_specs=(VM,) * 8,
        scratch_shapes=scratch,
        compiler_params=pltpu.CompilerParams(
            collective_id=3, has_side_effects=True, vmem_limit_bytes=63 << 20
        ),
        name="last",
    )(counts, inverse, d_query_t, d_kv, normed, joined, tokens, gain, gres, e_full, context_t, gain_mlp, *mlp)


def finish_kernel(*refs):
    sources = refs[:9]
    output, k_out, v_out, *outs = refs[9:18]
    out_buf, k_buf, v_buf, sem, load_sem = refs[18:23]
    base, near, kv_sum, *ready = refs[23:]
    loads = [
        pltpu.make_async_copy(src, dst, load_sem.at[i])
        for i, (src, dst) in enumerate(zip(sources, refs[23:]))
    ]
    for load in loads:
        load.start()
    copies = [pltpu.make_async_copy(src, dst, sem.at[i]) for i, (src, dst) in enumerate(zip(ready, outs))]
    for load, copy in zip(loads[3:], copies):
        load.wait()
        copy.start()
    for load in loads[:3]:
        load.wait()
    out_buf[...] = (base[...] + near[...].astype(floats)).astype(halves)
    kv_cols = k_buf.shape[1]
    k_buf[...] = kv_sum[:, :kv_cols]
    v_buf[...] = kv_sum[:, kv_cols:]
    more = [
        pltpu.make_async_copy(src, dst, sem.at[len(copies) + i])
        for i, (src, dst) in enumerate(((out_buf, output), (k_buf, k_out), (v_buf, v_out)))
    ]
    for copy in more:
        copy.start()
    for copy in copies + more:
        copy.wait()


def finish(base, near, kv_sum, *ready):
    shape = jax.ShapeDtypeStruct
    rows, cols = kv_sum.shape
    small = (rows, cols // 2)
    return pl.pallas_call(
        finish_kernel,
        out_shape=(
            shape(base.shape, halves),
            shape(small, floats),
            shape(small, floats),
            *[shape(a.shape, a.dtype) for a in ready],
        ),
        in_specs=[HM] * (3 + len(ready)),
        out_specs=(HM,) * (3 + len(ready)),
        scratch_shapes=[
            pltpu.VMEM(base.shape, halves),
            pltpu.VMEM(small, floats),
            pltpu.VMEM(small, floats),
            pltpu.SemaphoreType.DMA((3 + len(ready),)),
            pltpu.SemaphoreType.DMA((3 + len(ready),)),
            *[pltpu.VMEM(a.shape, a.dtype) for a in (base, near, kv_sum, *ready)],
        ],
        compiler_params=pltpu.CompilerParams(vmem_limit_bytes=63 << 20),
        name="finish",
    )(base, near, kv_sum, *ready)


def routes(target):
    pairs = []
    for index in range(32):
        dp, z = divmod(index, 4)
        there = target(dp // 4, dp // 2 % 2, dp % 2, z)
        if there is not None:
            y, x, c, z = there
            pairs.append((index, (y * 4 + x * 2 + c) * 4 + z))
    return pairs


ROUTES = {
    "core": routes(lambda y, x, c, z: (y, x, 1 - c, z)),
    "x": routes(lambda y, x, c, z: (y, 1 - x, c, z)),
    "y": routes(lambda y, x, c, z: (1 - y, x, c, z)),
    "near": routes(lambda y, x, c, z: (y, x, c, z ^ 1)),
    "far": routes(lambda y, x, c, z: (y, x, c, z ^ 2)),
    "cross": routes(lambda y, x, c, z: (y, x, 1 - c, z ^ 2)),
    "odd_far": routes(lambda y, x, c, z: (y, x, c, z ^ 2) if c else None),
    "odd_x": routes(lambda y, x, c, z: (y, 1 - x, c, z) if c else None),
    "odd_y": routes(lambda y, x, c, z: (1 - y, x, c, z) if c else None),
    "odd_xy": routes(lambda y, x, c, z: (1 - y, 1 - x, c, z) if c else None),
    "home": routes(lambda y, x, c, z: (y, x, 0, z ^ 2) if c else (y, x, 1, z)),
    "x_up": routes(lambda y, x, c, z: None if x else (y, 1, c, z)),
    "y_up": routes(lambda y, x, c, z: None if y else (1, x, c, z)),
    "x_down": routes(lambda y, x, c, z: (y, 0, c, z) if x else None),
    "y_down": routes(lambda y, x, c, z: (0, x, c, z) if y else None),
    "relay": routes(lambda y, x, c, z: (1, 0, c, z) if x and y else None),
    "unrelay": routes(lambda y, x, c, z: (1, 1, c, z) if y and not x else None),
}


def send(block, way):
    return lax.ppermute(block, ("dp", "tp"), ROUTES[way])


def local_regrouped(
    tokens,
    out_grad,
    segment_ids,
    attn_gain,
    query_weight,
    key_matrix,
    value_matrix,
    output_weight,
    mlp_gain,
    gate_weight,
    up_weight,
    down_weight,
):
    block = tokens.shape[0]
    dp = lax.axis_index("dp")
    half_width = HEAD_WIDTH // 2
    gain_attn, gain_mlp = attn_gain.astype(floats)[None, :], mlp_gain.astype(floats)[None, :]
    counts = jnp.sum(
        (segment_ids[None, :] < jnp.arange(1, 4, dtype=jnp.int32)[:, None]).astype(jnp.int32), axis=1
    )
    inverse = 1.0 / rope_base ** (jnp.arange(half_width, dtype=floats) * 2.0 / HEAD_WIDTH)
    inverse = inverse[:, None]
    q_t, pieces, normed_full, grad_full, joined, weight_o, weight_d, slice_g, slice_u = first_part(
        counts, inverse, tokens, out_grad, gain_attn,
        (query_weight, key_matrix.T, value_matrix.T),
        (output_weight, down_weight, gate_weight, up_weight),
    )
    slices = [send(part, "odd_far") for part in (slice_g, slice_u)]
    context_t, log_total = attend_forward(counts, q_t, pieces)
    (
        out_base, grad_residual, attn_grad_full, out_near, down_half, down_mine, gate_half, gate_mine,
        up_keep, up_send, d_context_t, delta, mlp_gain_part,
    ) = middle(
        context_t, tokens, gain_mlp, grad_full,
        (output_weight, down_weight, gate_weight, up_weight, weight_o, weight_d, *slices),
    )
    gate_come = send(gate_half, "x")
    up_come = send(up_send, "x")
    down_come = send(down_half, "y")
    out_near = send(out_near, "near")
    d_query_t, d_pieces = attend_backward(counts, q_t, d_context_t, log_total, delta, pieces)
    input_grad, gains, gate_sum, up_sum, down_sum, query_sum, kv_sum, output_sum = last_part(
        counts, inverse, d_query_t, d_pieces, normed_full, joined, tokens, gain_attn,
        grad_residual, attn_grad_full, context_t, mlp_gain_part,
        (down_mine, down_come, gate_mine, gate_come, up_keep, up_come),
    )
    per = gains.shape[1] // 8
    gains = lax.dynamic_slice_in_dim(gains, dp * per, per, axis=1)
    output, key_sum, value_sum, input_grad, query_sum, output_sum, gate_sum, up_sum, down_sum = finish(
        out_base, out_near, kv_sum, input_grad, query_sum, output_sum, gate_sum, up_sum, down_sum
    )
    return (
        output,
        input_grad,
        gains[1],
        query_sum,
        key_sum,
        value_sum,
        output_sum.T,
        gains[0],
        gate_sum,
        up_sum,
        down_sum.T,
    )


def solution(mesh):
    regroup = mesh.shape["dp"] == 8 and mesh.shape["tp"] == 4
    chosen = local_regrouped if regroup else local
    return jax.shard_map(
        chosen,
        mesh=mesh,
        in_specs=(
            P(("dp", "tp"), None),
            P(("dp", "tp"), None),
            P(),
            P(),
            P(None, "tp"),
            P(None, "tp"),
            P(None, "tp"),
            P("tp", None),
            P(),
            P(None, "tp"),
            P(None, "tp"),
            P("tp", None),
        ),
        out_specs=(
            P(("dp", "tp"), None),
            P(("dp", "tp"), None),
            P("dp"),
            P("dp", "tp"),
            P("dp", "tp"),
            P("dp", "tp"),
            P("tp", "dp"),
            P("dp"),
            P("dp", "tp"),
            P("dp", "tp"),
            P("tp", "dp"),
        ),
        check_vma=False,
    )
```
